32 devices in a mesh: ctx: 8 (over y, x, core), ch: 4 (over z).
Axes of the slice: x: 2, y: 2, z: 4, core: 2. Of those that a mesh axis runs over, the one named last changes fastest.
Arguments:
- queries: bfloat16 [1024, 8192], P('ctx', 'ch'), may hold values from -6 to 6
- key_input: bfloat16 [1024, 8192], P('ctx', 'ch'), may hold values from -6 to 6
- value_input: bfloat16 [1024, 8192], P('ctx', 'ch'), may hold values from -6 to 6
- cotangent: bfloat16 [1024, 8192], P('ctx', 'ch'), may hold values from -60 to 60, as said below
- residues: float32 [512, 16], replicated, may hold values from -1 to 1
- log_rates: float32 [512, 16], replicated, may hold values from -14 to -3
- skip_gain: float32 [8192], replicated, may hold values from -1 to 1
Outputs:
- grad_query: bfloat16 [1024, 8192], P('ctx', 'ch')
- grad_key: bfloat16 [1024, 8192], P('ctx', 'ch')
- grad_value: bfloat16 [1024, 8192], P('ctx', 'ch')
- grad_residue: float32 [512, 16], replicated
- grad_lograte: float32 [512, 16], replicated
- grad_skip: float32 [8192], replicated
The draws below stay inside these ranges and needn't reach their ends.
Inputs may be any that keep to these rules, and one draw needn't show every extreme that they name: Every row of the cotangent has its own scale.
All inputs are finite; a program needn't handle non-finite values.
Results may differ from the reference program's by a relative error of at most 0.017.
Values may be sent and summed in bfloat16 or wider, within the bound.
No kernel may reach another device: no remote copies, remote signals or barrier semaphores. Data moves between devices by JAX's collectives and lax.ppermute only.
A program may use at most 64 MiB of HBM per device.

```python
import math
import jax
import jax.numpy as jnp
from jax import lax

D = 8192
GROUP = 16
POLES = 16
TOKENS = 1024
GROUPS = 512


def pole_logs(key):
    base = jax.random.fold_in(key, 7)
    pick_key, slow_key, middle_key, fast_key = jax.random.split(base, 4)
    length = float(TOKENS)
    shape = (GROUPS, POLES)
    slow_share = 0.5
    middle_cut = 0.75
    fast_low = math.log(1.0 / 50.0)
    fast_high = math.log(1.0 / 30.0)
    slow_low = math.log(0.2 / length)
    slow_high = min(math.log(2.0 / length), fast_high)
    middle_low = min(math.log(2.0 / length), fast_low)
    choose = jax.random.uniform(pick_key, shape)
    slow = jax.random.uniform(slow_key, shape, minval=slow_low, maxval=slow_high)
    middle = jax.random.uniform(middle_key, shape, minval=middle_low, maxval=fast_low)
    fast = jax.random.uniform(fast_key, shape, minval=fast_low, maxval=fast_high)
    return jnp.where(choose < slow_share, slow, jnp.where(choose < middle_cut, middle, fast))


def draw_log_rates(key, part):
    return pole_logs(key).astype(jnp.float32)


def draw_residues(key, part):
    decay_rate = jnp.exp(pole_logs(key))
    noise_key = jax.random.fold_in(key, 8)
    shape = (GROUPS, POLES)
    noise = jnp.clip(jax.random.normal(noise_key, shape), -4.0, 4.0)
    return (noise * 0.3 * jnp.sqrt(2.0 * decay_rate)).astype(jnp.float32)


def draw_cotangent(key, part):
    noise_key = jax.random.fold_in(jax.random.fold_in(key, 9), 0)
    shape = (TOKENS, D)
    fraction = jnp.arange(TOKENS).astype(jnp.float32) / float(TOKENS)
    noise = jnp.clip(jax.random.normal(noise_key, shape), -5.0, 5.0)
    row_scale = 1.0 + 2.0 * fraction
    return (noise * row_scale[:, None]).astype(jnp.bfloat16)


def shard_levels(rng, dims, cuts, smallest, largest):
    gain = 1.0
    for position, blocks in cuts:
        steps = jax.random.uniform(jax.random.fold_in(jax.random.fold_in(rng, 6), position), (blocks,), jnp.float32, smallest / len(cuts), largest / len(cuts))
        gain = gain * jnp.repeat(jnp.exp(steps), dims[position] // blocks).reshape((-1,) + (1,) * (len(dims) - 1 - position))
    return gain


def centred(own_key, dims, deviation, most, shards=(), kind=jnp.bfloat16):
    result = jax.random.normal(own_key, dims, jnp.float32) * deviation
    if len(shards) > 0:
        result = shard_levels(own_key, dims, shards, -0.22, 0.18) * result
    return jnp.clip(result, min=-most, max=most).astype(kind)


def setup_inputs(seed: int = 0) -> dict:
    key_of = jax.random.split(jax.random.key(seed), 8)
    return {
        "queries": centred(key_of[0], (TOKENS, D), 1.0, 6.0, ((0, 8), (1, 4))),
        "key_input": centred(key_of[1], (TOKENS, D), 1.0, 6.0, ((0, 8), (1, 4))),
        "value_input": centred(key_of[2], (TOKENS, D), 1.0, 6.0, ((0, 8), (1, 4))),
        "cotangent": draw_cotangent(jax.random.fold_in(key_of[7], 71), 0),
        "residues": draw_residues(jax.random.fold_in(key_of[7], 71), 0),
        "log_rates": draw_log_rates(jax.random.fold_in(key_of[7], 71), 0),
        "skip_gain": jnp.clip(jax.random.uniform(key_of[6], (D,), jnp.float32, -1.0, 1.0), -1.0, 1.0),
    }


def reference(queries, key_input, value_input, cotangent, residues, log_rates, skip_gain):
    length = TOKENS
    padded = 2 * length
    groups = D // GROUP
    gated = (key_input.astype(jnp.float32) * value_input.astype(jnp.float32)).astype(jnp.bfloat16)
    dgate = (cotangent.astype(jnp.float32) * queries.astype(jnp.float32)).astype(jnp.bfloat16)
    decay_rate = jnp.exp(log_rates)
    positions = jnp.arange(length).astype(jnp.float32)
    gated_groups = gated.astype(jnp.float32).reshape(length, groups, GROUP).transpose(1, 2, 0)
    dgate_groups = dgate.astype(jnp.float32).reshape(length, groups, GROUP).transpose(1, 2, 0)

    def one_group(member):
        gated_one, dgate_one, residue_one, rate_one = member
        decays = jnp.exp(-rate_one[:, None] * positions[None, :])
        filter_taps = lax.optimization_barrier(jnp.sum(residue_one[:, None] * decays, axis=0))
        filter_spec = jnp.fft.rfft(filter_taps, n=padded)
        gated_spec = jnp.fft.rfft(gated_one, n=padded, axis=1)
        dgate_spec = jnp.fft.rfft(dgate_one, n=padded, axis=1)
        conv_z = jnp.fft.irfft(filter_spec[None, :] * gated_spec, n=padded, axis=1)[:, :length]
        conv_flow = jnp.fft.irfft(jnp.conj(filter_spec)[None, :] * dgate_spec, n=padded, axis=1)[:, :length]
        cross_spec = lax.optimization_barrier(jnp.sum(jnp.conj(gated_spec) * dgate_spec, axis=0))
        filter_grad = jnp.fft.irfft(cross_spec, n=padded)[:length].astype(jnp.float32)
        grad_res = jnp.dot(decays, filter_grad, precision=lax.Precision.HIGHEST)
        grad_log = -rate_one * residue_one * jnp.dot(decays * positions[None, :], filter_grad, precision=lax.Precision.HIGHEST)
        return (conv_z.astype(jnp.float32), conv_flow.astype(jnp.float32), grad_res, grad_log)
    conv_z, conv_flow, grad_res, grad_log = lax.map(one_group, (gated_groups, dgate_groups, residues, decay_rate))
    conv_z = conv_z.transpose(2, 0, 1).reshape(length, D)
    conv_flow = conv_flow.transpose(2, 0, 1).reshape(length, D)
    hidden_z = (skip_gain[None, :] * gated.astype(jnp.float32) + conv_z).astype(jnp.bfloat16)
    flow = (skip_gain[None, :] * dgate.astype(jnp.float32) + conv_flow).astype(jnp.bfloat16)
    grad_query = (cotangent.astype(jnp.float32) * hidden_z.astype(jnp.float32)).astype(jnp.bfloat16)
    grad_key = (flow.astype(jnp.float32) * value_input.astype(jnp.float32)).astype(jnp.bfloat16)
    grad_value = (flow.astype(jnp.float32) * key_input.astype(jnp.float32)).astype(jnp.bfloat16)
    grad_skip = lax.optimization_barrier(jnp.sum(dgate.astype(jnp.float32) * gated.astype(jnp.float32), axis=0)) / math.sqrt(length)
    return (grad_query, grad_key, grad_value, grad_res / length, grad_log / math.sqrt(length), grad_skip)
```

```python
import math

import jax
import jax.numpy as jnp
from jax import lax
from jax.experimental import pallas as pl
from jax.experimental.pallas import tpu as pltpu
from jax.sharding import PartitionSpec as P

LANES = 128
F32 = jnp.float32
BF16 = jnp.bfloat16
EXACT = lax.Precision.HIGHEST
VMEM_LIMIT = 48 * 1024 * 1024


def iota(shape, axis):
    return lax.broadcasted_iota(jnp.int32, shape, axis)


def mxu(left, right):
    return jnp.dot(left, right, preferred_element_type=F32)


def exact_dot(left, right):
    return jnp.dot(left, right, precision=EXACT, preferred_element_type=F32)


def gate(left, right):
    return (left.astype(F32) * right.astype(F32)).astype(BF16)


def reversal(size):
    return jnp.where(iota((size, size), 0) + iota((size, size), 1) == size - 1, 1.0, 0.0).astype(BF16)


def split_pair(value):
    high = value.astype(BF16).astype(F32)
    return high, value - high


def flat_rows(table, poles):
    groups = table.shape[0]
    per_row = LANES // poles
    spread = jnp.where(iota((poles, LANES), 0) == iota((poles, LANES), 1) % poles, 1.0, 0.0)
    wide = exact_dot(table, spread)
    keep = iota((groups, LANES), 0) % per_row == iota((groups, LANES), 1) // poles
    wide = jnp.where(keep, wide, 0.0)
    return jnp.sum(wide.reshape(groups // per_row, per_row, LANES), axis=1)


def states_kernel(logs_ref, res_ref, q_ref, k_ref, v_ref, c_ref, send_ref, pair_ref, rows_ref, *, group, poles):
    tokens, width = q_ref.shape
    per_block = LANES // group
    shard_groups = rows_ref.shape[1] * per_block
    owners, _, own_width = send_ref.shape
    step = pl.program_id(0)
    blocks = width // LANES

    @pl.when(step == 0)
    def _():
        first = lax.axis_index("ch") * shard_groups
        rows_ref[0] = jnp.exp(flat_rows(logs_ref[pl.ds(first, shard_groups), :], poles))
        rows_ref[1] = flat_rows(res_ref[pl.ds(first, shard_groups), :], poles)

    flip = reversal(tokens)
    back_pos = (tokens - 1 - iota((tokens, LANES), 0)).astype(F32)
    back_lane = (tokens - 1 - iota((per_block, tokens), 1)).astype(F32)
    lane_group = iota((tokens, LANES), 1) // group
    causal = iota((tokens, tokens), 0) + iota((tokens, tokens), 1) <= tokens - 1
    wide_group = (iota((poles, 2 * LANES), 1) % LANES) // group
    half = per_block // 2
    own_rows = iota((per_block, LANES), 0) == iota((per_block, LANES), 1) // poles
    zero = jnp.zeros((tokens, LANES), BF16)

    for j in range(blocks):
        cut = slice(j * LANES, (j + 1) * LANES)
        gated = gate(k_ref[:, cut], v_ref[:, cut])
        dgate = gate(c_ref[:, cut], q_ref[:, cut])
        skip = jnp.sum(gated.astype(F32) * dgate.astype(F32), axis=0, keepdims=True)
        turned = mxu(flip, dgate).astype(BF16)
        pair = jnp.concatenate([gated, turned], axis=1)
        pair_ref[:, 2 * j * LANES : 2 * (j + 1) * LANES] = pair
        rate = rows_ref[0, pl.ds(step * blocks + j, 1), :]
        table = jnp.exp(-rate * back_pos)
        table_low = table.astype(BF16)
        both = jnp.concatenate([table.T.astype(BF16), (table * back_pos).T.astype(BF16)], axis=0)
        summed = mxu(both, pair)
        folded = []
        for part in range(2):
            total = jnp.zeros((poles, 2 * LANES), F32)
            for g in range(per_block):
                start = part * LANES + g * poles
                total = jnp.where(wide_group == g, summed[start : start + poles], total)
            folded.append(total)
        left = [
            jnp.where((lane_group == i) | (lane_group == i + half), turned, zero) for i in range(half)
        ]
        right = [
            jnp.where(lane_group < half, gated, zero),
            jnp.where(lane_group >= half, gated, zero),
        ]
        outer = lax.dot_general(
            jnp.concatenate(left, axis=0),
            jnp.concatenate(right, axis=0),
            (((1,), (1,)), ((), ())),
            preferred_element_type=F32,
        )
        lags = []
        for h in range(2):
            for i in range(half):
                tile = outer[i * tokens : (i + 1) * tokens, h * tokens : (h + 1) * tokens]
                tile = jnp.where(causal, tile, 0.0)
                total = tile[:8]
                for a in range(1, tokens // 8):
                    total = total + pltpu.roll(tile[8 * a : 8 * a + 8], 8 * a, 1)
                total = pltpu.roll(total, 0, 1, stride=1, stride_axis=0)
                lags.append(jnp.sum(total, axis=0, keepdims=True))
        lag = jnp.concatenate(lags, axis=0)
        lag_high, lag_low = split_pair(lag)
        mom_high, mom_low = split_pair(lag * back_lane)
        stack = jnp.concatenate([lag_high, lag_low, mom_high, mom_low], axis=0).astype(BF16)
        local = mxu(stack, table_low)
        res_part = local[:per_block] + local[per_block : 2 * per_block]
        mom_part = local[2 * per_block : 3 * per_block] + local[3 * per_block :]
        res_row = jnp.sum(jnp.where(own_rows, res_part, 0.0), axis=0, keepdims=True)
        mom_row = jnp.sum(jnp.where(own_rows, mom_part, 0.0), axis=0, keepdims=True)
        extra = jnp.concatenate(
            [*split_pair(res_row), *split_pair(mom_row), *split_pair(skip), jnp.zeros((10, LANES), F32)],
            axis=0,
        )
        out = jnp.concatenate(
            [
                folded[0][:, :LANES],
                folded[0][:, LANES:],
                folded[1][:, :LANES],
                folded[1][:, LANES:],
                extra,
            ],
            axis=0,
        ).astype(BF16)
        if own_width >= LANES:
            place = j * LANES // own_width
            offset = j * LANES % own_width
            send_ref[place, :, offset : offset + LANES] = out
        else:
            for n in range(LANES // own_width):
                send_ref[j * (LANES // own_width) + n] = out[:, n * own_width : (n + 1) * own_width]


def conv_kernel(rows_ref, skip_ref, pair_ref, conv_ref, *, group, poles):
    tokens, width = pair_ref.shape
    per_block = LANES // group
    step = pl.program_id(0)
    blocks = width // (2 * LANES)
    all_blocks = rows_ref.shape[1]
    first = lax.axis_index("ch") * all_blocks
    back_pos = (tokens - 1 - iota((tokens, LANES), 0)).astype(F32)
    wide_group = (iota((tokens, 2 * LANES), 1) % LANES) // group
    causal = iota((tokens, tokens), 0) >= iota((tokens, tokens), 1)
    for j in range(blocks):
        cut = slice(2 * j * LANES, 2 * (j + 1) * LANES)
        pair = pair_ref[:, cut]
        here = step * blocks + j
        rate = rows_ref[0, pl.ds(here, 1), :]
        res = rows_ref[1, pl.ds(here, 1), :]
        table = (res * jnp.exp(-rate * back_pos)).T
        left, right = [], []
        for g in range(per_block):
            taps = jnp.sum(table[g * poles : (g + 1) * poles], axis=0, keepdims=True)
            base = pltpu.roll(jnp.broadcast_to(taps, (8, tokens)), 1, 1, stride=1, stride_axis=0)
            rolled = [base] + [pltpu.roll(base, 8 * a, 1) for a in range(1, tokens // 8)]
            left.append(jnp.where(causal, jnp.concatenate(rolled, axis=0), 0.0).astype(BF16))
            right.append(jnp.where(wide_group == g, pair, jnp.zeros_like(pair)))
        total = mxu(jnp.concatenate(left, axis=1), jnp.concatenate(right, axis=0))
        gain = skip_ref[pl.ds(first + here, 1), :]
        conv_ref[:, cut] = total + jnp.concatenate([gain, gain], axis=1) * pair.astype(F32)


def scan_kernel(logs_ref, res_ref, got_ref, back_ref, grad_ref, *, group, poles, tokens, first_of):
    parts, _, width = got_ref.shape
    groups = width // group
    first = first_of(groups)
    scale = tokens * parts
    spread = jnp.where(iota((poles, width), 0) == iota((poles, width), 1) % poles, 1.0, 0.0)
    keep = iota((groups, width), 0) == iota((groups, width), 1) // poles
    pick = iota((poles, width), 0) == iota((poles, width), 1) % poles
    same = jnp.where(iota((width, width), 0) // group == iota((width, width), 1) // group, 1.0, 0.0)

    def flat(ref):
        wide = exact_dot(ref[pl.ds(first, groups), :], spread)
        return jnp.sum(jnp.where(keep, wide, 0.0), axis=0, keepdims=True)

    rate = jnp.exp(flat(logs_ref))
    res = flat(res_ref)
    rates = exact_dot(jnp.where(pick, rate, 0.0), same)
    decay = jnp.exp(-rates * tokens)
    one = jnp.exp(-rates)

    def rows(i, n):
        return got_ref[i, n * poles : (n + 1) * poles, :].astype(F32)

    zeros = jnp.zeros((poles, width), F32)
    state, moment, sum_res, sum_mom = zeros, zeros, zeros, zeros
    extra = jnp.zeros((16, width), F32)
    for i in range(parts):
        back_ref[i, :poles, :] = state.astype(BF16)
        begin = rows(i, 1)
        sum_res += begin * state
        sum_mom += rows(i, 3) * state + begin * moment
        ahead = rows(i, 0)
        moment = decay * (moment + tokens * state) + rows(i, 2) + ahead
        state = decay * state + ahead
        extra += got_ref[i, 4 * poles :, :].astype(F32)
    state = zeros
    for i in reversed(range(parts)):
        back_ref[i, poles:, :] = state.astype(BF16)
        state = decay * state + rows(i, 1)

    def gather(total, high, low):
        wide = exact_dot(total * one, same)
        return jnp.sum(jnp.where(pick, wide, 0.0), axis=0, keepdims=True) + high + low

    grad_res = gather(sum_res, extra[0:1], extra[1:2]) / scale
    grad_log = -rate * res * gather(sum_mom, extra[2:3], extra[3:4]) / math.sqrt(scale)
    grad_skip = (extra[4:5] + extra[5:6]) / math.sqrt(scale)
    grad_ref[...] = jnp.concatenate(
        [grad_res, grad_log, grad_skip, jnp.zeros((5, width), F32)], axis=0
    )


def output_kernel(rows_ref, conv_ref, back_ref, k_ref, v_ref, c_ref, gq_ref, gk_ref, gv_ref, *, group, poles):
    tokens, width = k_ref.shape
    per_block = LANES // group
    own_width = back_ref.shape[2]
    step = pl.program_id(0)
    blocks = width // LANES
    flip = reversal(tokens)
    ahead = (1 + iota((tokens, LANES), 0)).astype(F32)
    wide_group = (iota((poles, 2 * LANES), 1) % LANES) // group
    for j in range(blocks):
        cut = slice(j * LANES, (j + 1) * LANES)
        here = step * blocks + j
        rate = rows_ref[0, pl.ds(here, 1), :]
        res = rows_ref[1, pl.ds(here, 1), :]
        table = (res * jnp.exp(-rate * ahead)).astype(BF16)
        if own_width >= LANES:
            place, offset = j * LANES // own_width, j * LANES % own_width
            states = back_ref[place, :, offset : offset + LANES]
        else:
            count = LANES // own_width
            states = jnp.concatenate([back_ref[j * count + n] for n in range(count)], axis=1)
        states = jnp.concatenate([states[:poles], states[poles:]], axis=1)
        stack = jnp.concatenate(
            [jnp.where(wide_group == g, states, jnp.zeros_like(states)) for g in range(per_block)], axis=0
        )
        total = (conv_ref[:, 2 * j * LANES : 2 * (j + 1) * LANES] + mxu(table, stack)).astype(BF16)
        flow = mxu(flip, total[:, LANES:])
        gq_ref[:, cut] = (c_ref[:, cut].astype(F32) * total[:, :LANES].astype(F32)).astype(BF16)
        gk_ref[:, cut] = (flow * v_ref[:, cut].astype(F32)).astype(BF16)
        gv_ref[:, cut] = (flow * k_ref[:, cut].astype(F32)).astype(BF16)


def local(queries, key_input, value_input, cotangent, residues, log_rates, skip_gain):
    tokens, width = queries.shape
    parts = lax.axis_size("ctx")
    shards = lax.axis_size("ch")
    all_groups, poles = residues.shape
    group = width * shards // all_groups
    own_width = width // parts
    step_width = min(width, max(4 * LANES, own_width))
    steps = width // step_width
    blocks = width // LANES
    payload = 4 * poles + 16
    owners = step_width // own_width
    sizes = dict(group=group, poles=poles)
    params = pltpu.CompilerParams(vmem_limit_bytes=VMEM_LIMIT)

    whole = pl.BlockSpec((all_groups, poles), lambda i: (0, 0))
    main = pl.BlockSpec((tokens, step_width), lambda i: (0, i))
    twice = pl.BlockSpec((tokens, 2 * step_width), lambda i: (0, i))
    row_table = pl.BlockSpec((2, blocks, LANES), lambda i: (0, 0, 0))

    send, pair, rows = pl.pallas_call(
        lambda *refs: states_kernel(*refs, **sizes),
        grid=(steps,),
        in_specs=[whole, whole, main, main, main, main],
        out_specs=[
            pl.BlockSpec((owners, payload, own_width), lambda i: (i, 0, 0)),
            twice,
            row_table,
        ],
        out_shape=[
            jax.ShapeDtypeStruct((parts, payload, own_width), BF16),
            jax.ShapeDtypeStruct((tokens, 2 * width), BF16),
            jax.ShapeDtypeStruct((2, blocks, LANES), F32),
        ],
        compiler_params=params,
        name="states",
    )(log_rates, residues, queries, key_input, value_input, cotangent)

    got = lax.all_to_all(send, "ctx", split_axis=0, concat_axis=0, tiled=True)

    skip_rows = skip_gain.reshape(-1, LANES)
    conv = pl.pallas_call(
        lambda *refs: conv_kernel(*refs, **sizes),
        grid=(steps,),
        in_specs=[row_table, pl.BlockSpec(skip_rows.shape, lambda i: (0, 0)), twice],
        out_specs=twice,
        out_shape=jax.ShapeDtypeStruct((tokens, 2 * width), F32),
        compiler_params=params,
        cost_estimate=pl.CostEstimate(
            flops=16 * tokens * tokens * width, bytes_accessed=12 * tokens * width, transcendentals=tokens * width
        ),
        name="conv",
    )(rows, skip_rows, pair)

    def first_of(groups):
        return (lax.axis_index("ch") * parts + lax.axis_index("ctx")) * groups

    vmem = pl.BlockSpec(memory_space=pltpu.VMEM)
    back, grads = pl.pallas_call(
        lambda *refs: scan_kernel(*refs, tokens=tokens, first_of=first_of, **sizes),
        in_specs=[vmem, vmem, vmem],
        out_specs=[vmem, vmem],
        out_shape=[
            jax.ShapeDtypeStruct((parts, 2 * poles, own_width), BF16),
            jax.ShapeDtypeStruct((8, own_width), F32),
        ],
        compiler_params=params,
        name="scan",
    )(log_rates, residues, got)

    states = lax.all_to_all(back, "ctx", split_axis=0, concat_axis=0, tiled=True)
    spread = jnp.broadcast_to(grads[None], (parts * shards, 8, own_width))
    final = lax.all_to_all(spread, ("ctx", "ch"), split_axis=0, concat_axis=0, tiled=True)

    grad_query, grad_key, grad_value = pl.pallas_call(
        lambda *refs: output_kernel(*refs, **sizes),
        grid=(steps,),
        in_specs=[
            row_table,
            twice,
            pl.BlockSpec((owners, 2 * poles, own_width), lambda i: (i, 0, 0)),
            main,
            main,
            main,
        ],
        out_specs=[main, main, main],
        out_shape=[jax.ShapeDtypeStruct((tokens, width), BF16)] * 3,
        compiler_params=params,
        name="outputs",
    )(rows, conv, states, key_input, value_input, cotangent)

    final = final.reshape(parts, shards, 8, own_width).transpose(2, 1, 0, 3)
    grad_residue = final[0].reshape(all_groups, poles)
    grad_lograte = final[1].reshape(all_groups, poles)
    grad_skip = final[2].reshape(-1)
    return (grad_query, grad_key, grad_value, grad_residue, grad_lograte, grad_skip)


def solution(mesh):
    placed = (P("ctx", "ch"), P("ctx", "ch"), P("ctx", "ch"), P("ctx", "ch"), P(), P(), P())
    return jax.shard_map(
        local,
        mesh=mesh,
        in_specs=placed,
        out_specs=(P("ctx", "ch"), P("ctx", "ch"), P("ctx", "ch"), P(), P(), P()),
        check_vma=False,
    )
```

```python
import math

import jax
import jax.numpy as jnp
from jax import lax
from jax.experimental import pallas as pl
from jax.experimental.pallas import tpu as pltpu
from jax.sharding import PartitionSpec as P

LANES = 128
F32 = jnp.float32
BF16 = jnp.bfloat16
EXACT = lax.Precision.HIGHEST
VMEM_LIMIT = 48 * 1024 * 1024


def iota(shape, axis):
    return lax.broadcasted_iota(jnp.int32, shape, axis)


def mxu(left, right):
    return jnp.dot(left, right, preferred_element_type=F32)


def exact_dot(left, right):
    return jnp.dot(left, right, precision=EXACT, preferred_element_type=F32)


def gate(left, right):
    return (left.astype(F32) * right.astype(F32)).astype(BF16)


def reversal(size):
    return jnp.where(iota((size, size), 0) + iota((size, size), 1) == size - 1, 1.0, 0.0).astype(BF16)


def split_pair(value):
    high = value.astype(BF16).astype(F32)
    return high, value - high


def flat_rows(table, poles):
    table = table.T
    groups = table.shape[0]
    per_row = LANES // poles
    spread = jnp.where(iota((poles, LANES), 0) == iota((poles, LANES), 1) % poles, 1.0, 0.0)
    wide = exact_dot(table, spread)
    keep = iota((groups, LANES), 0) % per_row == iota((groups, LANES), 1) // poles
    wide = jnp.where(keep, wide, 0.0)
    return jnp.sum(wide.reshape(groups // per_row, per_row, LANES), axis=1)


def states_kernel(logs_ref, res_ref, q_ref, k_ref, v_ref, c_ref, *rest, group, poles, parts):
    *slots, pair_ref, rows_ref, all_ref = rest
    tokens, width = q_ref.shape
    per_block = LANES // group
    shard_groups = rows_ref.shape[1] * per_block
    _, own_width = slots[0].shape
    owners = width // own_width
    step = pl.program_id(0)
    blocks = width // LANES

    @pl.when(step == 0)
    def _():
        first = pl.multiple_of(lax.axis_index("ch") * shard_groups, LANES)
        rows_ref[0] = jnp.exp(flat_rows(logs_ref[:, pl.ds(first, shard_groups)], poles))
        rows_ref[1] = flat_rows(res_ref[:, pl.ds(first, shard_groups)], poles)

    flip = reversal(tokens)
    back_pos = (tokens - 1 - iota((tokens, LANES), 0)).astype(F32)
    back_lane = (tokens - 1 - iota((per_block, tokens), 1)).astype(F32)
    lane_group = iota((tokens, LANES), 1) // group
    causal = iota((tokens, tokens), 0) + iota((tokens, tokens), 1) <= tokens - 1
    wide_group = (iota((poles, 2 * LANES), 1) % LANES) // group
    half = per_block // 2
    own_rows = iota((per_block, LANES), 0) == iota((per_block, LANES), 1) // poles
    zero = jnp.zeros((tokens, LANES), BF16)

    for j in range(blocks):
        cut = slice(j * LANES, (j + 1) * LANES)
        gated = gate(k_ref[:, cut], v_ref[:, cut])
        dgate = gate(c_ref[:, cut], q_ref[:, cut])
        skip = jnp.sum(gated.astype(F32) * dgate.astype(F32), axis=0, keepdims=True)
        turned = mxu(flip, dgate).astype(BF16)
        pair = jnp.concatenate([gated, turned], axis=1)
        pair_ref[:, 2 * j * LANES : 2 * (j + 1) * LANES] = pair
        rate = rows_ref[0, pl.ds(step * blocks + j, 1), :]
        table = jnp.exp(-rate * back_pos)
        table_low = table.astype(BF16)
        both = jnp.concatenate([table.T.astype(BF16), (table * back_pos).T.astype(BF16)], axis=0)
        summed = mxu(both, pair)
        folded = []
        for part in range(2):
            total = jnp.zeros((poles, 2 * LANES), F32)
            for g in range(per_block):
                start = part * LANES + g * poles
                total = jnp.where(wide_group == g, summed[start : start + poles], total)
            folded.append(total)
        left = [
            jnp.where((lane_group == i) | (lane_group == i + half), turned, zero) for i in range(half)
        ]
        right = [
            jnp.where(lane_group < half, gated, zero),
            jnp.where(lane_group >= half, gated, zero),
        ]
        outer = lax.dot_general(
            jnp.concatenate(left, axis=0),
            jnp.concatenate(right, axis=0),
            (((1,), (1,)), ((), ())),
            preferred_element_type=F32,
        )
        lags = []
        for h in range(2):
            for i in range(half):
                tile = outer[i * tokens : (i + 1) * tokens, h * tokens : (h + 1) * tokens]
                tile = jnp.where(causal, tile, 0.0)
                total = tile[:8]
                for a in range(1, tokens // 8):
                    total = total + pltpu.roll(tile[8 * a : 8 * a + 8], 8 * a, 1)
                total = pltpu.roll(total, 0, 1, stride=1, stride_axis=0)
                lags.append(jnp.sum(total, axis=0, keepdims=True))
        lag = jnp.concatenate(lags, axis=0)
        lag_high, lag_low = split_pair(lag)
        mom_high, mom_low = split_pair(lag * back_lane)
        stack = jnp.concatenate([lag_high, lag_low, mom_high, mom_low], axis=0).astype(BF16)
        local = mxu(stack, table_low)
        res_part = local[:per_block] + local[per_block : 2 * per_block]
        mom_part = local[2 * per_block : 3 * per_block] + local[3 * per_block :]
        res_row = jnp.sum(jnp.where(own_rows, res_part, 0.0), axis=0, keepdims=True)
        mom_row = jnp.sum(jnp.where(own_rows, mom_part, 0.0), axis=0, keepdims=True)
        extra = jnp.concatenate(
            [*split_pair(res_row), *split_pair(mom_row), *split_pair(skip), jnp.zeros((10, LANES), F32)],
            axis=0,
        )
        out = jnp.concatenate(
            [
                folded[0][:, :LANES],
                folded[0][:, LANES:],
                folded[1][:, :LANES],
                folded[1][:, LANES:],
                extra,
            ],
            axis=0,
        ).astype(BF16)
        if own_width >= LANES:
            place = j * LANES // own_width
            offset = j * LANES % own_width
            all_ref[step * owners + place, :, offset : offset + LANES] = out
        else:
            for n in range(LANES // own_width):
                place = j * (LANES // own_width) + n
                all_ref[step * owners + place] = out[:, n * own_width : (n + 1) * own_width]

    @pl.when(step == pl.num_programs(0) - 1)
    def _():
        for shift, slot in enumerate(slots):
            slot[...] = all_ref[lax.rem(lax.axis_index("ctx") + shift, parts)]


def conv_kernel(rows_ref, skip_ref, pair_ref, conv_ref, *, group, poles):
    tokens, width = pair_ref.shape
    per_block = LANES // group
    step = pl.program_id(0)
    blocks = width // (2 * LANES)
    all_blocks = rows_ref.shape[1]
    first = lax.axis_index("ch") * all_blocks
    back_pos = (tokens - 1 - iota((tokens, LANES), 0)).astype(F32)
    wide_group = (iota((tokens, 2 * LANES), 1) % LANES) // group
    causal = iota((tokens, tokens), 0) >= iota((tokens, tokens), 1)
    for j in range(blocks):
        cut = slice(2 * j * LANES, 2 * (j + 1) * LANES)
        pair = pair_ref[:, cut]
        here = step * blocks + j
        rate = rows_ref[0, pl.ds(here, 1), :]
        res = rows_ref[1, pl.ds(here, 1), :]
        table = (res * jnp.exp(-rate * back_pos)).T
        left, right = [], []
        for g in range(per_block):
            taps = jnp.sum(table[g * poles : (g + 1) * poles], axis=0, keepdims=True)
            base = pltpu.roll(jnp.broadcast_to(taps, (8, tokens)), 1, 1, stride=1, stride_axis=0)
            rolled = [base] + [pltpu.roll(base, 8 * a, 1) for a in range(1, tokens // 8)]
            left.append(jnp.where(causal, jnp.concatenate(rolled, axis=0), 0.0).astype(BF16))
            right.append(jnp.where(wide_group == g, pair, jnp.zeros_like(pair)))
        total = mxu(jnp.concatenate(left, axis=1), jnp.concatenate(right, axis=0))
        gain = skip_ref[pl.ds(first + here, 1), :]
        conv_ref[:, cut] = total + jnp.concatenate([gain, gain], axis=1) * pair.astype(F32)


def scan_kernel(logs_ref, res_ref, *rest, group, poles, tokens, parts):
    slots, backs = rest[:parts], rest[parts : 2 * parts]
    grad_ref, got_ref, back_ref = rest[2 * parts :]
    _, width = slots[0].shape
    groups = width // group
    me = lax.axis_index("ctx")
    for shift in range(parts):
        got_ref[lax.rem(me - shift + parts, parts)] = slots[shift][...]
    shard_groups = groups * parts
    start = pl.multiple_of(lax.axis_index("ch") * shard_groups, LANES)
    mine = jnp.where(
        iota((shard_groups, groups), 0) == me * groups + iota((shard_groups, groups), 1), 1.0, 0.0
    )
    scale = tokens * parts
    spread = jnp.where(iota((poles, width), 0) == iota((poles, width), 1) % poles, 1.0, 0.0)
    keep = iota((groups, width), 0) == iota((groups, width), 1) // poles
    pick = iota((poles, width), 0) == iota((poles, width), 1) % poles
    same = jnp.where(iota((width, width), 0) // group == iota((width, width), 1) // group, 1.0, 0.0)

    def flat(ref):
        table = exact_dot(ref[:, pl.ds(start, shard_groups)], mine).T
        wide = exact_dot(table, spread)
        return jnp.sum(jnp.where(keep, wide, 0.0), axis=0, keepdims=True)

    rate = jnp.exp(flat(logs_ref))
    res = flat(res_ref)
    rates = exact_dot(jnp.where(pick, rate, 0.0), same)
    decay = jnp.exp(-rates * tokens)
    one = jnp.exp(-rates)

    def rows(i, n):
        return got_ref[i, n * poles : (n + 1) * poles, :].astype(F32)

    zeros = jnp.zeros((poles, width), F32)
    state, moment, sum_res, sum_mom = zeros, zeros, zeros, zeros
    extra = jnp.zeros((16, width), F32)
    for i in range(parts):
        back_ref[i, :poles, :] = state.astype(BF16)
        begin = rows(i, 1)
        sum_res += begin * state
        sum_mom += rows(i, 3) * state + begin * moment
        ahead = rows(i, 0)
        moment = decay * (moment + tokens * state) + rows(i, 2) + ahead
        state = decay * state + ahead
        extra += got_ref[i, 4 * poles :, :].astype(F32)
    state = zeros
    for i in reversed(range(parts)):
        back_ref[i, poles:, :] = state.astype(BF16)
        state = decay * state + rows(i, 1)

    def gather(total, high, low):
        wide = exact_dot(total * one, same)
        return jnp.sum(jnp.where(pick, wide, 0.0), axis=0, keepdims=True) + high + low

    grad_res = gather(sum_res, extra[0:1], extra[1:2]) / scale
    grad_log = -rate * res * gather(sum_mom, extra[2:3], extra[3:4]) / math.sqrt(scale)
    grad_skip = (extra[4:5] + extra[5:6]) / math.sqrt(scale)
    for shift in range(parts):
        backs[shift][...] = back_ref[lax.rem(me + shift, parts)]
    grad_ref[...] = jnp.concatenate(
        [grad_res, grad_log, grad_skip, jnp.zeros((5, width), F32)], axis=0
    )


def output_kernel(rows_ref, conv_ref, k_ref, v_ref, c_ref, *rest, group, poles, parts):
    slots = rest[:parts]
    gq_ref, gk_ref, gv_ref, back_ref = rest[parts:]
    tokens, width = k_ref.shape
    per_block = LANES // group
    own_width = back_ref.shape[2]
    step = pl.program_id(0)
    blocks = width // LANES
    flip = reversal(tokens)
    ahead = (1 + iota((tokens, LANES), 0)).astype(F32)
    wide_group = (iota((poles, 2 * LANES), 1) % LANES) // group
    owners = max(1, width // own_width)

    @pl.when(step == 0)
    def _():
        for shift, slot in enumerate(slots):
            back_ref[lax.rem(lax.axis_index("ctx") - shift + parts, parts)] = slot[...]

    for j in range(blocks):
        cut = slice(j * LANES, (j + 1) * LANES)
        here = step * blocks + j
        rate = rows_ref[0, pl.ds(here, 1), :]
        res = rows_ref[1, pl.ds(here, 1), :]
        table = (res * jnp.exp(-rate * ahead)).astype(BF16)
        if own_width >= LANES:
            place, offset = j * LANES // own_width, j * LANES % own_width
            states = back_ref[step * owners + place, :, offset : offset + LANES]
        else:
            count = LANES // own_width
            states = jnp.concatenate([back_ref[step * owners + j * count + n] for n in range(count)], axis=1)
        states = jnp.concatenate([states[:poles], states[poles:]], axis=1)
        stack = jnp.concatenate(
            [jnp.where(wide_group == g, states, jnp.zeros_like(states)) for g in range(per_block)], axis=0
        )
        total = (conv_ref[:, 2 * j * LANES : 2 * (j + 1) * LANES] + mxu(table, stack)).astype(BF16)
        flow = mxu(flip, total[:, LANES:])
        gq_ref[:, cut] = (c_ref[:, cut].astype(F32) * total[:, :LANES].astype(F32)).astype(BF16)
        gk_ref[:, cut] = (flow * v_ref[:, cut].astype(F32)).astype(BF16)
        gv_ref[:, cut] = (flow * k_ref[:, cut].astype(F32)).astype(BF16)


def local(queries, key_input, value_input, cotangent, residues, log_rates, skip_gain):
    tokens, width = queries.shape
    parts = lax.axis_size("ctx")
    shards = lax.axis_size("ch")
    all_groups, poles = residues.shape
    group = width * shards // all_groups
    own_width = width // parts
    step_width = min(width, max(4 * LANES, own_width))
    steps = width // step_width
    blocks = width // LANES
    payload = 4 * poles + 16
    sizes = dict(group=group, poles=poles)
    params = pltpu.CompilerParams(vmem_limit_bytes=VMEM_LIMIT)

    def fixed(*shape):
        return pl.BlockSpec(shape, lambda i: (0,) * len(shape))

    def shifted(arrays):
        moved = [arrays[0]]
        for shift in range(1, parts):
            pairs = [(source, (source + shift) % parts) for source in range(parts)]
            moved.append(lax.ppermute(arrays[shift], "ctx", pairs))
        return moved

    log_rates, residues = log_rates.T, residues.T
    whole = fixed(poles, all_groups)
    main = pl.BlockSpec((tokens, step_width), lambda i: (0, i))
    twice = pl.BlockSpec((tokens, 2 * step_width), lambda i: (0, i))
    row_table = fixed(2, blocks, LANES)

    *send, pair, rows = pl.pallas_call(
        lambda *refs: states_kernel(*refs, parts=parts, **sizes),
        grid=(steps,),
        in_specs=[whole, whole, main, main, main, main],
        out_specs=[fixed(payload, own_width)] * parts + [twice, row_table],
        out_shape=[jax.ShapeDtypeStruct((payload, own_width), BF16)] * parts
        + [
            jax.ShapeDtypeStruct((tokens, 2 * width), BF16),
            jax.ShapeDtypeStruct((2, blocks, LANES), F32),
        ],
        scratch_shapes=[pltpu.VMEM((parts, payload, own_width), BF16)],
        compiler_params=params,
        name="states",
    )(log_rates, residues, queries, key_input, value_input, cotangent)

    got = shifted(send)

    skip_rows = skip_gain.reshape(-1, LANES)
    conv = pl.pallas_call(
        lambda *refs: conv_kernel(*refs, **sizes),
        grid=(steps,),
        in_specs=[row_table, fixed(*skip_rows.shape), twice],
        out_specs=twice,
        out_shape=jax.ShapeDtypeStruct((tokens, 2 * width), F32),
        compiler_params=params,
        cost_estimate=pl.CostEstimate(
            flops=16 * tokens * tokens * width, bytes_accessed=12 * tokens * width, transcendentals=tokens * width
        ),
        name="conv",
    )(rows, skip_rows, pair)

    vmem = pl.BlockSpec(memory_space=pltpu.VMEM)
    *back, grads = pl.pallas_call(
        lambda *refs: scan_kernel(*refs, tokens=tokens, parts=parts, **sizes),
        in_specs=[vmem] * (2 + parts),
        out_specs=[vmem] * (parts + 1),
        out_shape=[jax.ShapeDtypeStruct((2 * poles, own_width), BF16)] * parts
        + [jax.ShapeDtypeStruct((8, own_width), F32)],
        scratch_shapes=[
            pltpu.VMEM((parts, payload, own_width), BF16),
            pltpu.VMEM((parts, 2 * poles, own_width), BF16),
        ],
        compiler_params=params,
        name="scan",
    )(log_rates, residues, *got)

    states = shifted(back)
    spread = jnp.broadcast_to(grads[None], (parts * shards, 8, own_width))
    final = lax.all_to_all(spread, ("ctx", "ch"), split_axis=0, concat_axis=0, tiled=True)

    grad_query, grad_key, grad_value = pl.pallas_call(
        lambda *refs: output_kernel(*refs, parts=parts, **sizes),
        grid=(steps,),
        in_specs=[row_table, twice, main, main, main] + [fixed(2 * poles, own_width)] * parts,
        out_specs=[main, main, main],
        out_shape=[jax.ShapeDtypeStruct((tokens, width), BF16)] * 3,
        scratch_shapes=[pltpu.VMEM((parts, 2 * poles, own_width), BF16)],
        compiler_params=params,
        name="outputs",
    )(rows, conv, key_input, value_input, cotangent, *states)

    final = final.reshape(parts, shards, 8, own_width).transpose(2, 1, 0, 3)
    grad_residue = final[0].reshape(all_groups, poles)
    grad_lograte = final[1].reshape(all_groups, poles)
    grad_skip = final[2].reshape(-1)
    return (grad_query, grad_key, grad_value, grad_residue, grad_lograte, grad_skip)


def solution(mesh):
    placed = (P("ctx", "ch"), P("ctx", "ch"), P("ctx", "ch"), P("ctx", "ch"), P(), P(), P())
    return jax.shard_map(
        local,
        mesh=mesh,
        in_specs=placed,
        out_specs=(P("ctx", "ch"), P("ctx", "ch"), P("ctx", "ch"), P(), P(), P()),
        check_vma=False,
    )
```

```python
import math

import jax
import jax.numpy as jnp
from jax import lax
from jax.experimental import pallas as pl
from jax.experimental.pallas import tpu as pltpu
from jax.sharding import PartitionSpec as P

LANES = 128
SUB = 32
F32 = jnp.float32
BF16 = jnp.bfloat16
EXACT = lax.Precision.HIGHEST
VMEM_LIMIT = 40 * 1024 * 1024
PARAMS = pltpu.CompilerParams(vmem_limit_bytes=VMEM_LIMIT)


def iota(shape, axis):
    return lax.broadcasted_iota(jnp.int32, shape, axis)


def mxu(left, right):
    return jnp.dot(left, right, preferred_element_type=F32)


def mxu_t(left, right):
    return lax.dot_general(left, right, (((1,), (1,)), ((), ())), preferred_element_type=F32)


def exact_dot(left, right):
    return jnp.dot(left, right, precision=EXACT, preferred_element_type=F32)


def gate(left, right):
    return (left.astype(F32) * right.astype(F32)).astype(BF16)


def reversal(size):
    return jnp.where(iota((size, size), 0) + iota((size, size), 1) == size - 1, 1.0, 0.0).astype(BF16)


def split(value, pieces):
    parts = []
    for _ in range(pieces):
        parts.append(value.astype(BF16))
        value = value - parts[-1].astype(F32)
    return jnp.concatenate(parts, axis=0)


def join(stacked, rows):
    total = stacked[:rows].astype(F32)
    for start in range(rows, stacked.shape[0], rows):
        total = total + stacked[start : start + rows].astype(F32)
    return total


def flat_rows(table, poles):
    table = table.T
    groups = table.shape[0]
    per_row = LANES // poles
    spread = jnp.where(iota((poles, LANES), 0) == iota((poles, LANES), 1) % poles, 1.0, 0.0)
    wide = exact_dot(table, spread)
    keep = iota((groups, LANES), 0) % per_row == iota((groups, LANES), 1) // poles
    wide = jnp.where(keep, wide, 0.0)
    return jnp.sum(wide.reshape(groups // per_row, per_row, LANES), axis=1)


def members(groups, first, span, width):
    return jnp.where(iota((groups, width), 0) == first + iota((groups, width), 1) // span, 1.0, 0.0).astype(BF16)


def shard_start(groups):
    return pl.multiple_of(lax.axis_index("ch") * groups, LANES)


def states_kernel(logs_ref, res_ref, q_any, k_any, v_any, c_any, msg_ref, pair_ref, rows_ref, rates_ref,
                  q_ref, k_ref, v_ref, c_ref, skip_ref, sems, *, group, poles, steps):
    tokens, width = q_ref.shape
    per_block = LANES // group
    blocks, _, _ = rates_ref.shape
    groups = blocks * per_block
    inner = blocks // steps
    chunk = width // steps
    subs = tokens // SUB
    lag_width = per_block * SUB

    def copies(step):
        cut = pl.ds(pl.multiple_of(step * chunk, LANES), chunk)
        pairs = ((k_any, k_ref), (v_any, v_ref), (c_any, c_ref), (q_any, q_ref))
        return [
            pltpu.make_async_copy(far.at[:, cut], near.at[:, cut], sems.at[n, step])
            for n, (far, near) in enumerate(pairs)
        ]

    for step in range(steps):
        for copy in copies(step):
            copy.start()

    first = shard_start(groups)
    logs = logs_ref[:, pl.ds(first, groups)]
    rows_ref[0] = jnp.exp(flat_rows(logs, poles))
    rows_ref[1] = flat_rows(res_ref[:, pl.ds(first, groups)], poles)
    logs = split(logs, 3)

    flip = reversal(tokens)
    lag = (SUB - 1 - iota((poles, lag_width), 1) % SUB).astype(F32)
    wide_group = (iota((SUB, 2 * LANES), 1) % LANES) // group
    causal = iota((SUB, lag_width), 0) + iota((SUB, lag_width), 1) % SUB <= SUB - 1

    def body(step, sums):
        for copy in copies(step):
            copy.wait()
        for j in range(inner):
            block = step * inner + j
            cut = pl.ds(pl.multiple_of(block * LANES, LANES), LANES)
            gated = gate(k_ref[:, cut], v_ref[:, cut])
            dgate = gate(c_ref[:, cut], q_ref[:, cut])
            skip = jnp.sum(gated.astype(F32) * dgate.astype(F32), axis=0, keepdims=True)
            skip_ref[pl.ds(block, 1), :] = skip
            turned = mxu(flip, dgate).astype(BF16)
            pair = jnp.concatenate([gated, turned], axis=1)
            pair_ref[:, pl.ds(pl.multiple_of(2 * block * LANES, LANES), 2 * LANES)] = pair

            lag_of = members(groups, block * per_block, SUB, lag_width)
            lane_of = members(groups, block * per_block, group, LANES)
            spread = jnp.concatenate([lag_of, lane_of], axis=1)
            rates = jnp.exp(join(mxu(logs, spread), poles))
            lag_rate, rate = rates[:, :lag_width], rates[:, lag_width:]
            rates_ref[block] = rate
            table = jnp.exp(-lag_rate * lag)
            moment_table = table * lag
            tables = jnp.concatenate([table, moment_table], axis=0).astype(BF16)

            found, outer = [], jnp.zeros((SUB, lag_width), F32)
            for k in range(subs):
                part = pair[k * SUB : (k + 1) * SUB]
                stack = jnp.concatenate(
                    [jnp.where(wide_group == g, part, jnp.zeros_like(part)) for g in range(per_block)], axis=0
                )
                found.append(mxu(tables, stack))
                mate = turned[(subs - 1 - k) * SUB : (subs - k) * SUB]
                outer = outer + mxu_t(mate, stack[:, :LANES])
            outer = jnp.where(causal, outer, 0.0)
            outer = pltpu.roll(outer, 0, 1, stride=1, stride_axis=0)
            lags = jnp.sum(outer, axis=0, keepdims=True)

            once = jnp.exp(-rate)
            decay = jnp.exp(-rate * SUB)
            decay = jnp.concatenate([decay, decay], axis=1)
            state = jnp.zeros((poles, 2 * LANES), F32)
            moment = state
            cross_res = jnp.zeros((poles, LANES), F32)
            cross_mom = cross_res
            for k in range(subs):
                back = found[subs - 1 - k][:, LANES:]
                held, held_moment = state[:, :LANES], moment[:, :LANES]
                cross_res = cross_res + back[:poles] * held
                cross_mom = cross_mom + back[poles:] * held + back[:poles] * (held_moment + held)
                moment = decay * (moment + SUB * state) + found[k][poles:]
                state = decay * state + found[k][:poles]
            out = jnp.concatenate(
                [state[:, :LANES], state[:, LANES:], moment[:, :LANES], moment[:, LANES:]], axis=0
            )
            msg_ref[pl.ds(pl.multiple_of(block * 4 * poles, 16), 4 * poles), :] = out.astype(BF16)
            near = jnp.concatenate([lags * table, lags * moment_table], axis=0)
            far = jnp.concatenate([once * cross_res, once * cross_mom], axis=0)
            terms = split(jnp.concatenate([near, far], axis=1), 2)
            sums = sums + join(mxu_t(terms, spread), 2 * poles)
        return sums

    sums = lax.fori_loop(0, steps, body, jnp.zeros((2 * poles, groups), F32))
    tail = blocks * 4 * poles
    msg_ref[tail : tail + 4 * poles, :] = split(sums, 2)
    msg_ref[tail + 4 * poles :, :] = split(skip_ref[...], 2)


def conv_kernel(rows_ref, skip_ref, pair_ref, conv_ref, *, group, poles):
    tokens, width = pair_ref.shape
    per_block = LANES // group
    step = pl.program_id(0)
    blocks = width // (2 * LANES)
    all_blocks = rows_ref.shape[1]
    first = lax.axis_index("ch") * all_blocks
    back_pos = (tokens - 1 - iota((tokens, LANES), 0)).astype(F32)
    wide_group = (iota((tokens, 2 * LANES), 1) % LANES) // group
    causal = iota((tokens, tokens), 0) >= iota((tokens, tokens), 1)
    for j in range(blocks):
        cut = slice(2 * j * LANES, 2 * (j + 1) * LANES)
        pair = pair_ref[:, cut]
        here = step * blocks + j
        rate = rows_ref[0, pl.ds(here, 1), :]
        res = rows_ref[1, pl.ds(here, 1), :]
        table = (res * jnp.exp(-rate * back_pos)).T
        left, right = [], []
        for g in range(per_block):
            taps = jnp.sum(table[g * poles : (g + 1) * poles], axis=0, keepdims=True)
            base = pltpu.roll(jnp.broadcast_to(taps, (8, tokens)), 1, 1, stride=1, stride_axis=0)
            rolled = [base] + [pltpu.roll(base, 8 * a, 1) for a in range(1, tokens // 8)]
            left.append(jnp.where(causal, jnp.concatenate(rolled, axis=0), 0.0).astype(BF16))
            right.append(jnp.where(wide_group == g, pair, jnp.zeros_like(pair)))
        total = mxu(jnp.concatenate(left, axis=1), jnp.concatenate(right, axis=0))
        gain = skip_ref[pl.ds(first + here, 1), :]
        conv_ref[:, cut] = total + jnp.concatenate([gain, gain], axis=1) * pair.astype(F32)


def combine_kernel(*refs, level, levels, group, poles, tokens):
    last = level == levels - 1
    refs = list(refs)
    rates_ref, own_ref, got_ref = refs[:3]
    rest = refs[3:]
    held_ref = rest.pop(0) if level else None
    if last:
        logs_ref, res_ref = rest.pop(0), rest.pop(0)
    slim_ref = rest.pop() if level == levels - 2 else None
    out_ref, new_held_ref = rest
    blocks = rates_ref.shape[0]
    groups = blocks * (LANES // group)
    me = lax.axis_index("ctx")
    is_right = lax.rem(lax.shift_right_logical(me, level), 2) == 1
    before = lax.rem(me, 2**level)
    gap_left = (tokens * before).astype(F32)
    gap_right = (tokens * (2**level - 1 - before)).astype(F32)
    span = float(tokens * 2**level)
    next_right = lax.rem(lax.shift_right_logical(me, level + 1), 2) == 1
    own_rows = 4 * poles
    got_rows = 2 * poles if last else 4 * poles
    slim_rows = 2 * poles
    sums = jnp.zeros((4 * poles, groups), F32)
    for b in range(blocks):
        rate = rates_ref[b]
        own = own_ref[b * own_rows : (b + 1) * own_rows].astype(F32)
        got = got_ref[b * got_rows : (b + 1) * got_rows].astype(F32)
        own_f, own_b, own_fm, own_bm = (own[n * poles : (n + 1) * poles] for n in range(4))
        if last:
            got_f = got_b = got[:poles]
            got_fm = got_bm = got[poles:]
        else:
            got_f, got_b, got_fm, got_bm = (got[n * poles : (n + 1) * poles] for n in range(4))
        left_f = jnp.where(is_right, got_f, own_f)
        left_fm = jnp.where(is_right, got_fm, own_fm)
        right_b = jnp.where(is_right, own_b, got_b)
        right_bm = jnp.where(is_right, own_bm, got_bm)
        once = jnp.exp(-rate)
        cross_res = once * (right_b * left_f)
        cross_mom = once * (right_bm * left_f + right_b * (left_fm + left_f))
        terms = split(jnp.concatenate([cross_res, cross_mom], axis=0), 2)
        sums = sums + mxu_t(terms, members(groups, b * (LANES // group), group, LANES))
        if level:
            hold = held_ref[b]
        else:
            hold = jnp.zeros((2 * poles, LANES), F32)
        carry = jnp.exp(-rate * jnp.where(is_right, gap_left, gap_right)) * jnp.where(is_right, left_f, right_b)
        zero = jnp.zeros_like(carry)
        hold = hold + jnp.concatenate(
            [jnp.where(is_right, carry, zero), jnp.where(is_right, zero, carry)], axis=0
        )
        new_held_ref[b] = hold.astype(new_held_ref.dtype)
        if not last:
            right_f = jnp.where(is_right, own_f, got_f)
            right_fm = jnp.where(is_right, own_fm, got_fm)
            left_b = jnp.where(is_right, got_b, own_b)
            left_bm = jnp.where(is_right, got_bm, own_bm)
            decay = jnp.exp(-rate * span)
            new = [
                decay * left_f + right_f,
                left_b + decay * right_b,
                decay * (left_fm + span * left_f) + right_fm,
                left_bm + decay * (right_bm + span * right_b),
            ]
            out_ref[b * own_rows : (b + 1) * own_rows, :] = jnp.concatenate(new, axis=0).astype(BF16)
            if slim_ref is not None:
                chosen = jnp.concatenate(
                    [jnp.where(next_right, new[1], new[0]), jnp.where(next_right, new[3], new[2])], axis=0
                )
                slim_ref[b * slim_rows : (b + 1) * slim_rows, :] = chosen.astype(BF16)
    own_tail, got_tail = blocks * own_rows, blocks * got_rows
    total = (
        join(sums, 2 * poles)
        + join(own_ref[own_tail : own_tail + 4 * poles], 2 * poles)
        + join(got_ref[got_tail : got_tail + 4 * poles], 2 * poles)
    )
    skip = join(own_ref[own_tail + 4 * poles :], blocks) + join(got_ref[got_tail + 4 * poles :], blocks)
    if last:
        start = shard_start(groups)
        rate = jnp.exp(logs_ref[:, pl.ds(start, groups)])
        res = res_ref[:, pl.ds(start, groups)]
        length = 2 * span
        out_ref[:poles, :] = total[:poles] / length
        out_ref[poles : 2 * poles, :] = -rate * res * total[poles:] / math.sqrt(length)
        out_ref[2 * poles :, :] = skip / math.sqrt(length)
    else:
        rests = jnp.concatenate([split(total, 2), split(skip, 2)], axis=0)
        out_ref[own_tail:, :] = rests
        if slim_ref is not None:
            slim_ref[blocks * slim_rows :, :] = rests


def output_kernel(rows_ref, conv_ref, held_ref, k_ref, v_ref, c_ref, gq_ref, gk_ref, gv_ref, *, group, poles):
    tokens, width = k_ref.shape
    per_block = LANES // group
    step = pl.program_id(0)
    blocks = width // LANES
    flip = reversal(tokens)
    ahead = (1 + iota((tokens, LANES), 0)).astype(F32)
    wide_group = (iota((poles, 2 * LANES), 1) % LANES) // group
    for j in range(blocks):
        cut = slice(j * LANES, (j + 1) * LANES)
        here = step * blocks + j
        rate = rows_ref[0, pl.ds(here, 1), :]
        res = rows_ref[1, pl.ds(here, 1), :]
        table = (res * jnp.exp(-rate * ahead)).astype(BF16)
        held = held_ref[j]
        states = jnp.concatenate([held[:poles], held[poles:]], axis=1)
        stack = jnp.concatenate(
            [jnp.where(wide_group == g, states, jnp.zeros_like(states)) for g in range(per_block)], axis=0
        )
        total = (conv_ref[:, 2 * j * LANES : 2 * (j + 1) * LANES] + mxu(table, stack)).astype(BF16)
        flow = mxu(flip, total[:, LANES:])
        gq_ref[:, cut] = (c_ref[:, cut].astype(F32) * total[:, :LANES].astype(F32)).astype(BF16)
        gk_ref[:, cut] = (flow * v_ref[:, cut].astype(F32)).astype(BF16)
        gv_ref[:, cut] = (flow * k_ref[:, cut].astype(F32)).astype(BF16)


def assemble_kernel(*refs, shards, poles):
    slots = refs[:shards]
    res_ref, log_ref, skip_ref = refs[shards:]
    me = lax.axis_index("ch")
    groups = slots[0].shape[1]
    rows = slots[0].shape[0] - 2 * poles
    for shift, slot in enumerate(slots):
        source = lax.rem(me - shift + shards, shards)
        cut = pl.ds(pl.multiple_of(source * groups, LANES), groups)
        res_ref[:, cut] = slot[:poles, :]
        log_ref[:, cut] = slot[poles : 2 * poles, :]
        skip_ref[pl.ds(pl.multiple_of(source * rows, 8), rows), :] = slot[2 * poles :, :]


def local(queries, key_input, value_input, cotangent, residues, log_rates, skip_gain):
    tokens, width = queries.shape
    parts = lax.axis_size("ctx")
    shards = lax.axis_size("ch")
    levels = parts.bit_length() - 1
    all_groups, poles = residues.shape
    groups = all_groups // shards
    group = width // groups
    blocks = width // LANES
    steps = 4
    step_width = width // steps
    sizes = dict(group=group, poles=poles)
    tail = 4 * poles + 2 * blocks

    def fixed(*shape):
        return pl.BlockSpec(shape, lambda i: (0,) * len(shape))

    vmem = pl.BlockSpec(memory_space=pltpu.VMEM)
    far = pl.BlockSpec(memory_space=pltpu.HBM)
    log_rates, residues = log_rates.T, residues.T
    main = pl.BlockSpec((tokens, step_width), lambda i: (0, i))
    twice = pl.BlockSpec((tokens, 2 * step_width), lambda i: (0, i))
    row_table = fixed(2, blocks, LANES)

    message, pair, rows, rates = pl.pallas_call(
        lambda *refs: states_kernel(*refs, steps=steps, **sizes),
        in_specs=[vmem, vmem, far, far, far, far],
        out_specs=[vmem] * 4,
        out_shape=[
            jax.ShapeDtypeStruct((blocks * 4 * poles + tail, LANES), BF16),
            jax.ShapeDtypeStruct((tokens, 2 * width), BF16),
            jax.ShapeDtypeStruct((2, blocks, LANES), F32),
            jax.ShapeDtypeStruct((blocks, poles, LANES), F32),
        ],
        scratch_shapes=[pltpu.VMEM((tokens, width), BF16)] * 4
        + [pltpu.VMEM((blocks, LANES), F32), pltpu.SemaphoreType.DMA((4, steps))],
        compiler_params=PARAMS,
        name="states",
    )(log_rates, residues, queries, key_input, value_input, cotangent)

    skip_rows = skip_gain.reshape(-1, LANES)
    conv = pl.pallas_call(
        lambda *refs: conv_kernel(*refs, **sizes),
        grid=(steps,),
        in_specs=[row_table, fixed(*skip_rows.shape), twice],
        out_specs=twice,
        out_shape=jax.ShapeDtypeStruct((tokens, 2 * width), F32),
        compiler_params=PARAMS,
        cost_estimate=pl.CostEstimate(
            flops=16 * tokens * tokens * width, bytes_accessed=12 * tokens * width, transcendentals=tokens * width
        ),
        name="conv",
    )(rows, skip_rows, pair)

    held, outgoing = None, message
    for level in range(levels):
        last = level == levels - 1
        got = lax.ppermute(outgoing, "ctx", [(i, i ^ (1 << level)) for i in range(parts)])
        operands = [rates, message, got]
        if level:
            operands.append(held)
        if last:
            operands += [log_rates, residues]
            out = jax.ShapeDtypeStruct((2 * poles + blocks, LANES), F32)
        else:
            out = jax.ShapeDtypeStruct(message.shape, BF16)
        outs = [out, jax.ShapeDtypeStruct((blocks, 2 * poles, LANES), BF16 if last else F32)]
        if level == levels - 2:
            outs.append(jax.ShapeDtypeStruct((blocks * 2 * poles + tail, LANES), BF16))
        message, held, *slim = pl.pallas_call(
            lambda *refs, level=level: combine_kernel(*refs, level=level, levels=levels, tokens=tokens, **sizes),
            in_specs=[vmem] * len(operands),
            out_specs=[vmem] * len(outs),
            out_shape=outs,
            compiler_params=PARAMS,
            name="combine",
        )(*operands)
        outgoing = slim[0] if slim else message

    gathered = [message]
    for shift in range(1, shards):
        gathered.append(lax.ppermute(message, "ch", [(i, (i + shift) % shards) for i in range(shards)]))

    grad_query, grad_key, grad_value = pl.pallas_call(
        lambda *refs: output_kernel(*refs, **sizes),
        grid=(steps,),
        in_specs=[
            row_table,
            twice,
            pl.BlockSpec((blocks // steps, 2 * poles, LANES), lambda i: (i, 0, 0)),
            main,
            main,
            main,
        ],
        out_specs=[main, main, main],
        out_shape=[jax.ShapeDtypeStruct((tokens, width), BF16)] * 3,
        compiler_params=PARAMS,
        name="outputs",
    )(rows, conv, held, key_input, value_input, cotangent)

    grad_residue, grad_lograte, grad_skip = pl.pallas_call(
        lambda *refs: assemble_kernel(*refs, shards=shards, poles=poles),
        in_specs=[vmem] * shards,
        out_specs=[vmem] * 3,
        out_shape=[
            jax.ShapeDtypeStruct((poles, all_groups), F32),
            jax.ShapeDtypeStruct((poles, all_groups), F32),
            jax.ShapeDtypeStruct((shards * blocks, LANES), F32),
        ],
        compiler_params=PARAMS,
        name="assemble",
    )(*gathered)
    return (grad_query, grad_key, grad_value, grad_residue.T, grad_lograte.T, grad_skip.reshape(-1))


def solution(mesh):
    placed = (P("ctx", "ch"), P("ctx", "ch"), P("ctx", "ch"), P("ctx", "ch"), P(), P(), P())
    return jax.shard_map(
        local,
        mesh=mesh,
        in_specs=placed,
        out_specs=(P("ctx", "ch"), P("ctx", "ch"), P("ctx", "ch"), P(), P(), P()),
        check_vma=False,
    )
```

```python
import math

import jax
import jax.numpy as jnp
from jax import lax
from jax.experimental import pallas as pl
from jax.experimental.pallas import tpu as pltpu
from jax.sharding import PartitionSpec as P

LANES = 128
SUB = 32
F32 = jnp.float32
BF16 = jnp.bfloat16
EXACT = lax.Precision.HIGHEST
VMEM_LIMIT = 40 * 1024 * 1024
PARAMS = pltpu.CompilerParams(vmem_limit_bytes=VMEM_LIMIT)


def iota(shape, axis):
    return lax.broadcasted_iota(jnp.int32, shape, axis)


def over(value, size):
    return lax.shift_right_logical(value, size.bit_length() - 1)


def within(value, size):
    return lax.bitwise_and(value, size - 1)


def mxu(left, right):
    return jnp.dot(left, right, preferred_element_type=F32)


def mxu_t(left, right):
    return lax.dot_general(left, right, (((1,), (1,)), ((), ())), preferred_element_type=F32)


def exact_dot(left, right):
    return jnp.dot(left, right, precision=EXACT, preferred_element_type=F32)


def gate(left, right):
    return (left.astype(F32) * right.astype(F32)).astype(BF16)


def reversal(size):
    return jnp.where(iota((size, size), 0) + iota((size, size), 1) == size - 1, 1.0, 0.0).astype(BF16)


def split(value, pieces):
    parts = []
    for _ in range(pieces):
        parts.append(value.astype(BF16))
        value = value - parts[-1].astype(F32)
    return jnp.concatenate(parts, axis=0)


def join(stacked, rows):
    total = stacked[:rows].astype(F32)
    for start in range(rows, stacked.shape[0], rows):
        total = total + stacked[start : start + rows].astype(F32)
    return total


def flat_rows(table, poles):
    table = table.T
    groups = table.shape[0]
    per_row = LANES // poles
    spread = jnp.where(iota((poles, LANES), 0) == within(iota((poles, LANES), 1), poles), 1.0, 0.0)
    wide = exact_dot(table, spread)
    keep = within(iota((groups, LANES), 0), per_row) == over(iota((groups, LANES), 1), poles)
    wide = jnp.where(keep, wide, 0.0)
    return jnp.sum(wide.reshape(groups // per_row, per_row, LANES), axis=1)


def members(groups, first, span, width):
    return jnp.where(iota((groups, width), 0) == first + over(iota((groups, width), 1), span), 1.0, 0.0).astype(BF16)


def shard_start(groups):
    return pl.multiple_of(lax.axis_index("ch") * groups, LANES)


def states_kernel(logs_ref, res_ref, gated_ref, dgate_ref, msg_ref, pair_ref, rows_ref, rates_ref, skip_ref,
                  *, group, poles, steps):
    tokens, _ = gated_ref.shape
    per_block = LANES // group
    blocks, _, _ = rates_ref.shape
    groups = blocks * per_block
    inner = blocks // steps
    subs = tokens // SUB
    lag_width = per_block * SUB

    first = shard_start(groups)
    logs = logs_ref[:, pl.ds(first, groups)]
    rows_ref[0] = jnp.exp(flat_rows(logs, poles))
    rows_ref[1] = flat_rows(res_ref[:, pl.ds(first, groups)], poles)
    pieces = split(logs, 3).astype(F32)
    spread = jnp.concatenate(
        [members(groups, 0, SUB, lag_width), members(groups, 0, group, LANES)], axis=1
    )

    flip = reversal(tokens)
    lag = (SUB - 1 - within(iota((poles, lag_width), 1), SUB)).astype(F32)
    wide_group = over(within(iota((SUB, 2 * LANES), 1), LANES), group)
    causal = iota((SUB, lag_width), 0) + within(iota((SUB, lag_width), 1), SUB) <= SUB - 1

    def body(step, sums):
        for j in range(inner):
            block = step * inner + j
            cut = pl.ds(pl.multiple_of(block * LANES, LANES), LANES)
            gated, dgate = gated_ref[:, cut], dgate_ref[:, cut]
            skip = jnp.sum(gated.astype(F32) * dgate.astype(F32), axis=0, keepdims=True)
            skip_ref[pl.ds(block, 1), :] = skip
            turned = mxu(flip, dgate).astype(BF16)
            pair = jnp.concatenate([gated, turned], axis=1)
            pair_ref[:, pl.ds(pl.multiple_of(2 * block * LANES, LANES), 2 * LANES)] = pair

            turned_pieces = pltpu.roll(pieces, groups - block * per_block, 1).astype(BF16)
            rates = jnp.exp(join(mxu(turned_pieces, spread), poles))
            lag_rate, rate = rates[:, :lag_width], rates[:, lag_width:]
            rates_ref[block] = rate
            table = jnp.exp(-lag_rate * lag)
            moment_table = table * lag
            tables = jnp.concatenate([table, moment_table], axis=0).astype(BF16)

            found, outer = [], jnp.zeros((SUB, lag_width), F32)
            for k in range(subs):
                part = pair[k * SUB : (k + 1) * SUB]
                stack = jnp.concatenate(
                    [jnp.where(wide_group == g, part, jnp.zeros_like(part)) for g in range(per_block)], axis=0
                )
                found.append(mxu(tables, stack))
                mate = turned[(subs - 1 - k) * SUB : (subs - k) * SUB]
                outer = outer + mxu_t(mate, stack[:, :LANES])
            outer = jnp.where(causal, outer, 0.0)
            outer = pltpu.roll(outer, 0, 1, stride=1, stride_axis=0)
            lags = jnp.sum(outer, axis=0, keepdims=True)

            once = jnp.exp(-rate)
            decay = jnp.exp(-rate * SUB)
            decay = jnp.concatenate([decay, decay], axis=1)
            state = jnp.zeros((poles, 2 * LANES), F32)
            moment = state
            cross_res = jnp.zeros((poles, LANES), F32)
            cross_mom = cross_res
            for k in range(subs):
                back = found[subs - 1 - k][:, LANES:]
                held, held_moment = state[:, :LANES], moment[:, :LANES]
                cross_res = cross_res + back[:poles] * held
                cross_mom = cross_mom + back[poles:] * held + back[:poles] * (held_moment + held)
                moment = decay * (moment + SUB * state) + found[k][poles:]
                state = decay * state + found[k][:poles]
            out = jnp.concatenate(
                [state[:, :LANES], state[:, LANES:], moment[:, :LANES], moment[:, LANES:]], axis=0
            )
            msg_ref[pl.ds(pl.multiple_of(block * 4 * poles, 16), 4 * poles), :] = out.astype(BF16)
            near = jnp.concatenate([lags * table, lags * moment_table], axis=0)
            far = jnp.concatenate([once * cross_res, once * cross_mom], axis=0)
            terms = split(jnp.concatenate([near, far], axis=1), 2)
            sums = sums + pltpu.roll(join(mxu_t(terms, spread), 2 * poles), block * per_block, 1)
        return sums

    sums = lax.fori_loop(0, steps, body, jnp.zeros((2 * poles, groups), F32))
    tail = blocks * 4 * poles
    msg_ref[tail : tail + 4 * poles, :] = split(sums, 2)
    msg_ref[tail + 4 * poles :, :] = split(skip_ref[...], 2)


def conv_kernel(rows_ref, skip_ref, pair_ref, conv_ref, *, group, poles, steps):
    tokens, width = pair_ref.shape
    per_block = LANES // group
    all_blocks = rows_ref.shape[1]
    blocks = all_blocks // steps
    first = lax.axis_index("ch") * all_blocks
    back_pos = (tokens - 1 - iota((tokens, LANES), 0)).astype(F32)
    wide_group = over(within(iota((tokens, 2 * LANES), 1), LANES), group)
    causal = iota((tokens, tokens), 0) >= iota((tokens, tokens), 1)
    @pl.loop(0, steps)
    def _(step):
        for j in range(blocks):
            here = step * blocks + j
            cut = pl.ds(pl.multiple_of(2 * here * LANES, LANES), 2 * LANES)
            pair = pair_ref[:, cut]
            rate = rows_ref[0, pl.ds(here, 1), :]
            res = rows_ref[1, pl.ds(here, 1), :]
            table = (res * jnp.exp(-rate * back_pos)).T
            left, right = [], []
            for g in range(per_block):
                taps = jnp.sum(table[g * poles : (g + 1) * poles], axis=0, keepdims=True)
                base = pltpu.roll(jnp.broadcast_to(taps, (8, tokens)), 1, 1, stride=1, stride_axis=0)
                rolled = [base] + [pltpu.roll(base, 8 * a, 1) for a in range(1, tokens // 8)]
                left.append(jnp.where(causal, jnp.concatenate(rolled, axis=0), 0.0).astype(BF16))
                right.append(jnp.where(wide_group == g, pair, jnp.zeros_like(pair)))
            total = mxu(jnp.concatenate(left, axis=1), jnp.concatenate(right, axis=0))
            gain = skip_ref[pl.ds(first + here, 1), :]
            conv_ref[:, cut] = total + jnp.concatenate([gain, gain], axis=1) * pair.astype(F32)


def combine_kernel(*refs, level, levels, group, poles, tokens):
    last = level == levels - 1
    refs = list(refs)
    rates_ref, own_ref, got_ref = refs[:3]
    rest = refs[3:]
    held_ref = rest.pop(0) if level else None
    if level == 1:
        rest.pop(0)
    if last:
        logs_ref, res_ref = rest.pop(0), rest.pop(0)
    slim_ref = rest.pop() if level == levels - 2 else None
    out_ref, new_held_ref = rest
    blocks = rates_ref.shape[0]
    groups = blocks * (LANES // group)
    me = lax.axis_index("ctx")
    is_right = lax.rem(lax.shift_right_logical(me, level), 2) == 1
    before = lax.rem(me, 2**level)
    gap_left = (tokens * before).astype(F32)
    gap_right = (tokens * (2**level - 1 - before)).astype(F32)
    span = float(tokens * 2**level)
    next_right = lax.rem(lax.shift_right_logical(me, level + 1), 2) == 1
    own_rows = 4 * poles
    got_rows = 2 * poles if last else 4 * poles
    slim_rows = 2 * poles
    sums = jnp.zeros((4 * poles, groups), F32)
    for b in range(blocks):
        rate = rates_ref[b]
        own = own_ref[b * own_rows : (b + 1) * own_rows].astype(F32)
        got = got_ref[b * got_rows : (b + 1) * got_rows].astype(F32)
        own_f, own_b, own_fm, own_bm = (own[n * poles : (n + 1) * poles] for n in range(4))
        if last:
            got_f = got_b = got[:poles]
            got_fm = got_bm = got[poles:]
        else:
            got_f, got_b, got_fm, got_bm = (got[n * poles : (n + 1) * poles] for n in range(4))
        left_f = jnp.where(is_right, got_f, own_f)
        left_fm = jnp.where(is_right, got_fm, own_fm)
        right_b = jnp.where(is_right, own_b, got_b)
        right_bm = jnp.where(is_right, own_bm, got_bm)
        once = jnp.exp(-rate)
        cross_res = once * (right_b * left_f)
        cross_mom = once * (right_bm * left_f + right_b * (left_fm + left_f))
        terms = split(jnp.concatenate([cross_res, cross_mom], axis=0), 2)
        sums = sums + mxu_t(terms, members(groups, b * (LANES // group), group, LANES))
        if level:
            hold = held_ref[b]
        else:
            hold = jnp.zeros((2 * poles, LANES), F32)
        carry = jnp.exp(-rate * jnp.where(is_right, gap_left, gap_right)) * jnp.where(is_right, left_f, right_b)
        zero = jnp.zeros_like(carry)
        hold = hold + jnp.concatenate(
            [jnp.where(is_right, carry, zero), jnp.where(is_right, zero, carry)], axis=0
        )
        new_held_ref[b] = hold.astype(new_held_ref.dtype)
        if not last:
            right_f = jnp.where(is_right, own_f, got_f)
            right_fm = jnp.where(is_right, own_fm, got_fm)
            left_b = jnp.where(is_right, got_b, own_b)
            left_bm = jnp.where(is_right, got_bm, own_bm)
            decay = jnp.exp(-rate * span)
            new = [
                decay * left_f + right_f,
                left_b + decay * right_b,
                decay * (left_fm + span * left_f) + right_fm,
                left_bm + decay * (right_bm + span * right_b),
            ]
            out_ref[b * own_rows : (b + 1) * own_rows, :] = jnp.concatenate(new, axis=0).astype(BF16)
            if slim_ref is not None:
                chosen = jnp.concatenate(
                    [jnp.where(next_right, new[1], new[0]), jnp.where(next_right, new[3], new[2])], axis=0
                )
                slim_ref[b * slim_rows : (b + 1) * slim_rows, :] = chosen.astype(BF16)
    own_tail, got_tail = blocks * own_rows, blocks * got_rows
    total = (
        join(sums, 2 * poles)
        + join(own_ref[own_tail : own_tail + 4 * poles], 2 * poles)
        + join(got_ref[got_tail : got_tail + 4 * poles], 2 * poles)
    )
    skip = join(own_ref[own_tail + 4 * poles :], blocks) + join(got_ref[got_tail + 4 * poles :], blocks)
    if last:
        start = shard_start(groups)
        rate = jnp.exp(logs_ref[:, pl.ds(start, groups)])
        res = res_ref[:, pl.ds(start, groups)]
        length = 2 * span
        out_ref[:poles, :] = total[:poles] / length
        out_ref[poles : 2 * poles, :] = -rate * res * total[poles:] / math.sqrt(length)
        out_ref[2 * poles :, :] = skip / math.sqrt(length)
    else:
        rests = jnp.concatenate([split(total, 2), split(skip, 2)], axis=0)
        out_ref[own_tail:, :] = rests
        if slim_ref is not None:
            slim_ref[blocks * slim_rows :, :] = rests


def output_kernel(rows_ref, conv_ref, held_ref, k_ref, v_ref, c_ref, gq_ref, gk_ref, gv_ref, *, group, poles):
    tokens, width = gq_ref.shape
    per_block = LANES // group
    step = pl.program_id(0)
    blocks = width // LANES
    flip = reversal(tokens)
    ahead = (1 + iota((tokens, LANES), 0)).astype(F32)
    wide_group = over(within(iota((poles, 2 * LANES), 1), LANES), group)
    for j in range(blocks):
        cut = slice(j * LANES, (j + 1) * LANES)
        here = step * blocks + j
        wide = pl.ds(pl.multiple_of(here * LANES, LANES), LANES)
        both = pl.ds(pl.multiple_of(2 * here * LANES, LANES), 2 * LANES)
        rate = rows_ref[0, pl.ds(here, 1), :]
        res = rows_ref[1, pl.ds(here, 1), :]
        table = (res * jnp.exp(-rate * ahead)).astype(BF16)
        held = held_ref[here]
        states = jnp.concatenate([held[:poles], held[poles:]], axis=1)
        stack = jnp.concatenate(
            [jnp.where(wide_group == g, states, jnp.zeros_like(states)) for g in range(per_block)], axis=0
        )
        total = (conv_ref[:, both] + mxu(table, stack)).astype(BF16)
        flow = mxu(flip, total[:, LANES:])
        gq_ref[:, cut] = (c_ref[:, wide].astype(F32) * total[:, :LANES].astype(F32)).astype(BF16)
        gk_ref[:, cut] = (flow * v_ref[:, wide].astype(F32)).astype(BF16)
        gv_ref[:, cut] = (flow * k_ref[:, wide].astype(F32)).astype(BF16)


def assemble_kernel(*refs, shards, poles):
    slots = refs[:shards]
    res_ref, log_ref, skip_ref = refs[shards:]
    me = lax.axis_index("ch")
    groups = slots[0].shape[1]
    rows = slots[0].shape[0] - 2 * poles
    for shift, slot in enumerate(slots):
        source = lax.rem(me - shift + shards, shards)
        cut = pl.ds(pl.multiple_of(source * groups, LANES), groups)
        res_ref[:, cut] = slot[:poles, :]
        log_ref[:, cut] = slot[poles : 2 * poles, :]
        skip_ref[pl.ds(pl.multiple_of(source * rows, 8), rows), :] = slot[2 * poles :, :]


def local(queries, key_input, value_input, cotangent, residues, log_rates, skip_gain):
    tokens, width = queries.shape
    parts = lax.axis_size("ctx")
    shards = lax.axis_size("ch")
    levels = parts.bit_length() - 1
    all_groups, poles = residues.shape
    groups = all_groups // shards
    group = width // groups
    blocks = width // LANES
    steps = 4
    step_width = width // steps
    sizes = dict(group=group, poles=poles)
    tail = 4 * poles + 2 * blocks

    vmem = pl.BlockSpec(memory_space=pltpu.VMEM)
    log_rates, residues = log_rates.T, residues.T
    main = pl.BlockSpec((tokens, step_width), lambda i: (0, i))

    gated, dgate = gate(key_input, value_input), gate(cotangent, queries)
    message, pair, rows, rates = pl.pallas_call(
        lambda *refs: states_kernel(*refs, steps=steps, **sizes),
        in_specs=[vmem] * 4,
        out_specs=[vmem] * 4,
        out_shape=[
            jax.ShapeDtypeStruct((blocks * 4 * poles + tail, LANES), BF16),
            jax.ShapeDtypeStruct((tokens, 2 * width), BF16),
            jax.ShapeDtypeStruct((2, blocks, LANES), F32),
            jax.ShapeDtypeStruct((blocks, poles, LANES), F32),
        ],
        scratch_shapes=[pltpu.VMEM((blocks, LANES), F32)],
        compiler_params=PARAMS,
        name="states",
    )(log_rates, residues, gated, dgate)

    skip_rows = skip_gain.reshape(-1, LANES)
    conv = pl.pallas_call(
        lambda *refs: conv_kernel(*refs, steps=steps, **sizes),
        in_specs=[vmem] * 3,
        out_specs=vmem,
        out_shape=jax.ShapeDtypeStruct((tokens, 2 * width), F32),
        compiler_params=PARAMS,
        cost_estimate=pl.CostEstimate(
            flops=16 * tokens * tokens * width, bytes_accessed=12 * tokens * width, transcendentals=tokens * width
        ),
        name="conv",
    )(rows, skip_rows, pair)

    held, outgoing = None, message
    for level in range(levels):
        last = level == levels - 1
        got = lax.ppermute(outgoing, "ctx", [(i, i ^ (1 << level)) for i in range(parts)])
        operands = [rates, message, got]
        if level:
            operands.append(held)
        if level == 1:
            operands.append(conv)
        if last:
            operands += [log_rates, residues]
            out = jax.ShapeDtypeStruct((2 * poles + blocks, LANES), F32)
        else:
            out = jax.ShapeDtypeStruct(message.shape, BF16)
        outs = [out, jax.ShapeDtypeStruct((blocks, 2 * poles, LANES), BF16 if last else F32)]
        if level == levels - 2:
            outs.append(jax.ShapeDtypeStruct((blocks * 2 * poles + tail, LANES), BF16))
        message, held, *slim = pl.pallas_call(
            lambda *refs, level=level: combine_kernel(*refs, level=level, levels=levels, tokens=tokens, **sizes),
            in_specs=[pl.BlockSpec(memory_space=pl.ANY) if x is conv else vmem for x in operands],
            out_specs=[vmem] * len(outs),
            out_shape=outs,
            compiler_params=PARAMS,
            name="combine",
        )(*operands)
        outgoing = slim[0] if slim else message

    gathered = [message]
    for shift in range(1, shards):
        gathered.append(lax.ppermute(message, "ch", [(i, (i + shift) % shards) for i in range(shards)]))

    grad_query, grad_key, grad_value = pl.pallas_call(
        lambda *refs: output_kernel(*refs, **sizes),
        grid=(steps,),
        in_specs=[vmem] * 6,
        out_specs=[main, main, main],
        out_shape=[jax.ShapeDtypeStruct((tokens, width), BF16)] * 3,
        compiler_params=PARAMS,
        name="outputs",
    )(rows, conv, held, key_input, value_input, cotangent)

    grad_residue, grad_lograte, grad_skip = pl.pallas_call(
        lambda *refs: assemble_kernel(*refs, shards=shards, poles=poles),
        in_specs=[vmem] * shards,
        out_specs=[vmem] * 3,
        out_shape=[
            jax.ShapeDtypeStruct((poles, all_groups), F32),
            jax.ShapeDtypeStruct((poles, all_groups), F32),
            jax.ShapeDtypeStruct((shards * blocks, LANES), F32),
        ],
        compiler_params=PARAMS,
        name="assemble",
    )(*gathered)
    return (grad_query, grad_key, grad_value, grad_residue.T, grad_lograte.T, grad_skip.reshape(-1))


def solution(mesh):
    placed = (P("ctx", "ch"), P("ctx", "ch"), P("ctx", "ch"), P("ctx", "ch"), P(), P(), P())
    return jax.shard_map(
        local,
        mesh=mesh,
        in_specs=placed,
        out_specs=(P("ctx", "ch"), P("ctx", "ch"), P("ctx", "ch"), P(), P(), P()),
        check_vma=False,
    )
```

```python
import math

import jax
import jax.numpy as jnp
from jax import lax
from jax.experimental import pallas as pl
from jax.experimental.pallas import tpu as pltpu
from jax.sharding import PartitionSpec as P

LANES = 128
SUB = 32
F32 = jnp.float32
BF16 = jnp.bfloat16
EXACT = lax.Precision.HIGHEST
VMEM_LIMIT = 40 * 1024 * 1024
PARAMS = pltpu.CompilerParams(vmem_limit_bytes=VMEM_LIMIT)


def iota(shape, axis):
    return lax.broadcasted_iota(jnp.int32, shape, axis)


def over(value, size):
    return lax.shift_right_logical(value, size.bit_length() - 1)


def within(value, size):
    return lax.bitwise_and(value, size - 1)


def mxu(left, right):
    return jnp.dot(left, right, preferred_element_type=F32)


def mxu_t(left, right):
    return lax.dot_general(left, right, (((1,), (1,)), ((), ())), preferred_element_type=F32)


def exact_dot(left, right):
    return jnp.dot(left, right, precision=EXACT, preferred_element_type=F32)


def gate(left, right):
    return (left.astype(F32) * right.astype(F32)).astype(BF16)


def reversal(size):
    return jnp.where(iota((size, size), 0) + iota((size, size), 1) == size - 1, 1.0, 0.0).astype(BF16)


def split(value, pieces):
    parts = []
    for _ in range(pieces):
        parts.append(value.astype(BF16))
        value = value - parts[-1].astype(F32)
    return jnp.concatenate(parts, axis=0)


def join(stacked, rows):
    total = stacked[:rows].astype(F32)
    for start in range(rows, stacked.shape[0], rows):
        total = total + stacked[start : start + rows].astype(F32)
    return total


def flat_rows(table, poles):
    table = table.T
    groups = table.shape[0]
    per_row = LANES // poles
    spread = jnp.where(iota((poles, LANES), 0) == within(iota((poles, LANES), 1), poles), 1.0, 0.0)
    wide = exact_dot(table, spread)
    keep = within(iota((groups, LANES), 0), per_row) == over(iota((groups, LANES), 1), poles)
    wide = jnp.where(keep, wide, 0.0)
    return jnp.sum(wide.reshape(groups // per_row, per_row, LANES), axis=1)


def members(groups, first, span, width):
    return jnp.where(iota((groups, width), 0) == first + over(iota((groups, width), 1), span), 1.0, 0.0).astype(BF16)


def shard_start(groups):
    return pl.multiple_of(lax.axis_index("ch") * groups, LANES)


def pack_half(value, half):
    chosen = jnp.where(half > 0, pltpu.roll(value, LANES // 2, 1), value)
    high = chosen.astype(BF16).astype(F32)
    low = pltpu.roll(chosen - high, LANES // 2, 1)
    return jnp.where(iota(value.shape, 1) < LANES // 2, high, low).astype(BF16)


def open_half(packed):
    value = packed.astype(F32)
    return value + pltpu.roll(value, LANES // 2, 1)


def states_kernel(logs_ref, res_ref, gated_ref, dgate_ref, send_ref, keep_ref, turned_ref, rows_ref, rates_ref,
                  taps_ref, tables_ref, skip_ref, *, group, poles, inner):
    tokens, _ = gated_ref.shape
    per_block = LANES // group
    blocks, _, _ = rates_ref.shape
    half_blocks = blocks // 2
    groups = blocks * per_block
    subs = tokens // SUB
    lag_width = per_block * SUB
    step_groups = inner * per_block
    wide, lag_wide = inner * LANES, inner * lag_width
    core = lax.rem(lax.axis_index("ctx"), 2)

    first = shard_start(groups)
    logs = logs_ref[:, pl.ds(first, groups)]
    res = res_ref[:, pl.ds(first, groups)]
    rows_ref[0] = jnp.exp(flat_rows(logs, poles))
    rows_ref[1] = flat_rows(res, poles)
    pieces = jnp.concatenate([split(logs, 3), split(res, 3)], axis=0).astype(F32)
    spread = jnp.concatenate([members(groups, 0, SUB, lag_wide), members(groups, 0, group, wide)], axis=1)

    flip = reversal(tokens)
    lag = (SUB - 1 - within(iota((poles, lag_wide), 1), SUB)).astype(F32)
    wide_group = over(within(iota((SUB, 2 * LANES), 1), LANES), group)
    causal = iota((SUB, lag_wide), 0) + within(iota((SUB, lag_wide), 1), SUB) <= SUB - 1

    sums = jnp.zeros((2 * poles, groups), F32)
    for turn, msg_ref in enumerate((send_ref, keep_ref)):
        base = lax.rem(core + 1 + turn, 2) * half_blocks

        def body(step, sums, base=base, msg_ref=msg_ref):
            start = base + step * inner
            cut = pl.ds(pl.multiple_of(start * LANES, LANES), wide)
            gated, dgate = gated_ref[:, cut], dgate_ref[:, cut]
            turned = mxu(flip, dgate).astype(BF16)
            turned_ref[:, cut] = turned
            skip = jnp.sum(gated.astype(F32) * dgate.astype(F32), axis=0, keepdims=True)
            for j in range(inner):
                skip_ref[pl.ds(start + j, 1), :] = skip[:, j * LANES : (j + 1) * LANES]

            moved = pltpu.roll(pieces, groups - start * per_block, 1).astype(BF16)
            spreads = mxu(moved, spread)
            rates = jnp.exp(join(spreads[: 3 * poles], poles))
            res_lag = join(spreads[3 * poles :, :lag_wide], poles)
            lag_rate, rate = rates[:, :lag_wide], rates[:, lag_wide:]
            table = jnp.exp(-lag_rate * lag)
            moment_table = table * lag
            tables = jnp.concatenate([table, moment_table], axis=0).astype(BF16)
            taps = jnp.sum(res_lag * table, axis=0, keepdims=True)
            for j in range(inner):
                lanes = slice(j * lag_width, (j + 1) * lag_width)
                rates_ref[start + j] = rate[:, j * LANES : (j + 1) * LANES]
                taps_ref[pl.ds(start + j, 1), :] = taps[:, lanes]
                tables_ref[start + j] = tables[:poles, lanes]

            found = [[] for _ in range(subs)]
            outers = []
            for j in range(inner):
                lanes = slice(j * LANES, (j + 1) * LANES)
                mine = tables[:, j * lag_width : (j + 1) * lag_width]
                outer = None
                for k in range(subs):
                    part = jnp.concatenate(
                        [gated[k * SUB : (k + 1) * SUB, lanes], turned[k * SUB : (k + 1) * SUB, lanes]], axis=1
                    )
                    stack = jnp.concatenate(
                        [jnp.where(wide_group == g, part, jnp.zeros_like(part)) for g in range(per_block)], axis=0
                    )
                    found[k].append(mxu(mine, stack))
                    mate = turned[(subs - 1 - k) * SUB : (subs - k) * SUB, lanes]
                    term = mxu_t(mate, stack[:, :LANES])
                    outer = term if outer is None else outer + term
                outers.append(outer)
            outer = jnp.where(causal, jnp.concatenate(outers, axis=1), 0.0)
            outer = pltpu.roll(outer, 0, 1, stride=1, stride_axis=0)
            lags = jnp.sum(outer, axis=0, keepdims=True)

            ahead = [jnp.concatenate([f[:, :LANES] for f in found[k]], axis=1) for k in range(subs)]
            behind = [jnp.concatenate([f[:, LANES:] for f in found[k]], axis=1) for k in range(subs)]
            once = jnp.exp(-rate)
            decay = jnp.exp(-rate * SUB)
            state = jnp.zeros((poles, wide), F32)
            moment, back, back_moment, cross_res, cross_mom = state, state, state, state, state
            for k in range(subs):
                other = behind[subs - 1 - k]
                cross_res = cross_res + other[:poles] * state
                cross_mom = cross_mom + other[poles:] * state + other[:poles] * (moment + state)
                moment = decay * (moment + SUB * state) + ahead[k][poles:]
                state = decay * state + ahead[k][:poles]
                back_moment = decay * (back_moment + SUB * back) + behind[k][poles:]
                back = decay * back + behind[k][:poles]
            out = jnp.concatenate([state, back, moment, back_moment], axis=0).astype(BF16)
            for j in range(inner):
                row = pl.multiple_of((step * inner + j) * 4 * poles, 4 * poles)
                msg_ref[pl.ds(row, 4 * poles), :] = out[:, j * LANES : (j + 1) * LANES]
            near = jnp.concatenate([lags * table, lags * moment_table], axis=0)
            far = jnp.concatenate([once * cross_res, once * cross_mom], axis=0)
            terms = split(jnp.concatenate([near, far], axis=1), 2)
            return sums + pltpu.roll(join(mxu_t(terms, spread), 2 * poles), start * per_block, 1)

        sums = lax.fori_loop(0, half_blocks // inner, body, sums)
    tail = half_blocks * 4 * poles
    for turn, msg_ref in enumerate((send_ref, keep_ref)):
        half = lax.rem(core + 1 + turn, 2)
        msg_ref[tail : tail + 2 * poles, :] = pack_half(sums, half)
        skip = skip_ref[pl.ds(pl.multiple_of(half * half_blocks, 8), half_blocks), :]
        msg_ref[tail + 2 * poles :, :] = split(skip, 2)


def conv_kernel(rows_ref, skip_ref, rates_ref, taps_ref, tables_ref, gated_ref, turned_ref, conv_ref,
                *, group, poles, inner):
    tokens, _ = gated_ref.shape
    per_block = LANES // group
    blocks, _, _ = rates_ref.shape
    subs = tokens // SUB
    lag_width = per_block * SUB
    first = lax.axis_index("ch") * blocks
    lead = (1 + iota((SUB, LANES), 0)).astype(F32)
    wide_group = over(within(iota((SUB, 2 * LANES), 1), LANES), group)
    state_group = over(within(iota((poles, 2 * LANES), 1), LANES), group)
    causal = iota((SUB, lag_width), 0) >= within(iota((SUB, lag_width), 1), SUB)

    def body(step, carry):
        start = step * inner
        lefts, lead_tables, decays, pairs, gains = [], [], [], [], []
        for j in range(inner):
            here = start + j
            taps = jnp.broadcast_to(taps_ref[pl.ds(here, 1), :], (SUB, lag_width))
            taps = pltpu.roll(taps, lag_width - SUB + 1, 1, stride=1, stride_axis=0)
            taps = jnp.where(causal, taps, 0.0).astype(BF16)
            lefts.append(jnp.concatenate([taps, tables_ref[here]], axis=0))
            rate = rows_ref[0, pl.ds(here, 1), :]
            res = rows_ref[1, pl.ds(here, 1), :]
            lead_tables.append((res * jnp.exp(-rate * lead)).astype(BF16))
            decay = jnp.exp(-rates_ref[here] * SUB)
            decays.append(jnp.concatenate([decay, decay], axis=1))
            cut = pl.ds(pl.multiple_of(here * LANES, LANES), LANES)
            pairs.append(jnp.concatenate([gated_ref[:, cut], turned_ref[:, cut]], axis=1))
            gain = skip_ref[pl.ds(first + here, 1), :]
            gains.append(jnp.concatenate([gain, gain], axis=1))
        states = [jnp.zeros((poles, 2 * LANES), F32)] * inner
        totals = [[] for _ in range(inner)]
        for k in range(subs):
            rows = slice(k * SUB, (k + 1) * SUB)
            found = []
            for j in range(inner):
                part = pairs[j][rows]
                stack = [jnp.where(wide_group == g, part, jnp.zeros_like(part)) for g in range(per_block)]
                found.append(mxu(lefts[j], jnp.concatenate(stack, axis=0)))
            for j in range(inner):
                total = found[j][:SUB] + gains[j] * pairs[j][rows].astype(F32)
                if k:
                    held = states[j].astype(BF16)
                    stack = [jnp.where(state_group == g, held, jnp.zeros_like(held)) for g in range(per_block)]
                    total = total + mxu(lead_tables[j], jnp.concatenate(stack, axis=0))
                totals[j].append(total)
            states = [decays[j] * states[j] + found[j][SUB:] for j in range(inner)]
        for j in range(inner):
            cut = pl.ds(pl.multiple_of(2 * (start + j) * LANES, LANES), 2 * LANES)
            conv_ref[:, cut] = jnp.concatenate(totals[j], axis=0)
        return carry

    lax.fori_loop(0, blocks // inner, body, 0)


def combine_kernel(*refs, level, levels, group, poles, tokens):
    last = level == levels - 1
    refs = list(refs)
    rates_ref, own_ref, got_ref = refs[:3]
    rest = refs[3:]
    near_ref = held_ref = slim_ref = None
    if level == 0:
        out_ref, near_ref = rest[:2]
        rest = rest[2:]
    else:
        if level > 1:
            held_ref = rest.pop(0)
        else:
            rest.pop(0)
        if last:
            near_ref, logs_ref, res_ref = rest[:3]
            mine_ref, out_ref = rest[3:]
        else:
            out_ref, new_held_ref = rest[:2]
            rest = rest[2:]
    if level == levels - 2:
        slim_ref = rest[0]
    all_blocks = rates_ref.shape[0]
    blocks = all_blocks // 2
    per_block = LANES // group
    groups = all_blocks * per_block
    me = lax.axis_index("ctx")
    core = lax.rem(me, 2)
    is_right = lax.rem(lax.shift_right_logical(me, level), 2) == 1
    before = lax.rem(me, 2**level) - (core if level else 0)
    gap_left = (tokens * before).astype(F32)
    gap_right = (tokens * (2**level - 2 - before)).astype(F32)
    gap = jnp.where(is_right, gap_left, gap_right)
    span = float(tokens * 2**level)
    next_right = lax.rem(lax.shift_right_logical(me, level + 1), 2) == 1
    own_rows = 4 * poles
    got_rows = 2 * poles if last else 4 * poles
    slim_rows = 2 * poles

    def thirds(value):
        return [value[n * poles : (n + 1) * poles] for n in range(4)]

    wide_terms = []
    for b in range(blocks):
        rate = rates_ref[core * blocks + b]
        own_f, own_b, own_fm, own_bm = thirds(own_ref[b * own_rows : (b + 1) * own_rows].astype(F32))
        got = got_ref[b * got_rows : (b + 1) * got_rows].astype(F32)
        if last:
            got_f = got_b = got[:poles]
            got_fm = got_bm = got[poles:]
        else:
            got_f, got_b, got_fm, got_bm = thirds(got)
        left_f = jnp.where(is_right, got_f, own_f)
        left_fm = jnp.where(is_right, got_fm, own_fm)
        right_b = jnp.where(is_right, own_b, got_b)
        right_bm = jnp.where(is_right, own_bm, got_bm)
        once = jnp.exp(-rate)
        cross_res = once * (right_b * left_f)
        cross_mom = once * (right_bm * left_f + right_b * (left_fm + left_f))
        wide_terms.append(split(jnp.concatenate([cross_res, cross_mom], axis=0), 2))
        if level == 0:
            near_ref[b] = jnp.concatenate([left_f, right_b], axis=0)
        else:
            carry = jnp.exp(-rate * gap) * jnp.where(is_right, left_f, right_b)
            zero = jnp.zeros_like(carry)
            hold = jnp.concatenate([jnp.where(is_right, carry, zero), jnp.where(is_right, zero, carry)], axis=0)
            if level > 1:
                hold = hold + held_ref[b]
            if last:
                step = jnp.exp(-rate * tokens)
                near = near_ref[b]
                first_core = jnp.concatenate([hold[:poles], near[poles:] + step * hold[poles:]], axis=0)
                second_core = jnp.concatenate([near[:poles] + step * hold[:poles], hold[poles:]], axis=0)
                mine_ref[b] = jnp.where(core > 0, second_core, first_core).astype(BF16)
                out_ref[b * 2 * poles : (b + 1) * 2 * poles, :] = jnp.where(
                    core > 0, first_core, second_core
                ).astype(BF16)
            else:
                new_held_ref[b] = hold
        if not last:
            right_f = jnp.where(is_right, own_f, got_f)
            right_fm = jnp.where(is_right, own_fm, got_fm)
            left_b = jnp.where(is_right, got_b, own_b)
            left_bm = jnp.where(is_right, got_bm, own_bm)
            decay = jnp.exp(-rate * span)
            new = [
                decay * left_f + right_f,
                left_b + decay * right_b,
                decay * (left_fm + span * left_f) + right_fm,
                left_bm + decay * (right_bm + span * right_b),
            ]
            out_ref[b * own_rows : (b + 1) * own_rows, :] = jnp.concatenate(new, axis=0).astype(BF16)
            if slim_ref is not None:
                chosen = jnp.concatenate(
                    [jnp.where(next_right, new[1], new[0]), jnp.where(next_right, new[3], new[2])], axis=0
                )
                slim_ref[b * slim_rows : (b + 1) * slim_rows, :] = chosen.astype(BF16)
    own_tail, got_tail = blocks * own_rows, blocks * got_rows
    cross = mxu_t(jnp.concatenate(wide_terms, axis=1), members(groups, 0, group, blocks * LANES))
    total = (
        join(cross, 2 * poles)
        + open_half(own_ref[own_tail : own_tail + 2 * poles, :])
        + open_half(got_ref[got_tail : got_tail + 2 * poles, :])
    )
    skip = join(own_ref[own_tail + 2 * poles :, :], blocks) + join(got_ref[got_tail + 2 * poles :, :], blocks)
    if last:
        start = shard_start(groups)
        rate = jnp.exp(logs_ref[:, pl.ds(start, groups)])
        factor = -rate * res_ref[:, pl.ds(start, groups)]
        factor = jnp.where(core > 0, pltpu.roll(factor, LANES // 2, 1), factor)
        length = 2 * span
        total = jnp.concatenate(
            [total[:poles] / length, factor * total[poles:] / math.sqrt(length)], axis=0
        )
        skip = skip / math.sqrt(length)
    rests = jnp.concatenate([pack_half(total, 0), split(skip, 2)], axis=0)
    if last:
        out_ref[blocks * 2 * poles :, :] = rests
    else:
        out_ref[own_tail:, :] = rests
        if slim_ref is not None:
            slim_ref[blocks * slim_rows :, :] = rests


def merge_kernel(own_ref, got_ref, out_ref, *, poles):
    core = lax.rem(lax.axis_index("ctx"), 2)
    blocks = (out_ref.shape[0] - 2 * poles) // 2
    rows = own_ref.shape[0] - 2 * poles - 2 * blocks
    own, got = open_half(own_ref[rows : rows + 2 * poles, :]), open_half(got_ref[rows : rows + 2 * poles, :])
    left, right = jnp.where(core > 0, got, own), jnp.where(core > 0, own, got)
    out_ref[: 2 * poles, :] = jnp.where(iota(own.shape, 1) < LANES // 2, left, pltpu.roll(right, LANES // 2, 1))
    own, got = join(own_ref[rows + 2 * poles :, :], blocks), join(got_ref[rows + 2 * poles :, :], blocks)
    out_ref[2 * poles : 2 * poles + blocks, :] = jnp.where(core > 0, got, own)
    out_ref[2 * poles + blocks :, :] = jnp.where(core > 0, own, got)


def output_kernel(rows_ref, conv_ref, mine_ref, got_ref, k_ref, v_ref, c_ref, gq_ref, gk_ref, gv_ref,
                  *, group, poles):
    tokens, width = gq_ref.shape
    per_block = LANES // group
    step = pl.program_id(0)
    inner = width // LANES
    half_blocks = mine_ref.shape[0]
    core = lax.rem(lax.axis_index("ctx"), 2)
    flip = reversal(tokens)
    ahead = (1 + iota((tokens, LANES), 0)).astype(F32)
    state_group = over(within(iota((poles, 2 * LANES), 1), LANES), group)
    start = step * inner
    is_mine = over(start, half_blocks) == core
    totals = []
    for j in range(inner):
        here = start + j
        rate = rows_ref[0, pl.ds(here, 1), :]
        res = rows_ref[1, pl.ds(here, 1), :]
        table = (res * jnp.exp(-rate * ahead)).astype(BF16)
        place = within(here, half_blocks)
        held = jnp.where(
            is_mine, mine_ref[place], got_ref[pl.ds(pl.multiple_of(place * 2 * poles, 2 * poles), 2 * poles), :]
        )
        states = jnp.concatenate([held[:poles], held[poles:]], axis=1)
        stack = jnp.concatenate(
            [jnp.where(state_group == g, states, jnp.zeros_like(states)) for g in range(per_block)], axis=0
        )
        both = pl.ds(pl.multiple_of(2 * here * LANES, LANES), 2 * LANES)
        totals.append((conv_ref[:, both] + mxu(table, stack)).astype(BF16))
    hidden = jnp.concatenate([t[:, :LANES] for t in totals], axis=1)
    flow = mxu(flip, jnp.concatenate([t[:, LANES:] for t in totals], axis=1))
    cut = pl.ds(pl.multiple_of(start * LANES, LANES), width)
    gq_ref[...] = (c_ref[:, cut].astype(F32) * hidden.astype(F32)).astype(BF16)
    gk_ref[...] = (flow * v_ref[:, cut].astype(F32)).astype(BF16)
    gv_ref[...] = (flow * k_ref[:, cut].astype(F32)).astype(BF16)


def assemble_kernel(*refs, shards, poles):
    slots = refs[:shards]
    res_ref, log_ref, skip_ref = refs[shards:]
    me = lax.axis_index("ch")
    groups = slots[0].shape[1]
    rows = slots[0].shape[0] - 2 * poles
    for shift, slot in enumerate(slots):
        source = lax.rem(me - shift + shards, shards)
        cut = pl.ds(pl.multiple_of(source * groups, LANES), groups)
        res_ref[:, cut] = slot[:poles, :]
        log_ref[:, cut] = slot[poles : 2 * poles, :]
        skip_ref[pl.ds(pl.multiple_of(source * rows, 8), rows), :] = slot[2 * poles :, :]


def local(queries, key_input, value_input, cotangent, residues, log_rates, skip_gain):
    tokens, width = queries.shape
    parts = lax.axis_size("ctx")
    shards = lax.axis_size("ch")
    levels = parts.bit_length() - 1
    all_groups, poles = residues.shape
    groups = all_groups // shards
    group = width // groups
    blocks = width // LANES
    inner = 4
    steps = blocks // inner
    half_blocks = blocks // 2
    lag_width = LANES // group * SUB
    sizes = dict(group=group, poles=poles)
    tail = 2 * poles + blocks
    full_rows, slim_rows = half_blocks * 4 * poles + tail, half_blocks * 2 * poles + tail

    vmem = pl.BlockSpec(memory_space=pltpu.VMEM)
    anywhere = pl.BlockSpec(memory_space=pl.ANY)
    log_rates, residues = log_rates.T, residues.T
    main = pl.BlockSpec((tokens, inner * LANES), lambda i: (0, i))

    def shape(*dims, dtype=F32):
        return jax.ShapeDtypeStruct(dims, dtype)

    def swap(value, level):
        return lax.ppermute(value, "ctx", [(i, i ^ (1 << level)) for i in range(parts)])

    gated, dgate = gate(key_input, value_input), gate(cotangent, queries)
    outgoing, message, turned, rows, rates, taps, tables = pl.pallas_call(
        lambda *refs: states_kernel(*refs, inner=inner, **sizes),
        in_specs=[vmem] * 4,
        out_specs=[vmem] * 7,
        out_shape=[
            shape(full_rows, LANES, dtype=BF16),
            shape(full_rows, LANES, dtype=BF16),
            shape(tokens, width, dtype=BF16),
            shape(2, blocks, LANES),
            shape(blocks, poles, LANES),
            shape(blocks, lag_width),
            shape(blocks, poles, lag_width, dtype=BF16),
        ],
        scratch_shapes=[pltpu.VMEM((blocks, LANES), F32)],
        compiler_params=PARAMS,
        name="states",
    )(log_rates, residues, gated, dgate)

    skip_rows = skip_gain.reshape(-1, LANES)
    conv = pl.pallas_call(
        lambda *refs: conv_kernel(*refs, inner=inner, **sizes),
        in_specs=[vmem] * 7,
        out_specs=vmem,
        out_shape=shape(tokens, 2 * width),
        compiler_params=PARAMS,
        cost_estimate=pl.CostEstimate(
            flops=16 * tokens * tokens * width, bytes_accessed=12 * tokens * width, transcendentals=tokens * width
        ),
        name="conv",
    )(rows, skip_rows, rates, taps, tables, gated, turned)

    held = near = None
    for level in range(levels):
        last = level == levels - 1
        got = swap(outgoing, level)
        operands, specs = [rates, message, got], [vmem] * 3
        if level == 1:
            operands.append(conv)
            specs.append(anywhere)
        elif level > 1:
            operands.append(held)
            specs.append(vmem)
        if last:
            operands += [near, log_rates, residues]
            specs += [vmem] * 3
            outs = [shape(half_blocks, 2 * poles, LANES, dtype=BF16), shape(slim_rows, LANES, dtype=BF16)]
        else:
            outs = [shape(full_rows, LANES, dtype=BF16), shape(half_blocks, 2 * poles, LANES)]
        if level == levels - 2:
            outs.append(shape(slim_rows, LANES, dtype=BF16))
        results = pl.pallas_call(
            lambda *refs, level=level: combine_kernel(*refs, level=level, levels=levels, tokens=tokens, **sizes),
            in_specs=specs,
            out_specs=[vmem] * len(outs),
            out_shape=outs,
            compiler_params=PARAMS,
            name="combine",
        )(*operands)
        if last:
            mine, outgoing = results
        else:
            message = results[0]
            outgoing = results[-1] if level == levels - 2 else message
            if level == 0:
                near = results[1]
            else:
                held = results[1]
    got = swap(outgoing, 0)
    merged = pl.pallas_call(
        lambda *refs: merge_kernel(*refs, poles=poles),
        in_specs=[vmem] * 2,
        out_specs=vmem,
        out_shape=shape(2 * poles + blocks, LANES),
        compiler_params=PARAMS,
        name="merge",
    )(outgoing, got)

    gathered = [merged]
    for shift in range(1, shards):
        gathered.append(lax.ppermute(merged, "ch", [(i, (i + shift) % shards) for i in range(shards)]))

    grad_query, grad_key, grad_value = pl.pallas_call(
        lambda *refs: output_kernel(*refs, **sizes),
        grid=(steps,),
        in_specs=[vmem] * 7,
        out_specs=[main, main, main],
        out_shape=[jax.ShapeDtypeStruct((tokens, width), BF16)] * 3,
        compiler_params=PARAMS,
        name="outputs",
    )(rows, conv, mine, got, key_input, value_input, cotangent)

    grad_residue, grad_lograte, grad_skip = pl.pallas_call(
        lambda *refs: assemble_kernel(*refs, shards=shards, poles=poles),
        in_specs=[vmem] * shards,
        out_specs=[vmem] * 3,
        out_shape=[
            jax.ShapeDtypeStruct((poles, all_groups), F32),
            jax.ShapeDtypeStruct((poles, all_groups), F32),
            jax.ShapeDtypeStruct((shards * blocks, LANES), F32),
        ],
        compiler_params=PARAMS,
        name="assemble",
    )(*gathered)
    return (grad_query, grad_key, grad_value, grad_residue.T, grad_lograte.T, grad_skip.reshape(-1))


def solution(mesh):
    placed = (P("ctx", "ch"), P("ctx", "ch"), P("ctx", "ch"), P("ctx", "ch"), P(), P(), P())
    return jax.shard_map(
        local,
        mesh=mesh,
        in_specs=placed,
        out_specs=(P("ctx", "ch"), P("ctx", "ch"), P("ctx", "ch"), P(), P(), P()),
        check_vma=False,
    )
```

```python
import math

import jax
import jax.numpy as jnp
from jax import lax
from jax.experimental import pallas as pl
from jax.experimental.pallas import tpu as pltpu
from jax.sharding import PartitionSpec as P

LANES = 128
SUB = 32
F32 = jnp.float32
BF16 = jnp.bfloat16
EXACT = lax.Precision.HIGHEST
VMEM_LIMIT = 40 * 1024 * 1024
PARAMS = pltpu.CompilerParams(vmem_limit_bytes=VMEM_LIMIT)


def iota(shape, axis):
    return lax.broadcasted_iota(jnp.int32, shape, axis)


def over(value, size):
    return lax.shift_right_logical(value, size.bit_length() - 1)


def within(value, size):
    return lax.bitwise_and(value, size - 1)


def mxu(left, right):
    return jnp.dot(left, right, preferred_element_type=F32)


def mxu_t(left, right):
    return lax.dot_general(left, right, (((1,), (1,)), ((), ())), preferred_element_type=F32)


def exact_dot(left, right):
    return jnp.dot(left, right, precision=EXACT, preferred_element_type=F32)


def gate(left, right):
    return (left.astype(F32) * right.astype(F32)).astype(BF16)


def reversal(size):
    return jnp.where(iota((size, size), 0) + iota((size, size), 1) == size - 1, 1.0, 0.0).astype(BF16)


def split(value, pieces):
    parts = []
    for _ in range(pieces):
        parts.append(value.astype(BF16))
        value = value - parts[-1].astype(F32)
    return jnp.concatenate(parts, axis=0)


def join(stacked, rows):
    total = stacked[:rows].astype(F32)
    for start in range(rows, stacked.shape[0], rows):
        total = total + stacked[start : start + rows].astype(F32)
    return total


def flat_rows(table, poles):
    table = table.T
    groups = table.shape[0]
    per_row = LANES // poles
    spread = jnp.where(iota((poles, LANES), 0) == within(iota((poles, LANES), 1), poles), 1.0, 0.0)
    wide = exact_dot(table, spread)
    keep = within(iota((groups, LANES), 0), per_row) == over(iota((groups, LANES), 1), poles)
    wide = jnp.where(keep, wide, 0.0)
    return jnp.sum(wide.reshape(groups // per_row, per_row, LANES), axis=1)


def members(groups, first, span, width):
    return jnp.where(iota((groups, width), 0) == first + over(iota((groups, width), 1), span), 1.0, 0.0).astype(BF16)


def shard_start(groups):
    return pl.multiple_of(lax.axis_index("ch") * groups, LANES)


def pack_half(value, half):
    chosen = jnp.where(half > 0, pltpu.roll(value, LANES // 2, 1), value)
    high = chosen.astype(BF16).astype(F32)
    low = pltpu.roll(chosen - high, LANES // 2, 1)
    return jnp.where(iota(value.shape, 1) < LANES // 2, high, low).astype(BF16)


def open_half(packed):
    value = packed.astype(F32)
    return value + pltpu.roll(value, LANES // 2, 1)


def states_kernel(logs_ref, res_ref, gated_ref, dgate_ref, send_ref, keep_ref, turned_ref, rows_ref,
                  skip_ref, near_ref, *, group, poles, inner):
    tokens, _ = gated_ref.shape
    per_block = LANES // group
    _, blocks, _ = rows_ref.shape
    half_blocks = blocks // 2
    groups = blocks * per_block
    wide = inner * LANES
    core = lax.rem(lax.axis_index("ctx"), 2)

    first = shard_start(groups)
    rows_ref[0] = jnp.exp(flat_rows(logs_ref[:, pl.ds(first, groups)], poles))
    rows_ref[1] = flat_rows(res_ref[:, pl.ds(first, groups)], poles)

    flip = reversal(tokens)
    back_pos = (tokens - 1 - iota((tokens, LANES), 0)).astype(F32)
    back_lane = (tokens - 1 - iota((per_block, tokens), 1)).astype(F32)
    lane_group = over(iota((tokens, LANES), 1), group)
    causal = iota((tokens, tokens), 0) + iota((tokens, tokens), 1) <= tokens - 1
    wide_group = over(within(iota((poles, 2 * LANES), 1), LANES), group)
    own_rows = iota((per_block, LANES), 0) == over(iota((per_block, LANES), 1), poles)
    half = per_block // 2
    zero = jnp.zeros((tokens, LANES), BF16)

    for turn, msg_ref in enumerate((send_ref, keep_ref)):
        base = lax.rem(core + 1 + turn, 2) * half_blocks

        def body(step, carry, base=base, msg_ref=msg_ref):
            start = base + step * inner
            cut = pl.ds(pl.multiple_of(start * LANES, LANES), wide)
            gated, dgate = gated_ref[:, cut], dgate_ref[:, cut]
            turned = mxu(flip, dgate).astype(BF16)
            turned_ref[:, cut] = turned
            skip = jnp.sum(gated.astype(F32) * dgate.astype(F32), axis=0, keepdims=True)
            for j in range(inner):
                skip_ref[pl.ds(start + j, 1), :] = skip[:, j * LANES : (j + 1) * LANES]
            lanes = [slice(j * LANES, (j + 1) * LANES) for j in range(inner)]
            tables = [jnp.exp(-rows_ref[0, pl.ds(start + j, 1), :] * back_pos) for j in range(inner)]
            lows = [table.astype(BF16) for table in tables]
            found = []
            for j in range(inner):
                table = tables[j].T
                moment_table = table * back_lane[:1]
                both = jnp.concatenate([table.astype(BF16), moment_table.astype(BF16)], axis=0)
                pair = jnp.concatenate([gated[:, lanes[j]], turned[:, lanes[j]]], axis=1)
                found.append(mxu(both, pair))
            outers = []
            for j in range(inner):
                one, other = gated[:, lanes[j]], turned[:, lanes[j]]
                left = [
                    jnp.where((lane_group == i) | (lane_group == i + half), other, zero) for i in range(half)
                ]
                right = [jnp.where(lane_group < half, one, zero), jnp.where(lane_group >= half, one, zero)]
                outers.append(mxu_t(jnp.concatenate(left, axis=0), jnp.concatenate(right, axis=0)))
            for j in range(inner):
                folded = []
                for part in range(2):
                    total = found[j][part * LANES : part * LANES + poles]
                    for g in range(1, per_block):
                        row = part * LANES + g * poles
                        total = jnp.where(wide_group == g, found[j][row : row + poles], total)
                    folded.append(total)
                out = [folded[0][:, :LANES], folded[0][:, LANES:], folded[1][:, :LANES], folded[1][:, LANES:]]
                row = pl.multiple_of((step * inner + j) * 4 * poles, 4 * poles)
                msg_ref[pl.ds(row, 4 * poles), :] = jnp.concatenate(out, axis=0).astype(BF16)
            for j in range(inner):
                totals = []
                for g in range(per_block):
                    i, h = g % half, g // half
                    tile = outers[j][i * tokens : (i + 1) * tokens, h * tokens : (h + 1) * tokens]
                    tile = jnp.where(causal, tile, 0.0)
                    total = None
                    for a in range(tokens // 8):
                        shift = (8 * (a - g)) % tokens
                        piece = tile[8 * a : 8 * a + 8]
                        piece = pltpu.roll(piece, shift, 1) if shift else piece
                        total = piece if total is None else total + piece
                    totals.append(total)
                total = pltpu.roll(jnp.concatenate(totals, axis=0), 0, 1, stride=1, stride_axis=0)
                lag = jnp.sum(total.reshape(per_block, 8, tokens), axis=1)
                stack = jnp.concatenate([split(lag, 2), split(lag * back_lane, 2)], axis=0)
                local = mxu(stack, lows[j])
                for n in range(2):
                    part = join(local[2 * n * per_block : 2 * (n + 1) * per_block], per_block)
                    row = jnp.sum(jnp.where(own_rows, part, 0.0), axis=0, keepdims=True)
                    near_ref[n, pl.ds(start + j, 1), :] = row
            return carry

        lax.fori_loop(0, half_blocks // inner, body, 0)
    pick = iota((poles, LANES), 0) == within(iota((poles, LANES), 1), poles)
    terms = []
    for b in range(blocks):
        near = [jnp.where(pick, near_ref[n, b : b + 1, :], 0.0) for n in range(2)]
        terms.append(split(jnp.concatenate(near, axis=0), 2))
    sums = mxu_t(jnp.concatenate(terms, axis=1), members(groups, 0, poles, blocks * LANES))
    sums = join(sums, 2 * poles)
    tail = half_blocks * 4 * poles
    for turn, msg_ref in enumerate((send_ref, keep_ref)):
        half = lax.rem(core + 1 + turn, 2)
        msg_ref[tail : tail + 2 * poles, :] = pack_half(sums, half)
        skip = skip_ref[pl.ds(pl.multiple_of(half * half_blocks, 8), half_blocks), :]
        msg_ref[tail + 2 * poles :, :] = split(skip, 2)


def tables_kernel(logs_ref, res_ref, _, rates_ref, taps_ref, tables_ref, *, group, poles, inner):
    blocks, _, lag_width = tables_ref.shape
    per_block = LANES // group
    groups = blocks * per_block
    step_groups = inner * per_block
    wide, lag_wide = inner * LANES, inner * lag_width
    first = shard_start(groups)
    logs = logs_ref[:, pl.ds(first, groups)]
    res = res_ref[:, pl.ds(first, groups)]
    pieces = jnp.concatenate([split(logs, 3), split(res, 3)], axis=0)
    spread = jnp.concatenate([members(step_groups, 0, SUB, lag_wide), members(step_groups, 0, group, wide)], axis=1)
    lag = (SUB - 1 - within(iota((poles, lag_wide), 1), SUB)).astype(F32)
    for step in range(blocks // inner):
        spreads = mxu(pieces[:, step * step_groups : (step + 1) * step_groups], spread)
        rates = jnp.exp(join(spreads[: 3 * poles], poles))
        res_lag = join(spreads[3 * poles :, :lag_wide], poles)
        rate = rates[:, lag_wide:]
        table = jnp.exp(-rates[:, :lag_wide] * lag)
        taps = jnp.sum(res_lag * table, axis=0, keepdims=True)
        table = table.astype(BF16)
        for j in range(inner):
            here = step * inner + j
            lanes = slice(j * lag_width, (j + 1) * lag_width)
            rates_ref[here] = rate[:, j * LANES : (j + 1) * LANES]
            taps_ref[here : here + 1, :] = taps[:, lanes]
            tables_ref[here] = table[:, lanes]


def conv_kernel(rows_ref, skip_ref, rates_ref, taps_ref, tables_ref, gated_ref, turned_ref, conv_ref,
                *, group, poles, inner):
    tokens, _ = gated_ref.shape
    per_block = LANES // group
    blocks, _, _ = rates_ref.shape
    subs = tokens // SUB
    lag_width = per_block * SUB
    first = lax.axis_index("ch") * blocks
    lead = (1 + iota((SUB, LANES), 0)).astype(F32)
    wide_group = over(within(iota((SUB, 2 * LANES), 1), LANES), group)
    state_group = over(within(iota((poles, 2 * LANES), 1), LANES), group)
    causal = iota((SUB, lag_width), 0) >= within(iota((SUB, lag_width), 1), SUB)

    def body(step, carry):
        start = step * inner
        lefts, lead_tables, decays, pairs, gains = [], [], [], [], []
        for j in range(inner):
            here = start + j
            taps = jnp.broadcast_to(taps_ref[pl.ds(here, 1), :], (SUB, lag_width))
            taps = pltpu.roll(taps, lag_width - SUB + 1, 1, stride=1, stride_axis=0)
            taps = jnp.where(causal, taps, 0.0).astype(BF16)
            lefts.append(jnp.concatenate([taps, tables_ref[here]], axis=0))
            rate = rows_ref[0, pl.ds(here, 1), :]
            res = rows_ref[1, pl.ds(here, 1), :]
            lead_tables.append((res * jnp.exp(-rate * lead)).astype(BF16))
            decay = jnp.exp(-rates_ref[here] * SUB)
            decays.append(jnp.concatenate([decay, decay], axis=1))
            cut = pl.ds(pl.multiple_of(here * LANES, LANES), LANES)
            pairs.append(jnp.concatenate([gated_ref[:, cut], turned_ref[:, cut]], axis=1))
            gain = skip_ref[pl.ds(first + here, 1), :]
            gains.append(jnp.concatenate([gain, gain], axis=1))
        states = [jnp.zeros((poles, 2 * LANES), F32)] * inner
        totals = [[] for _ in range(inner)]
        for k in range(subs):
            rows = slice(k * SUB, (k + 1) * SUB)
            found = []
            for j in range(inner):
                part = pairs[j][rows]
                stack = [jnp.where(wide_group == g, part, jnp.zeros_like(part)) for g in range(per_block)]
                found.append(mxu(lefts[j], jnp.concatenate(stack, axis=0)))
            for j in range(inner):
                total = found[j][:SUB] + gains[j] * pairs[j][rows].astype(F32)
                if k:
                    held = states[j].astype(BF16)
                    stack = [jnp.where(state_group == g, held, jnp.zeros_like(held)) for g in range(per_block)]
                    total = total + mxu(lead_tables[j], jnp.concatenate(stack, axis=0))
                totals[j].append(total)
            states = [decays[j] * states[j] + found[j][SUB:] for j in range(inner)]
        for j in range(inner):
            cut = pl.ds(pl.multiple_of(2 * (start + j) * LANES, LANES), 2 * LANES)
            conv_ref[:, cut] = jnp.concatenate(totals[j], axis=0)
        return carry

    lax.fori_loop(0, blocks // inner, body, 0)


def combine_kernel(*refs, level, levels, group, poles, tokens):
    last = level == levels - 1
    refs = list(refs)
    rates_ref, own_ref, got_ref = refs[:3]
    rest = refs[3:]
    near_ref = held_ref = slim_ref = None
    if level == 0:
        out_ref, near_ref = rest[:2]
        rest = rest[2:]
    else:
        if level > 1:
            held_ref = rest.pop(0)
        else:
            rest.pop(0)
        if last:
            near_ref, logs_ref, res_ref = rest[:3]
            mine_ref, out_ref = rest[3:]
        else:
            out_ref, new_held_ref = rest[:2]
            rest = rest[2:]
    if level == levels - 2:
        slim_ref = rest[0]
    all_blocks = rates_ref.shape[0]
    blocks = all_blocks // 2
    per_block = LANES // group
    groups = all_blocks * per_block
    me = lax.axis_index("ctx")
    core = lax.rem(me, 2)
    is_right = lax.rem(lax.shift_right_logical(me, level), 2) == 1
    before = lax.rem(me, 2**level) - (core if level else 0)
    gap_left = (tokens * before).astype(F32)
    gap_right = (tokens * (2**level - 2 - before)).astype(F32)
    gap = jnp.where(is_right, gap_left, gap_right)
    span = float(tokens * 2**level)
    next_right = lax.rem(lax.shift_right_logical(me, level + 1), 2) == 1
    own_rows = 4 * poles
    got_rows = 2 * poles if last else 4 * poles
    slim_rows = 2 * poles

    def thirds(value):
        return [value[n * poles : (n + 1) * poles] for n in range(4)]

    wide_terms = []
    for b in range(blocks):
        rate = rates_ref[core * blocks + b]
        own_f, own_b, own_fm, own_bm = thirds(own_ref[b * own_rows : (b + 1) * own_rows].astype(F32))
        got = got_ref[b * got_rows : (b + 1) * got_rows].astype(F32)
        if last:
            got_f = got_b = got[:poles]
            got_fm = got_bm = got[poles:]
        else:
            got_f, got_b, got_fm, got_bm = thirds(got)
        left_f = jnp.where(is_right, got_f, own_f)
        left_fm = jnp.where(is_right, got_fm, own_fm)
        right_b = jnp.where(is_right, own_b, got_b)
        right_bm = jnp.where(is_right, own_bm, got_bm)
        once = jnp.exp(-rate)
        cross_res = once * (right_b * left_f)
        cross_mom = once * (right_bm * left_f + right_b * (left_fm + left_f))
        wide_terms.append(split(jnp.concatenate([cross_res, cross_mom], axis=0), 2))
        if level == 0:
            near_ref[b] = jnp.concatenate([left_f, right_b], axis=0)
        else:
            carry = jnp.exp(-rate * gap) * jnp.where(is_right, left_f, right_b)
            zero = jnp.zeros_like(carry)
            hold = jnp.concatenate([jnp.where(is_right, carry, zero), jnp.where(is_right, zero, carry)], axis=0)
            if level > 1:
                hold = hold + held_ref[b]
            if last:
                step = jnp.exp(-rate * tokens)
                near = near_ref[b]
                first_core = jnp.concatenate([hold[:poles], near[poles:] + step * hold[poles:]], axis=0)
                second_core = jnp.concatenate([near[:poles] + step * hold[:poles], hold[poles:]], axis=0)
                mine_ref[b] = jnp.where(core > 0, second_core, first_core).astype(BF16)
                out_ref[b * 2 * poles : (b + 1) * 2 * poles, :] = jnp.where(
                    core > 0, first_core, second_core
                ).astype(BF16)
            else:
                new_held_ref[b] = hold
        if not last:
            right_f = jnp.where(is_right, own_f, got_f)
            right_fm = jnp.where(is_right, own_fm, got_fm)
            left_b = jnp.where(is_right, got_b, own_b)
            left_bm = jnp.where(is_right, got_bm, own_bm)
            decay = jnp.exp(-rate * span)
            new = [
                decay * left_f + right_f,
                left_b + decay * right_b,
                decay * (left_fm + span * left_f) + right_fm,
                left_bm + decay * (right_bm + span * right_b),
            ]
            out_ref[b * own_rows : (b + 1) * own_rows, :] = jnp.concatenate(new, axis=0).astype(BF16)
            if slim_ref is not None:
                chosen = jnp.concatenate(
                    [jnp.where(next_right, new[1], new[0]), jnp.where(next_right, new[3], new[2])], axis=0
                )
                slim_ref[b * slim_rows : (b + 1) * slim_rows, :] = chosen.astype(BF16)
    own_tail, got_tail = blocks * own_rows, blocks * got_rows
    cross = mxu_t(jnp.concatenate(wide_terms, axis=1), members(groups, 0, group, blocks * LANES))
    total = (
        join(cross, 2 * poles)
        + open_half(own_ref[own_tail : own_tail + 2 * poles, :])
        + open_half(got_ref[got_tail : got_tail + 2 * poles, :])
    )
    skip = join(own_ref[own_tail + 2 * poles :, :], blocks) + join(got_ref[got_tail + 2 * poles :, :], blocks)
    if last:
        start = shard_start(groups)
        rate = jnp.exp(logs_ref[:, pl.ds(start, groups)])
        factor = -rate * res_ref[:, pl.ds(start, groups)]
        factor = jnp.where(core > 0, pltpu.roll(factor, LANES // 2, 1), factor)
        length = 2 * span
        total = jnp.concatenate(
            [total[:poles] / length, factor * total[poles:] / math.sqrt(length)], axis=0
        )
        skip = skip / math.sqrt(length)
    rests = jnp.concatenate([pack_half(total, 0), split(skip, 2)], axis=0)
    if last:
        out_ref[blocks * 2 * poles :, :] = rests
    else:
        out_ref[own_tail:, :] = rests
        if slim_ref is not None:
            slim_ref[blocks * slim_rows :, :] = rests


def merge_kernel(own_ref, got_ref, out_ref, *, poles):
    core = lax.rem(lax.axis_index("ctx"), 2)
    blocks = (out_ref.shape[0] - 2 * poles) // 2
    rows = own_ref.shape[0] - 2 * poles - 2 * blocks
    own, got = open_half(own_ref[rows : rows + 2 * poles, :]), open_half(got_ref[rows : rows + 2 * poles, :])
    left, right = jnp.where(core > 0, got, own), jnp.where(core > 0, own, got)
    out_ref[: 2 * poles, :] = jnp.where(iota(own.shape, 1) < LANES // 2, left, pltpu.roll(right, LANES // 2, 1))
    own, got = join(own_ref[rows + 2 * poles :, :], blocks), join(got_ref[rows + 2 * poles :, :], blocks)
    out_ref[2 * poles : 2 * poles + blocks, :] = jnp.where(core > 0, got, own)
    out_ref[2 * poles + blocks :, :] = jnp.where(core > 0, own, got)


def output_kernel(rows_ref, conv_ref, mine_ref, got_ref, k_ref, v_ref, c_ref, gq_ref, gk_ref, gv_ref,
                  *, group, poles):
    tokens, width = gq_ref.shape
    per_block = LANES // group
    step = pl.program_id(0)
    inner = width // LANES
    half_blocks = mine_ref.shape[0]
    core = lax.rem(lax.axis_index("ctx"), 2)
    flip = reversal(tokens)
    ahead = (1 + iota((tokens, LANES), 0)).astype(F32)
    state_group = over(within(iota((poles, 2 * LANES), 1), LANES), group)
    start = step * inner
    is_mine = over(start, half_blocks) == core
    totals = []
    for j in range(inner):
        here = start + j
        rate = rows_ref[0, pl.ds(here, 1), :]
        res = rows_ref[1, pl.ds(here, 1), :]
        table = (res * jnp.exp(-rate * ahead)).astype(BF16)
        place = within(here, half_blocks)
        held = jnp.where(
            is_mine, mine_ref[place], got_ref[pl.ds(pl.multiple_of(place * 2 * poles, 2 * poles), 2 * poles), :]
        )
        states = jnp.concatenate([held[:poles], held[poles:]], axis=1)
        stack = jnp.concatenate(
            [jnp.where(state_group == g, states, jnp.zeros_like(states)) for g in range(per_block)], axis=0
        )
        both = pl.ds(pl.multiple_of(2 * here * LANES, LANES), 2 * LANES)
        totals.append((conv_ref[:, both] + mxu(table, stack)).astype(BF16))
    hidden = jnp.concatenate([t[:, :LANES] for t in totals], axis=1)
    flow = mxu(flip, jnp.concatenate([t[:, LANES:] for t in totals], axis=1))
    cut = pl.ds(pl.multiple_of(start * LANES, LANES), width)
    gq_ref[...] = (c_ref[:, cut].astype(F32) * hidden.astype(F32)).astype(BF16)
    gk_ref[...] = (flow * v_ref[:, cut].astype(F32)).astype(BF16)
    gv_ref[...] = (flow * k_ref[:, cut].astype(F32)).astype(BF16)


def assemble_kernel(*refs, shards, poles):
    slots = refs[:shards]
    res_ref, log_ref, skip_ref = refs[shards:]
    me = lax.axis_index("ch")
    groups = slots[0].shape[1]
    rows = slots[0].shape[0] - 2 * poles
    for shift, slot in enumerate(slots):
        source = lax.rem(me - shift + shards, shards)
        cut = pl.ds(pl.multiple_of(source * groups, LANES), groups)
        res_ref[:, cut] = slot[:poles, :]
        log_ref[:, cut] = slot[poles : 2 * poles, :]
        skip_ref[pl.ds(pl.multiple_of(source * rows, 8), rows), :] = slot[2 * poles :, :]


def local(queries, key_input, value_input, cotangent, residues, log_rates, skip_gain):
    tokens, width = queries.shape
    parts = lax.axis_size("ctx")
    shards = lax.axis_size("ch")
    levels = parts.bit_length() - 1
    all_groups, poles = residues.shape
    groups = all_groups // shards
    group = width // groups
    blocks = width // LANES
    inner = 4
    steps = blocks // inner
    half_blocks = blocks // 2
    lag_width = LANES // group * SUB
    sizes = dict(group=group, poles=poles)
    tail = 2 * poles + blocks
    full_rows, slim_rows = half_blocks * 4 * poles + tail, half_blocks * 2 * poles + tail

    vmem = pl.BlockSpec(memory_space=pltpu.VMEM)
    anywhere = pl.BlockSpec(memory_space=pl.ANY)
    log_rates, residues = log_rates.T, residues.T
    main = pl.BlockSpec((tokens, inner * LANES), lambda i: (0, i))

    def shape(*dims, dtype=F32):
        return jax.ShapeDtypeStruct(dims, dtype)

    def swap(value, level):
        return lax.ppermute(value, "ctx", [(i, i ^ (1 << level)) for i in range(parts)])

    gated, dgate = gate(key_input, value_input), gate(cotangent, queries)
    outgoing, message, turned, rows = pl.pallas_call(
        lambda *refs: states_kernel(*refs, inner=inner, **sizes),
        in_specs=[vmem] * 4,
        out_specs=[vmem] * 4,
        out_shape=[
            shape(full_rows, LANES, dtype=BF16),
            shape(full_rows, LANES, dtype=BF16),
            shape(tokens, width, dtype=BF16),
            shape(2, blocks, LANES),
        ],
        scratch_shapes=[pltpu.VMEM((blocks, LANES), F32), pltpu.VMEM((2, blocks, LANES), F32)],
        compiler_params=PARAMS,
        name="states",
    )(log_rates, residues, gated, dgate)

    rates, taps, tables = pl.pallas_call(
        lambda *refs: tables_kernel(*refs, inner=inner, **sizes),
        in_specs=[vmem, vmem, anywhere],
        out_specs=[vmem] * 3,
        out_shape=[
            shape(blocks, poles, LANES),
            shape(blocks, lag_width),
            shape(blocks, poles, lag_width, dtype=BF16),
        ],
        compiler_params=PARAMS,
        cost_estimate=pl.CostEstimate(flops=10**9, bytes_accessed=10**6, transcendentals=10**5),
        name="tables",
    )(log_rates, residues, rows)

    skip_rows = skip_gain.reshape(-1, LANES)
    conv = pl.pallas_call(
        lambda *refs: conv_kernel(*refs, inner=inner, **sizes),
        in_specs=[vmem] * 7,
        out_specs=vmem,
        out_shape=shape(tokens, 2 * width),
        compiler_params=PARAMS,
        cost_estimate=pl.CostEstimate(
            flops=16 * tokens * tokens * width, bytes_accessed=12 * tokens * width, transcendentals=tokens * width
        ),
        name="conv",
    )(rows, skip_rows, rates, taps, tables, gated, turned)

    held = near = None
    for level in range(levels):
        last = level == levels - 1
        got = swap(outgoing, level)
        operands, specs = [rates, message, got], [vmem] * 3
        if level == 1:
            operands.append(conv)
            specs.append(anywhere)
        elif level > 1:
            operands.append(held)
            specs.append(vmem)
        if last:
            operands += [near, log_rates, residues]
            specs += [vmem] * 3
            outs = [shape(half_blocks, 2 * poles, LANES, dtype=BF16), shape(slim_rows, LANES, dtype=BF16)]
        else:
            outs = [shape(full_rows, LANES, dtype=BF16), shape(half_blocks, 2 * poles, LANES)]
        if level == levels - 2:
            outs.append(shape(slim_rows, LANES, dtype=BF16))
        results = pl.pallas_call(
            lambda *refs, level=level: combine_kernel(*refs, level=level, levels=levels, tokens=tokens, **sizes),
            in_specs=specs,
            out_specs=[vmem] * len(outs),
            out_shape=outs,
            compiler_params=PARAMS,
            name="combine",
        )(*operands)
        if last:
            mine, outgoing = results
        else:
            message = results[0]
            outgoing = results[-1] if level == levels - 2 else message
            if level == 0:
                near = results[1]
            else:
                held = results[1]
    got = swap(outgoing, 0)
    merged = pl.pallas_call(
        lambda *refs: merge_kernel(*refs, poles=poles),
        in_specs=[vmem] * 2,
        out_specs=vmem,
        out_shape=shape(2 * poles + blocks, LANES),
        compiler_params=PARAMS,
        name="merge",
    )(outgoing, got)

    gathered = [merged]
    for shift in range(1, shards):
        gathered.append(lax.ppermute(merged, "ch", [(i, (i + shift) % shards) for i in range(shards)]))

    grad_query, grad_key, grad_value = pl.pallas_call(
        lambda *refs: output_kernel(*refs, **sizes),
        grid=(steps,),
        in_specs=[vmem] * 7,
        out_specs=[main, main, main],
        out_shape=[jax.ShapeDtypeStruct((tokens, width), BF16)] * 3,
        compiler_params=PARAMS,
        name="outputs",
    )(rows, conv, mine, got, key_input, value_input, cotangent)

    grad_residue, grad_lograte, grad_skip = pl.pallas_call(
        lambda *refs: assemble_kernel(*refs, shards=shards, poles=poles),
        in_specs=[vmem] * shards,
        out_specs=[vmem] * 3,
        out_shape=[
            jax.ShapeDtypeStruct((poles, all_groups), F32),
            jax.ShapeDtypeStruct((poles, all_groups), F32),
            jax.ShapeDtypeStruct((shards * blocks, LANES), F32),
        ],
        compiler_params=PARAMS,
        name="assemble",
    )(*gathered)
    return (grad_query, grad_key, grad_value, grad_residue.T, grad_lograte.T, grad_skip.reshape(-1))


def solution(mesh):
    placed = (P("ctx", "ch"), P("ctx", "ch"), P("ctx", "ch"), P("ctx", "ch"), P(), P(), P())
    return jax.shard_map(
        local,
        mesh=mesh,
        in_specs=placed,
        out_specs=(P("ctx", "ch"), P("ctx", "ch"), P("ctx", "ch"), P(), P(), P()),
        check_vma=False,
    )
```

```python
import math

import jax
import jax.numpy as jnp
from jax import lax
from jax.experimental import pallas as pl
from jax.experimental.pallas import tpu as pltpu
from jax.sharding import PartitionSpec as P

LANES = 128
SUB = 32
F32 = jnp.float32
BF16 = jnp.bfloat16
EXACT = lax.Precision.HIGHEST
VMEM_LIMIT = 40 * 1024 * 1024
PARAMS = pltpu.CompilerParams(vmem_limit_bytes=VMEM_LIMIT)


def iota(shape, axis):
    return lax.broadcasted_iota(jnp.int32, shape, axis)


def over(value, size):
    return lax.shift_right_logical(value, size.bit_length() - 1)


def within(value, size):
    return lax.bitwise_and(value, size - 1)


def mxu(left, right):
    return jnp.dot(left, right, preferred_element_type=F32)


def mxu_t(left, right):
    return lax.dot_general(left, right, (((1,), (1,)), ((), ())), preferred_element_type=F32)


def exact_dot(left, right):
    return jnp.dot(left, right, precision=EXACT, preferred_element_type=F32)


def gate(left, right):
    return (left.astype(F32) * right.astype(F32)).astype(BF16)


def reversal(size):
    return jnp.where(iota((size, size), 0) + iota((size, size), 1) == size - 1, 1.0, 0.0).astype(BF16)


def split(value, pieces):
    parts = []
    for _ in range(pieces):
        parts.append(value.astype(BF16))
        value = value - parts[-1].astype(F32)
    return jnp.concatenate(parts, axis=0)


def join(stacked, rows):
    total = stacked[:rows].astype(F32)
    for start in range(rows, stacked.shape[0], rows):
        total = total + stacked[start : start + rows].astype(F32)
    return total


def flat_rows(table, poles):
    table = table.T
    groups = table.shape[0]
    per_row = LANES // poles
    spread = jnp.where(iota((poles, LANES), 0) == within(iota((poles, LANES), 1), poles), 1.0, 0.0)
    wide = exact_dot(table, spread)
    keep = within(iota((groups, LANES), 0), per_row) == over(iota((groups, LANES), 1), poles)
    wide = jnp.where(keep, wide, 0.0)
    return jnp.sum(wide.reshape(groups // per_row, per_row, LANES), axis=1)


def members(groups, first, span, width):
    return jnp.where(iota((groups, width), 0) == first + over(iota((groups, width), 1), span), 1.0, 0.0).astype(BF16)


def shard_start(groups):
    return pl.multiple_of(lax.axis_index("ch") * groups, LANES)


def states_kernel(logs_ref, res_ref, gated_ref, dgate_ref, send_ref, keep_ref, turned_ref, rows_ref,
                  *, group, poles, inner):
    tokens, _ = gated_ref.shape
    per_block = LANES // group
    _, blocks, _ = rows_ref.shape
    half_blocks = blocks // 2
    groups = blocks * per_block
    wide = inner * LANES
    core = lax.rem(lax.axis_index("ctx"), 2)

    first = shard_start(groups)
    rows_ref[0] = jnp.exp(flat_rows(logs_ref[:, pl.ds(first, groups)], poles))
    rows_ref[1] = flat_rows(res_ref[:, pl.ds(first, groups)], poles)

    flip = reversal(tokens)
    back_pos = (tokens - 1 - iota((tokens, LANES), 0)).astype(F32)
    back_lane = (tokens - 1 - iota((1, tokens), 1)).astype(F32)
    wide_group = over(within(iota((poles, 2 * LANES), 1), LANES), group)
    lanes = [slice(j * LANES, (j + 1) * LANES) for j in range(inner)]

    for turn, msg_ref in enumerate((send_ref, keep_ref)):
        base = lax.rem(core + 1 + turn, 2) * half_blocks

        def body(step, carry, base=base, msg_ref=msg_ref):
            start = base + step * inner
            cut = pl.ds(pl.multiple_of(start * LANES, LANES), wide)
            gated, dgate = gated_ref[:, cut], dgate_ref[:, cut]
            turned = mxu(flip, dgate).astype(BF16)
            turned_ref[:, cut] = turned
            tables = [jnp.exp(-rows_ref[0, pl.ds(start + j, 1), :] * back_pos).T for j in range(inner)]
            found = []
            for j in range(inner):
                both = jnp.concatenate([tables[j].astype(BF16), (tables[j] * back_lane).astype(BF16)], axis=0)
                pair = jnp.concatenate([gated[:, lanes[j]], turned[:, lanes[j]]], axis=1)
                found.append(mxu(both, pair))
            for j in range(inner):
                folded = []
                for part in range(2):
                    total = found[j][part * LANES : part * LANES + poles]
                    for g in range(1, per_block):
                        row = part * LANES + g * poles
                        total = jnp.where(wide_group == g, found[j][row : row + poles], total)
                    folded.append(total)
                out = [folded[0][:, :LANES], folded[0][:, LANES:], folded[1][:, :LANES], folded[1][:, LANES:]]
                row = pl.multiple_of((step * inner + j) * 4 * poles, 4 * poles)
                msg_ref[pl.ds(row, 4 * poles), :] = jnp.concatenate(out, axis=0).astype(BF16)
            return carry

        lax.fori_loop(0, half_blocks // inner, body, 0)


def lags_kernel(rows_ref, gated_ref, dgate_ref, turned_ref, _, sums_ref, skip_ref, near_ref, *, group, poles, inner):
    tokens, _ = gated_ref.shape
    per_block = LANES // group
    _, blocks, _ = rows_ref.shape
    groups = blocks * per_block
    wide = inner * LANES
    back_pos = (tokens - 1 - iota((tokens, LANES), 0)).astype(F32)
    back_lane = (tokens - 1 - iota((per_block, tokens), 1)).astype(F32)
    lane_group = over(iota((tokens, LANES), 1), group)
    causal = iota((tokens, tokens), 0) + iota((tokens, tokens), 1) <= tokens - 1
    own_rows = iota((per_block, LANES), 0) == over(iota((per_block, LANES), 1), poles)
    half = per_block // 2
    zero = jnp.zeros((tokens, LANES), BF16)
    lanes = [slice(j * LANES, (j + 1) * LANES) for j in range(inner)]

    def body(step, carry):
        start = step * inner
        cut = pl.ds(pl.multiple_of(start * LANES, LANES), wide)
        gated, turned = gated_ref[:, cut], turned_ref[:, cut]
        skip = jnp.sum(gated.astype(F32) * dgate_ref[:, cut].astype(F32), axis=0, keepdims=True)
        for j in range(inner):
            skip_ref[pl.ds(start + j, 1), :] = skip[:, lanes[j]]
        lows = [jnp.exp(-rows_ref[0, pl.ds(start + j, 1), :] * back_pos).astype(BF16) for j in range(inner)]
        outers = []
        for j in range(inner):
            one, other = gated[:, lanes[j]], turned[:, lanes[j]]
            left = [jnp.where((lane_group == i) | (lane_group == i + half), other, zero) for i in range(half)]
            right = [jnp.where(lane_group < half, one, zero), jnp.where(lane_group >= half, one, zero)]
            outers.append(mxu_t(jnp.concatenate(left, axis=0), jnp.concatenate(right, axis=0)))
        for j in range(inner):
            totals = []
            for g in range(per_block):
                i, h = g % half, g // half
                tile = outers[j][i * tokens : (i + 1) * tokens, h * tokens : (h + 1) * tokens]
                tile = jnp.where(causal, tile, 0.0)
                total = None
                for a in range(tokens // 8):
                    shift = (8 * (a - g)) % tokens
                    piece = tile[8 * a : 8 * a + 8]
                    piece = pltpu.roll(piece, shift, 1) if shift else piece
                    total = piece if total is None else total + piece
                totals.append(total)
            total = pltpu.roll(jnp.concatenate(totals, axis=0), 0, 1, stride=1, stride_axis=0)
            lag = jnp.sum(total.reshape(per_block, 8, tokens), axis=1)
            stack = jnp.concatenate([split(lag, 2), split(lag * back_lane, 2)], axis=0)
            local = mxu(stack, lows[j])
            for n in range(2):
                part = join(local[2 * n * per_block : 2 * (n + 1) * per_block], per_block)
                row = jnp.sum(jnp.where(own_rows, part, 0.0), axis=0, keepdims=True)
                near_ref[n, pl.ds(start + j, 1), :] = row
        return carry

    lax.fori_loop(0, blocks // inner, body, 0)
    pick = iota((poles, LANES), 0) == within(iota((poles, LANES), 1), poles)
    terms = []
    for b in range(blocks):
        near = [jnp.where(pick, near_ref[n, b : b + 1, :], 0.0) for n in range(2)]
        terms.append(split(jnp.concatenate(near, axis=0), 2))
    sums = mxu_t(jnp.concatenate(terms, axis=1), members(groups, 0, poles, blocks * LANES))
    sums_ref[: 4 * poles, :] = split(join(sums, 2 * poles), 2)
    sums_ref[4 * poles :, :] = split(skip_ref[...], 2)


def tables_kernel(logs_ref, res_ref, _, rates_ref, taps_ref, tables_ref, *, group, poles, inner):
    blocks, _, lag_width = tables_ref.shape
    per_block = LANES // group
    groups = blocks * per_block
    step_groups = inner * per_block
    wide, lag_wide = inner * LANES, inner * lag_width
    first = shard_start(groups)
    logs = logs_ref[:, pl.ds(first, groups)]
    res = res_ref[:, pl.ds(first, groups)]
    pieces = jnp.concatenate([split(logs, 3), split(res, 3)], axis=0)
    spread = jnp.concatenate([members(step_groups, 0, SUB, lag_wide), members(step_groups, 0, group, wide)], axis=1)
    lag = (SUB - 1 - within(iota((poles, lag_wide), 1), SUB)).astype(F32)
    for step in range(blocks // inner):
        spreads = mxu(pieces[:, step * step_groups : (step + 1) * step_groups], spread)
        rates = jnp.exp(join(spreads[: 3 * poles], poles))
        res_lag = join(spreads[3 * poles :, :lag_wide], poles)
        rate = rates[:, lag_wide:]
        table = jnp.exp(-rates[:, :lag_wide] * lag)
        taps = jnp.sum(res_lag * table, axis=0, keepdims=True)
        table = table.astype(BF16)
        for j in range(inner):
            here = step * inner + j
            lanes = slice(j * lag_width, (j + 1) * lag_width)
            rates_ref[here] = rate[:, j * LANES : (j + 1) * LANES]
            taps_ref[here : here + 1, :] = taps[:, lanes]
            tables_ref[here] = table[:, lanes]


def conv_kernel(rows_ref, skip_ref, rates_ref, taps_ref, tables_ref, gated_ref, turned_ref, _, conv_ref,
                *, group, poles, inner):
    tokens, _ = gated_ref.shape
    per_block = LANES // group
    blocks, _, _ = rates_ref.shape
    subs = tokens // SUB
    lag_width = per_block * SUB
    first = lax.axis_index("ch") * blocks
    lead = (1 + iota((SUB, LANES), 0)).astype(F32)
    wide_group = over(within(iota((SUB, 2 * LANES), 1), LANES), group)
    state_group = over(within(iota((poles, 2 * LANES), 1), LANES), group)
    causal = iota((SUB, lag_width), 0) >= within(iota((SUB, lag_width), 1), SUB)

    def body(step, carry):
        start = step * inner
        lefts, lead_tables, decays, pairs, gains = [], [], [], [], []
        for j in range(inner):
            here = start + j
            taps = jnp.broadcast_to(taps_ref[pl.ds(here, 1), :], (SUB, lag_width))
            taps = pltpu.roll(taps, lag_width - SUB + 1, 1, stride=1, stride_axis=0)
            taps = jnp.where(causal, taps, 0.0).astype(BF16)
            lefts.append(jnp.concatenate([taps, tables_ref[here]], axis=0))
            rate = rows_ref[0, pl.ds(here, 1), :]
            res = rows_ref[1, pl.ds(here, 1), :]
            lead_tables.append((res * jnp.exp(-rate * lead)).astype(BF16))
            decay = jnp.exp(-rates_ref[here] * SUB)
            decays.append(jnp.concatenate([decay, decay], axis=1))
            cut = pl.ds(pl.multiple_of(here * LANES, LANES), LANES)
            pairs.append(jnp.concatenate([gated_ref[:, cut], turned_ref[:, cut]], axis=1))
            gain = skip_ref[pl.ds(first + here, 1), :]
            gains.append(jnp.concatenate([gain, gain], axis=1))
        states = [jnp.zeros((poles, 2 * LANES), F32)] * inner
        totals = [[] for _ in range(inner)]
        for k in range(subs):
            rows = slice(k * SUB, (k + 1) * SUB)
            found = []
            for j in range(inner):
                part = pairs[j][rows]
                stack = [jnp.where(wide_group == g, part, jnp.zeros_like(part)) for g in range(per_block)]
                found.append(mxu(lefts[j], jnp.concatenate(stack, axis=0)))
            for j in range(inner):
                total = found[j][:SUB] + gains[j] * pairs[j][rows].astype(F32)
                if k:
                    held = states[j].astype(BF16)
                    stack = [jnp.where(state_group == g, held, jnp.zeros_like(held)) for g in range(per_block)]
                    total = total + mxu(lead_tables[j], jnp.concatenate(stack, axis=0))
                totals[j].append(total)
            states = [decays[j] * states[j] + found[j][SUB:] for j in range(inner)]
        for j in range(inner):
            cut = pl.ds(pl.multiple_of(2 * (start + j) * LANES, LANES), 2 * LANES)
            conv_ref[:, cut] = jnp.concatenate(totals[j], axis=0)
        return carry

    lax.fori_loop(0, blocks // inner, body, 0)


def combine_kernel(*refs, level, levels, group, poles, tokens):
    last = level == levels - 1
    refs = list(refs)
    rates_ref, own_ref, got_ref = refs[:3]
    rest = refs[3:]
    near_ref = held_ref = slim_ref = None
    if level == 0:
        out_ref, near_ref = rest[:2]
        rest = rest[2:]
    else:
        if level > 1:
            held_ref = rest.pop(0)
        else:
            own_sums_ref, got_sums_ref = rest.pop(0), rest.pop(0)
        if level == min(2, levels - 1):
            rest.pop(0)
        if last:
            near_ref, mine_ref, out_ref = rest
        else:
            out_ref, new_held_ref = rest[:2]
            rest = rest[2:]
    if level == levels - 2:
        slim_ref = rest[0]
    all_blocks = rates_ref.shape[0]
    blocks = all_blocks // 2
    per_block = LANES // group
    groups = all_blocks * per_block
    me = lax.axis_index("ctx")
    core = lax.rem(me, 2)
    is_right = lax.rem(lax.shift_right_logical(me, level), 2) == 1
    before = lax.rem(me, 2**level) - (core if level else 0)
    gap_left = (tokens * before).astype(F32)
    gap_right = (tokens * (2**level - 2 - before)).astype(F32)
    gap = jnp.where(is_right, gap_left, gap_right)
    span = float(tokens * 2**level)
    next_right = lax.rem(lax.shift_right_logical(me, level + 1), 2) == 1
    own_rows = 4 * poles
    got_rows = 2 * poles if last else 4 * poles
    slim_rows = 2 * poles

    def thirds(value):
        return [value[n * poles : (n + 1) * poles] for n in range(4)]

    wide_terms = []
    for b in range(blocks):
        rate = rates_ref[core * blocks + b]
        own_f, own_b, own_fm, own_bm = thirds(own_ref[b * own_rows : (b + 1) * own_rows].astype(F32))
        got = got_ref[b * got_rows : (b + 1) * got_rows].astype(F32)
        if last:
            got_f = got_b = got[:poles]
            got_fm = got_bm = got[poles:]
        else:
            got_f, got_b, got_fm, got_bm = thirds(got)
        left_f = jnp.where(is_right, got_f, own_f)
        left_fm = jnp.where(is_right, got_fm, own_fm)
        right_b = jnp.where(is_right, own_b, got_b)
        right_bm = jnp.where(is_right, own_bm, got_bm)
        once = jnp.exp(-rate)
        cross_res = once * (right_b * left_f)
        cross_mom = once * (right_bm * left_f + right_b * (left_fm + left_f))
        wide_terms.append(split(jnp.concatenate([cross_res, cross_mom], axis=0), 2))
        if level == 0:
            near_ref[b] = jnp.concatenate([left_f, right_b], axis=0)
        else:
            carry = jnp.exp(-rate * gap) * jnp.where(is_right, left_f, right_b)
            zero = jnp.zeros_like(carry)
            hold = jnp.concatenate([jnp.where(is_right, carry, zero), jnp.where(is_right, zero, carry)], axis=0)
            if level > 1:
                hold = hold + held_ref[b]
            if last:
                step = jnp.exp(-rate * tokens)
                near = near_ref[b]
                first_core = jnp.concatenate([hold[:poles], near[poles:] + step * hold[poles:]], axis=0)
                second_core = jnp.concatenate([near[:poles] + step * hold[:poles], hold[poles:]], axis=0)
                mine_ref[b] = jnp.where(core > 0, second_core, first_core).astype(BF16)
                out_ref[b * 2 * poles : (b + 1) * 2 * poles, :] = jnp.where(
                    core > 0, first_core, second_core
                ).astype(BF16)
            else:
                new_held_ref[b] = hold
        if not last:
            right_f = jnp.where(is_right, own_f, got_f)
            right_fm = jnp.where(is_right, own_fm, got_fm)
            left_b = jnp.where(is_right, got_b, own_b)
            left_bm = jnp.where(is_right, got_bm, own_bm)
            decay = jnp.exp(-rate * span)
            new = [
                decay * left_f + right_f,
                left_b + decay * right_b,
                decay * (left_fm + span * left_f) + right_fm,
                left_bm + decay * (right_bm + span * right_b),
            ]
            out_ref[b * own_rows : (b + 1) * own_rows, :] = jnp.concatenate(new, axis=0).astype(BF16)
            if slim_ref is not None:
                chosen = jnp.concatenate(
                    [jnp.where(next_right, new[1], new[0]), jnp.where(next_right, new[3], new[2])], axis=0
                )
                slim_ref[b * slim_rows : (b + 1) * slim_rows, :] = chosen.astype(BF16)
    own_tail, got_tail = blocks * own_rows, blocks * got_rows
    cross = mxu_t(jnp.concatenate(wide_terms, axis=1), members(groups, 0, group, blocks * LANES))
    cross = join(cross, 2 * poles)
    total = jnp.where(core > 0, pltpu.roll(cross, groups // 2, 1), cross)
    if level:
        own_tail, got_tail = own_ref[own_tail:, :], got_ref[got_tail:, :]
        tails = [own_tail, got_tail]
        if level == 1:
            tails += [own_sums_ref[...], got_sums_ref[...]]
        for part in tails:
            total = total + join(part[: 4 * poles], 2 * poles)
        skip = sum(join(part[4 * poles :], all_blocks) for part in tails if part.shape[0] > 4 * poles)
        rests = jnp.concatenate([split(total, 2), split(skip, 2)], axis=0)
    else:
        rests = split(total, 2)
    out_ref[blocks * (2 * poles if last else own_rows) :, :] = rests
    if slim_ref is not None:
        slim_ref[blocks * slim_rows :, :] = rests


def merge_kernel(logs_ref, res_ref, own_ref, got_ref, out_ref, *, poles, length):
    blocks = out_ref.shape[0] - 2 * poles
    groups = out_ref.shape[1]
    start = own_ref.shape[0] - 4 * poles - 2 * blocks
    own, got = own_ref[start:, :], got_ref[start:, :]
    total = join(own[: 4 * poles], 2 * poles) + join(got[: 4 * poles], 2 * poles)
    skip = join(own[4 * poles :], blocks) + join(got[4 * poles :], blocks)
    first = shard_start(groups)
    factor = -jnp.exp(logs_ref[:, pl.ds(first, groups)]) * res_ref[:, pl.ds(first, groups)]
    out_ref[:poles, :] = total[:poles] / length
    out_ref[poles : 2 * poles, :] = factor * total[poles:] / math.sqrt(length)
    out_ref[2 * poles :, :] = skip / math.sqrt(length)


def output_kernel(rows_ref, conv_ref, mine_ref, got_ref, k_ref, v_ref, c_ref, gq_ref, gk_ref, gv_ref,
                  *, group, poles):
    tokens, width = gq_ref.shape
    per_block = LANES // group
    step = pl.program_id(0)
    inner = width // LANES
    half_blocks = mine_ref.shape[0]
    core = lax.rem(lax.axis_index("ctx"), 2)
    flip = reversal(tokens)
    ahead = (1 + iota((tokens, LANES), 0)).astype(F32)
    state_group = over(within(iota((poles, 2 * LANES), 1), LANES), group)
    start = step * inner
    is_mine = over(start, half_blocks) == core
    totals = []
    for j in range(inner):
        here = start + j
        rate = rows_ref[0, pl.ds(here, 1), :]
        res = rows_ref[1, pl.ds(here, 1), :]
        table = (res * jnp.exp(-rate * ahead)).astype(BF16)
        place = within(here, half_blocks)
        held = jnp.where(
            is_mine, mine_ref[place], got_ref[pl.ds(pl.multiple_of(place * 2 * poles, 2 * poles), 2 * poles), :]
        )
        states = jnp.concatenate([held[:poles], held[poles:]], axis=1)
        stack = jnp.concatenate(
            [jnp.where(state_group == g, states, jnp.zeros_like(states)) for g in range(per_block)], axis=0
        )
        both = pl.ds(pl.multiple_of(2 * here * LANES, LANES), 2 * LANES)
        totals.append((conv_ref[:, both] + mxu(table, stack)).astype(BF16))
    hidden = jnp.concatenate([t[:, :LANES] for t in totals], axis=1)
    flow = mxu(flip, jnp.concatenate([t[:, LANES:] for t in totals], axis=1))
    cut = pl.ds(pl.multiple_of(start * LANES, LANES), width)
    gq_ref[...] = (c_ref[:, cut].astype(F32) * hidden.astype(F32)).astype(BF16)
    gk_ref[...] = (flow * v_ref[:, cut].astype(F32)).astype(BF16)
    gv_ref[...] = (flow * k_ref[:, cut].astype(F32)).astype(BF16)


def assemble_kernel(*refs, shards, poles):
    slots = refs[:shards]
    res_ref, log_ref, skip_ref = refs[shards:]
    me = lax.axis_index("ch")
    groups = slots[0].shape[1]
    rows = slots[0].shape[0] - 2 * poles
    for shift, slot in enumerate(slots):
        source = lax.rem(me - shift + shards, shards)
        cut = pl.ds(pl.multiple_of(source * groups, LANES), groups)
        res_ref[:, cut] = slot[:poles, :]
        log_ref[:, cut] = slot[poles : 2 * poles, :]
        skip_ref[pl.ds(pl.multiple_of(source * rows, 8), rows), :] = slot[2 * poles :, :]


def local(queries, key_input, value_input, cotangent, residues, log_rates, skip_gain):
    tokens, width = queries.shape
    parts = lax.axis_size("ctx")
    shards = lax.axis_size("ch")
    levels = parts.bit_length() - 1
    all_groups, poles = residues.shape
    groups = all_groups // shards
    group = width // groups
    blocks = width // LANES
    inner = 4
    steps = blocks // inner
    half_blocks = blocks // 2
    lag_width = LANES // group * SUB
    sizes = dict(group=group, poles=poles)
    near_tail, tail = 4 * poles, 4 * poles + 2 * blocks
    full_rows, half_rows = half_blocks * 4 * poles, half_blocks * 2 * poles

    vmem = pl.BlockSpec(memory_space=pltpu.VMEM)
    anywhere = pl.BlockSpec(memory_space=pl.ANY)
    log_rates, residues = log_rates.T, residues.T
    main = pl.BlockSpec((tokens, inner * LANES), lambda i: (0, i))

    def shape(*dims, dtype=F32):
        return jax.ShapeDtypeStruct(dims, dtype)

    def swap(value, level):
        return lax.ppermute(value, "ctx", [(i, i ^ (1 << level)) for i in range(parts)])

    gated, dgate = gate(key_input, value_input), gate(cotangent, queries)
    outgoing, message, turned, rows = pl.pallas_call(
        lambda *refs: states_kernel(*refs, inner=inner, **sizes),
        in_specs=[vmem] * 4,
        out_specs=[vmem] * 4,
        out_shape=[
            shape(full_rows, LANES, dtype=BF16),
            shape(full_rows, LANES, dtype=BF16),
            shape(tokens, width, dtype=BF16),
            shape(2, blocks, LANES),
        ],
        compiler_params=PARAMS,
        name="states",
    )(log_rates, residues, gated, dgate)

    rates, taps, tables = pl.pallas_call(
        lambda *refs: tables_kernel(*refs, inner=inner, **sizes),
        in_specs=[vmem, vmem, anywhere],
        out_specs=[vmem] * 3,
        out_shape=[
            shape(blocks, poles, LANES),
            shape(blocks, lag_width),
            shape(blocks, poles, lag_width, dtype=BF16),
        ],
        compiler_params=PARAMS,
        cost_estimate=pl.CostEstimate(flops=10**9, bytes_accessed=10**6, transcendentals=10**5),
        name="tables",
    )(log_rates, residues, rows)

    def local_sums(after):
        return pl.pallas_call(
            lambda *refs: lags_kernel(*refs, inner=inner, **sizes),
            in_specs=[vmem] * 4 + [anywhere],
            out_specs=vmem,
            out_shape=shape(tail, LANES, dtype=BF16),
            scratch_shapes=[pltpu.VMEM((blocks, LANES), F32), pltpu.VMEM((2, blocks, LANES), F32)],
            compiler_params=PARAMS,
            cost_estimate=pl.CostEstimate(
                flops=16 * tokens * tokens * width, bytes_accessed=12 * tokens * width, transcendentals=tokens * width
            ),
            name="lags",
        )(rows, gated, dgate, turned, after)

    def convolve(after):
        skip_rows = skip_gain.reshape(-1, LANES)
        return pl.pallas_call(
            lambda *refs: conv_kernel(*refs, inner=inner, **sizes),
            in_specs=[vmem] * 7 + [anywhere],
            out_specs=vmem,
            out_shape=shape(tokens, 2 * width),
            compiler_params=PARAMS,
            cost_estimate=pl.CostEstimate(
                flops=16 * tokens * tokens * width, bytes_accessed=12 * tokens * width, transcendentals=tokens * width
            ),
            name="conv",
        )(rows, skip_rows, rates, taps, tables, gated, turned, after)

    held = near = None
    for level in range(levels):
        last = level == levels - 1
        got = swap(outgoing, level)
        operands, specs = [rates, message, got], [vmem] * 3
        if level == 1:
            sums = local_sums(near)
            operands += [sums, swap(sums, level)]
            specs += [vmem] * 2
        elif level > 1:
            operands.append(held)
            specs.append(vmem)
        if level == min(2, levels - 1):
            conv = convolve(near if held is None else held)
            operands.append(conv)
            specs.append(anywhere)
        if last:
            operands.append(near)
            specs.append(vmem)
            outs = [shape(half_blocks, 2 * poles, LANES, dtype=BF16), shape(half_rows + tail, LANES, dtype=BF16)]
        else:
            outs = [
                shape(full_rows + (tail if level else near_tail), LANES, dtype=BF16),
                shape(half_blocks, 2 * poles, LANES),
            ]
        if level == levels - 2:
            outs.append(shape(half_rows + (tail if level else near_tail), LANES, dtype=BF16))
        results = pl.pallas_call(
            lambda *refs, level=level: combine_kernel(*refs, level=level, levels=levels, tokens=tokens, **sizes),
            in_specs=specs,
            out_specs=[vmem] * len(outs),
            out_shape=outs,
            compiler_params=PARAMS,
            name="combine",
        )(*operands)
        if last:
            mine, outgoing = results
        else:
            message = results[0]
            outgoing = results[-1] if level == levels - 2 else message
            if level == 0:
                near = results[1]
            else:
                held = results[1]
    got = swap(outgoing, 0)
    merged = pl.pallas_call(
        lambda *refs: merge_kernel(*refs, poles=poles, length=tokens * parts),
        in_specs=[vmem] * 4,
        out_specs=vmem,
        out_shape=shape(2 * poles + blocks, LANES),
        compiler_params=PARAMS,
        name="merge",
    )(log_rates, residues, outgoing, got)

    gathered = [merged]
    for shift in range(1, shards):
        gathered.append(lax.ppermute(merged, "ch", [(i, (i + shift) % shards) for i in range(shards)]))

    grad_query, grad_key, grad_value = pl.pallas_call(
        lambda *refs: output_kernel(*refs, **sizes),
        grid=(steps,),
        in_specs=[vmem] * 7,
        out_specs=[main, main, main],
        out_shape=[jax.ShapeDtypeStruct((tokens, width), BF16)] * 3,
        compiler_params=PARAMS,
        name="outputs",
    )(rows, conv, mine, got, key_input, value_input, cotangent)

    grad_residue, grad_lograte, grad_skip = pl.pallas_call(
        lambda *refs: assemble_kernel(*refs, shards=shards, poles=poles),
        in_specs=[vmem] * shards,
        out_specs=[vmem] * 3,
        out_shape=[
            jax.ShapeDtypeStruct((poles, all_groups), F32),
            jax.ShapeDtypeStruct((poles, all_groups), F32),
            jax.ShapeDtypeStruct((shards * blocks, LANES), F32),
        ],
        compiler_params=PARAMS,
        name="assemble",
    )(*gathered)
    return (grad_query, grad_key, grad_value, grad_residue.T, grad_lograte.T, grad_skip.reshape(-1))


def solution(mesh):
    placed = (P("ctx", "ch"), P("ctx", "ch"), P("ctx", "ch"), P("ctx", "ch"), P(), P(), P())
    return jax.shard_map(
        local,
        mesh=mesh,
        in_specs=placed,
        out_specs=(P("ctx", "ch"), P("ctx", "ch"), P("ctx", "ch"), P(), P(), P()),
        check_vma=False,
    )
```

```python
import math

import jax
import jax.numpy as jnp
from jax import lax
from jax.experimental import pallas as pl
from jax.experimental.pallas import tpu as pltpu
from jax.sharding import PartitionSpec as P

LANES = 128
SUB = 32
F32 = jnp.float32
BF16 = jnp.bfloat16
EXACT = lax.Precision.HIGHEST
VMEM_LIMIT = 40 * 1024 * 1024
PARAMS = pltpu.CompilerParams(vmem_limit_bytes=VMEM_LIMIT)


def iota(shape, axis):
    return lax.broadcasted_iota(jnp.int32, shape, axis)


def over(value, size):
    return lax.shift_right_logical(value, size.bit_length() - 1)


def within(value, size):
    return lax.bitwise_and(value, size - 1)


def mxu(left, right):
    return jnp.dot(left, right, preferred_element_type=F32)


def mxu_t(left, right):
    return lax.dot_general(left, right, (((1,), (1,)), ((), ())), preferred_element_type=F32)


def exact_dot(left, right):
    return jnp.dot(left, right, precision=EXACT, preferred_element_type=F32)


def gate(left, right):
    return (left.astype(F32) * right.astype(F32)).astype(BF16)


def reversal(size):
    return jnp.where(iota((size, size), 0) + iota((size, size), 1) == size - 1, 1.0, 0.0).astype(BF16)


def split(value, pieces):
    parts = []
    for _ in range(pieces):
        parts.append(value.astype(BF16))
        value = value - parts[-1].astype(F32)
    return jnp.concatenate(parts, axis=0)


def join(stacked, rows):
    total = stacked[:rows].astype(F32)
    for start in range(rows, stacked.shape[0], rows):
        total = total + stacked[start : start + rows].astype(F32)
    return total


def flat_rows(table, poles):
    table = table.T
    groups = table.shape[0]
    per_row = LANES // poles
    spread = jnp.where(iota((poles, LANES), 0) == within(iota((poles, LANES), 1), poles), 1.0, 0.0)
    wide = exact_dot(table, spread)
    keep = within(iota((groups, LANES), 0), per_row) == over(iota((groups, LANES), 1), poles)
    wide = jnp.where(keep, wide, 0.0)
    return jnp.sum(wide.reshape(groups // per_row, per_row, LANES), axis=1)


def members(groups, first, span, width):
    return jnp.where(iota((groups, width), 0) == first + over(iota((groups, width), 1), span), 1.0, 0.0).astype(BF16)


def shard_start(groups):
    return pl.multiple_of(lax.axis_index("ch") * groups, LANES)


def states_kernel(logs_ref, res_ref, gated_ref, dgate_ref, send_ref, keep_ref, turned_ref, rows_ref,
                  *, group, poles, inner):
    tokens, _ = gated_ref.shape
    per_block = LANES // group
    _, blocks, _ = rows_ref.shape
    half_blocks = blocks // 2
    groups = blocks * per_block
    wide = inner * LANES
    core = lax.rem(lax.axis_index("ctx"), 2)

    first = shard_start(groups)
    rows_ref[0] = jnp.exp(flat_rows(logs_ref[:, pl.ds(first, groups)], poles))
    rows_ref[1] = flat_rows(res_ref[:, pl.ds(first, groups)], poles)

    flip = reversal(tokens)
    back_pos = (tokens - 1 - iota((tokens, LANES), 0)).astype(F32)
    back_lane = (tokens - 1 - iota((1, tokens), 1)).astype(F32)
    wide_group = over(within(iota((poles, 2 * LANES), 1), LANES), group)
    lanes = [slice(j * LANES, (j + 1) * LANES) for j in range(inner)]

    for turn, msg_ref in enumerate((send_ref, keep_ref)):
        base = lax.rem(core + 1 + turn, 2) * half_blocks

        def body(step, carry, base=base, msg_ref=msg_ref):
            start = base + step * inner
            cut = pl.ds(pl.multiple_of(start * LANES, LANES), wide)
            gated, dgate = gated_ref[:, cut], dgate_ref[:, cut]
            turned = mxu(flip, dgate).astype(BF16)
            turned_ref[:, cut] = turned
            tables = [jnp.exp(-rows_ref[0, pl.ds(start + j, 1), :] * back_pos).T for j in range(inner)]
            found = []
            for j in range(inner):
                both = jnp.concatenate([tables[j].astype(BF16), (tables[j] * back_lane).astype(BF16)], axis=0)
                pair = jnp.concatenate([gated[:, lanes[j]], turned[:, lanes[j]]], axis=1)
                found.append(mxu(both, pair))
            for j in range(inner):
                folded = []
                for part in range(2):
                    total = found[j][part * LANES : part * LANES + poles]
                    for g in range(1, per_block):
                        row = part * LANES + g * poles
                        total = jnp.where(wide_group == g, found[j][row : row + poles], total)
                    folded.append(total)
                out = [folded[0][:, :LANES], folded[0][:, LANES:], folded[1][:, :LANES], folded[1][:, LANES:]]
                row = pl.multiple_of((step * inner + j) * 4 * poles, 4 * poles)
                msg_ref[pl.ds(row, 4 * poles), :] = jnp.concatenate(out, axis=0).astype(BF16)
            return carry

        lax.fori_loop(0, half_blocks // inner, body, 0)


def lags_kernel(rows_ref, gated_ref, dgate_ref, turned_ref, _, sums_ref, skip_ref, near_ref, lag_ref, *, group, poles):
    tokens, _ = gated_ref.shape
    per_block = LANES // group
    _, blocks, _ = rows_ref.shape
    groups = blocks * per_block
    back_pos = (tokens - 1 - iota((tokens, LANES), 0)).astype(F32)
    back_lane = (tokens - 1 - iota((per_block, tokens), 1)).astype(F32)
    lane_group = over(iota((tokens, LANES), 1), group)
    causal = iota((tokens, tokens), 0) + iota((tokens, tokens), 1) <= tokens - 1
    own_rows = iota((per_block, LANES), 0) == over(iota((per_block, LANES), 1), poles)
    half = per_block // 2
    zero = jnp.zeros((tokens, LANES), BF16)
    lanes = [slice(b * LANES, (b + 1) * LANES) for b in range(blocks)]

    def outer_of(b):
        one, other = gated_ref[:, lanes[b]], turned_ref[:, lanes[b]]
        left = [jnp.where((lane_group == i) | (lane_group == i + half), other, zero) for i in range(half)]
        right = [jnp.where(lane_group < half, one, zero), jnp.where(lane_group >= half, one, zero)]
        return mxu_t(jnp.concatenate(left, axis=0), jnp.concatenate(right, axis=0))

    def diagonals(b, outer):
        totals = []
        for g in range(per_block):
            i, h = g % half, g // half
            total = None
            for a in range(tokens // 8):
                rows = slice(i * tokens + 8 * a, i * tokens + 8 * a + 8)
                piece = jnp.where(causal[8 * a : 8 * a + 8], outer[rows, h * tokens : (h + 1) * tokens], 0.0)
                shift = (8 * (a - g)) % tokens
                piece = pltpu.roll(piece, shift, 1) if shift else piece
                total = piece if total is None else total + piece
            totals.append(total)
        total = pltpu.roll(jnp.concatenate(totals, axis=0), 0, 1, stride=1, stride_axis=0)
        lag_ref[b * per_block : (b + 1) * per_block, :] = jnp.sum(total.reshape(per_block, 8, tokens), axis=1)

    ahead = outer_of(0)
    for b in range(blocks):
        outer, ahead = ahead, outer_of(b + 1) if b + 1 < blocks else None
        diagonals(b, outer)
    for b in range(blocks):
        product = gated_ref[:, lanes[b]].astype(F32) * dgate_ref[:, lanes[b]].astype(F32)
        skip_ref[b : b + 1, :] = jnp.sum(product, axis=0, keepdims=True)
    locals_ = []
    for b in range(blocks):
        lag = lag_ref[b * per_block : (b + 1) * per_block, :]
        stack = jnp.concatenate([split(lag, 2), split(lag * back_lane, 2)], axis=0)
        low = jnp.exp(-rows_ref[0, b : b + 1, :] * back_pos).astype(BF16)
        locals_.append(mxu(stack, low))
    for b in range(blocks):
        for n in range(2):
            part = join(locals_[b][2 * n * per_block : 2 * (n + 1) * per_block], per_block)
            near_ref[n, b : b + 1, :] = jnp.sum(jnp.where(own_rows, part, 0.0), axis=0, keepdims=True)
    pick = iota((poles, LANES), 0) == within(iota((poles, LANES), 1), poles)
    terms = []
    for b in range(blocks):
        near = [jnp.where(pick, near_ref[n, b : b + 1, :], 0.0) for n in range(2)]
        terms.append(split(jnp.concatenate(near, axis=0), 2))
    sums = mxu_t(jnp.concatenate(terms, axis=1), members(groups, 0, poles, blocks * LANES))
    sums_ref[: 4 * poles, :] = split(join(sums, 2 * poles), 2)
    sums_ref[4 * poles :, :] = split(skip_ref[...], 2)


def tables_kernel(logs_ref, res_ref, _, rates_ref, taps_ref, tables_ref, *, group, poles, inner):
    blocks, _, lag_width = tables_ref.shape
    per_block = LANES // group
    groups = blocks * per_block
    step_groups = inner * per_block
    wide, lag_wide = inner * LANES, inner * lag_width
    first = shard_start(groups)
    logs = logs_ref[:, pl.ds(first, groups)]
    res = res_ref[:, pl.ds(first, groups)]
    pieces = jnp.concatenate([split(logs, 3), split(res, 3)], axis=0)
    spread = jnp.concatenate([members(step_groups, 0, SUB, lag_wide), members(step_groups, 0, group, wide)], axis=1)
    lag = (SUB - 1 - within(iota((poles, lag_wide), 1), SUB)).astype(F32)
    for step in range(blocks // inner):
        spreads = mxu(pieces[:, step * step_groups : (step + 1) * step_groups], spread)
        rates = jnp.exp(join(spreads[: 3 * poles], poles))
        res_lag = join(spreads[3 * poles :, :lag_wide], poles)
        rate = rates[:, lag_wide:]
        table = jnp.exp(-rates[:, :lag_wide] * lag)
        taps = jnp.sum(res_lag * table, axis=0, keepdims=True)
        table = table.astype(BF16)
        for j in range(inner):
            here = step * inner + j
            lanes = slice(j * lag_width, (j + 1) * lag_width)
            rates_ref[here] = rate[:, j * LANES : (j + 1) * LANES]
            taps_ref[here : here + 1, :] = taps[:, lanes]
            tables_ref[here] = table[:, lanes]


def conv_kernel(rows_ref, skip_ref, rates_ref, taps_ref, tables_ref, gated_ref, turned_ref, _, conv_ref,
                *, group, poles, inner):
    tokens, _ = gated_ref.shape
    per_block = LANES // group
    blocks, _, _ = rates_ref.shape
    subs = tokens // SUB
    lag_width = per_block * SUB
    first = lax.axis_index("ch") * blocks
    lead = (1 + iota((SUB, LANES), 0)).astype(F32)
    wide_group = over(within(iota((SUB, 2 * LANES), 1), LANES), group)
    state_group = over(within(iota((poles, 2 * LANES), 1), LANES), group)
    causal = iota((SUB, lag_width), 0) >= within(iota((SUB, lag_width), 1), SUB)

    def body(step, carry):
        start = step * inner
        lefts, lead_tables, decays, pairs, gains = [], [], [], [], []
        for j in range(inner):
            here = start + j
            taps = jnp.broadcast_to(taps_ref[pl.ds(here, 1), :], (SUB, lag_width))
            taps = pltpu.roll(taps, lag_width - SUB + 1, 1, stride=1, stride_axis=0)
            taps = jnp.where(causal, taps, 0.0).astype(BF16)
            lefts.append(jnp.concatenate([taps, tables_ref[here]], axis=0))
            rate = rows_ref[0, pl.ds(here, 1), :]
            res = rows_ref[1, pl.ds(here, 1), :]
            lead_tables.append((res * jnp.exp(-rate * lead)).astype(BF16))
            decay = jnp.exp(-rates_ref[here] * SUB)
            decays.append(jnp.concatenate([decay, decay], axis=1))
            cut = pl.ds(pl.multiple_of(here * LANES, LANES), LANES)
            pairs.append(jnp.concatenate([gated_ref[:, cut], turned_ref[:, cut]], axis=1))
            gain = skip_ref[pl.ds(first + here, 1), :]
            gains.append(jnp.concatenate([gain, gain], axis=1))
        states = [jnp.zeros((poles, 2 * LANES), F32)] * inner
        totals = [[] for _ in range(inner)]
        for k in range(subs):
            rows = slice(k * SUB, (k + 1) * SUB)
            found = []
            for j in range(inner):
                part = pairs[j][rows]
                stack = [jnp.where(wide_group == g, part, jnp.zeros_like(part)) for g in range(per_block)]
                found.append(mxu(lefts[j], jnp.concatenate(stack, axis=0)))
            for j in range(inner):
                total = found[j][:SUB] + gains[j] * pairs[j][rows].astype(F32)
                if k:
                    held = states[j].astype(BF16)
                    stack = [jnp.where(state_group == g, held, jnp.zeros_like(held)) for g in range(per_block)]
                    total = total + mxu(lead_tables[j], jnp.concatenate(stack, axis=0))
                totals[j].append(total)
            states = [decays[j] * states[j] + found[j][SUB:] for j in range(inner)]
        for j in range(inner):
            cut = pl.ds(pl.multiple_of(2 * (start + j) * LANES, LANES), 2 * LANES)
            conv_ref[:, cut] = jnp.concatenate(totals[j], axis=0)
        return carry

    lax.fori_loop(0, blocks // inner, body, 0)


def combine_kernel(*refs, level, levels, group, poles, tokens):
    last = level == levels - 1
    refs = list(refs)
    rates_ref, own_ref, got_ref = refs[:3]
    rest = refs[3:]
    near_ref = held_ref = slim_ref = None
    if level == 0:
        out_ref, near_ref = rest[:2]
        rest = rest[2:]
    else:
        if level > 1:
            held_ref = rest.pop(0)
        else:
            own_sums_ref, got_sums_ref = rest.pop(0), rest.pop(0)
        if level == min(2, levels - 1):
            rest.pop(0)
        if last:
            near_ref, mine_ref, out_ref = rest
        else:
            out_ref, new_held_ref = rest[:2]
            rest = rest[2:]
    if level == levels - 2:
        slim_ref = rest[0]
    all_blocks = rates_ref.shape[0]
    blocks = all_blocks // 2
    per_block = LANES // group
    groups = all_blocks * per_block
    me = lax.axis_index("ctx")
    core = lax.rem(me, 2)
    is_right = lax.rem(lax.shift_right_logical(me, level), 2) == 1
    before = lax.rem(me, 2**level) - (core if level else 0)
    gap_left = (tokens * before).astype(F32)
    gap_right = (tokens * (2**level - 2 - before)).astype(F32)
    gap = jnp.where(is_right, gap_left, gap_right)
    span = float(tokens * 2**level)
    next_right = lax.rem(lax.shift_right_logical(me, level + 1), 2) == 1
    own_rows = 4 * poles
    got_rows = 2 * poles if last else 4 * poles
    slim_rows = 2 * poles

    def thirds(value):
        return [value[n * poles : (n + 1) * poles] for n in range(4)]

    wide_terms = []
    for b in range(blocks):
        rate = rates_ref[core * blocks + b]
        own_f, own_b, own_fm, own_bm = thirds(own_ref[b * own_rows : (b + 1) * own_rows].astype(F32))
        got = got_ref[b * got_rows : (b + 1) * got_rows].astype(F32)
        if last:
            got_f = got_b = got[:poles]
            got_fm = got_bm = got[poles:]
        else:
            got_f, got_b, got_fm, got_bm = thirds(got)
        left_f = jnp.where(is_right, got_f, own_f)
        left_fm = jnp.where(is_right, got_fm, own_fm)
        right_b = jnp.where(is_right, own_b, got_b)
        right_bm = jnp.where(is_right, own_bm, got_bm)
        once = jnp.exp(-rate)
        cross_res = once * (right_b * left_f)
        cross_mom = once * (right_bm * left_f + right_b * (left_fm + left_f))
        wide_terms.append(split(jnp.concatenate([cross_res, cross_mom], axis=0), 2))
        if level == 0:
            near_ref[b] = jnp.concatenate([left_f, right_b], axis=0)
        else:
            carry = jnp.exp(-rate * gap) * jnp.where(is_right, left_f, right_b)
            zero = jnp.zeros_like(carry)
            hold = jnp.concatenate([jnp.where(is_right, carry, zero), jnp.where(is_right, zero, carry)], axis=0)
            if level > 1:
                hold = hold + held_ref[b]
            if last:
                step = jnp.exp(-rate * tokens)
                near = near_ref[b]
                first_core = jnp.concatenate([hold[:poles], near[poles:] + step * hold[poles:]], axis=0)
                second_core = jnp.concatenate([near[:poles] + step * hold[:poles], hold[poles:]], axis=0)
                mine_ref[b] = jnp.where(core > 0, second_core, first_core).astype(BF16)
                out_ref[b * 2 * poles : (b + 1) * 2 * poles, :] = jnp.where(
                    core > 0, first_core, second_core
                ).astype(BF16)
            else:
                new_held_ref[b] = hold
        if not last:
            right_f = jnp.where(is_right, own_f, got_f)
            right_fm = jnp.where(is_right, own_fm, got_fm)
            left_b = jnp.where(is_right, got_b, own_b)
            left_bm = jnp.where(is_right, got_bm, own_bm)
            decay = jnp.exp(-rate * span)
            new = [
                decay * left_f + right_f,
                left_b + decay * right_b,
                decay * (left_fm + span * left_f) + right_fm,
                left_bm + decay * (right_bm + span * right_b),
            ]
            out_ref[b * own_rows : (b + 1) * own_rows, :] = jnp.concatenate(new, axis=0).astype(BF16)
            if slim_ref is not None:
                chosen = jnp.concatenate(
                    [jnp.where(next_right, new[1], new[0]), jnp.where(next_right, new[3], new[2])], axis=0
                )
                slim_ref[b * slim_rows : (b + 1) * slim_rows, :] = chosen.astype(BF16)
    own_tail, got_tail = blocks * own_rows, blocks * got_rows
    cross = mxu_t(jnp.concatenate(wide_terms, axis=1), members(groups, 0, group, blocks * LANES))
    cross = join(cross, 2 * poles)
    total = jnp.where(core > 0, pltpu.roll(cross, groups // 2, 1), cross)
    if level:
        own_tail, got_tail = own_ref[own_tail:, :], got_ref[got_tail:, :]
        tails = [own_tail, got_tail]
        if level == 1:
            tails += [own_sums_ref[...], got_sums_ref[...]]
        for part in tails:
            total = total + join(part[: 4 * poles], 2 * poles)
        skip = sum(join(part[4 * poles :], all_blocks) for part in tails if part.shape[0] > 4 * poles)
        rests = jnp.concatenate([split(total, 2), split(skip, 2)], axis=0)
    else:
        rests = split(total, 2)
    out_ref[blocks * (2 * poles if last else own_rows) :, :] = rests
    if slim_ref is not None:
        slim_ref[blocks * slim_rows :, :] = rests


def merge_kernel(logs_ref, res_ref, own_ref, got_ref, out_ref, *, poles, length):
    blocks = out_ref.shape[0] - 2 * poles
    groups = out_ref.shape[1]
    start = own_ref.shape[0] - 4 * poles - 2 * blocks
    own, got = own_ref[start:, :], got_ref[start:, :]
    total = join(own[: 4 * poles], 2 * poles) + join(got[: 4 * poles], 2 * poles)
    skip = join(own[4 * poles :], blocks) + join(got[4 * poles :], blocks)
    first = shard_start(groups)
    factor = -jnp.exp(logs_ref[:, pl.ds(first, groups)]) * res_ref[:, pl.ds(first, groups)]
    out_ref[:poles, :] = total[:poles] / length
    out_ref[poles : 2 * poles, :] = factor * total[poles:] / math.sqrt(length)
    out_ref[2 * poles :, :] = skip / math.sqrt(length)


def output_kernel(rows_ref, conv_ref, mine_ref, got_ref, k_ref, v_ref, c_ref, gq_ref, gk_ref, gv_ref,
                  *, group, poles):
    tokens, width = gq_ref.shape
    per_block = LANES // group
    step = pl.program_id(0)
    inner = width // LANES
    half_blocks = mine_ref.shape[0]
    core = lax.rem(lax.axis_index("ctx"), 2)
    flip = reversal(tokens)
    ahead = (1 + iota((tokens, LANES), 0)).astype(F32)
    state_group = over(within(iota((poles, 2 * LANES), 1), LANES), group)
    start = step * inner
    is_mine = over(start, half_blocks) == core
    totals = []
    for j in range(inner):
        here = start + j
        rate = rows_ref[0, pl.ds(here, 1), :]
        res = rows_ref[1, pl.ds(here, 1), :]
        table = (res * jnp.exp(-rate * ahead)).astype(BF16)
        place = within(here, half_blocks)
        held = jnp.where(
            is_mine, mine_ref[place], got_ref[pl.ds(pl.multiple_of(place * 2 * poles, 2 * poles), 2 * poles), :]
        )
        states = jnp.concatenate([held[:poles], held[poles:]], axis=1)
        stack = jnp.concatenate(
            [jnp.where(state_group == g, states, jnp.zeros_like(states)) for g in range(per_block)], axis=0
        )
        both = pl.ds(pl.multiple_of(2 * here * LANES, LANES), 2 * LANES)
        totals.append((conv_ref[:, both] + mxu(table, stack)).astype(BF16))
    hidden = jnp.concatenate([t[:, :LANES] for t in totals], axis=1)
    flow = mxu(flip, jnp.concatenate([t[:, LANES:] for t in totals], axis=1))
    cut = pl.ds(pl.multiple_of(start * LANES, LANES), width)
    gq_ref[...] = (c_ref[:, cut].astype(F32) * hidden.astype(F32)).astype(BF16)
    gk_ref[...] = (flow * v_ref[:, cut].astype(F32)).astype(BF16)
    gv_ref[...] = (flow * k_ref[:, cut].astype(F32)).astype(BF16)


def assemble_kernel(*refs, shards, poles):
    slots = refs[:shards]
    res_ref, log_ref, skip_ref = refs[shards:]
    me = lax.axis_index("ch")
    groups = slots[0].shape[1]
    rows = slots[0].shape[0] - 2 * poles
    for shift, slot in enumerate(slots):
        source = lax.rem(me - shift + shards, shards)
        cut = pl.ds(pl.multiple_of(source * groups, LANES), groups)
        res_ref[:, cut] = slot[:poles, :]
        log_ref[:, cut] = slot[poles : 2 * poles, :]
        skip_ref[pl.ds(pl.multiple_of(source * rows, 8), rows), :] = slot[2 * poles :, :]


def local(queries, key_input, value_input, cotangent, residues, log_rates, skip_gain):
    tokens, width = queries.shape
    parts = lax.axis_size("ctx")
    shards = lax.axis_size("ch")
    levels = parts.bit_length() - 1
    all_groups, poles = residues.shape
    groups = all_groups // shards
    group = width // groups
    blocks = width // LANES
    inner = 4
    steps = blocks // inner
    half_blocks = blocks // 2
    lag_width = LANES // group * SUB
    sizes = dict(group=group, poles=poles)
    near_tail, tail = 4 * poles, 4 * poles + 2 * blocks
    full_rows, half_rows = half_blocks * 4 * poles, half_blocks * 2 * poles

    vmem = pl.BlockSpec(memory_space=pltpu.VMEM)
    anywhere = pl.BlockSpec(memory_space=pl.ANY)
    log_rates, residues = log_rates.T, residues.T
    main = pl.BlockSpec((tokens, inner * LANES), lambda i: (0, i))

    def shape(*dims, dtype=F32):
        return jax.ShapeDtypeStruct(dims, dtype)

    def swap(value, level):
        return lax.ppermute(value, "ctx", [(i, i ^ (1 << level)) for i in range(parts)])

    gated, dgate = gate(key_input, value_input), gate(cotangent, queries)
    outgoing, message, turned, rows = pl.pallas_call(
        lambda *refs: states_kernel(*refs, inner=inner, **sizes),
        in_specs=[vmem] * 4,
        out_specs=[vmem] * 4,
        out_shape=[
            shape(full_rows, LANES, dtype=BF16),
            shape(full_rows, LANES, dtype=BF16),
            shape(tokens, width, dtype=BF16),
            shape(2, blocks, LANES),
        ],
        compiler_params=PARAMS,
        name="states",
    )(log_rates, residues, gated, dgate)

    rates, taps, tables = pl.pallas_call(
        lambda *refs: tables_kernel(*refs, inner=inner, **sizes),
        in_specs=[vmem, vmem, anywhere],
        out_specs=[vmem] * 3,
        out_shape=[
            shape(blocks, poles, LANES),
            shape(blocks, lag_width),
            shape(blocks, poles, lag_width, dtype=BF16),
        ],
        compiler_params=PARAMS,
        cost_estimate=pl.CostEstimate(flops=10**9, bytes_accessed=10**6, transcendentals=10**5),
        name="tables",
    )(log_rates, residues, rows)

    def local_sums(after):
        return pl.pallas_call(
            lambda *refs: lags_kernel(*refs, **sizes),
            in_specs=[vmem] * 4 + [anywhere],
            out_specs=vmem,
            out_shape=shape(tail, LANES, dtype=BF16),
            scratch_shapes=[
                pltpu.VMEM((blocks, LANES), F32),
                pltpu.VMEM((2, blocks, LANES), F32),
                pltpu.VMEM((groups, tokens), F32),
            ],
            compiler_params=PARAMS,
            cost_estimate=pl.CostEstimate(
                flops=16 * tokens * tokens * width, bytes_accessed=12 * tokens * width, transcendentals=tokens * width
            ),
            name="lags",
        )(rows, gated, dgate, turned, after)

    def convolve(after):
        skip_rows = skip_gain.reshape(-1, LANES)
        return pl.pallas_call(
            lambda *refs: conv_kernel(*refs, inner=inner, **sizes),
            in_specs=[vmem] * 7 + [anywhere],
            out_specs=vmem,
            out_shape=shape(tokens, 2 * width),
            compiler_params=PARAMS,
            cost_estimate=pl.CostEstimate(
                flops=16 * tokens * tokens * width, bytes_accessed=12 * tokens * width, transcendentals=tokens * width
            ),
            name="conv",
        )(rows, skip_rows, rates, taps, tables, gated, turned, after)

    held = near = None
    for level in range(levels):
        last = level == levels - 1
        got = swap(outgoing, level)
        operands, specs = [rates, message, got], [vmem] * 3
        if level == 1:
            sums = local_sums(near)
            operands += [sums, swap(sums, level)]
            specs += [vmem] * 2
        elif level > 1:
            operands.append(held)
            specs.append(vmem)
        if level == min(2, levels - 1):
            conv = convolve(near if held is None else held)
            operands.append(conv)
            specs.append(anywhere)
        if last:
            operands.append(near)
            specs.append(vmem)
            outs = [shape(half_blocks, 2 * poles, LANES, dtype=BF16), shape(half_rows + tail, LANES, dtype=BF16)]
        else:
            outs = [
                shape(full_rows + (tail if level else near_tail), LANES, dtype=BF16),
                shape(half_blocks, 2 * poles, LANES),
            ]
        if level == levels - 2:
            outs.append(shape(half_rows + (tail if level else near_tail), LANES, dtype=BF16))
        results = pl.pallas_call(
            lambda *refs, level=level: combine_kernel(*refs, level=level, levels=levels, tokens=tokens, **sizes),
            in_specs=specs,
            out_specs=[vmem] * len(outs),
            out_shape=outs,
            compiler_params=PARAMS,
            name="combine",
        )(*operands)
        if last:
            mine, outgoing = results
        else:
            message = results[0]
            outgoing = results[-1] if level == levels - 2 else message
            if level == 0:
                near = results[1]
            else:
                held = results[1]
    got = swap(outgoing, 0)
    merged = pl.pallas_call(
        lambda *refs: merge_kernel(*refs, poles=poles, length=tokens * parts),
        in_specs=[vmem] * 4,
        out_specs=vmem,
        out_shape=shape(2 * poles + blocks, LANES),
        compiler_params=PARAMS,
        name="merge",
    )(log_rates, residues, outgoing, got)

    gathered = [merged]
    for shift in range(1, shards):
        gathered.append(lax.ppermute(merged, "ch", [(i, (i + shift) % shards) for i in range(shards)]))

    grad_query, grad_key, grad_value = pl.pallas_call(
        lambda *refs: output_kernel(*refs, **sizes),
        grid=(steps,),
        in_specs=[vmem] * 7,
        out_specs=[main, main, main],
        out_shape=[jax.ShapeDtypeStruct((tokens, width), BF16)] * 3,
        compiler_params=PARAMS,
        name="outputs",
    )(rows, conv, mine, got, key_input, value_input, cotangent)

    grad_residue, grad_lograte, grad_skip = pl.pallas_call(
        lambda *refs: assemble_kernel(*refs, shards=shards, poles=poles),
        in_specs=[vmem] * shards,
        out_specs=[vmem] * 3,
        out_shape=[
            jax.ShapeDtypeStruct((poles, all_groups), F32),
            jax.ShapeDtypeStruct((poles, all_groups), F32),
            jax.ShapeDtypeStruct((shards * blocks, LANES), F32),
        ],
        compiler_params=PARAMS,
        name="assemble",
    )(*gathered)
    return (grad_query, grad_key, grad_value, grad_residue.T, grad_lograte.T, grad_skip.reshape(-1))


def solution(mesh):
    placed = (P("ctx", "ch"), P("ctx", "ch"), P("ctx", "ch"), P("ctx", "ch"), P(), P(), P())
    return jax.shard_map(
        local,
        mesh=mesh,
        in_specs=placed,
        out_specs=(P("ctx", "ch"), P("ctx", "ch"), P("ctx", "ch"), P(), P(), P()),
        check_vma=False,
    )
```

```python
import math

import jax
import jax.numpy as jnp
from jax import lax
from jax.experimental import pallas as pl
from jax.experimental.pallas import tpu as pltpu
from jax.sharding import PartitionSpec as P

LANES = 128
SUB = 32
F32 = jnp.float32
BF16 = jnp.bfloat16
EXACT = lax.Precision.HIGHEST
VMEM_LIMIT = 40 * 1024 * 1024
PARAMS = pltpu.CompilerParams(vmem_limit_bytes=VMEM_LIMIT)


def iota(shape, axis):
    return lax.broadcasted_iota(jnp.int32, shape, axis)


def over(value, size):
    return lax.shift_right_logical(value, size.bit_length() - 1)


def within(value, size):
    return lax.bitwise_and(value, size - 1)


def mxu(left, right):
    return jnp.dot(left, right, preferred_element_type=F32)


def mxu_t(left, right):
    return lax.dot_general(left, right, (((1,), (1,)), ((), ())), preferred_element_type=F32)


def exact_dot(left, right):
    return jnp.dot(left, right, precision=EXACT, preferred_element_type=F32)


def gate(left, right):
    return (left.astype(F32) * right.astype(F32)).astype(BF16)


def reversal(size):
    return jnp.where(iota((size, size), 0) + iota((size, size), 1) == size - 1, 1.0, 0.0).astype(BF16)


def split(value, pieces):
    parts = []
    for _ in range(pieces):
        parts.append(value.astype(BF16))
        value = value - parts[-1].astype(F32)
    return jnp.concatenate(parts, axis=0)


def join(stacked, rows):
    total = stacked[:rows].astype(F32)
    for start in range(rows, stacked.shape[0], rows):
        total = total + stacked[start : start + rows].astype(F32)
    return total


def flat_rows(table, poles):
    table = table.T
    groups = table.shape[0]
    per_row = LANES // poles
    spread = jnp.where(iota((poles, LANES), 0) == within(iota((poles, LANES), 1), poles), 1.0, 0.0)
    wide = exact_dot(table, spread)
    keep = within(iota((groups, LANES), 0), per_row) == over(iota((groups, LANES), 1), poles)
    wide = jnp.where(keep, wide, 0.0)
    return jnp.sum(wide.reshape(groups // per_row, per_row, LANES), axis=1)


def members(groups, first, span, width):
    return jnp.where(iota((groups, width), 0) == first + over(iota((groups, width), 1), span), 1.0, 0.0).astype(BF16)


def shard_start(groups):
    return pl.multiple_of(lax.axis_index("ch") * groups, LANES)


def states_kernel(logs_ref, res_ref, gated_ref, dgate_ref, send_ref, keep_ref, turned_ref, rows_ref,
                  *, group, poles, inner):
    tokens, _ = gated_ref.shape
    per_block = LANES // group
    _, blocks, _ = rows_ref.shape
    half_blocks = blocks // 2
    groups = blocks * per_block
    wide = inner * LANES
    core = lax.rem(lax.axis_index("ctx"), 2)

    first = shard_start(groups)
    rows_ref[0] = jnp.exp(flat_rows(logs_ref[:, pl.ds(first, groups)], poles))
    rows_ref[1] = flat_rows(res_ref[:, pl.ds(first, groups)], poles)

    flip = reversal(tokens)
    back_pos = (tokens - 1 - iota((tokens, LANES), 0)).astype(F32)
    back_lane = (tokens - 1 - iota((1, tokens), 1)).astype(F32)
    wide_group = over(within(iota((poles, 2 * LANES), 1), LANES), group)
    lanes = [slice(j * LANES, (j + 1) * LANES) for j in range(inner)]

    for turn, msg_ref in enumerate((send_ref, keep_ref)):
        base = lax.rem(core + 1 + turn, 2) * half_blocks

        def body(step, carry, base=base, msg_ref=msg_ref):
            start = base + step * inner
            cut = pl.ds(pl.multiple_of(start * LANES, LANES), wide)
            gated, dgate = gated_ref[:, cut], dgate_ref[:, cut]
            turned = mxu(flip, dgate).astype(BF16)
            turned_ref[:, cut] = turned
            tables = [jnp.exp(-rows_ref[0, pl.ds(start + j, 1), :] * back_pos).T for j in range(inner)]
            found = []
            for j in range(inner):
                both = jnp.concatenate([tables[j].astype(BF16), (tables[j] * back_lane).astype(BF16)], axis=0)
                pair = jnp.concatenate([gated[:, lanes[j]], turned[:, lanes[j]]], axis=1)
                found.append(mxu(both, pair))
            for j in range(inner):
                folded = []
                for part in range(2):
                    total = found[j][part * LANES : part * LANES + poles]
                    for g in range(1, per_block):
                        row = part * LANES + g * poles
                        total = jnp.where(wide_group == g, found[j][row : row + poles], total)
                    folded.append(total)
                out = [folded[0][:, :LANES], folded[0][:, LANES:], folded[1][:, :LANES], folded[1][:, LANES:]]
                row = pl.multiple_of((step * inner + j) * 4 * poles, 4 * poles)
                msg_ref[pl.ds(row, 4 * poles), :] = jnp.concatenate(out, axis=0).astype(BF16)
            return carry

        lax.fori_loop(0, half_blocks // inner, body, 0)


def lags_kernel(lag_rates_ref, gated_ref, dgate_ref, turned_ref, _, sums_ref, skip_ref, *, group, poles, inner):
    tokens, _ = gated_ref.shape
    per_block = LANES // group
    blocks, _, lag_width = lag_rates_ref.shape
    subs = tokens // SUB
    step_groups = inner * per_block
    lane_group = over(iota((SUB, LANES), 1), group)
    row, lane = iota((SUB, lag_width), 0), within(iota((SUB, lag_width), 1), SUB)
    near_side, no_wrap = row + lane <= SUB - 1, lane >= row
    lag = (SUB - 1 - within(iota((poles, lag_width), 1), SUB)).astype(F32)
    spread = members(step_groups, 0, SUB, inner * lag_width)
    sums = []
    for step in range(blocks // inner):
        outers = []
        for j in range(inner):
            lanes = slice((step * inner + j) * LANES, (step * inner + j + 1) * LANES)
            found = [None] * subs
            for k in range(subs):
                part = gated_ref[k * SUB : (k + 1) * SUB, lanes]
                stack = jnp.concatenate(
                    [jnp.where(lane_group == g, part, jnp.zeros_like(part)) for g in range(per_block)], axis=0
                )
                outer = mxu_t(turned_ref[: (subs - k) * SUB, lanes], stack)
                for n in range(subs - k):
                    far = subs - 1 - k - n
                    piece = outer[n * SUB : (n + 1) * SUB]
                    found[far] = piece if found[far] is None else found[far] + piece
            outers.append(found)
        terms = []
        for j in range(inner):
            found = outers[j] + [jnp.zeros((SUB, lag_width), F32)]
            lags = []
            for far in range(subs):
                total = jnp.where(near_side, found[far], found[far + 1])
                straight = pltpu.roll(total, 0, 1, stride=1, stride_axis=0)
                wrapped = pltpu.roll(total, lag_width - SUB, 1, stride=1, stride_axis=0)
                lags.append(jnp.sum(jnp.where(no_wrap, straight, wrapped), axis=0, keepdims=True))
            rate = lag_rates_ref[step * inner + j]
            decay = jnp.exp(-rate * SUB)
            total = jnp.zeros((poles, lag_width), F32)
            weighted = total
            for far in reversed(range(subs)):
                weighted = decay * weighted + far * lags[far]
                total = decay * total + lags[far]
            table = jnp.exp(-rate * lag)
            terms.append(
                split(jnp.concatenate([table * total, table * (lag * total + SUB * weighted)], axis=0), 2)
            )
        sums.append(mxu_t(jnp.concatenate(terms, axis=1), spread))
    for b in range(blocks):
        lanes = slice(b * LANES, (b + 1) * LANES)
        product = gated_ref[:, lanes].astype(F32) * dgate_ref[:, lanes].astype(F32)
        skip_ref[b : b + 1, :] = jnp.sum(product, axis=0, keepdims=True)
    sums = jnp.concatenate(sums, axis=1)
    sums_ref[: 4 * poles, :] = split(join(sums, 2 * poles), 2)
    sums_ref[4 * poles :, :] = split(skip_ref[...], 2)


def tables_kernel(logs_ref, res_ref, _, rates_ref, lag_rates_ref, taps_ref, tables_ref, *, group, poles, inner):
    blocks, _, lag_width = tables_ref.shape
    per_block = LANES // group
    groups = blocks * per_block
    step_groups = inner * per_block
    wide, lag_wide = inner * LANES, inner * lag_width
    first = shard_start(groups)
    logs = logs_ref[:, pl.ds(first, groups)]
    res = res_ref[:, pl.ds(first, groups)]
    pieces = jnp.concatenate([split(logs, 3), split(res, 3)], axis=0)
    spread = jnp.concatenate([members(step_groups, 0, SUB, lag_wide), members(step_groups, 0, group, wide)], axis=1)
    lag = (SUB - 1 - within(iota((poles, lag_wide), 1), SUB)).astype(F32)
    for step in range(blocks // inner):
        spreads = mxu(pieces[:, step * step_groups : (step + 1) * step_groups], spread)
        rates = jnp.exp(join(spreads[: 3 * poles], poles))
        res_lag = join(spreads[3 * poles :, :lag_wide], poles)
        rate = rates[:, lag_wide:]
        table = jnp.exp(-rates[:, :lag_wide] * lag)
        taps = jnp.sum(res_lag * table, axis=0, keepdims=True)
        table = table.astype(BF16)
        for j in range(inner):
            here = step * inner + j
            lanes = slice(j * lag_width, (j + 1) * lag_width)
            rates_ref[here] = rate[:, j * LANES : (j + 1) * LANES]
            lag_rates_ref[here] = rates[:, lanes]
            taps_ref[here : here + 1, :] = taps[:, lanes]
            tables_ref[here] = table[:, lanes]


def conv_kernel(rows_ref, skip_ref, rates_ref, taps_ref, tables_ref, gated_ref, turned_ref, _, conv_ref,
                *, group, poles, inner):
    tokens, _ = gated_ref.shape
    per_block = LANES // group
    blocks, _, _ = rates_ref.shape
    subs = tokens // SUB
    lag_width = per_block * SUB
    first = lax.axis_index("ch") * blocks
    lead = (1 + iota((SUB, LANES), 0)).astype(F32)
    wide_group = over(within(iota((SUB, 2 * LANES), 1), LANES), group)
    state_group = over(within(iota((poles, 2 * LANES), 1), LANES), group)
    causal = iota((SUB, lag_width), 0) >= within(iota((SUB, lag_width), 1), SUB)

    def body(step, carry):
        start = step * inner
        lefts, lead_tables, decays, pairs, gains = [], [], [], [], []
        for j in range(inner):
            here = start + j
            taps = jnp.broadcast_to(taps_ref[pl.ds(here, 1), :], (SUB, lag_width))
            taps = pltpu.roll(taps, lag_width - SUB + 1, 1, stride=1, stride_axis=0)
            taps = jnp.where(causal, taps, 0.0).astype(BF16)
            lefts.append(jnp.concatenate([taps, tables_ref[here]], axis=0))
            rate = rows_ref[0, pl.ds(here, 1), :]
            res = rows_ref[1, pl.ds(here, 1), :]
            lead_tables.append((res * jnp.exp(-rate * lead)).astype(BF16))
            decay = jnp.exp(-rates_ref[here] * SUB)
            decays.append(jnp.concatenate([decay, decay], axis=1))
            cut = pl.ds(pl.multiple_of(here * LANES, LANES), LANES)
            pairs.append(jnp.concatenate([gated_ref[:, cut], turned_ref[:, cut]], axis=1))
            gain = skip_ref[pl.ds(first + here, 1), :]
            gains.append(jnp.concatenate([gain, gain], axis=1))
        states = [jnp.zeros((poles, 2 * LANES), F32)] * inner
        totals = [[] for _ in range(inner)]
        for k in range(subs):
            rows = slice(k * SUB, (k + 1) * SUB)
            found = []
            for j in range(inner):
                part = pairs[j][rows]
                stack = [jnp.where(wide_group == g, part, jnp.zeros_like(part)) for g in range(per_block)]
                found.append(mxu(lefts[j], jnp.concatenate(stack, axis=0)))
            for j in range(inner):
                total = found[j][:SUB] + gains[j] * pairs[j][rows].astype(F32)
                if k:
                    held = states[j].astype(BF16)
                    stack = [jnp.where(state_group == g, held, jnp.zeros_like(held)) for g in range(per_block)]
                    total = total + mxu(lead_tables[j], jnp.concatenate(stack, axis=0))
                totals[j].append(total)
            states = [decays[j] * states[j] + found[j][SUB:] for j in range(inner)]
        for j in range(inner):
            cut = pl.ds(pl.multiple_of(2 * (start + j) * LANES, LANES), 2 * LANES)
            conv_ref[:, cut] = jnp.concatenate(totals[j], axis=0)
        return carry

    lax.fori_loop(0, blocks // inner, body, 0)


def combine_kernel(*refs, level, levels, group, poles, tokens):
    last = level == levels - 1
    refs = list(refs)
    rates_ref, own_ref, got_ref = refs[:3]
    rest = refs[3:]
    near_ref = held_ref = slim_ref = None
    if level == 0:
        out_ref, near_ref = rest[:2]
        rest = rest[2:]
    else:
        if level > 1:
            held_ref = rest.pop(0)
        else:
            own_sums_ref, got_sums_ref = rest.pop(0), rest.pop(0)
        if level == min(2, levels - 1):
            rest.pop(0)
        if last:
            near_ref, mine_ref, out_ref = rest
        else:
            out_ref, new_held_ref = rest[:2]
            rest = rest[2:]
    if level == levels - 2:
        slim_ref = rest[0]
    all_blocks = rates_ref.shape[0]
    blocks = all_blocks // 2
    per_block = LANES // group
    groups = all_blocks * per_block
    me = lax.axis_index("ctx")
    core = lax.rem(me, 2)
    is_right = lax.rem(lax.shift_right_logical(me, level), 2) == 1
    before = lax.rem(me, 2**level) - (core if level else 0)
    gap_left = (tokens * before).astype(F32)
    gap_right = (tokens * (2**level - 2 - before)).astype(F32)
    gap = jnp.where(is_right, gap_left, gap_right)
    span = float(tokens * 2**level)
    next_right = lax.rem(lax.shift_right_logical(me, level + 1), 2) == 1
    own_rows = 4 * poles
    got_rows = 2 * poles if last else 4 * poles
    slim_rows = 2 * poles

    def thirds(value):
        return [value[n * poles : (n + 1) * poles] for n in range(4)]

    wide_terms = []
    for b in range(blocks):
        rate = rates_ref[core * blocks + b]
        own_f, own_b, own_fm, own_bm = thirds(own_ref[b * own_rows : (b + 1) * own_rows].astype(F32))
        got = got_ref[b * got_rows : (b + 1) * got_rows].astype(F32)
        if last:
            got_f = got_b = got[:poles]
            got_fm = got_bm = got[poles:]
        else:
            got_f, got_b, got_fm, got_bm = thirds(got)
        left_f = jnp.where(is_right, got_f, own_f)
        left_fm = jnp.where(is_right, got_fm, own_fm)
        right_b = jnp.where(is_right, own_b, got_b)
        right_bm = jnp.where(is_right, own_bm, got_bm)
        once = jnp.exp(-rate)
        cross_res = once * (right_b * left_f)
        cross_mom = once * (right_bm * left_f + right_b * (left_fm + left_f))
        wide_terms.append(split(jnp.concatenate([cross_res, cross_mom], axis=0), 2))
        if level == 0:
            near_ref[b] = jnp.concatenate([left_f, right_b], axis=0)
        else:
            carry = jnp.exp(-rate * gap) * jnp.where(is_right, left_f, right_b)
            zero = jnp.zeros_like(carry)
            hold = jnp.concatenate([jnp.where(is_right, carry, zero), jnp.where(is_right, zero, carry)], axis=0)
            if level > 1:
                hold = hold + held_ref[b]
            if last:
                step = jnp.exp(-rate * tokens)
                near = near_ref[b]
                first_core = jnp.concatenate([hold[:poles], near[poles:] + step * hold[poles:]], axis=0)
                second_core = jnp.concatenate([near[:poles] + step * hold[:poles], hold[poles:]], axis=0)
                mine_ref[b] = jnp.where(core > 0, second_core, first_core).astype(BF16)
                out_ref[b * 2 * poles : (b + 1) * 2 * poles, :] = jnp.where(
                    core > 0, first_core, second_core
                ).astype(BF16)
            else:
                new_held_ref[b] = hold
        if not last:
            right_f = jnp.where(is_right, own_f, got_f)
            right_fm = jnp.where(is_right, own_fm, got_fm)
            left_b = jnp.where(is_right, got_b, own_b)
            left_bm = jnp.where(is_right, got_bm, own_bm)
            decay = jnp.exp(-rate * span)
            new = [
                decay * left_f + right_f,
                left_b + decay * right_b,
                decay * (left_fm + span * left_f) + right_fm,
                left_bm + decay * (right_bm + span * right_b),
            ]
            out_ref[b * own_rows : (b + 1) * own_rows, :] = jnp.concatenate(new, axis=0).astype(BF16)
            if slim_ref is not None:
                chosen = jnp.concatenate(
                    [jnp.where(next_right, new[1], new[0]), jnp.where(next_right, new[3], new[2])], axis=0
                )
                slim_ref[b * slim_rows : (b + 1) * slim_rows, :] = chosen.astype(BF16)
    own_tail, got_tail = blocks * own_rows, blocks * got_rows
    cross = mxu_t(jnp.concatenate(wide_terms, axis=1), members(groups, 0, group, blocks * LANES))
    cross = join(cross, 2 * poles)
    total = jnp.where(core > 0, pltpu.roll(cross, groups // 2, 1), cross)
    if level:
        own_tail, got_tail = own_ref[own_tail:, :], got_ref[got_tail:, :]
        tails = [own_tail, got_tail]
        if level == 1:
            tails += [own_sums_ref[...], got_sums_ref[...]]
        for part in tails:
            total = total + join(part[: 4 * poles], 2 * poles)
        skip = sum(join(part[4 * poles :], all_blocks) for part in tails if part.shape[0] > 4 * poles)
        rests = jnp.concatenate([split(total, 2), split(skip, 2)], axis=0)
    else:
        rests = split(total, 2)
    out_ref[blocks * (2 * poles if last else own_rows) :, :] = rests
    if slim_ref is not None:
        slim_ref[blocks * slim_rows :, :] = rests


def merge_kernel(logs_ref, res_ref, own_ref, got_ref, out_ref, *, poles, length):
    blocks = out_ref.shape[0] - 2 * poles
    groups = out_ref.shape[1]
    start = own_ref.shape[0] - 4 * poles - 2 * blocks
    own, got = own_ref[start:, :], got_ref[start:, :]
    total = join(own[: 4 * poles], 2 * poles) + join(got[: 4 * poles], 2 * poles)
    skip = join(own[4 * poles :], blocks) + join(got[4 * poles :], blocks)
    first = shard_start(groups)
    factor = -jnp.exp(logs_ref[:, pl.ds(first, groups)]) * res_ref[:, pl.ds(first, groups)]
    out_ref[:poles, :] = total[:poles] / length
    out_ref[poles : 2 * poles, :] = factor * total[poles:] / math.sqrt(length)
    out_ref[2 * poles :, :] = skip / math.sqrt(length)


def output_kernel(rows_ref, conv_ref, mine_ref, got_ref, k_ref, v_ref, c_ref, gq_ref, gk_ref, gv_ref,
                  *, group, poles):
    tokens, width = gq_ref.shape
    per_block = LANES // group
    step = pl.program_id(0)
    inner = width // LANES
    half_blocks = mine_ref.shape[0]
    core = lax.rem(lax.axis_index("ctx"), 2)
    flip = reversal(tokens)
    ahead = (1 + iota((tokens, LANES), 0)).astype(F32)
    state_group = over(within(iota((poles, 2 * LANES), 1), LANES), group)
    start = step * inner
    is_mine = over(start, half_blocks) == core
    totals = []
    for j in range(inner):
        here = start + j
        rate = rows_ref[0, pl.ds(here, 1), :]
        res = rows_ref[1, pl.ds(here, 1), :]
        table = (res * jnp.exp(-rate * ahead)).astype(BF16)
        place = within(here, half_blocks)
        held = jnp.where(
            is_mine, mine_ref[place], got_ref[pl.ds(pl.multiple_of(place * 2 * poles, 2 * poles), 2 * poles), :]
        )
        states = jnp.concatenate([held[:poles], held[poles:]], axis=1)
        stack = jnp.concatenate(
            [jnp.where(state_group == g, states, jnp.zeros_like(states)) for g in range(per_block)], axis=0
        )
        both = pl.ds(pl.multiple_of(2 * here * LANES, LANES), 2 * LANES)
        totals.append((conv_ref[:, both] + mxu(table, stack)).astype(BF16))
    hidden = jnp.concatenate([t[:, :LANES] for t in totals], axis=1)
    flow = mxu(flip, jnp.concatenate([t[:, LANES:] for t in totals], axis=1))
    cut = pl.ds(pl.multiple_of(start * LANES, LANES), width)
    gq_ref[...] = (c_ref[:, cut].astype(F32) * hidden.astype(F32)).astype(BF16)
    gk_ref[...] = (flow * v_ref[:, cut].astype(F32)).astype(BF16)
    gv_ref[...] = (flow * k_ref[:, cut].astype(F32)).astype(BF16)


def assemble_kernel(*refs, shards, poles):
    slots = refs[:shards]
    res_ref, log_ref, skip_ref = refs[shards:]
    me = lax.axis_index("ch")
    groups = slots[0].shape[1]
    rows = slots[0].shape[0] - 2 * poles
    for shift, slot in enumerate(slots):
        source = lax.rem(me - shift + shards, shards)
        cut = pl.ds(pl.multiple_of(source * groups, LANES), groups)
        res_ref[:, cut] = slot[:poles, :]
        log_ref[:, cut] = slot[poles : 2 * poles, :]
        skip_ref[pl.ds(pl.multiple_of(source * rows, 8), rows), :] = slot[2 * poles :, :]


def local(queries, key_input, value_input, cotangent, residues, log_rates, skip_gain):
    tokens, width = queries.shape
    parts = lax.axis_size("ctx")
    shards = lax.axis_size("ch")
    levels = parts.bit_length() - 1
    all_groups, poles = residues.shape
    groups = all_groups // shards
    group = width // groups
    blocks = width // LANES
    inner = 4
    steps = blocks // inner
    half_blocks = blocks // 2
    lag_width = LANES // group * SUB
    sizes = dict(group=group, poles=poles)
    near_tail, tail = 4 * poles, 4 * poles + 2 * blocks
    full_rows, half_rows = half_blocks * 4 * poles, half_blocks * 2 * poles

    vmem = pl.BlockSpec(memory_space=pltpu.VMEM)
    anywhere = pl.BlockSpec(memory_space=pl.ANY)
    log_rates, residues = log_rates.T, residues.T
    main = pl.BlockSpec((tokens, inner * LANES), lambda i: (0, i))

    def shape(*dims, dtype=F32):
        return jax.ShapeDtypeStruct(dims, dtype)

    def swap(value, level):
        return lax.ppermute(value, "ctx", [(i, i ^ (1 << level)) for i in range(parts)])

    gated, dgate = gate(key_input, value_input), gate(cotangent, queries)
    outgoing, message, turned, rows = pl.pallas_call(
        lambda *refs: states_kernel(*refs, inner=inner, **sizes),
        in_specs=[vmem] * 4,
        out_specs=[vmem] * 4,
        out_shape=[
            shape(full_rows, LANES, dtype=BF16),
            shape(full_rows, LANES, dtype=BF16),
            shape(tokens, width, dtype=BF16),
            shape(2, blocks, LANES),
        ],
        compiler_params=PARAMS,
        name="states",
    )(log_rates, residues, gated, dgate)

    rates, lag_rates, taps, tables = pl.pallas_call(
        lambda *refs: tables_kernel(*refs, inner=inner, **sizes),
        in_specs=[vmem, vmem, anywhere],
        out_specs=[vmem] * 4,
        out_shape=[
            shape(blocks, poles, LANES),
            shape(blocks, poles, lag_width),
            shape(blocks, lag_width),
            shape(blocks, poles, lag_width, dtype=BF16),
        ],
        compiler_params=PARAMS,
        cost_estimate=pl.CostEstimate(flops=10**9, bytes_accessed=10**6, transcendentals=10**5),
        name="tables",
    )(log_rates, residues, rows)

    def local_sums(after):
        return pl.pallas_call(
            lambda *refs: lags_kernel(*refs, inner=inner, **sizes),
            in_specs=[vmem] * 4 + [anywhere],
            out_specs=vmem,
            out_shape=shape(tail, LANES, dtype=BF16),
            scratch_shapes=[pltpu.VMEM((blocks, LANES), F32)],
            compiler_params=PARAMS,
            cost_estimate=pl.CostEstimate(
                flops=16 * tokens * tokens * width, bytes_accessed=12 * tokens * width, transcendentals=tokens * width
            ),
            name="lags",
        )(lag_rates, gated, dgate, turned, after)

    def convolve(after):
        skip_rows = skip_gain.reshape(-1, LANES)
        return pl.pallas_call(
            lambda *refs: conv_kernel(*refs, inner=inner, **sizes),
            in_specs=[vmem] * 7 + [anywhere],
            out_specs=vmem,
            out_shape=shape(tokens, 2 * width),
            compiler_params=PARAMS,
            cost_estimate=pl.CostEstimate(
                flops=16 * tokens * tokens * width, bytes_accessed=12 * tokens * width, transcendentals=tokens * width
            ),
            name="conv",
        )(rows, skip_rows, rates, taps, tables, gated, turned, after)

    held = near = None
    for level in range(levels):
        last = level == levels - 1
        got = swap(outgoing, level)
        operands, specs = [rates, message, got], [vmem] * 3
        if level == 1:
            sums = local_sums(near)
            operands += [sums, swap(sums, level)]
            specs += [vmem] * 2
        elif level > 1:
            operands.append(held)
            specs.append(vmem)
        if level == min(2, levels - 1):
            conv = convolve(near if held is None else held)
            operands.append(conv)
            specs.append(anywhere)
        if last:
            operands.append(near)
            specs.append(vmem)
            outs = [shape(half_blocks, 2 * poles, LANES, dtype=BF16), shape(half_rows + tail, LANES, dtype=BF16)]
        else:
            outs = [
                shape(full_rows + (tail if level else near_tail), LANES, dtype=BF16),
                shape(half_blocks, 2 * poles, LANES),
            ]
        if level == levels - 2:
            outs.append(shape(half_rows + (tail if level else near_tail), LANES, dtype=BF16))
        results = pl.pallas_call(
            lambda *refs, level=level: combine_kernel(*refs, level=level, levels=levels, tokens=tokens, **sizes),
            in_specs=specs,
            out_specs=[vmem] * len(outs),
            out_shape=outs,
            compiler_params=PARAMS,
            name="combine",
        )(*operands)
        if last:
            mine, outgoing = results
        else:
            message = results[0]
            outgoing = results[-1] if level == levels - 2 else message
            if level == 0:
                near = results[1]
            else:
                held = results[1]
    got = swap(outgoing, 0)
    merged = pl.pallas_call(
        lambda *refs: merge_kernel(*refs, poles=poles, length=tokens * parts),
        in_specs=[vmem] * 4,
        out_specs=vmem,
        out_shape=shape(2 * poles + blocks, LANES),
        compiler_params=PARAMS,
        name="merge",
    )(log_rates, residues, outgoing, got)

    gathered = [merged]
    for shift in range(1, shards):
        gathered.append(lax.ppermute(merged, "ch", [(i, (i + shift) % shards) for i in range(shards)]))

    grad_query, grad_key, grad_value = pl.pallas_call(
        lambda *refs: output_kernel(*refs, **sizes),
        grid=(steps,),
        in_specs=[vmem] * 7,
        out_specs=[main, main, main],
        out_shape=[jax.ShapeDtypeStruct((tokens, width), BF16)] * 3,
        compiler_params=PARAMS,
        name="outputs",
    )(rows, conv, mine, got, key_input, value_input, cotangent)

    grad_residue, grad_lograte, grad_skip = pl.pallas_call(
        lambda *refs: assemble_kernel(*refs, shards=shards, poles=poles),
        in_specs=[vmem] * shards,
        out_specs=[vmem] * 3,
        out_shape=[
            jax.ShapeDtypeStruct((poles, all_groups), F32),
            jax.ShapeDtypeStruct((poles, all_groups), F32),
            jax.ShapeDtypeStruct((shards * blocks, LANES), F32),
        ],
        compiler_params=PARAMS,
        name="assemble",
    )(*gathered)
    return (grad_query, grad_key, grad_value, grad_residue.T, grad_lograte.T, grad_skip.reshape(-1))


def solution(mesh):
    placed = (P("ctx", "ch"), P("ctx", "ch"), P("ctx", "ch"), P("ctx", "ch"), P(), P(), P())
    return jax.shard_map(
        local,
        mesh=mesh,
        in_specs=placed,
        out_specs=(P("ctx", "ch"), P("ctx", "ch"), P("ctx", "ch"), P(), P(), P()),
        check_vma=False,
    )
```

```python
import math

import jax
import jax.numpy as jnp
from jax import lax
from jax.experimental import pallas as pl
from jax.experimental.pallas import tpu as pltpu
from jax.sharding import PartitionSpec as P

LANES = 128
SUB = 32
F32 = jnp.float32
BF16 = jnp.bfloat16
EXACT = lax.Precision.HIGHEST
VMEM_LIMIT = 40 * 1024 * 1024
PARAMS = pltpu.CompilerParams(vmem_limit_bytes=VMEM_LIMIT)


def iota(shape, axis):
    return lax.broadcasted_iota(jnp.int32, shape, axis)


def over(value, size):
    return lax.shift_right_logical(value, size.bit_length() - 1)


def within(value, size):
    return lax.bitwise_and(value, size - 1)


def mxu(left, right):
    return jnp.dot(left, right, preferred_element_type=F32)


def mxu_t(left, right):
    return lax.dot_general(left, right, (((1,), (1,)), ((), ())), preferred_element_type=F32)


def exact_dot(left, right):
    return jnp.dot(left, right, precision=EXACT, preferred_element_type=F32)


def gate(left, right):
    return (left.astype(F32) * right.astype(F32)).astype(BF16)


def reversal(size):
    return jnp.where(iota((size, size), 0) + iota((size, size), 1) == size - 1, 1.0, 0.0).astype(BF16)


def split(value, pieces):
    parts = []
    for _ in range(pieces):
        parts.append(value.astype(BF16))
        value = value - parts[-1].astype(F32)
    return jnp.concatenate(parts, axis=0)


def join(stacked, rows):
    total = stacked[:rows].astype(F32)
    for start in range(rows, stacked.shape[0], rows):
        total = total + stacked[start : start + rows].astype(F32)
    return total


def flat_rows(table, poles):
    table = table.T
    groups = table.shape[0]
    per_row = LANES // poles
    spread = jnp.where(iota((poles, LANES), 0) == within(iota((poles, LANES), 1), poles), 1.0, 0.0)
    wide = exact_dot(table, spread)
    keep = within(iota((groups, LANES), 0), per_row) == over(iota((groups, LANES), 1), poles)
    wide = jnp.where(keep, wide, 0.0)
    return jnp.sum(wide.reshape(groups // per_row, per_row, LANES), axis=1)


def members(groups, first, span, width):
    return jnp.where(iota((groups, width), 0) == first + over(iota((groups, width), 1), span), 1.0, 0.0).astype(BF16)


def shard_start(groups):
    return pl.multiple_of(lax.axis_index("ch") * groups, LANES)


def states_kernel(logs_ref, res_ref, gated_ref, dgate_ref, send_ref, keep_ref, turned_ref, rows_ref,
                  *, group, poles, inner):
    tokens, _ = gated_ref.shape
    per_block = LANES // group
    _, blocks, _ = rows_ref.shape
    half_blocks = blocks // 2
    groups = blocks * per_block
    wide = inner * LANES
    core = lax.rem(lax.axis_index("ctx"), 2)

    first = shard_start(groups)
    rows_ref[0] = jnp.exp(flat_rows(logs_ref[:, pl.ds(first, groups)], poles))
    rows_ref[1] = flat_rows(res_ref[:, pl.ds(first, groups)], poles)

    flip = reversal(tokens)
    back_pos = (tokens - 1 - iota((tokens, LANES), 0)).astype(F32)
    back_lane = (tokens - 1 - iota((1, tokens), 1)).astype(F32)
    wide_group = over(within(iota((poles, 2 * LANES), 1), LANES), group)
    lanes = [slice(j * LANES, (j + 1) * LANES) for j in range(inner)]

    for turn, msg_ref in enumerate((send_ref, keep_ref)):
        base = lax.rem(core + 1 + turn, 2) * half_blocks

        def body(step, carry, base=base, msg_ref=msg_ref):
            start = base + step * inner
            cut = pl.ds(pl.multiple_of(start * LANES, LANES), wide)
            gated, dgate = gated_ref[:, cut], dgate_ref[:, cut]
            turned = mxu(flip, dgate).astype(BF16)
            turned_ref[:, cut] = turned
            tables = [jnp.exp(-rows_ref[0, pl.ds(start + j, 1), :] * back_pos).T for j in range(inner)]
            found = []
            for j in range(inner):
                both = jnp.concatenate([tables[j].astype(BF16), (tables[j] * back_lane).astype(BF16)], axis=0)
                pair = jnp.concatenate([gated[:, lanes[j]], turned[:, lanes[j]]], axis=1)
                found.append(mxu(both, pair))
            for j in range(inner):
                folded = []
                for part in range(2):
                    total = found[j][part * LANES : part * LANES + poles]
                    for g in range(1, per_block):
                        row = part * LANES + g * poles
                        total = jnp.where(wide_group == g, found[j][row : row + poles], total)
                    folded.append(total)
                out = [folded[0][:, :LANES], folded[0][:, LANES:], folded[1][:, :LANES], folded[1][:, LANES:]]
                row = pl.multiple_of((step * inner + j) * 4 * poles, 4 * poles)
                msg_ref[pl.ds(row, 4 * poles), :] = jnp.concatenate(out, axis=0).astype(BF16)
            return carry

        lax.fori_loop(0, half_blocks // inner, body, 0)


def lags_kernel(lag_rates_ref, gated_ref, dgate_ref, turned_ref, _, sums_ref, skip_ref, *, second, group, poles, inner):
    tokens, _ = gated_ref.shape
    per_block = LANES // group
    blocks, _, lag_width = lag_rates_ref.shape
    subs = tokens // SUB
    step_groups = inner * per_block
    lane_group = over(iota((SUB, LANES), 1), group)
    row, lane = iota((SUB, lag_width), 0), within(iota((SUB, lag_width), 1), SUB)
    near_side, no_wrap = row + lane <= SUB - 1, lane >= row
    lag = (SUB - 1 - within(iota((poles, lag_width), 1), SUB)).astype(F32)
    spread = members(step_groups, 0, SUB, inner * lag_width)
    half_steps = blocks // inner // 2
    sums = []
    for step in range(half_steps * second, half_steps * (second + 1)):
        outers = []
        for j in range(inner):
            lanes = slice((step * inner + j) * LANES, (step * inner + j + 1) * LANES)
            found = [None] * subs
            for k in range(subs):
                part = gated_ref[k * SUB : (k + 1) * SUB, lanes]
                stack = jnp.concatenate(
                    [jnp.where(lane_group == g, part, jnp.zeros_like(part)) for g in range(per_block)], axis=0
                )
                outer = mxu_t(turned_ref[: (subs - k) * SUB, lanes], stack)
                for n in range(subs - k):
                    far = subs - 1 - k - n
                    piece = outer[n * SUB : (n + 1) * SUB]
                    found[far] = piece if found[far] is None else found[far] + piece
            outers.append(found)
        terms = []
        for j in range(inner):
            found = outers[j] + [jnp.zeros((SUB, lag_width), F32)]
            lags = []
            for far in range(subs):
                total = jnp.where(near_side, found[far], found[far + 1])
                straight = pltpu.roll(total, 0, 1, stride=1, stride_axis=0)
                wrapped = pltpu.roll(total, lag_width - SUB, 1, stride=1, stride_axis=0)
                lags.append(jnp.sum(jnp.where(no_wrap, straight, wrapped), axis=0, keepdims=True))
            rate = lag_rates_ref[step * inner + j]
            decay = jnp.exp(-rate * SUB)
            total = jnp.zeros((poles, lag_width), F32)
            weighted = total
            for far in reversed(range(subs)):
                weighted = decay * weighted + far * lags[far]
                total = decay * total + lags[far]
            table = jnp.exp(-rate * lag)
            terms.append(
                split(jnp.concatenate([table * total, table * (lag * total + SUB * weighted)], axis=0), 2)
            )
        sums.append(mxu_t(jnp.concatenate(terms, axis=1), spread))
    sums = jnp.concatenate(sums, axis=1)
    zeros = jnp.zeros_like(sums)
    sums = jnp.concatenate([zeros, sums] if second else [sums, zeros], axis=1)
    sums_ref[: 4 * poles, :] = split(join(sums, 2 * poles), 2)
    if second:
        for b in range(blocks):
            lanes = slice(b * LANES, (b + 1) * LANES)
            product = gated_ref[:, lanes].astype(F32) * dgate_ref[:, lanes].astype(F32)
            skip_ref[b : b + 1, :] = jnp.sum(product, axis=0, keepdims=True)
        sums_ref[4 * poles :, :] = split(skip_ref[...], 2)


def tables_kernel(logs_ref, res_ref, _, rates_ref, lag_rates_ref, taps_ref, tables_ref, *, group, poles, inner):
    blocks, _, lag_width = tables_ref.shape
    per_block = LANES // group
    groups = blocks * per_block
    step_groups = inner * per_block
    wide, lag_wide = inner * LANES, inner * lag_width
    first = shard_start(groups)
    logs = logs_ref[:, pl.ds(first, groups)]
    res = res_ref[:, pl.ds(first, groups)]
    pieces = jnp.concatenate([split(logs, 3), split(res, 3)], axis=0)
    spread = jnp.concatenate([members(step_groups, 0, SUB, lag_wide), members(step_groups, 0, group, wide)], axis=1)
    lag = (SUB - 1 - within(iota((poles, lag_wide), 1), SUB)).astype(F32)
    for step in range(blocks // inner):
        spreads = mxu(pieces[:, step * step_groups : (step + 1) * step_groups], spread)
        rates = jnp.exp(join(spreads[: 3 * poles], poles))
        res_lag = join(spreads[3 * poles :, :lag_wide], poles)
        rate = rates[:, lag_wide:]
        table = jnp.exp(-rates[:, :lag_wide] * lag)
        taps = jnp.sum(res_lag * table, axis=0, keepdims=True)
        table = table.astype(BF16)
        for j in range(inner):
            here = step * inner + j
            lanes = slice(j * lag_width, (j + 1) * lag_width)
            rates_ref[here] = rate[:, j * LANES : (j + 1) * LANES]
            lag_rates_ref[here] = rates[:, lanes]
            taps_ref[here : here + 1, :] = taps[:, lanes]
            tables_ref[here] = table[:, lanes]


def conv_kernel(rows_ref, skip_ref, rates_ref, taps_ref, tables_ref, gated_ref, turned_ref, _, conv_ref,
                *, group, poles, inner):
    tokens, _ = gated_ref.shape
    per_block = LANES // group
    blocks, _, _ = rates_ref.shape
    subs = tokens // SUB
    lag_width = per_block * SUB
    first = lax.axis_index("ch") * blocks
    lead = (1 + iota((SUB, LANES), 0)).astype(F32)
    wide_group = over(within(iota((SUB, 2 * LANES), 1), LANES), group)
    state_group = over(within(iota((poles, 2 * LANES), 1), LANES), group)
    causal = iota((SUB, lag_width), 0) >= within(iota((SUB, lag_width), 1), SUB)

    def body(step, carry):
        start = step * inner
        lefts, lead_tables, decays, pairs, gains = [], [], [], [], []
        for j in range(inner):
            here = start + j
            taps = jnp.broadcast_to(taps_ref[pl.ds(here, 1), :], (SUB, lag_width))
            taps = pltpu.roll(taps, lag_width - SUB + 1, 1, stride=1, stride_axis=0)
            taps = jnp.where(causal, taps, 0.0).astype(BF16)
            lefts.append(jnp.concatenate([taps, tables_ref[here]], axis=0))
            rate = rows_ref[0, pl.ds(here, 1), :]
            res = rows_ref[1, pl.ds(here, 1), :]
            lead_tables.append((res * jnp.exp(-rate * lead)).astype(BF16))
            decay = jnp.exp(-rates_ref[here] * SUB)
            decays.append(jnp.concatenate([decay, decay], axis=1))
            cut = pl.ds(pl.multiple_of(here * LANES, LANES), LANES)
            pairs.append(jnp.concatenate([gated_ref[:, cut], turned_ref[:, cut]], axis=1))
            gain = skip_ref[pl.ds(first + here, 1), :]
            gains.append(jnp.concatenate([gain, gain], axis=1))
        states = [jnp.zeros((poles, 2 * LANES), F32)] * inner
        totals = [[] for _ in range(inner)]
        for k in range(subs):
            rows = slice(k * SUB, (k + 1) * SUB)
            found = []
            for j in range(inner):
                part = pairs[j][rows]
                stack = [jnp.where(wide_group == g, part, jnp.zeros_like(part)) for g in range(per_block)]
                found.append(mxu(lefts[j], jnp.concatenate(stack, axis=0)))
            for j in range(inner):
                total = found[j][:SUB] + gains[j] * pairs[j][rows].astype(F32)
                if k:
                    held = states[j].astype(BF16)
                    stack = [jnp.where(state_group == g, held, jnp.zeros_like(held)) for g in range(per_block)]
                    total = total + mxu(lead_tables[j], jnp.concatenate(stack, axis=0))
                totals[j].append(total)
            states = [decays[j] * states[j] + found[j][SUB:] for j in range(inner)]
        for j in range(inner):
            cut = pl.ds(pl.multiple_of(2 * (start + j) * LANES, LANES), 2 * LANES)
            conv_ref[:, cut] = jnp.concatenate(totals[j], axis=0)
        return carry

    lax.fori_loop(0, blocks // inner, body, 0)


def combine_kernel(*refs, level, levels, group, poles, tokens):
    last = level == levels - 1
    refs = list(refs)
    rates_ref, own_ref, got_ref = refs[:3]
    rest = refs[3:]
    near_ref = held_ref = slim_ref = None
    if level == 0:
        own_sums_ref, out_ref, near_ref = rest[:3]
        rest = rest[3:]
    else:
        if level > 1:
            held_ref = rest.pop(0)
        else:
            own_sums_ref, got_sums_ref = rest.pop(0), rest.pop(0)
        if level == min(2, levels - 1):
            rest.pop(0)
        if last:
            near_ref, mine_ref, out_ref = rest
        else:
            out_ref, new_held_ref = rest[:2]
            rest = rest[2:]
    if level == levels - 2:
        slim_ref = rest[0]
    all_blocks = rates_ref.shape[0]
    blocks = all_blocks // 2
    per_block = LANES // group
    groups = all_blocks * per_block
    me = lax.axis_index("ctx")
    core = lax.rem(me, 2)
    is_right = lax.rem(lax.shift_right_logical(me, level), 2) == 1
    before = lax.rem(me, 2**level) - (core if level else 0)
    gap_left = (tokens * before).astype(F32)
    gap_right = (tokens * (2**level - 2 - before)).astype(F32)
    gap = jnp.where(is_right, gap_left, gap_right)
    span = float(tokens * 2**level)
    next_right = lax.rem(lax.shift_right_logical(me, level + 1), 2) == 1
    own_rows = 4 * poles
    got_rows = 2 * poles if last else 4 * poles
    slim_rows = 2 * poles

    def thirds(value):
        return [value[n * poles : (n + 1) * poles] for n in range(4)]

    wide_terms = []
    for b in range(blocks):
        rate = rates_ref[core * blocks + b]
        own_f, own_b, own_fm, own_bm = thirds(own_ref[b * own_rows : (b + 1) * own_rows].astype(F32))
        got = got_ref[b * got_rows : (b + 1) * got_rows].astype(F32)
        if last:
            got_f = got_b = got[:poles]
            got_fm = got_bm = got[poles:]
        else:
            got_f, got_b, got_fm, got_bm = thirds(got)
        left_f = jnp.where(is_right, got_f, own_f)
        left_fm = jnp.where(is_right, got_fm, own_fm)
        right_b = jnp.where(is_right, own_b, got_b)
        right_bm = jnp.where(is_right, own_bm, got_bm)
        once = jnp.exp(-rate)
        cross_res = once * (right_b * left_f)
        cross_mom = once * (right_bm * left_f + right_b * (left_fm + left_f))
        wide_terms.append(split(jnp.concatenate([cross_res, cross_mom], axis=0), 2))
        if level == 0:
            near_ref[b] = jnp.concatenate([left_f, right_b], axis=0)
        else:
            carry = jnp.exp(-rate * gap) * jnp.where(is_right, left_f, right_b)
            zero = jnp.zeros_like(carry)
            hold = jnp.concatenate([jnp.where(is_right, carry, zero), jnp.where(is_right, zero, carry)], axis=0)
            if level > 1:
                hold = hold + held_ref[b]
            if last:
                step = jnp.exp(-rate * tokens)
                near = near_ref[b]
                first_core = jnp.concatenate([hold[:poles], near[poles:] + step * hold[poles:]], axis=0)
                second_core = jnp.concatenate([near[:poles] + step * hold[:poles], hold[poles:]], axis=0)
                mine_ref[b] = jnp.where(core > 0, second_core, first_core).astype(BF16)
                out_ref[b * 2 * poles : (b + 1) * 2 * poles, :] = jnp.where(
                    core > 0, first_core, second_core
                ).astype(BF16)
            else:
                new_held_ref[b] = hold
        if not last:
            right_f = jnp.where(is_right, own_f, got_f)
            right_fm = jnp.where(is_right, own_fm, got_fm)
            left_b = jnp.where(is_right, got_b, own_b)
            left_bm = jnp.where(is_right, got_bm, own_bm)
            decay = jnp.exp(-rate * span)
            new = [
                decay * left_f + right_f,
                left_b + decay * right_b,
                decay * (left_fm + span * left_f) + right_fm,
                left_bm + decay * (right_bm + span * right_b),
            ]
            out_ref[b * own_rows : (b + 1) * own_rows, :] = jnp.concatenate(new, axis=0).astype(BF16)
            if slim_ref is not None:
                chosen = jnp.concatenate(
                    [jnp.where(next_right, new[1], new[0]), jnp.where(next_right, new[3], new[2])], axis=0
                )
                slim_ref[b * slim_rows : (b + 1) * slim_rows, :] = chosen.astype(BF16)
    own_tail, got_tail = blocks * own_rows, blocks * got_rows
    cross = mxu_t(jnp.concatenate(wide_terms, axis=1), members(groups, 0, group, blocks * LANES))
    cross = join(cross, 2 * poles)
    total = jnp.where(core > 0, pltpu.roll(cross, groups // 2, 1), cross)
    if level:
        own_tail, got_tail = own_ref[own_tail:, :], got_ref[got_tail:, :]
        tails = [own_tail, got_tail]
        if level == 1:
            tails += [own_sums_ref[...], got_sums_ref[...]]
        for part in tails:
            total = total + join(part[: 4 * poles], 2 * poles)
        skip = sum(join(part[4 * poles :], all_blocks) for part in tails if part.shape[0] > 4 * poles)
        rests = jnp.concatenate([split(total, 2), split(skip, 2)], axis=0)
    else:
        rests = split(total + join(own_sums_ref[...], 2 * poles), 2)
    out_ref[blocks * (2 * poles if last else own_rows) :, :] = rests
    if slim_ref is not None:
        slim_ref[blocks * slim_rows :, :] = rests


def merge_kernel(logs_ref, res_ref, own_ref, got_ref, out_ref, *, poles, length):
    blocks = out_ref.shape[0] - 2 * poles
    groups = out_ref.shape[1]
    start = own_ref.shape[0] - 4 * poles - 2 * blocks
    own, got = own_ref[start:, :], got_ref[start:, :]
    total = join(own[: 4 * poles], 2 * poles) + join(got[: 4 * poles], 2 * poles)
    skip = join(own[4 * poles :], blocks) + join(got[4 * poles :], blocks)
    first = shard_start(groups)
    factor = -jnp.exp(logs_ref[:, pl.ds(first, groups)]) * res_ref[:, pl.ds(first, groups)]
    out_ref[:poles, :] = total[:poles] / length
    out_ref[poles : 2 * poles, :] = factor * total[poles:] / math.sqrt(length)
    out_ref[2 * poles :, :] = skip / math.sqrt(length)


def output_kernel(rows_ref, conv_ref, mine_ref, got_ref, k_ref, v_ref, c_ref, *rest, offset, group, poles):
    gq_ref, gk_ref, gv_ref, mark_ref = rest[-4:]
    mark_ref[...] = jnp.zeros_like(mark_ref)
    tokens, width = gq_ref.shape
    per_block = LANES // group
    step = pl.program_id(0) + offset
    inner = width // LANES
    half_blocks = mine_ref.shape[0]
    core = lax.rem(lax.axis_index("ctx"), 2)
    flip = reversal(tokens)
    ahead = (1 + iota((tokens, LANES), 0)).astype(F32)
    state_group = over(within(iota((poles, 2 * LANES), 1), LANES), group)
    start = step * inner
    is_mine = over(start, half_blocks) == core
    totals = []
    for j in range(inner):
        here = start + j
        rate = rows_ref[0, pl.ds(here, 1), :]
        res = rows_ref[1, pl.ds(here, 1), :]
        table = (res * jnp.exp(-rate * ahead)).astype(BF16)
        place = within(here, half_blocks)
        held = jnp.where(
            is_mine, mine_ref[place], got_ref[pl.ds(pl.multiple_of(place * 2 * poles, 2 * poles), 2 * poles), :]
        )
        states = jnp.concatenate([held[:poles], held[poles:]], axis=1)
        stack = jnp.concatenate(
            [jnp.where(state_group == g, states, jnp.zeros_like(states)) for g in range(per_block)], axis=0
        )
        both = pl.ds(pl.multiple_of(2 * here * LANES, LANES), 2 * LANES)
        totals.append((conv_ref[:, both] + mxu(table, stack)).astype(BF16))
    hidden = jnp.concatenate([t[:, :LANES] for t in totals], axis=1)
    flow = mxu(flip, jnp.concatenate([t[:, LANES:] for t in totals], axis=1))
    cut = pl.ds(pl.multiple_of(start * LANES, LANES), width)
    gq_ref[...] = (c_ref[:, cut].astype(F32) * hidden.astype(F32)).astype(BF16)
    gk_ref[...] = (flow * v_ref[:, cut].astype(F32)).astype(BF16)
    gv_ref[...] = (flow * k_ref[:, cut].astype(F32)).astype(BF16)


def stack_kernel(own_ref, got_ref, _, out_ref):
    rows = own_ref.shape[0]
    out_ref[:rows, :] = own_ref[...]
    out_ref[rows:, :] = got_ref[...]


def assemble_kernel(own_ref, got_ref, res_ref, log_ref, skip_ref, *, shards, poles):
    me = lax.axis_index("ch")
    groups = own_ref.shape[1]
    half = shards // 2
    piece = own_ref.shape[0] // half
    rows = piece - 2 * poles
    for k in range(shards):
        source = lax.bitwise_xor(me, k)
        value = (own_ref if k < half else got_ref)[k % half * piece : (k % half + 1) * piece, :]
        cut = pl.ds(pl.multiple_of(source * groups, LANES), groups)
        res_ref[:, cut] = value[:poles]
        log_ref[:, cut] = value[poles : 2 * poles]
        skip_ref[pl.ds(pl.multiple_of(source * rows, 8), rows), :] = value[2 * poles :]


def local(queries, key_input, value_input, cotangent, residues, log_rates, skip_gain):
    tokens, width = queries.shape
    parts = lax.axis_size("ctx")
    shards = lax.axis_size("ch")
    levels = parts.bit_length() - 1
    all_groups, poles = residues.shape
    groups = all_groups // shards
    group = width // groups
    blocks = width // LANES
    inner = 4
    steps = blocks // inner
    half_blocks = blocks // 2
    lag_width = LANES // group * SUB
    sizes = dict(group=group, poles=poles)
    near_tail, tail = 4 * poles, 4 * poles + 2 * blocks
    full_rows, half_rows = half_blocks * 4 * poles, half_blocks * 2 * poles

    vmem = pl.BlockSpec(memory_space=pltpu.VMEM)
    anywhere = pl.BlockSpec(memory_space=pl.ANY)
    log_rates, residues = log_rates.T, residues.T
    def shape(*dims, dtype=F32):
        return jax.ShapeDtypeStruct(dims, dtype)

    def swap(value, level):
        return lax.ppermute(value, "ctx", [(i, i ^ (1 << level)) for i in range(parts)])

    gated, dgate = gate(key_input, value_input), gate(cotangent, queries)
    outgoing, message, turned, rows = pl.pallas_call(
        lambda *refs: states_kernel(*refs, inner=inner, **sizes),
        in_specs=[vmem] * 4,
        out_specs=[vmem] * 4,
        out_shape=[
            shape(full_rows, LANES, dtype=BF16),
            shape(full_rows, LANES, dtype=BF16),
            shape(tokens, width, dtype=BF16),
            shape(2, blocks, LANES),
        ],
        compiler_params=PARAMS,
        name="states",
    )(log_rates, residues, gated, dgate)

    rates, lag_rates, taps, tables = pl.pallas_call(
        lambda *refs: tables_kernel(*refs, inner=inner, **sizes),
        in_specs=[vmem, vmem, anywhere],
        out_specs=[vmem] * 4,
        out_shape=[
            shape(blocks, poles, LANES),
            shape(blocks, poles, lag_width),
            shape(blocks, lag_width),
            shape(blocks, poles, lag_width, dtype=BF16),
        ],
        compiler_params=PARAMS,
        cost_estimate=pl.CostEstimate(flops=10**9, bytes_accessed=10**6, transcendentals=10**5),
        name="tables",
    )(log_rates, residues, rows)

    def local_sums(after, second):
        return pl.pallas_call(
            lambda *refs: lags_kernel(*refs, second=second, inner=inner, **sizes),
            in_specs=[vmem] * 4 + [anywhere],
            out_specs=vmem,
            out_shape=shape(tail if second else near_tail, LANES, dtype=BF16),
            scratch_shapes=[pltpu.VMEM((blocks, LANES), F32)],
            compiler_params=PARAMS,
            cost_estimate=pl.CostEstimate(
                flops=16 * tokens * tokens * width, bytes_accessed=12 * tokens * width, transcendentals=tokens * width
            ),
            name="lags",
        )(lag_rates, gated, dgate, turned, after)

    def convolve(after):
        skip_rows = skip_gain.reshape(-1, LANES)
        return pl.pallas_call(
            lambda *refs: conv_kernel(*refs, inner=inner, **sizes),
            in_specs=[vmem] * 7 + [anywhere],
            out_specs=vmem,
            out_shape=shape(tokens, 2 * width),
            compiler_params=PARAMS,
            cost_estimate=pl.CostEstimate(
                flops=16 * tokens * tokens * width, bytes_accessed=12 * tokens * width, transcendentals=tokens * width
            ),
            name="conv",
        )(rows, skip_rows, rates, taps, tables, gated, turned, after)

    held = near = None
    for level in range(levels):
        last = level == levels - 1
        got = swap(outgoing, level)
        operands, specs = [rates, message, got], [vmem] * 3
        if level == 0:
            operands.append(local_sums(rows, 0))
            specs.append(vmem)
        elif level == 1:
            sums = local_sums(near, 1)
            operands += [sums, swap(sums, level)]
            specs += [vmem] * 2
        else:
            operands.append(held)
            specs.append(vmem)
        if level == min(2, levels - 1):
            conv = convolve(near if held is None else held)
            operands.append(conv)
            specs.append(anywhere)
        if last:
            operands.append(near)
            specs.append(vmem)
            outs = [shape(half_blocks, 2 * poles, LANES, dtype=BF16), shape(half_rows + tail, LANES, dtype=BF16)]
        else:
            outs = [
                shape(full_rows + (tail if level else near_tail), LANES, dtype=BF16),
                shape(half_blocks, 2 * poles, LANES),
            ]
        if level == levels - 2:
            outs.append(shape(half_rows + (tail if level else near_tail), LANES, dtype=BF16))
        results = pl.pallas_call(
            lambda *refs, level=level: combine_kernel(*refs, level=level, levels=levels, tokens=tokens, **sizes),
            in_specs=specs,
            out_specs=[vmem] * len(outs),
            out_shape=outs,
            compiler_params=PARAMS,
            name="combine",
        )(*operands)
        if last:
            mine, outgoing = results
        else:
            message = results[0]
            outgoing = results[-1] if level == levels - 2 else message
            if level == 0:
                near = results[1]
            else:
                held = results[1]
    got = swap(outgoing, 0)
    merged = pl.pallas_call(
        lambda *refs: merge_kernel(*refs, poles=poles, length=tokens * parts),
        in_specs=[vmem] * 4,
        out_specs=vmem,
        out_shape=shape(2 * poles + blocks, LANES),
        compiler_params=PARAMS,
        name="merge",
    )(log_rates, residues, outgoing, got)

    def emit(offset, before):
        count = steps // 2
        main = pl.BlockSpec((tokens, inner * LANES), lambda i: (0, i + offset))
        return pl.pallas_call(
            lambda *refs: output_kernel(*refs, offset=offset, **sizes),
            grid=(count,),
            in_specs=[vmem] * 7 + [anywhere] * len(before),
            out_specs=[main] * 3 + [pl.BlockSpec((8, LANES), lambda i: (0, 0))],
            out_shape=[shape(tokens, width, dtype=BF16)] * 3 + [shape(8, LANES)],
            input_output_aliases={7 + n: n for n in range(3)} if offset else {},
            compiler_params=PARAMS,
            cost_estimate=pl.CostEstimate(
                flops=4 * tokens * tokens * width, bytes_accessed=8 * tokens * width, transcendentals=tokens * width
            ),
            name="outputs",
        )(rows, conv, mine, got, key_input, value_input, cotangent, *before)

    own, after = merged, []
    for level in range(shards.bit_length() - 1):
        other = lax.ppermute(own, "ch", [(i, i ^ (1 << level)) for i in range(shards)])
        if level == shards.bit_length() - 2:
            break
        if not after:
            after = emit(0, [])
        own = pl.pallas_call(
            stack_kernel,
            in_specs=[vmem, vmem, anywhere],
            out_specs=vmem,
            out_shape=shape(2 * own.shape[0], LANES),
            compiler_params=PARAMS,
            name="stack",
        )(own, other, after[3])
    grad_query, grad_key, grad_value, _ = emit(steps // 2, [*after[:3], own])

    grad_residue, grad_lograte, grad_skip = pl.pallas_call(
        lambda *refs: assemble_kernel(*refs, shards=shards, poles=poles),
        in_specs=[vmem] * 2,
        out_specs=[vmem] * 3,
        out_shape=[shape(poles, all_groups), shape(poles, all_groups), shape(shards * blocks, LANES)],
        compiler_params=PARAMS,
        name="assemble",
    )(own, other)
    return (grad_query, grad_key, grad_value, grad_residue.T, grad_lograte.T, grad_skip.reshape(-1))


def solution(mesh):
    placed = (P("ctx", "ch"), P("ctx", "ch"), P("ctx", "ch"), P("ctx", "ch"), P(), P(), P())
    return jax.shard_map(
        local,
        mesh=mesh,
        in_specs=placed,
        out_specs=(P("ctx", "ch"), P("ctx", "ch"), P("ctx", "ch"), P(), P(), P()),
        check_vma=False,
    )
```

```python
import math

import jax
import jax.numpy as jnp
from jax import lax
from jax.experimental import pallas as pl
from jax.experimental.pallas import tpu as pltpu
from jax.sharding import PartitionSpec as P

LANES = 128
SUB = 32
F32 = jnp.float32
BF16 = jnp.bfloat16
EXACT = lax.Precision.HIGHEST
VMEM_LIMIT = 40 * 1024 * 1024
PARAMS = pltpu.CompilerParams(vmem_limit_bytes=VMEM_LIMIT)


def iota(shape, axis):
    return lax.broadcasted_iota(jnp.int32, shape, axis)


def over(value, size):
    return lax.shift_right_logical(value, size.bit_length() - 1)


def within(value, size):
    return lax.bitwise_and(value, size - 1)


def mxu(left, right):
    return jnp.dot(left, right, preferred_element_type=F32)


def mxu_t(left, right):
    return lax.dot_general(left, right, (((1,), (1,)), ((), ())), preferred_element_type=F32)


def exact_dot(left, right):
    return jnp.dot(left, right, precision=EXACT, preferred_element_type=F32)


def gate(left, right):
    return (left.astype(F32) * right.astype(F32)).astype(BF16)


def reversal(size):
    return jnp.where(iota((size, size), 0) + iota((size, size), 1) == size - 1, 1.0, 0.0).astype(BF16)


def split(value, pieces):
    parts = []
    for _ in range(pieces):
        parts.append(value.astype(BF16))
        value = value - parts[-1].astype(F32)
    return jnp.concatenate(parts, axis=0)


def join(stacked, rows):
    total = stacked[:rows].astype(F32)
    for start in range(rows, stacked.shape[0], rows):
        total = total + stacked[start : start + rows].astype(F32)
    return total


def flat_rows(table, poles):
    table = table.T
    groups = table.shape[0]
    per_row = LANES // poles
    spread = jnp.where(iota((poles, LANES), 0) == within(iota((poles, LANES), 1), poles), 1.0, 0.0)
    wide = exact_dot(table, spread)
    keep = within(iota((groups, LANES), 0), per_row) == over(iota((groups, LANES), 1), poles)
    wide = jnp.where(keep, wide, 0.0)
    return jnp.sum(wide.reshape(groups // per_row, per_row, LANES), axis=1)


def members(groups, first, span, width):
    return jnp.where(iota((groups, width), 0) == first + over(iota((groups, width), 1), span), 1.0, 0.0).astype(BF16)


def shard_start(groups):
    return pl.multiple_of(lax.axis_index("ch") * groups, LANES)


def states_kernel(logs_ref, res_ref, gated_ref, dgate_ref, send_ref, keep_ref, turned_ref, rows_ref,
                  *, group, poles, inner):
    tokens, _ = gated_ref.shape
    per_block = LANES // group
    _, blocks, _ = rows_ref.shape
    half_blocks = blocks // 2
    groups = blocks * per_block
    wide = inner * LANES
    core = lax.rem(lax.axis_index("ctx"), 2)

    first = shard_start(groups)
    rows_ref[0] = jnp.exp(flat_rows(logs_ref[:, pl.ds(first, groups)], poles))
    rows_ref[1] = flat_rows(res_ref[:, pl.ds(first, groups)], poles)

    flip = reversal(tokens)
    back_pos = (tokens - 1 - iota((tokens, LANES), 0)).astype(F32)
    back_lane = (tokens - 1 - iota((1, tokens), 1)).astype(F32)
    wide_group = over(within(iota((poles, 2 * LANES), 1), LANES), group)
    lanes = [slice(j * LANES, (j + 1) * LANES) for j in range(inner)]

    for turn, msg_ref in enumerate((send_ref, keep_ref)):
        base = lax.rem(core + 1 + turn, 2) * half_blocks

        def body(step, carry, base=base, msg_ref=msg_ref):
            start = base + step * inner
            cut = pl.ds(pl.multiple_of(start * LANES, LANES), wide)
            gated, dgate = gated_ref[:, cut], dgate_ref[:, cut]
            turned = mxu(flip, dgate).astype(BF16)
            turned_ref[:, cut] = turned
            tables = [jnp.exp(-rows_ref[0, pl.ds(start + j, 1), :] * back_pos).T for j in range(inner)]
            found = []
            for j in range(inner):
                both = jnp.concatenate([tables[j].astype(BF16), (tables[j] * back_lane).astype(BF16)], axis=0)
                pair = jnp.concatenate([gated[:, lanes[j]], turned[:, lanes[j]]], axis=1)
                found.append(mxu(both, pair))
            for j in range(inner):
                folded = []
                for part in range(2):
                    total = found[j][part * LANES : part * LANES + poles]
                    for g in range(1, per_block):
                        row = part * LANES + g * poles
                        total = jnp.where(wide_group == g, found[j][row : row + poles], total)
                    folded.append(total)
                out = [folded[0][:, :LANES], folded[0][:, LANES:], folded[1][:, :LANES], folded[1][:, LANES:]]
                row = pl.multiple_of((step * inner + j) * 4 * poles, 4 * poles)
                msg_ref[pl.ds(row, 4 * poles), :] = jnp.concatenate(out, axis=0).astype(BF16)
            return carry

        lax.fori_loop(0, half_blocks // inner, body, 0)


def lags_kernel(lag_rates_ref, gated_ref, dgate_ref, turned_ref, *rest, second, group, poles, inner):
    if second:
        first_ref, out_ref, skip_ref = rest
    else:
        (out_ref,) = rest
    tokens, _ = gated_ref.shape
    per_block = LANES // group
    blocks, _, lag_width = lag_rates_ref.shape
    subs = tokens // SUB
    step_groups = inner * per_block
    lane_group = over(iota((SUB, LANES), 1), group)
    row, lane = iota((SUB, lag_width), 0), within(iota((SUB, lag_width), 1), SUB)
    near_side, no_wrap = row + lane <= SUB - 1, lane >= row
    lag = (SUB - 1 - within(iota((poles, lag_width), 1), SUB)).astype(F32)
    spread = members(step_groups, 0, SUB, inner * lag_width)
    half_steps = blocks // inner // 2
    sums = []
    for step in range(half_steps * second, half_steps * (second + 1)):
        outers = []
        for j in range(inner):
            lanes = slice((step * inner + j) * LANES, (step * inner + j + 1) * LANES)
            found = [None] * subs
            for k in range(subs):
                part = gated_ref[k * SUB : (k + 1) * SUB, lanes]
                stack = jnp.concatenate(
                    [jnp.where(lane_group == g, part, jnp.zeros_like(part)) for g in range(per_block)], axis=0
                )
                outer = mxu_t(turned_ref[: (subs - k) * SUB, lanes], stack)
                for n in range(subs - k):
                    far = subs - 1 - k - n
                    piece = outer[n * SUB : (n + 1) * SUB]
                    found[far] = piece if found[far] is None else found[far] + piece
            outers.append(found)
        terms = []
        for j in range(inner):
            found = outers[j] + [jnp.zeros((SUB, lag_width), F32)]
            lags = []
            for far in range(subs):
                total = jnp.where(near_side, found[far], found[far + 1])
                straight = pltpu.roll(total, 0, 1, stride=1, stride_axis=0)
                wrapped = pltpu.roll(total, lag_width - SUB, 1, stride=1, stride_axis=0)
                lags.append(jnp.sum(jnp.where(no_wrap, straight, wrapped), axis=0, keepdims=True))
            rate = lag_rates_ref[step * inner + j]
            decay = jnp.exp(-rate * SUB)
            total = jnp.zeros((poles, lag_width), F32)
            weighted = total
            for far in reversed(range(subs)):
                weighted = decay * weighted + far * lags[far]
                total = decay * total + lags[far]
            table = jnp.exp(-rate * lag)
            terms.append(
                split(jnp.concatenate([table * total, table * (lag * total + SUB * weighted)], axis=0), 2)
            )
        sums.append(mxu_t(jnp.concatenate(terms, axis=1), spread))
    sums = jnp.concatenate(sums, axis=1)
    zeros = jnp.zeros_like(sums)
    sums = jnp.concatenate([zeros, sums] if second else [sums, zeros], axis=1)
    sums = join(sums, 2 * poles)
    if not second:
        out_ref[...] = sums
        return
    for b in range(blocks):
        lanes = slice(b * LANES, (b + 1) * LANES)
        product = gated_ref[:, lanes].astype(F32) * dgate_ref[:, lanes].astype(F32)
        skip_ref[b : b + 1, :] = jnp.sum(product, axis=0, keepdims=True)
    out_ref[: 2 * poles, :] = (first_ref[...] + sums).astype(BF16)
    out_ref[2 * poles :, :] = skip_ref[...].astype(BF16)


def tables_kernel(logs_ref, _, rates_ref, lag_rates_ref, *, group, poles, inner):
    blocks, _, lag_width = lag_rates_ref.shape
    per_block = LANES // group
    groups = blocks * per_block
    step_groups = inner * per_block
    lag_wide = inner * lag_width
    pieces = split(logs_ref[:, pl.ds(shard_start(groups), groups)], 3)
    spread = jnp.concatenate(
        [members(step_groups, 0, SUB, lag_wide), members(step_groups, 0, group, inner * LANES)], axis=1
    )
    for step in range(blocks // inner):
        spreads = mxu(pieces[:, step * step_groups : (step + 1) * step_groups], spread)
        rates = jnp.exp(join(spreads, poles))
        for j in range(inner):
            here = step * inner + j
            lag_rates_ref[here] = rates[:, j * lag_width : (j + 1) * lag_width]
            rates_ref[here] = rates[:, lag_wide + j * LANES : lag_wide + (j + 1) * LANES]


def conv_kernel(res_ref, rows_ref, skip_ref, rates_ref, lag_rates_ref, gated_ref, turned_ref, _, conv_ref,
                *, group, poles, inner):
    tokens, _ = gated_ref.shape
    per_block = LANES // group
    blocks, _, _ = rates_ref.shape
    subs = tokens // SUB
    lag_width = per_block * SUB
    first = lax.axis_index("ch") * blocks
    lead = (1 + iota((SUB, LANES), 0)).astype(F32)
    wide_group = over(within(iota((SUB, 2 * LANES), 1), LANES), group)
    state_group = over(within(iota((poles, 2 * LANES), 1), LANES), group)
    causal = iota((SUB, lag_width), 0) >= within(iota((SUB, lag_width), 1), SUB)
    lag = (SUB - 1 - within(iota((poles, lag_width), 1), SUB)).astype(F32)
    groups = blocks * per_block
    pieces = split(res_ref[:, pl.ds(shard_start(groups), groups)], 3).astype(F32)
    spread = members(groups, 0, SUB, inner * lag_width)

    def body(step, carry):
        start = step * inner
        moved = pltpu.roll(pieces, groups - start * per_block, 1).astype(BF16)
        lag_res = join(mxu(moved, spread), poles)
        lefts, lead_tables, decays, pairs, gains = [], [], [], [], []
        for j in range(inner):
            here = start + j
            table = jnp.exp(-lag_rates_ref[here] * lag)
            taps = jnp.sum(lag_res[:, j * lag_width : (j + 1) * lag_width] * table, axis=0, keepdims=True)
            taps = jnp.broadcast_to(taps, (SUB, lag_width))
            taps = pltpu.roll(taps, lag_width - SUB + 1, 1, stride=1, stride_axis=0)
            taps = jnp.where(causal, taps, 0.0).astype(BF16)
            lefts.append(jnp.concatenate([taps, table.astype(BF16)], axis=0))
            rate = rows_ref[0, pl.ds(here, 1), :]
            res = rows_ref[1, pl.ds(here, 1), :]
            lead_tables.append((res * jnp.exp(-rate * lead)).astype(BF16))
            decay = jnp.exp(-rates_ref[here] * SUB)
            decays.append(jnp.concatenate([decay, decay], axis=1))
            cut = pl.ds(pl.multiple_of(here * LANES, LANES), LANES)
            pairs.append(jnp.concatenate([gated_ref[:, cut], turned_ref[:, cut]], axis=1))
            gain = skip_ref[pl.ds(first + here, 1), :]
            gains.append(jnp.concatenate([gain, gain], axis=1))
        states = [jnp.zeros((poles, 2 * LANES), F32)] * inner
        totals = [[] for _ in range(inner)]
        for k in range(subs):
            rows = slice(k * SUB, (k + 1) * SUB)
            found = []
            for j in range(inner):
                part = pairs[j][rows]
                stack = [jnp.where(wide_group == g, part, jnp.zeros_like(part)) for g in range(per_block)]
                found.append(mxu(lefts[j], jnp.concatenate(stack, axis=0)))
            for j in range(inner):
                total = found[j][:SUB] + gains[j] * pairs[j][rows].astype(F32)
                if k:
                    held = states[j].astype(BF16)
                    stack = [jnp.where(state_group == g, held, jnp.zeros_like(held)) for g in range(per_block)]
                    total = total + mxu(lead_tables[j], jnp.concatenate(stack, axis=0))
                totals[j].append(total)
            states = [decays[j] * states[j] + found[j][SUB:] for j in range(inner)]
        for j in range(inner):
            cut = pl.ds(pl.multiple_of(2 * (start + j) * LANES, LANES), 2 * LANES)
            conv_ref[:, cut] = jnp.concatenate(totals[j], axis=0)
        return carry

    lax.fori_loop(0, blocks // inner, body, 0)


def combine_kernel(*refs, level, levels, group, poles, tokens):
    last = level == levels - 1
    refs = list(refs)
    rates_ref = refs.pop(0)
    all_blocks = rates_ref.shape[0]
    blocks = all_blocks // 2
    per_block = LANES // group
    groups = all_blocks * per_block
    rows = 2 * poles
    if level == 0:
        own_ref, got_ref, sums_ref, states_ref, total_ref, near_ref = refs
    else:
        own_ref, own_tail_ref, got_ref = refs.pop(0), refs.pop(0), refs.pop(0)
        got_tail_ref = None if last else refs.pop(0)
        held_ref = refs.pop(0) if level > 1 else None
        if level == min(2, levels - 1):
            refs.pop(0)
        if last:
            near_ref, mine_ref, out_ref = refs
        else:
            states_ref, tail_ref, new_held_ref = refs[:3]
            slim_ref = refs[3] if level == levels - 2 else None
    me = lax.axis_index("ctx")
    core = lax.rem(me, 2)
    is_right = lax.rem(lax.shift_right_logical(me, level), 2) == 1
    before = lax.rem(me, 2**level) - (core if level else 0)
    gap_left = (tokens * before).astype(F32)
    gap_right = (tokens * (2**level - 2 - before)).astype(F32)
    gap = jnp.where(is_right, gap_left, gap_right)
    span = float(tokens * 2**level)
    next_right = lax.rem(lax.shift_right_logical(me, level + 1), 2) == 1

    def quarters(ref, b):
        value = ref[2 * b * rows : 2 * (b + 1) * rows].astype(F32)
        return [value[n * poles : (n + 1) * poles] for n in range(4)]

    wide_terms = []
    for b in range(blocks):
        rate = rates_ref[core * blocks + b]
        own_f, own_b, own_fm, own_bm = quarters(own_ref, b)
        if last:
            got = got_ref[b * rows : (b + 1) * rows].astype(F32)
            got_f = got_b = got[:poles]
            got_fm = got_bm = got[poles:]
        else:
            got_f, got_b, got_fm, got_bm = quarters(got_ref, b)
        left_f = jnp.where(is_right, got_f, own_f)
        left_fm = jnp.where(is_right, got_fm, own_fm)
        right_b = jnp.where(is_right, own_b, got_b)
        right_bm = jnp.where(is_right, own_bm, got_bm)
        once = jnp.exp(-rate)
        cross_res = once * (right_b * left_f)
        cross_mom = once * (right_bm * left_f + right_b * (left_fm + left_f))
        wide_terms.append(split(jnp.concatenate([cross_res, cross_mom], axis=0), 2))
        if level == 0:
            near_ref[b] = jnp.concatenate([left_f, right_b], axis=0)
        else:
            carry = jnp.exp(-rate * gap) * jnp.where(is_right, left_f, right_b)
            zero = jnp.zeros_like(carry)
            hold = jnp.concatenate([jnp.where(is_right, carry, zero), jnp.where(is_right, zero, carry)], axis=0)
            if level > 1:
                hold = hold + held_ref[b]
            if last:
                step = jnp.exp(-rate * tokens)
                near = near_ref[b]
                first_core = jnp.concatenate([hold[:poles], near[poles:] + step * hold[poles:]], axis=0)
                second_core = jnp.concatenate([near[:poles] + step * hold[:poles], hold[poles:]], axis=0)
                mine_ref[b] = jnp.where(core > 0, second_core, first_core).astype(BF16)
                out_ref[b * rows : (b + 1) * rows, :] = jnp.where(core > 0, first_core, second_core).astype(BF16)
            else:
                new_held_ref[b] = hold
        if not last:
            right_f = jnp.where(is_right, own_f, got_f)
            right_fm = jnp.where(is_right, own_fm, got_fm)
            left_b = jnp.where(is_right, got_b, own_b)
            left_bm = jnp.where(is_right, got_bm, own_bm)
            decay = jnp.exp(-rate * span)
            new_f, new_b = decay * left_f + right_f, left_b + decay * right_b
            new_fm = decay * (left_fm + span * left_f) + right_fm
            new_bm = left_bm + decay * (right_bm + span * right_b)
            here = slice(b * rows, (b + 1) * rows)
            new = jnp.concatenate([new_f, new_b, new_fm, new_bm], axis=0).astype(BF16)
            states_ref[2 * b * rows : 2 * (b + 1) * rows, :] = new
            if level == levels - 2 and level:
                chosen = [jnp.where(next_right, new_b, new_f), jnp.where(next_right, new_bm, new_fm)]
                slim_ref[here, :] = jnp.concatenate(chosen, axis=0).astype(BF16)
    cross = join(mxu_t(jnp.concatenate(wide_terms, axis=1), members(groups, 0, group, blocks * LANES)), rows)
    cross = jnp.where(core > 0, pltpu.roll(cross, groups // 2, 1), cross)
    tail = blocks * rows
    if level == 0:
        total_ref[...] = cross + sums_ref[...]
        return
    got_tail = got_ref[tail:, :] if last else got_tail_ref[...]
    both = own_tail_ref[...].astype(F32) + got_tail.astype(F32)
    rests = jnp.concatenate([both[:rows] + cross, both[rows:]], axis=0).astype(BF16)
    if last:
        out_ref[tail:, :] = rests
    else:
        tail_ref[...] = rests
        if slim_ref is not None:
            slim_ref[tail:, :] = rests


def merge_kernel(logs_ref, res_ref, own_ref, got_ref, out_ref, *, poles, length):
    groups = out_ref.shape[1]
    start = own_ref.shape[0] - out_ref.shape[0]
    both = own_ref[start:, :].astype(F32) + got_ref[start:, :].astype(F32)
    first = shard_start(groups)
    factor = -jnp.exp(logs_ref[:, pl.ds(first, groups)]) * res_ref[:, pl.ds(first, groups)]
    scaled = [
        both[:poles] / length,
        factor * both[poles : 2 * poles] / math.sqrt(length),
        both[2 * poles :] / math.sqrt(length),
    ]
    out_ref[...] = jnp.concatenate(scaled, axis=0).astype(BF16)


def output_kernel(rows_ref, conv_ref, mine_ref, got_ref, k_ref, v_ref, c_ref, *rest, offset, group, poles):
    gq_ref, gk_ref, gv_ref, mark_ref = rest[-4:]
    mark_ref[...] = jnp.zeros_like(mark_ref)
    tokens, width = gq_ref.shape
    per_block = LANES // group
    step = pl.program_id(0) + offset
    inner = width // LANES
    half_blocks = mine_ref.shape[0]
    core = lax.rem(lax.axis_index("ctx"), 2)
    flip = reversal(tokens)
    ahead = (1 + iota((tokens, LANES), 0)).astype(F32)
    state_group = over(within(iota((poles, 2 * LANES), 1), LANES), group)
    start = step * inner
    is_mine = over(start, half_blocks) == core
    totals = []
    for j in range(inner):
        here = start + j
        rate = rows_ref[0, pl.ds(here, 1), :]
        res = rows_ref[1, pl.ds(here, 1), :]
        table = (res * jnp.exp(-rate * ahead)).astype(BF16)
        place = within(here, half_blocks)
        held = jnp.where(
            is_mine, mine_ref[place], got_ref[pl.ds(pl.multiple_of(place * 2 * poles, 2 * poles), 2 * poles), :]
        )
        states = jnp.concatenate([held[:poles], held[poles:]], axis=1)
        stack = jnp.concatenate(
            [jnp.where(state_group == g, states, jnp.zeros_like(states)) for g in range(per_block)], axis=0
        )
        both = pl.ds(pl.multiple_of(2 * here * LANES, LANES), 2 * LANES)
        totals.append((conv_ref[:, both] + mxu(table, stack)).astype(BF16))
    hidden = jnp.concatenate([t[:, :LANES] for t in totals], axis=1)
    flow = mxu(flip, jnp.concatenate([t[:, LANES:] for t in totals], axis=1))
    cut = pl.ds(pl.multiple_of(start * LANES, LANES), width)
    gq_ref[...] = (c_ref[:, cut].astype(F32) * hidden.astype(F32)).astype(BF16)
    gk_ref[...] = (flow * v_ref[:, cut].astype(F32)).astype(BF16)
    gv_ref[...] = (flow * k_ref[:, cut].astype(F32)).astype(BF16)


def stack_kernel(own_ref, got_ref, _, out_ref):
    rows = own_ref.shape[0]
    out_ref[:rows, :] = own_ref[...]
    out_ref[rows:, :] = got_ref[...]


def assemble_kernel(own_ref, got_ref, res_ref, log_ref, skip_ref, *, masks, poles):
    shards = len(masks)
    me = lax.axis_index("ch")
    groups = own_ref.shape[1]
    half = shards // 2
    piece = own_ref.shape[0] // half
    rows = piece - 2 * poles
    for k, mask in enumerate(masks):
        source = lax.bitwise_xor(me, mask)
        value = (own_ref if k < half else got_ref)[k % half * piece : (k % half + 1) * piece, :].astype(F32)
        cut = pl.ds(pl.multiple_of(source * groups, LANES), groups)
        res_ref[:, cut] = value[:poles]
        log_ref[:, cut] = value[poles : 2 * poles]
        skip_ref[pl.ds(pl.multiple_of(source * rows, 8), rows), :] = value[2 * poles :]


def local(queries, key_input, value_input, cotangent, residues, log_rates, skip_gain):
    tokens, width = queries.shape
    parts = lax.axis_size("ctx")
    shards = lax.axis_size("ch")
    levels = parts.bit_length() - 1
    all_groups, poles = residues.shape
    groups = all_groups // shards
    group = width // groups
    blocks = width // LANES
    inner = 4
    steps = blocks // inner
    half_blocks = blocks // 2
    lag_width = LANES // group * SUB
    sizes = dict(group=group, poles=poles)
    half_rows, tail = half_blocks * 2 * poles, 2 * poles + blocks

    vmem = pl.BlockSpec(memory_space=pltpu.VMEM)
    anywhere = pl.BlockSpec(memory_space=pl.ANY)
    log_rates, residues = log_rates.T, residues.T
    def shape(*dims, dtype=F32):
        return jax.ShapeDtypeStruct(dims, dtype)

    def swap(value, level):
        return lax.ppermute(value, "ctx", [(i, i ^ (1 << level)) for i in range(parts)])

    gated, dgate = gate(key_input, value_input), gate(cotangent, queries)
    outgoing, message, turned, rows = pl.pallas_call(
        lambda *refs: states_kernel(*refs, inner=inner, **sizes),
        in_specs=[vmem] * 4,
        out_specs=[vmem] * 4,
        out_shape=[
            shape(2 * half_rows, LANES, dtype=BF16),
            shape(2 * half_rows, LANES, dtype=BF16),
            shape(tokens, width, dtype=BF16),
            shape(2, blocks, LANES),
        ],
        compiler_params=PARAMS,
        name="states",
    )(log_rates, residues, gated, dgate)

    rates, lag_rates = pl.pallas_call(
        lambda *refs: tables_kernel(*refs, inner=inner, **sizes),
        in_specs=[vmem, anywhere],
        out_specs=[vmem] * 2,
        out_shape=[shape(blocks, poles, LANES), shape(blocks, poles, lag_width)],
        compiler_params=PARAMS,
        cost_estimate=pl.CostEstimate(flops=10**9, bytes_accessed=10**6, transcendentals=10**5),
        name="tables",
    )(log_rates, rows)

    work = pl.CostEstimate(
        flops=16 * tokens * tokens * width, bytes_accessed=12 * tokens * width, transcendentals=tokens * width
    )

    def local_sums(second, *more):
        return pl.pallas_call(
            lambda *refs: lags_kernel(*refs, second=second, inner=inner, **sizes),
            in_specs=[vmem] * (4 + len(more)),
            out_specs=vmem,
            out_shape=shape(tail, LANES, dtype=BF16) if second else shape(2 * poles, LANES),
            scratch_shapes=[pltpu.VMEM((blocks, LANES), F32)] if second else [],
            compiler_params=PARAMS,
            cost_estimate=work,
            name="lags",
        )(lag_rates, gated, dgate, turned, *more)

    def convolve(after):
        skip_rows = skip_gain.reshape(-1, LANES)
        return pl.pallas_call(
            lambda *refs: conv_kernel(*refs, inner=inner, **sizes),
            in_specs=[vmem] * 7 + [anywhere],
            out_specs=vmem,
            out_shape=shape(tokens, 2 * width),
            compiler_params=PARAMS,
            cost_estimate=work,
            name="conv",
        )(residues, rows, skip_rows, rates, lag_rates, gated, turned, after)

    def combine(level, operands, outs):
        return pl.pallas_call(
            lambda *refs: combine_kernel(*refs, level=level, levels=levels, tokens=tokens, **sizes),
            in_specs=[anywhere if x is conv else vmem for x in operands],
            out_specs=[vmem] * len(outs),
            out_shape=outs,
            compiler_params=PARAMS,
            name="combine",
        )(*operands)

    conv = None
    states_shape = shape(2 * half_rows, LANES, dtype=BF16)
    tail_shape = shape(tail, LANES, dtype=BF16)
    slim_shape = shape(half_rows + tail, LANES, dtype=BF16)
    held_shape = shape(half_blocks, 2 * poles, LANES)
    got = swap(outgoing, 0)
    states, total, near = combine(
        0, [rates, message, got, local_sums(0)], [states_shape, shape(2 * poles, LANES), held_shape]
    )
    held = slim = None
    for level in range(1, levels):
        last = level == levels - 1
        if last and slim is not None:
            received = [swap(slim, level)]
        else:
            received = [swap(states, level)]
            if level == 1:
                carried = local_sums(1, total)
            received.append(swap(carried, level))
        operands = [rates, states, carried, *received]
        if level > 1:
            operands.append(held)
        if level == min(2, levels - 1):
            conv = convolve(near if held is None else held)
            operands.append(conv)
        if last:
            outs = [shape(half_blocks, 2 * poles, LANES, dtype=BF16), slim_shape]
            mine, outgoing = combine(level, [*operands, near], outs)
        else:
            outs = [states_shape, tail_shape, held_shape]
            if level == levels - 2:
                outs.append(slim_shape)
            states, carried, held, *more = combine(level, operands, outs)
            slim = more[0] if more else None
    got = swap(outgoing, 0)
    merged = pl.pallas_call(
        lambda *refs: merge_kernel(*refs, poles=poles, length=tokens * parts),
        in_specs=[vmem] * 4,
        out_specs=vmem,
        out_shape=shape(tail, LANES, dtype=BF16),
        compiler_params=PARAMS,
        name="merge",
    )(log_rates, residues, outgoing, got)

    def emit(offset, before):
        count = steps // 2
        main = pl.BlockSpec((tokens, inner * LANES), lambda i: (0, i + offset))
        return pl.pallas_call(
            lambda *refs: output_kernel(*refs, offset=offset, **sizes),
            grid=(count,),
            in_specs=[vmem] * 7 + [anywhere] * len(before),
            out_specs=[main] * 3 + [pl.BlockSpec((8, LANES), lambda i: (0, 0))],
            out_shape=[shape(tokens, width, dtype=BF16)] * 3 + [shape(8, LANES)],
            input_output_aliases={7 + n: n for n in range(3)} if offset else {},
            compiler_params=PARAMS,
            cost_estimate=pl.CostEstimate(
                flops=4 * tokens * tokens * width, bytes_accessed=8 * tokens * width, transcendentals=tokens * width
            ),
            name="outputs",
        )(rows, conv, mine, got, key_input, value_input, cotangent, *before)

    own, after, masks = merged, [], [0]
    for level in reversed(range(shards.bit_length() - 1)):
        other = lax.ppermute(own, "ch", [(i, i ^ (1 << level)) for i in range(shards)])
        masks += [mask ^ (1 << level) for mask in masks]
        if level == 0:
            break
        if not after:
            after = emit(0, [])
        own = pl.pallas_call(
            stack_kernel,
            in_specs=[vmem, vmem, anywhere],
            out_specs=vmem,
            out_shape=shape(2 * own.shape[0], LANES, dtype=BF16),
            compiler_params=PARAMS,
            name="stack",
        )(own, other, after[3])
    grad_query, grad_key, grad_value, _ = emit(steps // 2, [*after[:3], own])

    grad_residue, grad_lograte, grad_skip = pl.pallas_call(
        lambda *refs: assemble_kernel(*refs, masks=masks, poles=poles),
        in_specs=[vmem] * 2,
        out_specs=[vmem] * 3,
        out_shape=[shape(poles, all_groups), shape(poles, all_groups), shape(shards * blocks, LANES)],
        compiler_params=PARAMS,
        name="assemble",
    )(own, other)
    return (grad_query, grad_key, grad_value, grad_residue.T, grad_lograte.T, grad_skip.reshape(-1))


def solution(mesh):
    placed = (P("ctx", "ch"), P("ctx", "ch"), P("ctx", "ch"), P("ctx", "ch"), P(), P(), P())
    return jax.shard_map(
        local,
        mesh=mesh,
        in_specs=placed,
        out_specs=(P("ctx", "ch"), P("ctx", "ch"), P("ctx", "ch"), P(), P(), P()),
        check_vma=False,
    )
```

```python
import math

import jax
import jax.numpy as jnp
from jax import lax
from jax.experimental import pallas as pl
from jax.experimental.pallas import tpu as pltpu
from jax.sharding import PartitionSpec as P

LANES = 128
SUB = 32
F32 = jnp.float32
BF16 = jnp.bfloat16
EXACT = lax.Precision.HIGHEST
VMEM_LIMIT = 40 * 1024 * 1024
PARAMS = pltpu.CompilerParams(vmem_limit_bytes=VMEM_LIMIT)


def iota(shape, axis):
    return lax.broadcasted_iota(jnp.int32, shape, axis)


def over(value, size):
    return lax.shift_right_logical(value, size.bit_length() - 1)


def within(value, size):
    return lax.bitwise_and(value, size - 1)


def mxu(left, right):
    return jnp.dot(left, right, preferred_element_type=F32)


def mxu_t(left, right):
    return lax.dot_general(left, right, (((1,), (1,)), ((), ())), preferred_element_type=F32)


def exact_dot(left, right):
    return jnp.dot(left, right, precision=EXACT, preferred_element_type=F32)


def gate(left, right):
    return (left.astype(F32) * right.astype(F32)).astype(BF16)


def reversal(size):
    return jnp.where(iota((size, size), 0) + iota((size, size), 1) == size - 1, 1.0, 0.0).astype(BF16)


def split(value, pieces):
    parts = []
    for _ in range(pieces):
        parts.append(value.astype(BF16))
        value = value - parts[-1].astype(F32)
    return jnp.concatenate(parts, axis=0)


def join(stacked, rows):
    total = stacked[:rows].astype(F32)
    for start in range(rows, stacked.shape[0], rows):
        total = total + stacked[start : start + rows].astype(F32)
    return total


def flat_rows(table, poles):
    table = table.T
    groups = table.shape[0]
    per_row = LANES // poles
    spread = jnp.where(iota((poles, LANES), 0) == within(iota((poles, LANES), 1), poles), 1.0, 0.0)
    wide = exact_dot(table, spread)
    keep = within(iota((groups, LANES), 0), per_row) == over(iota((groups, LANES), 1), poles)
    wide = jnp.where(keep, wide, 0.0)
    return jnp.sum(wide.reshape(groups // per_row, per_row, LANES), axis=1)


def members(groups, first, span, width):
    return jnp.where(iota((groups, width), 0) == first + over(iota((groups, width), 1), span), 1.0, 0.0).astype(BF16)


def shard_start(groups):
    return pl.multiple_of(lax.axis_index("ch") * groups, LANES)


def states_kernel(logs_ref, res_ref, gated_ref, dgate_ref, send_ref, keep_ref, turned_ref, rows_ref,
                  *, group, poles, inner):
    tokens, _ = gated_ref.shape
    per_block = LANES // group
    _, blocks, _ = rows_ref.shape
    half_blocks = blocks // 2
    groups = blocks * per_block
    wide = inner * LANES
    core = lax.rem(lax.axis_index("ctx"), 2)

    first = shard_start(groups)
    rows_ref[0] = jnp.exp(flat_rows(logs_ref[:, pl.ds(first, groups)], poles))
    rows_ref[1] = flat_rows(res_ref[:, pl.ds(first, groups)], poles)

    flip = reversal(tokens)
    back_pos = (tokens - 1 - iota((tokens, LANES), 0)).astype(F32)
    back_lane = (tokens - 1 - iota((1, tokens), 1)).astype(F32)
    wide_group = over(within(iota((poles, 2 * LANES), 1), LANES), group)
    lanes = [slice(j * LANES, (j + 1) * LANES) for j in range(inner)]

    for turn, msg_ref in enumerate((send_ref, keep_ref)):
        base = lax.rem(core + 1 + turn, 2) * half_blocks

        def body(step, carry, base=base, msg_ref=msg_ref):
            start = base + step * inner
            cut = pl.ds(pl.multiple_of(start * LANES, LANES), wide)
            gated, dgate = gated_ref[:, cut], dgate_ref[:, cut]
            turned = mxu(flip, dgate).astype(BF16)
            turned_ref[:, cut] = turned
            tables = [jnp.exp(-rows_ref[0, pl.ds(start + j, 1), :] * back_pos).T for j in range(inner)]
            found = []
            for j in range(inner):
                both = jnp.concatenate([tables[j].astype(BF16), (tables[j] * back_lane).astype(BF16)], axis=0)
                pair = jnp.concatenate([gated[:, lanes[j]], turned[:, lanes[j]]], axis=1)
                found.append(mxu(both, pair))
            for j in range(inner):
                folded = []
                for part in range(2):
                    total = found[j][part * LANES : part * LANES + poles]
                    for g in range(1, per_block):
                        row = part * LANES + g * poles
                        total = jnp.where(wide_group == g, found[j][row : row + poles], total)
                    folded.append(total)
                out = [folded[0][:, :LANES], folded[0][:, LANES:], folded[1][:, :LANES], folded[1][:, LANES:]]
                row = pl.multiple_of((step * inner + j) * 4 * poles, 4 * poles)
                msg_ref[pl.ds(row, 4 * poles), :] = jnp.concatenate(out, axis=0).astype(BF16)
            return carry

        lax.fori_loop(0, half_blocks // inner, body, 0)


def lags_kernel(lag_rates_ref, gated_ref, dgate_ref, turned_ref, *rest, second, group, poles, inner):
    if second:
        first_ref, out_ref, skip_ref = rest
    else:
        (out_ref,) = rest
    tokens, _ = gated_ref.shape
    per_block = LANES // group
    blocks, _, lag_width = lag_rates_ref.shape
    subs = tokens // SUB
    step_groups = inner * per_block
    lane_group = over(iota((SUB, LANES), 1), group)
    row, lane = iota((SUB, lag_width), 0), within(iota((SUB, lag_width), 1), SUB)
    near_side, no_wrap = row + lane <= SUB - 1, lane >= row
    lag = (SUB - 1 - within(iota((poles, lag_width), 1), SUB)).astype(F32)
    spread = members(step_groups, 0, SUB, inner * lag_width)
    half_steps = blocks // inner // 2
    sums = []
    for step in range(half_steps * second, half_steps * (second + 1)):
        outers = []
        for j in range(inner):
            lanes = slice((step * inner + j) * LANES, (step * inner + j + 1) * LANES)
            found = [None] * subs
            for k in range(subs):
                part = gated_ref[k * SUB : (k + 1) * SUB, lanes]
                stack = jnp.concatenate(
                    [jnp.where(lane_group == g, part, jnp.zeros_like(part)) for g in range(per_block)], axis=0
                )
                outer = mxu_t(turned_ref[: (subs - k) * SUB, lanes], stack)
                for n in range(subs - k):
                    far = subs - 1 - k - n
                    piece = outer[n * SUB : (n + 1) * SUB]
                    found[far] = piece if found[far] is None else found[far] + piece
            outers.append(found)
        terms = []
        for j in range(inner):
            found = outers[j] + [jnp.zeros((SUB, lag_width), F32)]
            lags = []
            for far in range(subs):
                total = jnp.where(near_side, found[far], found[far + 1])
                straight = pltpu.roll(total, 0, 1, stride=1, stride_axis=0)
                wrapped = pltpu.roll(total, lag_width - SUB, 1, stride=1, stride_axis=0)
                lags.append(jnp.sum(jnp.where(no_wrap, straight, wrapped), axis=0, keepdims=True))
            rate = lag_rates_ref[step * inner + j]
            decay = jnp.exp(-rate * SUB)
            total = jnp.zeros((poles, lag_width), F32)
            weighted = total
            for far in reversed(range(subs)):
                weighted = decay * weighted + far * lags[far]
                total = decay * total + lags[far]
            table = jnp.exp(-rate * lag)
            terms.append(
                split(jnp.concatenate([table * total, table * (lag * total + SUB * weighted)], axis=0), 2)
            )
        sums.append(mxu_t(jnp.concatenate(terms, axis=1), spread))
    sums = jnp.concatenate(sums, axis=1)
    zeros = jnp.zeros_like(sums)
    sums = jnp.concatenate([zeros, sums] if second else [sums, zeros], axis=1)
    sums = join(sums, 2 * poles)
    if not second:
        out_ref[...] = sums
        return
    for b in range(blocks):
        lanes = slice(b * LANES, (b + 1) * LANES)
        product = gated_ref[:, lanes].astype(F32) * dgate_ref[:, lanes].astype(F32)
        skip_ref[b : b + 1, :] = jnp.sum(product, axis=0, keepdims=True)
    out_ref[: 2 * poles, :] = (first_ref[...] + sums).astype(BF16)
    out_ref[2 * poles :, :] = skip_ref[...].astype(BF16)


def tables_kernel(logs_ref, _, rates_ref, lag_rates_ref, *, group, poles, inner):
    blocks, _, lag_width = lag_rates_ref.shape
    per_block = LANES // group
    groups = blocks * per_block
    step_groups = inner * per_block
    lag_wide = inner * lag_width
    pieces = split(logs_ref[:, pl.ds(shard_start(groups), groups)], 3)
    spread = jnp.concatenate(
        [members(step_groups, 0, SUB, lag_wide), members(step_groups, 0, group, inner * LANES)], axis=1
    )
    for step in range(blocks // inner):
        spreads = mxu(pieces[:, step * step_groups : (step + 1) * step_groups], spread)
        rates = jnp.exp(join(spreads, poles))
        for j in range(inner):
            here = step * inner + j
            lag_rates_ref[here] = rates[:, j * lag_width : (j + 1) * lag_width]
            rates_ref[here] = rates[:, lag_wide + j * LANES : lag_wide + (j + 1) * LANES]


def conv_kernel(res_ref, rows_ref, skip_ref, rates_ref, lag_rates_ref, gated_ref, turned_ref, _, conv_ref,
                *, group, poles, inner):
    tokens, _ = gated_ref.shape
    per_block = LANES // group
    blocks, _, _ = rates_ref.shape
    subs = tokens // SUB
    lag_width = per_block * SUB
    first = lax.axis_index("ch") * blocks
    lead = (1 + iota((SUB, LANES), 0)).astype(F32)
    wide_group = over(within(iota((SUB, 2 * LANES), 1), LANES), group)
    state_group = over(within(iota((poles, 2 * LANES), 1), LANES), group)
    causal = iota((SUB, lag_width), 0) >= within(iota((SUB, lag_width), 1), SUB)
    lag = (SUB - 1 - within(iota((poles, lag_width), 1), SUB)).astype(F32)
    groups = blocks * per_block
    pieces = split(res_ref[:, pl.ds(shard_start(groups), groups)], 3).astype(F32)
    spread = members(groups, 0, SUB, inner * lag_width)

    def body(step, carry):
        start = step * inner
        moved = pltpu.roll(pieces, groups - start * per_block, 1).astype(BF16)
        lag_res = join(mxu(moved, spread), poles)
        lefts, lead_tables, decays, pairs, gains = [], [], [], [], []
        for j in range(inner):
            here = start + j
            table = jnp.exp(-lag_rates_ref[here] * lag)
            taps = jnp.sum(lag_res[:, j * lag_width : (j + 1) * lag_width] * table, axis=0, keepdims=True)
            taps = jnp.broadcast_to(taps, (SUB, lag_width))
            taps = pltpu.roll(taps, lag_width - SUB + 1, 1, stride=1, stride_axis=0)
            taps = jnp.where(causal, taps, 0.0).astype(BF16)
            lefts.append(jnp.concatenate([taps, table.astype(BF16)], axis=0))
            rate = rows_ref[0, pl.ds(here, 1), :]
            res = rows_ref[1, pl.ds(here, 1), :]
            lead_tables.append((res * jnp.exp(-rate * lead)).astype(BF16))
            decay = jnp.exp(-rates_ref[here] * SUB)
            decays.append(jnp.concatenate([decay, decay], axis=1))
            cut = pl.ds(pl.multiple_of(here * LANES, LANES), LANES)
            pairs.append(jnp.concatenate([gated_ref[:, cut], turned_ref[:, cut]], axis=1))
            gain = skip_ref[pl.ds(first + here, 1), :]
            gains.append(jnp.concatenate([gain, gain], axis=1))
        states = [jnp.zeros((poles, 2 * LANES), F32)] * inner
        totals = [[] for _ in range(inner)]
        for k in range(subs):
            rows = slice(k * SUB, (k + 1) * SUB)
            found = []
            for j in range(inner):
                part = pairs[j][rows]
                stack = [jnp.where(wide_group == g, part, jnp.zeros_like(part)) for g in range(per_block)]
                found.append(mxu(lefts[j], jnp.concatenate(stack, axis=0)))
            for j in range(inner):
                total = found[j][:SUB] + gains[j] * pairs[j][rows].astype(F32)
                if k:
                    held = states[j].astype(BF16)
                    stack = [jnp.where(state_group == g, held, jnp.zeros_like(held)) for g in range(per_block)]
                    total = total + mxu(lead_tables[j], jnp.concatenate(stack, axis=0))
                totals[j].append(total)
            states = [decays[j] * states[j] + found[j][SUB:] for j in range(inner)]
        for j in range(inner):
            cut = pl.ds(pl.multiple_of(2 * (start + j) * LANES, LANES), 2 * LANES)
            conv_ref[:, cut] = jnp.concatenate(totals[j], axis=0)
        return carry

    lax.fori_loop(0, blocks // inner, body, 0)


def combine_kernel(*refs, level, levels, group, poles, tokens):
    last = level == levels - 1
    refs = list(refs)
    rates_ref = refs.pop(0)
    all_blocks = rates_ref.shape[0]
    blocks = all_blocks // 2
    per_block = LANES // group
    groups = all_blocks * per_block
    rows = 2 * poles
    if level == 0:
        own_ref, got_ref, sums_ref, states_ref, total_ref, near_ref = refs
    else:
        own_ref, own_tail_ref, got_ref = refs.pop(0), refs.pop(0), refs.pop(0)
        got_tail_ref = None if last else refs.pop(0)
        held_ref = refs.pop(0) if level > 1 else None
        if level == min(2, levels - 1):
            refs.pop(0)
        if last:
            near_ref, mine_ref, out_ref = refs
        else:
            states_ref, tail_ref, new_held_ref = refs[:3]
            slim_ref = refs[3] if level == levels - 2 else None
    me = lax.axis_index("ctx")
    core = lax.rem(me, 2)
    is_right = lax.rem(lax.shift_right_logical(me, level), 2) == 1
    before = lax.rem(me, 2**level) - (core if level else 0)
    gap_left = (tokens * before).astype(F32)
    gap_right = (tokens * (2**level - 2 - before)).astype(F32)
    gap = jnp.where(is_right, gap_left, gap_right)
    span = float(tokens * 2**level)
    next_right = lax.rem(lax.shift_right_logical(me, level + 1), 2) == 1

    def quarters(ref, b):
        value = ref[2 * b * rows : 2 * (b + 1) * rows].astype(F32)
        return [value[n * poles : (n + 1) * poles] for n in range(4)]

    wide_terms = []
    for b in range(blocks):
        rate = rates_ref[core * blocks + b]
        own_f, own_b, own_fm, own_bm = quarters(own_ref, b)
        if last:
            got = got_ref[b * rows : (b + 1) * rows].astype(F32)
            got_f = got_b = got[:poles]
            got_fm = got_bm = got[poles:]
        else:
            got_f, got_b, got_fm, got_bm = quarters(got_ref, b)
        left_f = jnp.where(is_right, got_f, own_f)
        left_fm = jnp.where(is_right, got_fm, own_fm)
        right_b = jnp.where(is_right, own_b, got_b)
        right_bm = jnp.where(is_right, own_bm, got_bm)
        once = jnp.exp(-rate)
        cross_res = once * (right_b * left_f)
        cross_mom = once * (right_bm * left_f + right_b * (left_fm + left_f))
        wide_terms.append(split(jnp.concatenate([cross_res, cross_mom], axis=0), 2))
        if level == 0:
            near_ref[b] = jnp.concatenate([left_f, right_b], axis=0)
        else:
            carry = jnp.exp(-rate * gap) * jnp.where(is_right, left_f, right_b)
            zero = jnp.zeros_like(carry)
            hold = jnp.concatenate([jnp.where(is_right, carry, zero), jnp.where(is_right, zero, carry)], axis=0)
            if level > 1:
                hold = hold + held_ref[b]
            if last:
                step = jnp.exp(-rate * tokens)
                near = near_ref[b]
                first_core = jnp.concatenate([hold[:poles], near[poles:] + step * hold[poles:]], axis=0)
                second_core = jnp.concatenate([near[:poles] + step * hold[:poles], hold[poles:]], axis=0)
                mine_ref[b] = jnp.where(core > 0, second_core, first_core).astype(BF16)
                out_ref[b * rows : (b + 1) * rows, :] = jnp.where(core > 0, first_core, second_core).astype(BF16)
            else:
                new_held_ref[b] = hold
        if not last:
            right_f = jnp.where(is_right, own_f, got_f)
            right_fm = jnp.where(is_right, own_fm, got_fm)
            left_b = jnp.where(is_right, got_b, own_b)
            left_bm = jnp.where(is_right, got_bm, own_bm)
            decay = jnp.exp(-rate * span)
            new_f, new_b = decay * left_f + right_f, left_b + decay * right_b
            new_fm = decay * (left_fm + span * left_f) + right_fm
            new_bm = left_bm + decay * (right_bm + span * right_b)
            here = slice(b * rows, (b + 1) * rows)
            new = jnp.concatenate([new_f, new_b, new_fm, new_bm], axis=0).astype(BF16)
            states_ref[2 * b * rows : 2 * (b + 1) * rows, :] = new
            if level == levels - 2 and level:
                chosen = [jnp.where(next_right, new_b, new_f), jnp.where(next_right, new_bm, new_fm)]
                slim_ref[here, :] = jnp.concatenate(chosen, axis=0).astype(BF16)
    cross = join(mxu_t(jnp.concatenate(wide_terms, axis=1), members(groups, 0, group, blocks * LANES)), rows)
    cross = jnp.where(core > 0, pltpu.roll(cross, groups // 2, 1), cross)
    tail = blocks * rows
    if level == 0:
        total_ref[...] = cross + sums_ref[...]
        return
    got_tail = got_ref[tail:, :] if last else got_tail_ref[...]
    both = own_tail_ref[...].astype(F32) + got_tail.astype(F32)
    rests = jnp.concatenate([both[:rows] + cross, both[rows:]], axis=0).astype(BF16)
    if last:
        out_ref[tail:, :] = rests
    else:
        tail_ref[...] = rests
        if slim_ref is not None:
            slim_ref[tail:, :] = rests


def merge_kernel(logs_ref, res_ref, own_ref, got_ref, out_ref, *, poles, length):
    groups = out_ref.shape[2]
    start = own_ref.shape[0] - out_ref.shape[1]
    both = own_ref[start:, :].astype(F32) + got_ref[start:, :].astype(F32)
    first = shard_start(groups)
    factor = -jnp.exp(logs_ref[:, pl.ds(first, groups)]) * res_ref[:, pl.ds(first, groups)]
    scaled = [
        both[:poles] / length,
        factor * both[poles : 2 * poles] / math.sqrt(length),
        both[2 * poles :] / math.sqrt(length),
    ]
    scaled = jnp.concatenate(scaled, axis=0).astype(BF16)
    for n in range(out_ref.shape[0]):
        out_ref[n] = scaled


def output_kernel(rows_ref, conv_ref, mine_ref, got_ref, k_ref, v_ref, c_ref, gq_ref, gk_ref, gv_ref,
                  mark_ref, *, group, poles):
    mark_ref[...] = jnp.zeros_like(mark_ref)
    tokens, width = gq_ref.shape
    per_block = LANES // group
    step = pl.program_id(0)
    inner = width // LANES
    half_blocks = mine_ref.shape[0]
    core = lax.rem(lax.axis_index("ctx"), 2)
    flip = reversal(tokens)
    ahead = (1 + iota((tokens, LANES), 0)).astype(F32)
    state_group = over(within(iota((poles, 2 * LANES), 1), LANES), group)
    start = step * inner
    is_mine = over(start, half_blocks) == core
    totals = []
    for j in range(inner):
        here = start + j
        rate = rows_ref[0, pl.ds(here, 1), :]
        res = rows_ref[1, pl.ds(here, 1), :]
        table = (res * jnp.exp(-rate * ahead)).astype(BF16)
        place = within(here, half_blocks)
        held = jnp.where(
            is_mine, mine_ref[place], got_ref[pl.ds(pl.multiple_of(place * 2 * poles, 2 * poles), 2 * poles), :]
        )
        states = jnp.concatenate([held[:poles], held[poles:]], axis=1)
        stack = jnp.concatenate(
            [jnp.where(state_group == g, states, jnp.zeros_like(states)) for g in range(per_block)], axis=0
        )
        both = pl.ds(pl.multiple_of(2 * here * LANES, LANES), 2 * LANES)
        totals.append((conv_ref[:, both] + mxu(table, stack)).astype(BF16))
    hidden = jnp.concatenate([t[:, :LANES] for t in totals], axis=1)
    flow = mxu(flip, jnp.concatenate([t[:, LANES:] for t in totals], axis=1))
    cut = pl.ds(pl.multiple_of(start * LANES, LANES), width)
    gq_ref[...] = (c_ref[:, cut].astype(F32) * hidden.astype(F32)).astype(BF16)
    gk_ref[...] = (flow * v_ref[:, cut].astype(F32)).astype(BF16)
    gv_ref[...] = (flow * k_ref[:, cut].astype(F32)).astype(BF16)


def assemble_kernel(pieces_ref, _, res_ref, log_ref, skip_ref, *, poles):
    shards, rows, groups = pieces_ref.shape
    rows -= 2 * poles
    for n in range(shards):
        value = pieces_ref[n].astype(F32)
        cut = slice(n * groups, (n + 1) * groups)
        res_ref[:, cut] = value[:poles]
        log_ref[:, cut] = value[poles : 2 * poles]
        skip_ref[n * rows : (n + 1) * rows, :] = value[2 * poles :]


def local(queries, key_input, value_input, cotangent, residues, log_rates, skip_gain):
    tokens, width = queries.shape
    parts = lax.axis_size("ctx")
    shards = lax.axis_size("ch")
    levels = parts.bit_length() - 1
    all_groups, poles = residues.shape
    groups = all_groups // shards
    group = width // groups
    blocks = width // LANES
    inner = 4
    steps = blocks // inner
    half_blocks = blocks // 2
    lag_width = LANES // group * SUB
    sizes = dict(group=group, poles=poles)
    half_rows, tail = half_blocks * 2 * poles, 2 * poles + blocks

    vmem = pl.BlockSpec(memory_space=pltpu.VMEM)
    anywhere = pl.BlockSpec(memory_space=pl.ANY)
    log_rates, residues = log_rates.T, residues.T
    def shape(*dims, dtype=F32):
        return jax.ShapeDtypeStruct(dims, dtype)

    def swap(value, level):
        return lax.ppermute(value, "ctx", [(i, i ^ (1 << level)) for i in range(parts)])

    gated, dgate = gate(key_input, value_input), gate(cotangent, queries)
    outgoing, message, turned, rows = pl.pallas_call(
        lambda *refs: states_kernel(*refs, inner=inner, **sizes),
        in_specs=[vmem] * 4,
        out_specs=[vmem] * 4,
        out_shape=[
            shape(2 * half_rows, LANES, dtype=BF16),
            shape(2 * half_rows, LANES, dtype=BF16),
            shape(tokens, width, dtype=BF16),
            shape(2, blocks, LANES),
        ],
        compiler_params=PARAMS,
        name="states",
    )(log_rates, residues, gated, dgate)

    rates, lag_rates = pl.pallas_call(
        lambda *refs: tables_kernel(*refs, inner=inner, **sizes),
        in_specs=[vmem, anywhere],
        out_specs=[vmem] * 2,
        out_shape=[shape(blocks, poles, LANES), shape(blocks, poles, lag_width)],
        compiler_params=PARAMS,
        cost_estimate=pl.CostEstimate(flops=10**9, bytes_accessed=10**6, transcendentals=10**5),
        name="tables",
    )(log_rates, rows)

    work = pl.CostEstimate(
        flops=16 * tokens * tokens * width, bytes_accessed=12 * tokens * width, transcendentals=tokens * width
    )

    def local_sums(second, *more):
        return pl.pallas_call(
            lambda *refs: lags_kernel(*refs, second=second, inner=inner, **sizes),
            in_specs=[vmem] * (4 + len(more)),
            out_specs=vmem,
            out_shape=shape(tail, LANES, dtype=BF16) if second else shape(2 * poles, LANES),
            scratch_shapes=[pltpu.VMEM((blocks, LANES), F32)] if second else [],
            compiler_params=PARAMS,
            cost_estimate=work,
            name="lags",
        )(lag_rates, gated, dgate, turned, *more)

    def convolve(after):
        skip_rows = skip_gain.reshape(-1, LANES)
        return pl.pallas_call(
            lambda *refs: conv_kernel(*refs, inner=inner, **sizes),
            in_specs=[vmem] * 7 + [anywhere],
            out_specs=vmem,
            out_shape=shape(tokens, 2 * width),
            compiler_params=PARAMS,
            cost_estimate=work,
            name="conv",
        )(residues, rows, skip_rows, rates, lag_rates, gated, turned, after)

    def combine(level, operands, outs):
        return pl.pallas_call(
            lambda *refs: combine_kernel(*refs, level=level, levels=levels, tokens=tokens, **sizes),
            in_specs=[anywhere if x is conv else vmem for x in operands],
            out_specs=[vmem] * len(outs),
            out_shape=outs,
            compiler_params=PARAMS,
            name="combine",
        )(*operands)

    conv = None
    states_shape = shape(2 * half_rows, LANES, dtype=BF16)
    tail_shape = shape(tail, LANES, dtype=BF16)
    slim_shape = shape(half_rows + tail, LANES, dtype=BF16)
    held_shape = shape(half_blocks, 2 * poles, LANES)
    got = swap(outgoing, 0)
    states, total, near = combine(
        0, [rates, message, got, local_sums(0)], [states_shape, shape(2 * poles, LANES), held_shape]
    )
    held = slim = None
    for level in range(1, levels):
        last = level == levels - 1
        if last and slim is not None:
            received = [swap(slim, level)]
        else:
            received = [swap(states, level)]
            if level == 1:
                carried = local_sums(1, total)
            received.append(swap(carried, level))
        operands = [rates, states, carried, *received]
        if level > 1:
            operands.append(held)
        if level == min(2, levels - 1):
            conv = convolve(near if held is None else held)
            operands.append(conv)
        if last:
            outs = [shape(half_blocks, 2 * poles, LANES, dtype=BF16), slim_shape]
            mine, outgoing = combine(level, [*operands, near], outs)
        else:
            outs = [states_shape, tail_shape, held_shape]
            if level == levels - 2:
                outs.append(slim_shape)
            states, carried, held, *more = combine(level, operands, outs)
            slim = more[0] if more else None
    got = swap(outgoing, 0)
    merged = pl.pallas_call(
        lambda *refs: merge_kernel(*refs, poles=poles, length=tokens * parts),
        in_specs=[vmem] * 4,
        out_specs=vmem,
        out_shape=shape(shards, tail, LANES, dtype=BF16),
        compiler_params=PARAMS,
        name="merge",
    )(log_rates, residues, outgoing, got)

    pieces = lax.all_to_all(merged, "ch", split_axis=0, concat_axis=0, tiled=True)

    main = pl.BlockSpec((tokens, inner * LANES), lambda i: (0, i))
    grad_query, grad_key, grad_value, mark = pl.pallas_call(
        lambda *refs: output_kernel(*refs, **sizes),
        grid=(steps,),
        in_specs=[vmem] * 7,
        out_specs=[main] * 3 + [pl.BlockSpec((8, LANES), lambda i: (0, 0))],
        out_shape=[shape(tokens, width, dtype=BF16)] * 3 + [shape(8, LANES)],
        compiler_params=PARAMS,
        cost_estimate=work,
        name="outputs",
    )(rows, conv, mine, got, key_input, value_input, cotangent)

    grad_residue, grad_lograte, grad_skip = pl.pallas_call(
        lambda *refs: assemble_kernel(*refs, poles=poles),
        in_specs=[vmem] * 2,
        out_specs=[vmem] * 3,
        out_shape=[shape(poles, all_groups), shape(poles, all_groups), shape(shards * blocks, LANES)],
        compiler_params=PARAMS,
        name="assemble",
    )(pieces, mark)
    return (grad_query, grad_key, grad_value, grad_residue.T, grad_lograte.T, grad_skip.reshape(-1))


def solution(mesh):
    placed = (P("ctx", "ch"), P("ctx", "ch"), P("ctx", "ch"), P("ctx", "ch"), P(), P(), P())
    return jax.shard_map(
        local,
        mesh=mesh,
        in_specs=placed,
        out_specs=(P("ctx", "ch"), P("ctx", "ch"), P("ctx", "ch"), P(), P(), P()),
        check_vma=False,
    )
```

```python
import math

import jax
import jax.numpy as jnp
from jax import lax
from jax.experimental import pallas as pl
from jax.experimental.pallas import tpu as pltpu
from jax.sharding import PartitionSpec as P

LANES = 128
SUB = 32
F32 = jnp.float32
BF16 = jnp.bfloat16
EXACT = lax.Precision.HIGHEST
VMEM_LIMIT = 40 * 1024 * 1024
PARAMS = pltpu.CompilerParams(vmem_limit_bytes=VMEM_LIMIT)


def iota(shape, axis):
    return lax.broadcasted_iota(jnp.int32, shape, axis)


def over(value, size):
    return lax.shift_right_logical(value, size.bit_length() - 1)


def within(value, size):
    return lax.bitwise_and(value, size - 1)


def mxu(left, right):
    return jnp.dot(left, right, preferred_element_type=F32)


def mxu_t(left, right):
    return lax.dot_general(left, right, (((1,), (1,)), ((), ())), preferred_element_type=F32)


def exact_dot(left, right):
    return jnp.dot(left, right, precision=EXACT, preferred_element_type=F32)


def gate(left, right):
    return (left.astype(F32) * right.astype(F32)).astype(BF16)


def reversal(size):
    return jnp.where(iota((size, size), 0) + iota((size, size), 1) == size - 1, 1.0, 0.0).astype(BF16)


def split(value, pieces):
    parts = []
    for _ in range(pieces):
        parts.append(value.astype(BF16))
        value = value - parts[-1].astype(F32)
    return jnp.concatenate(parts, axis=0)


def join(stacked, rows):
    total = stacked[:rows].astype(F32)
    for start in range(rows, stacked.shape[0], rows):
        total = total + stacked[start : start + rows].astype(F32)
    return total


def flat_rows(table, poles):
    table = table.T
    groups = table.shape[0]
    per_row = LANES // poles
    spread = jnp.where(iota((poles, LANES), 0) == within(iota((poles, LANES), 1), poles), 1.0, 0.0)
    wide = exact_dot(table, spread)
    keep = within(iota((groups, LANES), 0), per_row) == over(iota((groups, LANES), 1), poles)
    wide = jnp.where(keep, wide, 0.0)
    return jnp.sum(wide.reshape(groups // per_row, per_row, LANES), axis=1)


def members(groups, first, span, width):
    return jnp.where(iota((groups, width), 0) == first + over(iota((groups, width), 1), span), 1.0, 0.0).astype(BF16)


def shard_start(groups):
    return pl.multiple_of(lax.axis_index("ch") * groups, LANES)


def states_kernel(logs_ref, res_ref, gated_ref, dgate_ref, send_ref, keep_ref, turned_ref, rows_ref,
                  *, group, poles, inner):
    tokens, _ = gated_ref.shape
    per_block = LANES // group
    _, blocks, _ = rows_ref.shape
    half_blocks = blocks // 2
    groups = blocks * per_block
    wide = inner * LANES
    core = lax.rem(lax.axis_index("ctx"), 2)

    first = shard_start(groups)
    rows_ref[0] = jnp.exp(flat_rows(logs_ref[:, pl.ds(first, groups)], poles))
    rows_ref[1] = flat_rows(res_ref[:, pl.ds(first, groups)], poles)

    flip = reversal(tokens)
    back_pos = (tokens - 1 - iota((tokens, LANES), 0)).astype(F32)
    back_lane = (tokens - 1 - iota((1, tokens), 1)).astype(F32)
    wide_group = over(within(iota((poles, 2 * LANES), 1), LANES), group)
    lanes = [slice(j * LANES, (j + 1) * LANES) for j in range(inner)]

    for turn, msg_ref in enumerate((send_ref, keep_ref)):
        base = lax.rem(core + 1 + turn, 2) * half_blocks

        def body(step, carry, base=base, msg_ref=msg_ref):
            start = base + step * inner
            cut = pl.ds(pl.multiple_of(start * LANES, LANES), wide)
            gated, dgate = gated_ref[:, cut], dgate_ref[:, cut]
            turned = mxu(flip, dgate).astype(BF16)
            turned_ref[:, cut] = turned
            tables = [jnp.exp(-rows_ref[0, pl.ds(start + j, 1), :] * back_pos).T for j in range(inner)]
            found = []
            for j in range(inner):
                both = jnp.concatenate([tables[j].astype(BF16), (tables[j] * back_lane).astype(BF16)], axis=0)
                pair = jnp.concatenate([gated[:, lanes[j]], turned[:, lanes[j]]], axis=1)
                found.append(mxu(both, pair))
            for j in range(inner):
                folded = []
                for part in range(2):
                    total = found[j][part * LANES : part * LANES + poles]
                    for g in range(1, per_block):
                        row = part * LANES + g * poles
                        total = jnp.where(wide_group == g, found[j][row : row + poles], total)
                    folded.append(total)
                out = [folded[0][:, :LANES], folded[0][:, LANES:], folded[1][:, :LANES], folded[1][:, LANES:]]
                row = pl.multiple_of((step * inner + j) * 4 * poles, 4 * poles)
                msg_ref[pl.ds(row, 4 * poles), :] = jnp.concatenate(out, axis=0).astype(BF16)
            return carry

        lax.fori_loop(0, half_blocks // inner, body, 0)


def lags_kernel(lag_rates_ref, gated_ref, dgate_ref, turned_ref, *rest, second, group, poles, inner):
    if second:
        first_ref, out_ref, skip_ref = rest
    else:
        (out_ref,) = rest
    tokens, _ = gated_ref.shape
    per_block = LANES // group
    blocks, _, lag_width = lag_rates_ref.shape
    subs = tokens // SUB
    step_groups = inner * per_block
    lane_group = over(iota((SUB, LANES), 1), group)
    row, lane = iota((SUB, lag_width), 0), within(iota((SUB, lag_width), 1), SUB)
    near_side, no_wrap = row + lane <= SUB - 1, lane >= row
    lag = (SUB - 1 - within(iota((poles, lag_width), 1), SUB)).astype(F32)
    spread = members(step_groups, 0, SUB, inner * lag_width)
    steps = blocks // inner
    sums = []
    for step in range(1, steps) if second else range(1):
        outers = []
        for j in range(inner):
            lanes = slice((step * inner + j) * LANES, (step * inner + j + 1) * LANES)
            found = [None] * subs
            for k in range(subs):
                part = gated_ref[k * SUB : (k + 1) * SUB, lanes]
                stack = jnp.concatenate(
                    [jnp.where(lane_group == g, part, jnp.zeros_like(part)) for g in range(per_block)], axis=0
                )
                outer = mxu_t(turned_ref[: (subs - k) * SUB, lanes], stack)
                for n in range(subs - k):
                    far = subs - 1 - k - n
                    piece = outer[n * SUB : (n + 1) * SUB]
                    found[far] = piece if found[far] is None else found[far] + piece
            outers.append(found)
        terms = []
        for j in range(inner):
            found = outers[j] + [jnp.zeros((SUB, lag_width), F32)]
            lags = []
            for far in range(subs):
                total = jnp.where(near_side, found[far], found[far + 1])
                straight = pltpu.roll(total, 0, 1, stride=1, stride_axis=0)
                wrapped = pltpu.roll(total, lag_width - SUB, 1, stride=1, stride_axis=0)
                lags.append(jnp.sum(jnp.where(no_wrap, straight, wrapped), axis=0, keepdims=True))
            rate = lag_rates_ref[step * inner + j]
            decay = jnp.exp(-rate * SUB)
            total = jnp.zeros((poles, lag_width), F32)
            weighted = total
            for far in reversed(range(subs)):
                weighted = decay * weighted + far * lags[far]
                total = decay * total + lags[far]
            table = jnp.exp(-rate * lag)
            terms.append(
                split(jnp.concatenate([table * total, table * (lag * total + SUB * weighted)], axis=0), 2)
            )
        sums.append(mxu_t(jnp.concatenate(terms, axis=1), spread))
    sums = jnp.concatenate(sums, axis=1)
    zeros = jnp.zeros((sums.shape[0], blocks * per_block - sums.shape[1]), F32)
    sums = jnp.concatenate([zeros, sums] if second else [sums, zeros], axis=1)
    sums = join(sums, 2 * poles)
    if not second:
        out_ref[...] = sums
        return
    for b in range(blocks):
        lanes = slice(b * LANES, (b + 1) * LANES)
        product = gated_ref[:, lanes].astype(F32) * dgate_ref[:, lanes].astype(F32)
        skip_ref[b : b + 1, :] = jnp.sum(product, axis=0, keepdims=True)
    out_ref[: 2 * poles, :] = (first_ref[...] + sums).astype(BF16)
    out_ref[2 * poles :, :] = skip_ref[...].astype(BF16)


def tables_kernel(logs_ref, _, rates_ref, lag_rates_ref, *, group, poles, inner):
    blocks, _, lag_width = lag_rates_ref.shape
    per_block = LANES // group
    groups = blocks * per_block
    step_groups = inner * per_block
    lag_wide = inner * lag_width
    pieces = split(logs_ref[:, pl.ds(shard_start(groups), groups)], 3)
    spread = jnp.concatenate(
        [members(step_groups, 0, SUB, lag_wide), members(step_groups, 0, group, inner * LANES)], axis=1
    )
    for step in range(blocks // inner):
        spreads = mxu(pieces[:, step * step_groups : (step + 1) * step_groups], spread)
        rates = jnp.exp(join(spreads, poles))
        for j in range(inner):
            here = step * inner + j
            lag_rates_ref[here] = rates[:, j * lag_width : (j + 1) * lag_width]
            rates_ref[here] = rates[:, lag_wide + j * LANES : lag_wide + (j + 1) * LANES]


def conv_kernel(res_ref, rows_ref, skip_ref, rates_ref, lag_rates_ref, gated_ref, turned_ref, _, conv_ref,
                *, first_step, group, poles, inner):
    tokens, _ = gated_ref.shape
    per_block = LANES // group
    blocks, _, _ = rates_ref.shape
    subs = tokens // SUB
    lag_width = per_block * SUB
    first = lax.axis_index("ch") * blocks
    lead = (1 + iota((SUB, LANES), 0)).astype(F32)
    wide_group = over(within(iota((SUB, 2 * LANES), 1), LANES), group)
    state_group = over(within(iota((poles, 2 * LANES), 1), LANES), group)
    causal = iota((SUB, lag_width), 0) >= within(iota((SUB, lag_width), 1), SUB)
    lag = (SUB - 1 - within(iota((poles, lag_width), 1), SUB)).astype(F32)
    groups = blocks * per_block
    pieces = split(res_ref[:, pl.ds(shard_start(groups), groups)], 3).astype(F32)
    spread = members(groups, 0, SUB, inner * lag_width)

    def body(step, carry):
        start = (step + first_step) * inner
        moved = pltpu.roll(pieces, groups - start * per_block, 1).astype(BF16)
        lag_res = join(mxu(moved, spread), poles)
        lefts, lead_tables, decays, pairs, gains = [], [], [], [], []
        for j in range(inner):
            here = start + j
            table = jnp.exp(-lag_rates_ref[here] * lag)
            taps = jnp.sum(lag_res[:, j * lag_width : (j + 1) * lag_width] * table, axis=0, keepdims=True)
            taps = jnp.broadcast_to(taps, (SUB, lag_width))
            taps = pltpu.roll(taps, lag_width - SUB + 1, 1, stride=1, stride_axis=0)
            taps = jnp.where(causal, taps, 0.0).astype(BF16)
            lefts.append(jnp.concatenate([taps, table.astype(BF16)], axis=0))
            rate = rows_ref[0, pl.ds(here, 1), :]
            res = rows_ref[1, pl.ds(here, 1), :]
            lead_tables.append((res * jnp.exp(-rate * lead)).astype(BF16))
            decay = jnp.exp(-rates_ref[here] * SUB)
            decays.append(jnp.concatenate([decay, decay], axis=1))
            cut = pl.ds(pl.multiple_of(here * LANES, LANES), LANES)
            pairs.append(jnp.concatenate([gated_ref[:, cut], turned_ref[:, cut]], axis=1))
            gain = skip_ref[pl.ds(first + here, 1), :]
            gains.append(jnp.concatenate([gain, gain], axis=1))
        states = [jnp.zeros((poles, 2 * LANES), F32)] * inner
        totals = [[] for _ in range(inner)]
        for k in range(subs):
            rows = slice(k * SUB, (k + 1) * SUB)
            found = []
            for j in range(inner):
                part = pairs[j][rows]
                stack = [jnp.where(wide_group == g, part, jnp.zeros_like(part)) for g in range(per_block)]
                found.append(mxu(lefts[j], jnp.concatenate(stack, axis=0)))
            for j in range(inner):
                total = found[j][:SUB] + gains[j] * pairs[j][rows].astype(F32)
                if k:
                    held = states[j].astype(BF16)
                    stack = [jnp.where(state_group == g, held, jnp.zeros_like(held)) for g in range(per_block)]
                    total = total + mxu(lead_tables[j], jnp.concatenate(stack, axis=0))
                totals[j].append(total)
            states = [decays[j] * states[j] + found[j][SUB:] for j in range(inner)]
        for j in range(inner):
            cut = pl.ds(pl.multiple_of(2 * (step * inner + j) * LANES, LANES), 2 * LANES)
            conv_ref[:, cut] = jnp.concatenate(totals[j], axis=0)
        return carry

    lax.fori_loop(0, conv_ref.shape[1] // (2 * inner * LANES), body, 0)


def combine_kernel(*refs, level, levels, group, poles, tokens):
    last = level == levels - 1
    refs = list(refs)
    rates_ref = refs.pop(0)
    all_blocks = rates_ref.shape[0]
    blocks = all_blocks // 2
    per_block = LANES // group
    groups = all_blocks * per_block
    rows = 2 * poles
    if level == 0:
        own_ref, got_ref, sums_ref, states_ref, total_ref, near_ref = refs
    else:
        own_ref, own_tail_ref, got_ref = refs.pop(0), refs.pop(0), refs.pop(0)
        got_tail_ref = None if last else refs.pop(0)
        held_ref = refs.pop(0) if level > 1 else None
        if level == min(2, levels - 1):
            refs.pop(0)
        if last:
            near_ref, mine_ref, out_ref = refs
        else:
            states_ref, tail_ref, new_held_ref = refs[:3]
            slim_ref = refs[3] if level == levels - 2 else None
    me = lax.axis_index("ctx")
    core = lax.rem(me, 2)
    is_right = lax.rem(lax.shift_right_logical(me, level), 2) == 1
    before = lax.rem(me, 2**level) - (core if level else 0)
    gap_left = (tokens * before).astype(F32)
    gap_right = (tokens * (2**level - 2 - before)).astype(F32)
    gap = jnp.where(is_right, gap_left, gap_right)
    span = float(tokens * 2**level)
    next_right = lax.rem(lax.shift_right_logical(me, level + 1), 2) == 1

    def quarters(ref, b):
        value = ref[2 * b * rows : 2 * (b + 1) * rows].astype(F32)
        return [value[n * poles : (n + 1) * poles] for n in range(4)]

    wide_terms = []
    for b in range(blocks):
        rate = rates_ref[core * blocks + b]
        own_f, own_b, own_fm, own_bm = quarters(own_ref, b)
        if last:
            got = got_ref[b * rows : (b + 1) * rows].astype(F32)
            got_f = got_b = got[:poles]
            got_fm = got_bm = got[poles:]
        else:
            got_f, got_b, got_fm, got_bm = quarters(got_ref, b)
        left_f = jnp.where(is_right, got_f, own_f)
        left_fm = jnp.where(is_right, got_fm, own_fm)
        right_b = jnp.where(is_right, own_b, got_b)
        right_bm = jnp.where(is_right, own_bm, got_bm)
        once = jnp.exp(-rate)
        cross_res = once * (right_b * left_f)
        cross_mom = once * (right_bm * left_f + right_b * (left_fm + left_f))
        wide_terms.append(split(jnp.concatenate([cross_res, cross_mom], axis=0), 2))
        if level == 0:
            near_ref[b] = jnp.concatenate([left_f, right_b], axis=0)
        else:
            carry = jnp.exp(-rate * gap) * jnp.where(is_right, left_f, right_b)
            zero = jnp.zeros_like(carry)
            hold = jnp.concatenate([jnp.where(is_right, carry, zero), jnp.where(is_right, zero, carry)], axis=0)
            if level > 1:
                hold = hold + held_ref[b]
            if last:
                step = jnp.exp(-rate * tokens)
                near = near_ref[b]
                first_core = jnp.concatenate([hold[:poles], near[poles:] + step * hold[poles:]], axis=0)
                second_core = jnp.concatenate([near[:poles] + step * hold[:poles], hold[poles:]], axis=0)
                mine_ref[b] = jnp.where(core > 0, second_core, first_core).astype(BF16)
                out_ref[b * rows : (b + 1) * rows, :] = jnp.where(core > 0, first_core, second_core).astype(BF16)
            else:
                new_held_ref[b] = hold
        if not last:
            right_f = jnp.where(is_right, own_f, got_f)
            right_fm = jnp.where(is_right, own_fm, got_fm)
            left_b = jnp.where(is_right, got_b, own_b)
            left_bm = jnp.where(is_right, got_bm, own_bm)
            decay = jnp.exp(-rate * span)
            new_f, new_b = decay * left_f + right_f, left_b + decay * right_b
            new_fm = decay * (left_fm + span * left_f) + right_fm
            new_bm = left_bm + decay * (right_bm + span * right_b)
            here = slice(b * rows, (b + 1) * rows)
            new = jnp.concatenate([new_f, new_b, new_fm, new_bm], axis=0).astype(BF16)
            states_ref[2 * b * rows : 2 * (b + 1) * rows, :] = new
            if level == levels - 2 and level:
                chosen = [jnp.where(next_right, new_b, new_f), jnp.where(next_right, new_bm, new_fm)]
                slim_ref[here, :] = jnp.concatenate(chosen, axis=0).astype(BF16)
    cross = join(mxu_t(jnp.concatenate(wide_terms, axis=1), members(groups, 0, group, blocks * LANES)), rows)
    cross = jnp.where(core > 0, pltpu.roll(cross, groups // 2, 1), cross)
    tail = blocks * rows
    if level == 0:
        total_ref[...] = cross + sums_ref[...]
        return
    got_tail = got_ref[tail:, :] if last else got_tail_ref[...]
    both = own_tail_ref[...].astype(F32) + got_tail.astype(F32)
    rests = jnp.concatenate([both[:rows] + cross, both[rows:]], axis=0).astype(BF16)
    if last:
        out_ref[tail:, :] = rests
    else:
        tail_ref[...] = rests
        if slim_ref is not None:
            slim_ref[tail:, :] = rests


def merge_kernel(logs_ref, res_ref, own_ref, got_ref, _, out_ref, *, poles, length):
    groups = out_ref.shape[1]
    start = own_ref.shape[0] - out_ref.shape[0]
    both = own_ref[start:, :].astype(F32) + got_ref[start:, :].astype(F32)
    first = shard_start(groups)
    factor = -jnp.exp(logs_ref[:, pl.ds(first, groups)]) * res_ref[:, pl.ds(first, groups)]
    scaled = [
        both[:poles] / length,
        factor * both[poles : 2 * poles] / math.sqrt(length),
        both[2 * poles :] / math.sqrt(length),
    ]
    out_ref[...] = jnp.concatenate(scaled, axis=0).astype(BF16)


def output_kernel(rows_ref, conv_ref, last_ref, mine_ref, got_ref, k_ref, v_ref, c_ref, gq_ref, gk_ref, gv_ref,
                  *, group, poles):
    tokens, width = gq_ref.shape
    per_block = LANES // group
    step = pl.program_id(0)
    steps = pl.num_programs(0)
    inner = width // LANES
    half_blocks = mine_ref.shape[0]
    core = lax.rem(lax.axis_index("ctx"), 2)
    flip = reversal(tokens)
    ahead = (1 + iota((tokens, LANES), 0)).astype(F32)
    state_group = over(within(iota((poles, 2 * LANES), 1), LANES), group)
    start = step * inner
    is_mine = over(start, half_blocks) == core
    cut = pl.ds(pl.multiple_of(start * LANES, LANES), width)

    def emit(conv_ref, base):
        totals = []
        for j in range(inner):
            here = start + j
            rate = rows_ref[0, pl.ds(here, 1), :]
            res = rows_ref[1, pl.ds(here, 1), :]
            table = (res * jnp.exp(-rate * ahead)).astype(BF16)
            place = within(here, half_blocks)
            held = jnp.where(
                is_mine, mine_ref[place], got_ref[pl.ds(pl.multiple_of(place * 2 * poles, 2 * poles), 2 * poles), :]
            )
            states = jnp.concatenate([held[:poles], held[poles:]], axis=1)
            stack = jnp.concatenate(
                [jnp.where(state_group == g, states, jnp.zeros_like(states)) for g in range(per_block)], axis=0
            )
            both = pl.ds(pl.multiple_of(2 * (here - base) * LANES, LANES), 2 * LANES)
            totals.append((conv_ref[:, both] + mxu(table, stack)).astype(BF16))
        hidden = jnp.concatenate([t[:, :LANES] for t in totals], axis=1)
        flow = mxu(flip, jnp.concatenate([t[:, LANES:] for t in totals], axis=1))
        gq_ref[...] = (c_ref[:, cut].astype(F32) * hidden.astype(F32)).astype(BF16)
        gk_ref[...] = (flow * v_ref[:, cut].astype(F32)).astype(BF16)
        gv_ref[...] = (flow * k_ref[:, cut].astype(F32)).astype(BF16)

    @pl.when(step < steps - 1)
    def _():
        emit(conv_ref, 0)

    @pl.when(step == steps - 1)
    def _():
        emit(last_ref, (steps - 1) * inner)


def assemble_kernel(*refs, poles):
    *slots, res_ref, log_ref, skip_ref = refs
    shards = len(slots)
    me = lax.axis_index("ch")
    groups = slots[0].shape[1]
    rows = slots[0].shape[0] - 2 * poles
    for shift, slot in enumerate(slots):
        source = lax.rem(me - shift + shards, shards)
        value = slot[...].astype(F32)
        cut = pl.ds(pl.multiple_of(source * groups, LANES), groups)
        res_ref[:, cut] = value[:poles]
        log_ref[:, cut] = value[poles : 2 * poles]
        skip_ref[pl.ds(pl.multiple_of(source * rows, 8), rows), :] = value[2 * poles :]


def local(queries, key_input, value_input, cotangent, residues, log_rates, skip_gain):
    tokens, width = queries.shape
    parts = lax.axis_size("ctx")
    shards = lax.axis_size("ch")
    levels = parts.bit_length() - 1
    all_groups, poles = residues.shape
    groups = all_groups // shards
    group = width // groups
    blocks = width // LANES
    inner = 4
    steps = blocks // inner
    half_blocks = blocks // 2
    lag_width = LANES // group * SUB
    sizes = dict(group=group, poles=poles)
    half_rows, tail = half_blocks * 2 * poles, 2 * poles + blocks

    vmem = pl.BlockSpec(memory_space=pltpu.VMEM)
    anywhere = pl.BlockSpec(memory_space=pl.ANY)
    log_rates, residues = log_rates.T, residues.T
    def shape(*dims, dtype=F32):
        return jax.ShapeDtypeStruct(dims, dtype)

    def swap(value, level):
        return lax.ppermute(value, "ctx", [(i, i ^ (1 << level)) for i in range(parts)])

    gated, dgate = gate(key_input, value_input), gate(cotangent, queries)
    outgoing, message, turned, rows = pl.pallas_call(
        lambda *refs: states_kernel(*refs, inner=inner, **sizes),
        in_specs=[vmem] * 4,
        out_specs=[vmem] * 4,
        out_shape=[
            shape(2 * half_rows, LANES, dtype=BF16),
            shape(2 * half_rows, LANES, dtype=BF16),
            shape(tokens, width, dtype=BF16),
            shape(2, blocks, LANES),
        ],
        compiler_params=PARAMS,
        name="states",
    )(log_rates, residues, gated, dgate)

    rates, lag_rates = pl.pallas_call(
        lambda *refs: tables_kernel(*refs, inner=inner, **sizes),
        in_specs=[vmem, anywhere],
        out_specs=[vmem] * 2,
        out_shape=[shape(blocks, poles, LANES), shape(blocks, poles, lag_width)],
        compiler_params=PARAMS,
        cost_estimate=pl.CostEstimate(flops=10**9, bytes_accessed=10**6, transcendentals=10**5),
        name="tables",
    )(log_rates, rows)

    work = pl.CostEstimate(
        flops=16 * tokens * tokens * width, bytes_accessed=12 * tokens * width, transcendentals=tokens * width
    )

    def local_sums(second, *more):
        return pl.pallas_call(
            lambda *refs: lags_kernel(*refs, second=second, inner=inner, **sizes),
            in_specs=[vmem] * (4 + len(more)),
            out_specs=vmem,
            out_shape=shape(tail, LANES, dtype=BF16) if second else shape(2 * poles, LANES),
            scratch_shapes=[pltpu.VMEM((blocks, LANES), F32)] if second else [],
            compiler_params=PARAMS,
            cost_estimate=work,
            name="lags",
        )(lag_rates, gated, dgate, turned, *more)

    def convolve(first_step, count, after):
        skip_rows = skip_gain.reshape(-1, LANES)
        return pl.pallas_call(
            lambda *refs: conv_kernel(*refs, first_step=first_step, inner=inner, **sizes),
            in_specs=[vmem] * 7 + [anywhere],
            out_specs=vmem,
            out_shape=shape(tokens, 2 * count * inner * LANES),
            compiler_params=PARAMS,
            cost_estimate=work,
            name="conv",
        )(residues, rows, skip_rows, rates, lag_rates, gated, turned, after)

    def combine(level, operands, outs):
        return pl.pallas_call(
            lambda *refs: combine_kernel(*refs, level=level, levels=levels, tokens=tokens, **sizes),
            in_specs=[anywhere if x is conv else vmem for x in operands],
            out_specs=[vmem] * len(outs),
            out_shape=outs,
            compiler_params=PARAMS,
            name="combine",
        )(*operands)

    conv = None
    states_shape = shape(2 * half_rows, LANES, dtype=BF16)
    tail_shape = shape(tail, LANES, dtype=BF16)
    slim_shape = shape(half_rows + tail, LANES, dtype=BF16)
    held_shape = shape(half_blocks, 2 * poles, LANES)
    got = swap(outgoing, 0)
    states, total, near = combine(
        0, [rates, message, got, local_sums(0)], [states_shape, shape(2 * poles, LANES), held_shape]
    )
    held = slim = None
    for level in range(1, levels):
        last = level == levels - 1
        if last and slim is not None:
            received = [swap(slim, level)]
        else:
            received = [swap(states, level)]
            if level == 1:
                carried = local_sums(1, total)
            received.append(swap(carried, level))
        operands = [rates, states, carried, *received]
        if level > 1:
            operands.append(held)
        if level == min(2, levels - 1):
            conv = convolve(0, steps - 1, near if held is None else held)
            operands.append(conv)
        if last:
            outs = [shape(half_blocks, 2 * poles, LANES, dtype=BF16), slim_shape]
            mine, outgoing = combine(level, [*operands, near], outs)
        else:
            outs = [states_shape, tail_shape, held_shape]
            if level == levels - 2:
                outs.append(slim_shape)
            states, carried, held, *more = combine(level, operands, outs)
            slim = more[0] if more else None
    got = swap(outgoing, 0)
    last_conv = convolve(steps - 1, 1, outgoing)
    merged = pl.pallas_call(
        lambda *refs: merge_kernel(*refs, poles=poles, length=tokens * parts),
        in_specs=[vmem] * 4 + [anywhere],
        out_specs=vmem,
        out_shape=shape(tail, LANES, dtype=BF16),
        compiler_params=PARAMS,
        name="merge",
    )(log_rates, residues, outgoing, got, last_conv)

    gathered = [merged]
    for shift in range(1, shards):
        gathered.append(lax.ppermute(merged, "ch", [(i, (i + shift) % shards) for i in range(shards)]))

    main = pl.BlockSpec((tokens, inner * LANES), lambda i: (0, i))
    grad_query, grad_key, grad_value = pl.pallas_call(
        lambda *refs: output_kernel(*refs, **sizes),
        grid=(steps,),
        in_specs=[vmem] * 8,
        out_specs=[main] * 3,
        out_shape=[shape(tokens, width, dtype=BF16)] * 3,
        compiler_params=PARAMS,
        cost_estimate=work,
        name="outputs",
    )(rows, conv, last_conv, mine, got, key_input, value_input, cotangent)

    grad_residue, grad_lograte, grad_skip = pl.pallas_call(
        lambda *refs: assemble_kernel(*refs, poles=poles),
        in_specs=[vmem] * shards,
        out_specs=[vmem] * 3,
        out_shape=[shape(poles, all_groups), shape(poles, all_groups), shape(shards * blocks, LANES)],
        compiler_params=PARAMS,
        name="assemble",
    )(*gathered)
    return (grad_query, grad_key, grad_value, grad_residue.T, grad_lograte.T, grad_skip.reshape(-1))


def solution(mesh):
    placed = (P("ctx", "ch"), P("ctx", "ch"), P("ctx", "ch"), P("ctx", "ch"), P(), P(), P())
    return jax.shard_map(
        local,
        mesh=mesh,
        in_specs=placed,
        out_specs=(P("ctx", "ch"), P("ctx", "ch"), P("ctx", "ch"), P(), P(), P()),
        check_vma=False,
    )
```

```python
import math

import jax
import jax.numpy as jnp
from jax import lax
from jax.experimental import pallas as pl
from jax.experimental.pallas import tpu as pltpu
from jax.sharding import PartitionSpec as P

LANES = 128
SUB = 32
F32 = jnp.float32
BF16 = jnp.bfloat16
EXACT = lax.Precision.HIGHEST
VMEM_LIMIT = 40 * 1024 * 1024
PARAMS = pltpu.CompilerParams(vmem_limit_bytes=VMEM_LIMIT)


def iota(shape, axis):
    return lax.broadcasted_iota(jnp.int32, shape, axis)


def over(value, size):
    return lax.shift_right_logical(value, size.bit_length() - 1)


def within(value, size):
    return lax.bitwise_and(value, size - 1)


def mxu(left, right):
    return jnp.dot(left, right, preferred_element_type=F32)


def mxu_t(left, right):
    return lax.dot_general(left, right, (((1,), (1,)), ((), ())), preferred_element_type=F32)


def exact_dot(left, right):
    return jnp.dot(left, right, precision=EXACT, preferred_element_type=F32)


def gate(left, right):
    return (left.astype(F32) * right.astype(F32)).astype(BF16)


def reversal(size):
    return jnp.where(iota((size, size), 0) + iota((size, size), 1) == size - 1, 1.0, 0.0).astype(BF16)


def split(value, pieces):
    parts = []
    for _ in range(pieces):
        parts.append(value.astype(BF16))
        value = value - parts[-1].astype(F32)
    return jnp.concatenate(parts, axis=0)


def join(stacked, rows):
    total = stacked[:rows].astype(F32)
    for start in range(rows, stacked.shape[0], rows):
        total = total + stacked[start : start + rows].astype(F32)
    return total


def flat_rows(table, poles):
    table = table.T
    groups = table.shape[0]
    per_row = LANES // poles
    spread = jnp.where(iota((poles, LANES), 0) == within(iota((poles, LANES), 1), poles), 1.0, 0.0)
    wide = exact_dot(table, spread)
    keep = within(iota((groups, LANES), 0), per_row) == over(iota((groups, LANES), 1), poles)
    wide = jnp.where(keep, wide, 0.0)
    return jnp.sum(wide.reshape(groups // per_row, per_row, LANES), axis=1)


def members(groups, first, span, width):
    return jnp.where(iota((groups, width), 0) == first + over(iota((groups, width), 1), span), 1.0, 0.0).astype(BF16)


def shard_start(groups):
    return pl.multiple_of(lax.axis_index("ch") * groups, LANES)


def states_kernel(logs_ref, res_ref, gated_ref, dgate_ref, send_ref, keep_ref, turned_ref, rows_ref,
                  *, group, poles, inner):
    tokens, _ = gated_ref.shape
    per_block = LANES // group
    _, blocks, _ = rows_ref.shape
    half_blocks = blocks // 2
    groups = blocks * per_block
    wide = inner * LANES
    core = lax.rem(lax.axis_index("ctx"), 2)

    first = shard_start(groups)
    rows_ref[0] = jnp.exp(flat_rows(logs_ref[:, pl.ds(first, groups)], poles))
    rows_ref[1] = flat_rows(res_ref[:, pl.ds(first, groups)], poles)

    flip = reversal(tokens)
    back_pos = (tokens - 1 - iota((tokens, LANES), 0)).astype(F32)
    back_lane = (tokens - 1 - iota((1, tokens), 1)).astype(F32)
    wide_group = over(within(iota((poles, 2 * LANES), 1), LANES), group)
    lanes = [slice(j * LANES, (j + 1) * LANES) for j in range(inner)]

    for turn, msg_ref in enumerate((send_ref, keep_ref)):
        base = lax.rem(core + 1 + turn, 2) * half_blocks

        def body(step, carry, base=base, msg_ref=msg_ref):
            start = base + step * inner
            cut = pl.ds(pl.multiple_of(start * LANES, LANES), wide)
            gated, dgate = gated_ref[:, cut], dgate_ref[:, cut]
            turned = mxu(flip, dgate).astype(BF16)
            turned_ref[:, cut] = turned
            tables = [jnp.exp(-rows_ref[0, pl.ds(start + j, 1), :] * back_pos).T for j in range(inner)]
            found = []
            for j in range(inner):
                both = jnp.concatenate([tables[j].astype(BF16), (tables[j] * back_lane).astype(BF16)], axis=0)
                pair = jnp.concatenate([gated[:, lanes[j]], turned[:, lanes[j]]], axis=1)
                found.append(mxu(both, pair))
            for j in range(inner):
                folded = []
                for part in range(2):
                    total = found[j][part * LANES : part * LANES + poles]
                    for g in range(1, per_block):
                        row = part * LANES + g * poles
                        total = jnp.where(wide_group == g, found[j][row : row + poles], total)
                    folded.append(total)
                out = [folded[0][:, :LANES], folded[0][:, LANES:], folded[1][:, :LANES], folded[1][:, LANES:]]
                row = pl.multiple_of((step * inner + j) * 4 * poles, 4 * poles)
                msg_ref[pl.ds(row, 4 * poles), :] = jnp.concatenate(out, axis=0).astype(BF16)
            return carry

        lax.fori_loop(0, half_blocks // inner, body, 0)


def lags_kernel(lag_rates_ref, gated_ref, dgate_ref, turned_ref, *rest, second, group, poles, inner):
    if second:
        first_ref, out_ref, skip_ref = rest
    else:
        (out_ref,) = rest
    tokens, _ = gated_ref.shape
    per_block = LANES // group
    blocks, _, lag_width = lag_rates_ref.shape
    subs = tokens // SUB
    step_groups = inner * per_block
    lane_group = over(iota((SUB, LANES), 1), group)
    row, lane = iota((SUB, lag_width), 0), within(iota((SUB, lag_width), 1), SUB)
    near_side, no_wrap = row + lane <= SUB - 1, lane >= row
    lag = (SUB - 1 - within(iota((poles, lag_width), 1), SUB)).astype(F32)
    spread = members(step_groups, 0, SUB, inner * lag_width)
    steps = blocks // inner
    sums = []
    for step in range(1, steps) if second else range(1):
        outers = []
        for j in range(inner):
            lanes = slice((step * inner + j) * LANES, (step * inner + j + 1) * LANES)
            found = [None] * subs
            for k in range(subs):
                part = gated_ref[k * SUB : (k + 1) * SUB, lanes]
                stack = jnp.concatenate(
                    [jnp.where(lane_group == g, part, jnp.zeros_like(part)) for g in range(per_block)], axis=0
                )
                outer = mxu_t(turned_ref[: (subs - k) * SUB, lanes], stack)
                for n in range(subs - k):
                    far = subs - 1 - k - n
                    piece = outer[n * SUB : (n + 1) * SUB]
                    found[far] = piece if found[far] is None else found[far] + piece
            outers.append(found)
        terms = []
        for j in range(inner):
            found = outers[j] + [jnp.zeros((SUB, lag_width), F32)]
            lags = []
            for far in range(subs):
                total = jnp.where(near_side, found[far], found[far + 1])
                straight = pltpu.roll(total, 0, 1, stride=1, stride_axis=0)
                wrapped = pltpu.roll(total, lag_width - SUB, 1, stride=1, stride_axis=0)
                lags.append(jnp.sum(jnp.where(no_wrap, straight, wrapped), axis=0, keepdims=True))
            rate = lag_rates_ref[step * inner + j]
            decay = jnp.exp(-rate * SUB)
            total = jnp.zeros((poles, lag_width), F32)
            weighted = total
            for far in reversed(range(subs)):
                weighted = decay * weighted + far * lags[far]
                total = decay * total + lags[far]
            table = jnp.exp(-rate * lag)
            terms.append(
                split(jnp.concatenate([table * total, table * (lag * total + SUB * weighted)], axis=0), 2)
            )
        sums.append(mxu_t(jnp.concatenate(terms, axis=1), spread))
    sums = jnp.concatenate(sums, axis=1)
    zeros = jnp.zeros((sums.shape[0], blocks * per_block - sums.shape[1]), F32)
    sums = jnp.concatenate([zeros, sums] if second else [sums, zeros], axis=1)
    sums = join(sums, 2 * poles)
    if not second:
        out_ref[...] = sums
        return
    for b in range(blocks):
        lanes = slice(b * LANES, (b + 1) * LANES)
        product = gated_ref[:, lanes].astype(F32) * dgate_ref[:, lanes].astype(F32)
        skip_ref[b : b + 1, :] = jnp.sum(product, axis=0, keepdims=True)
    out_ref[: 2 * poles, :] = (first_ref[...] + sums).astype(BF16)
    out_ref[2 * poles :, :] = skip_ref[...].astype(BF16)


def tables_kernel(logs_ref, _, rates_ref, lag_rates_ref, *, group, poles, inner):
    blocks, _, lag_width = lag_rates_ref.shape
    per_block = LANES // group
    groups = blocks * per_block
    step_groups = inner * per_block
    lag_wide = inner * lag_width
    pieces = split(logs_ref[:, pl.ds(shard_start(groups), groups)], 3)
    spread = jnp.concatenate(
        [members(step_groups, 0, SUB, lag_wide), members(step_groups, 0, group, inner * LANES)], axis=1
    )
    for step in range(blocks // inner):
        spreads = mxu(pieces[:, step * step_groups : (step + 1) * step_groups], spread)
        rates = jnp.exp(join(spreads, poles))
        for j in range(inner):
            here = step * inner + j
            lag_rates_ref[here] = rates[:, j * lag_width : (j + 1) * lag_width]
            rates_ref[here] = rates[:, lag_wide + j * LANES : lag_wide + (j + 1) * LANES]


def conv_kernel(res_ref, rows_ref, skip_ref, rates_ref, lag_rates_ref, gated_ref, turned_ref, _, conv_ref,
                *, first_step, group, poles, inner):
    tokens, _ = gated_ref.shape
    per_block = LANES // group
    blocks, _, _ = rates_ref.shape
    subs = tokens // SUB
    lag_width = per_block * SUB
    first = lax.axis_index("ch") * blocks
    lead = (1 + iota((SUB, LANES), 0)).astype(F32)
    wide_group = over(within(iota((SUB, 2 * LANES), 1), LANES), group)
    state_group = over(within(iota((poles, 2 * LANES), 1), LANES), group)
    causal = iota((SUB, lag_width), 0) >= within(iota((SUB, lag_width), 1), SUB)
    lag = (SUB - 1 - within(iota((poles, lag_width), 1), SUB)).astype(F32)
    groups = blocks * per_block
    pieces = split(res_ref[:, pl.ds(shard_start(groups), groups)], 3).astype(F32)
    spread = members(groups, 0, SUB, inner * lag_width)

    def body(step, carry):
        start = (step + first_step) * inner
        moved = pltpu.roll(pieces, groups - start * per_block, 1).astype(BF16)
        lag_res = join(mxu(moved, spread), poles)
        lefts, lead_tables, decays, pairs, gains = [], [], [], [], []
        for j in range(inner):
            here = start + j
            table = jnp.exp(-lag_rates_ref[here] * lag)
            taps = jnp.sum(lag_res[:, j * lag_width : (j + 1) * lag_width] * table, axis=0, keepdims=True)
            taps = jnp.broadcast_to(taps, (SUB, lag_width))
            taps = pltpu.roll(taps, lag_width - SUB + 1, 1, stride=1, stride_axis=0)
            taps = jnp.where(causal, taps, 0.0).astype(BF16)
            lefts.append(jnp.concatenate([taps, table.astype(BF16)], axis=0))
            rate = rows_ref[0, pl.ds(here, 1), :]
            res = rows_ref[1, pl.ds(here, 1), :]
            lead_tables.append((res * jnp.exp(-rate * lead)).astype(BF16))
            decay = jnp.exp(-rates_ref[here] * SUB)
            decays.append(jnp.concatenate([decay, decay], axis=1))
            cut = pl.ds(pl.multiple_of(here * LANES, LANES), LANES)
            pairs.append(jnp.concatenate([gated_ref[:, cut], turned_ref[:, cut]], axis=1))
            gain = skip_ref[pl.ds(first + here, 1), :]
            gains.append(jnp.concatenate([gain, gain], axis=1))
        states = [jnp.zeros((poles, 2 * LANES), F32)] * inner
        totals = [[] for _ in range(inner)]
        for k in range(subs):
            rows = slice(k * SUB, (k + 1) * SUB)
            found = []
            for j in range(inner):
                part = pairs[j][rows]
                stack = [jnp.where(wide_group == g, part, jnp.zeros_like(part)) for g in range(per_block)]
                found.append(mxu(lefts[j], jnp.concatenate(stack, axis=0)))
            for j in range(inner):
                total = found[j][:SUB] + gains[j] * pairs[j][rows].astype(F32)
                if k:
                    held = states[j].astype(BF16)
                    stack = [jnp.where(state_group == g, held, jnp.zeros_like(held)) for g in range(per_block)]
                    total = total + mxu(lead_tables[j], jnp.concatenate(stack, axis=0))
                totals[j].append(total)
            states = [decays[j] * states[j] + found[j][SUB:] for j in range(inner)]
        for j in range(inner):
            cut = pl.ds(pl.multiple_of(2 * (step * inner + j) * LANES, LANES), 2 * LANES)
            conv_ref[:, cut] = jnp.concatenate(totals[j], axis=0)
        return carry

    lax.fori_loop(0, conv_ref.shape[1] // (2 * inner * LANES), body, 0)


def combine_kernel(*refs, level, levels, group, poles, tokens):
    last = level == levels - 1
    refs = list(refs)
    rates_ref = refs.pop(0)
    all_blocks = rates_ref.shape[0]
    blocks = all_blocks // 2
    per_block = LANES // group
    groups = all_blocks * per_block
    rows = 2 * poles
    if level == 0:
        own_ref, got_ref, sums_ref, states_ref, total_ref, near_ref = refs
    else:
        own_ref, own_tail_ref, got_ref = refs.pop(0), refs.pop(0), refs.pop(0)
        got_tail_ref = None if last else refs.pop(0)
        held_ref = refs.pop(0) if level > 1 else None
        if level == min(2, levels - 1):
            refs.pop(0)
        if last:
            near_ref, mine_ref, out_ref = refs
        else:
            states_ref, tail_ref, new_held_ref = refs[:3]
            slim_ref = refs[3] if level == levels - 2 else None
    me = lax.axis_index("ctx")
    core = lax.rem(me, 2)
    is_right = lax.rem(lax.shift_right_logical(me, level), 2) == 1
    before = lax.rem(me, 2**level) - (core if level else 0)
    gap_left = (tokens * before).astype(F32)
    gap_right = (tokens * (2**level - 2 - before)).astype(F32)
    gap = jnp.where(is_right, gap_left, gap_right)
    span = float(tokens * 2**level)
    next_right = lax.rem(lax.shift_right_logical(me, level + 1), 2) == 1

    def quarters(ref, b):
        value = ref[2 * b * rows : 2 * (b + 1) * rows].astype(F32)
        return [value[n * poles : (n + 1) * poles] for n in range(4)]

    wide_terms = []
    for b in range(blocks):
        rate = rates_ref[core * blocks + b]
        own_f, own_b, own_fm, own_bm = quarters(own_ref, b)
        if last:
            got = got_ref[b * rows : (b + 1) * rows].astype(F32)
            got_f = got_b = got[:poles]
            got_fm = got_bm = got[poles:]
        else:
            got_f, got_b, got_fm, got_bm = quarters(got_ref, b)
        left_f = jnp.where(is_right, got_f, own_f)
        left_fm = jnp.where(is_right, got_fm, own_fm)
        right_b = jnp.where(is_right, own_b, got_b)
        right_bm = jnp.where(is_right, own_bm, got_bm)
        once = jnp.exp(-rate)
        cross_res = once * (right_b * left_f)
        cross_mom = once * (right_bm * left_f + right_b * (left_fm + left_f))
        wide_terms.append(split(jnp.concatenate([cross_res, cross_mom], axis=0), 2))
        if level == 0:
            near_ref[b] = jnp.concatenate([left_f, right_b], axis=0)
        else:
            carry = jnp.exp(-rate * gap) * jnp.where(is_right, left_f, right_b)
            zero = jnp.zeros_like(carry)
            hold = jnp.concatenate([jnp.where(is_right, carry, zero), jnp.where(is_right, zero, carry)], axis=0)
            if level > 1:
                hold = hold + held_ref[b]
            if last:
                step = jnp.exp(-rate * tokens)
                near = near_ref[b]
                first_core = jnp.concatenate([hold[:poles], near[poles:] + step * hold[poles:]], axis=0)
                second_core = jnp.concatenate([near[:poles] + step * hold[:poles], hold[poles:]], axis=0)
                mine_ref[b] = jnp.where(core > 0, second_core, first_core).astype(BF16)
                out_ref[b * rows : (b + 1) * rows, :] = jnp.where(core > 0, first_core, second_core).astype(BF16)
            else:
                new_held_ref[b] = hold
        if not last:
            right_f = jnp.where(is_right, own_f, got_f)
            right_fm = jnp.where(is_right, own_fm, got_fm)
            left_b = jnp.where(is_right, got_b, own_b)
            left_bm = jnp.where(is_right, got_bm, own_bm)
            decay = jnp.exp(-rate * span)
            new_f, new_b = decay * left_f + right_f, left_b + decay * right_b
            new_fm = decay * (left_fm + span * left_f) + right_fm
            new_bm = left_bm + decay * (right_bm + span * right_b)
            here = slice(b * rows, (b + 1) * rows)
            new = jnp.concatenate([new_f, new_b, new_fm, new_bm], axis=0).astype(BF16)
            states_ref[2 * b * rows : 2 * (b + 1) * rows, :] = new
            if level == levels - 2 and level:
                chosen = [jnp.where(next_right, new_b, new_f), jnp.where(next_right, new_bm, new_fm)]
                slim_ref[here, :] = jnp.concatenate(chosen, axis=0).astype(BF16)
    cross = join(mxu_t(jnp.concatenate(wide_terms, axis=1), members(groups, 0, group, blocks * LANES)), rows)
    cross = jnp.where(core > 0, pltpu.roll(cross, groups // 2, 1), cross)
    tail = blocks * rows
    if level == 0:
        total_ref[...] = cross + sums_ref[...]
        return
    got_tail = got_ref[tail:, :] if last else got_tail_ref[...]
    both = own_tail_ref[...].astype(F32) + got_tail.astype(F32)
    rests = jnp.concatenate([both[:rows] + cross, both[rows:]], axis=0).astype(BF16)
    if last:
        out_ref[tail:, :] = rests
    else:
        tail_ref[...] = rests
        if slim_ref is not None:
            slim_ref[tail:, :] = rests


def merge_kernel(logs_ref, res_ref, own_ref, got_ref, _, out_ref, *, poles, length):
    groups = out_ref.shape[1]
    start = own_ref.shape[0] - out_ref.shape[0]
    both = own_ref[start:, :].astype(F32) + got_ref[start:, :].astype(F32)
    first = shard_start(groups)
    factor = -jnp.exp(logs_ref[:, pl.ds(first, groups)]) * res_ref[:, pl.ds(first, groups)]
    scaled = [
        both[:poles] / length,
        factor * both[poles : 2 * poles] / math.sqrt(length),
        both[2 * poles :] / math.sqrt(length),
    ]
    out_ref[...] = jnp.concatenate(scaled, axis=0).astype(BF16)


def output_kernel(rows_ref, conv_ref, last_ref, mine_ref, got_ref, k_ref, v_ref, c_ref, gq_ref, gk_ref, gv_ref,
                  *, group, poles):
    tokens, width = gq_ref.shape
    per_block = LANES // group
    step = pl.program_id(0)
    steps = pl.num_programs(0)
    inner = width // LANES
    half_blocks = mine_ref.shape[0]
    core = lax.rem(lax.axis_index("ctx"), 2)
    flip = reversal(tokens)
    ahead = (1 + iota((tokens, LANES), 0)).astype(F32)
    state_group = over(within(iota((poles, 2 * LANES), 1), LANES), group)
    start = step * inner
    is_mine = over(start, half_blocks) == core
    cut = pl.ds(pl.multiple_of(start * LANES, LANES), width)

    def emit(conv_ref, base):
        totals = []
        for j in range(inner):
            here = start + j
            rate = rows_ref[0, pl.ds(here, 1), :]
            res = rows_ref[1, pl.ds(here, 1), :]
            table = (res * jnp.exp(-rate * ahead)).astype(BF16)
            place = within(here, half_blocks)
            held = jnp.where(
                is_mine, mine_ref[place], got_ref[pl.ds(pl.multiple_of(place * 2 * poles, 2 * poles), 2 * poles), :]
            )
            states = jnp.concatenate([held[:poles], held[poles:]], axis=1)
            stack = jnp.concatenate(
                [jnp.where(state_group == g, states, jnp.zeros_like(states)) for g in range(per_block)], axis=0
            )
            both = pl.ds(pl.multiple_of(2 * (here - base) * LANES, LANES), 2 * LANES)
            totals.append((conv_ref[:, both] + mxu(table, stack)).astype(BF16))
        hidden = jnp.concatenate([t[:, :LANES] for t in totals], axis=1)
        flow = mxu(flip, jnp.concatenate([t[:, LANES:] for t in totals], axis=1))
        gq_ref[...] = (c_ref[:, cut].astype(F32) * hidden.astype(F32)).astype(BF16)
        gk_ref[...] = (flow * v_ref[:, cut].astype(F32)).astype(BF16)
        gv_ref[...] = (flow * k_ref[:, cut].astype(F32)).astype(BF16)

    @pl.when(step < steps - 1)
    def _():
        emit(conv_ref, 0)

    @pl.when(step == steps - 1)
    def _():
        emit(last_ref, (steps - 1) * inner)


def assemble_kernel(*refs, poles):
    *slots, res_ref, log_ref, skip_ref = refs
    me = lax.axis_index("ch")
    groups = slots[0].shape[1]
    rows = slots[0].shape[0] - 2 * poles
    for mask, slot in enumerate(slots):
        source = lax.bitwise_xor(me, mask)
        value = slot[...].astype(F32)
        cut = pl.ds(pl.multiple_of(source * groups, LANES), groups)
        res_ref[:, cut] = value[:poles]
        log_ref[:, cut] = value[poles : 2 * poles]
        skip_ref[pl.ds(pl.multiple_of(source * rows, 8), rows), :] = value[2 * poles :]


def local(queries, key_input, value_input, cotangent, residues, log_rates, skip_gain):
    tokens, width = queries.shape
    parts = lax.axis_size("ctx")
    shards = lax.axis_size("ch")
    levels = parts.bit_length() - 1
    all_groups, poles = residues.shape
    groups = all_groups // shards
    group = width // groups
    blocks = width // LANES
    inner = 4
    steps = blocks // inner
    half_blocks = blocks // 2
    lag_width = LANES // group * SUB
    sizes = dict(group=group, poles=poles)
    half_rows, tail = half_blocks * 2 * poles, 2 * poles + blocks

    vmem = pl.BlockSpec(memory_space=pltpu.VMEM)
    anywhere = pl.BlockSpec(memory_space=pl.ANY)
    log_rates, residues = log_rates.T, residues.T
    def shape(*dims, dtype=F32):
        return jax.ShapeDtypeStruct(dims, dtype)

    def swap(value, level):
        return lax.ppermute(value, "ctx", [(i, i ^ (1 << level)) for i in range(parts)])

    gated, dgate = gate(key_input, value_input), gate(cotangent, queries)
    outgoing, message, turned, rows = pl.pallas_call(
        lambda *refs: states_kernel(*refs, inner=inner, **sizes),
        in_specs=[vmem] * 4,
        out_specs=[vmem] * 4,
        out_shape=[
            shape(2 * half_rows, LANES, dtype=BF16),
            shape(2 * half_rows, LANES, dtype=BF16),
            shape(tokens, width, dtype=BF16),
            shape(2, blocks, LANES),
        ],
        compiler_params=PARAMS,
        name="states",
    )(log_rates, residues, gated, dgate)

    rates, lag_rates = pl.pallas_call(
        lambda *refs: tables_kernel(*refs, inner=inner, **sizes),
        in_specs=[vmem, anywhere],
        out_specs=[vmem] * 2,
        out_shape=[shape(blocks, poles, LANES), shape(blocks, poles, lag_width)],
        compiler_params=PARAMS,
        cost_estimate=pl.CostEstimate(flops=10**9, bytes_accessed=10**6, transcendentals=10**5),
        name="tables",
    )(log_rates, rows)

    work = pl.CostEstimate(
        flops=16 * tokens * tokens * width, bytes_accessed=12 * tokens * width, transcendentals=tokens * width
    )

    def local_sums(second, *more):
        return pl.pallas_call(
            lambda *refs: lags_kernel(*refs, second=second, inner=inner, **sizes),
            in_specs=[vmem] * (4 + len(more)),
            out_specs=vmem,
            out_shape=shape(tail, LANES, dtype=BF16) if second else shape(2 * poles, LANES),
            scratch_shapes=[pltpu.VMEM((blocks, LANES), F32)] if second else [],
            compiler_params=PARAMS,
            cost_estimate=work,
            name="lags",
        )(lag_rates, gated, dgate, turned, *more)

    def convolve(first_step, count, after):
        skip_rows = skip_gain.reshape(-1, LANES)
        return pl.pallas_call(
            lambda *refs: conv_kernel(*refs, first_step=first_step, inner=inner, **sizes),
            in_specs=[vmem] * 7 + [anywhere],
            out_specs=vmem,
            out_shape=shape(tokens, 2 * count * inner * LANES),
            compiler_params=PARAMS,
            cost_estimate=work,
            name="conv",
        )(residues, rows, skip_rows, rates, lag_rates, gated, turned, after)

    def combine(level, operands, outs):
        return pl.pallas_call(
            lambda *refs: combine_kernel(*refs, level=level, levels=levels, tokens=tokens, **sizes),
            in_specs=[anywhere if x is conv else vmem for x in operands],
            out_specs=[vmem] * len(outs),
            out_shape=outs,
            compiler_params=PARAMS,
            name="combine",
        )(*operands)

    conv = None
    states_shape = shape(2 * half_rows, LANES, dtype=BF16)
    tail_shape = shape(tail, LANES, dtype=BF16)
    slim_shape = shape(half_rows + tail, LANES, dtype=BF16)
    held_shape = shape(half_blocks, 2 * poles, LANES)
    got = swap(outgoing, 0)
    states, total, near = combine(
        0, [rates, message, got, local_sums(0)], [states_shape, shape(2 * poles, LANES), held_shape]
    )
    held = slim = None
    for level in range(1, levels):
        last = level == levels - 1
        if last and slim is not None:
            received = [swap(slim, level)]
        else:
            received = [swap(states, level)]
            if level == 1:
                carried = local_sums(1, total)
            received.append(swap(carried, level))
        operands = [rates, states, carried, *received]
        if level > 1:
            operands.append(held)
        if level == min(2, levels - 1):
            conv = convolve(0, steps - 1, near if held is None else held)
            operands.append(conv)
        if last:
            outs = [shape(half_blocks, 2 * poles, LANES, dtype=BF16), slim_shape]
            mine, outgoing = combine(level, [*operands, near], outs)
        else:
            outs = [states_shape, tail_shape, held_shape]
            if level == levels - 2:
                outs.append(slim_shape)
            states, carried, held, *more = combine(level, operands, outs)
            slim = more[0] if more else None
    got = swap(outgoing, 0)
    last_conv = convolve(steps - 1, 1, outgoing)
    merged = pl.pallas_call(
        lambda *refs: merge_kernel(*refs, poles=poles, length=tokens * parts),
        in_specs=[vmem] * 4 + [anywhere],
        out_specs=vmem,
        out_shape=shape(tail, LANES, dtype=BF16),
        compiler_params=PARAMS,
        name="merge",
    )(log_rates, residues, outgoing, got, last_conv)

    gathered = [merged]
    for mask in range(1, shards):
        gathered.append(lax.ppermute(merged, "ch", [(i, i ^ mask) for i in range(shards)]))

    main = pl.BlockSpec((tokens, inner * LANES), lambda i: (0, i))
    grad_query, grad_key, grad_value = pl.pallas_call(
        lambda *refs: output_kernel(*refs, **sizes),
        grid=(steps,),
        in_specs=[vmem] * 8,
        out_specs=[main] * 3,
        out_shape=[shape(tokens, width, dtype=BF16)] * 3,
        compiler_params=PARAMS,
        cost_estimate=work,
        name="outputs",
    )(rows, conv, last_conv, mine, got, key_input, value_input, cotangent)

    grad_residue, grad_lograte, grad_skip = pl.pallas_call(
        lambda *refs: assemble_kernel(*refs, poles=poles),
        in_specs=[vmem] * shards,
        out_specs=[vmem] * 3,
        out_shape=[shape(poles, all_groups), shape(poles, all_groups), shape(shards * blocks, LANES)],
        compiler_params=PARAMS,
        name="assemble",
    )(*gathered)
    return (grad_query, grad_key, grad_value, grad_residue.T, grad_lograte.T, grad_skip.reshape(-1))


def solution(mesh):
    placed = (P("ctx", "ch"), P("ctx", "ch"), P("ctx", "ch"), P("ctx", "ch"), P(), P(), P())
    return jax.shard_map(
        local,
        mesh=mesh,
        in_specs=placed,
        out_specs=(P("ctx", "ch"), P("ctx", "ch"), P("ctx", "ch"), P(), P(), P()),
        check_vma=False,
    )
```

```python
import math

import jax
import jax.numpy as jnp
from jax import lax
from jax.experimental import pallas as pl
from jax.experimental.pallas import tpu as pltpu
from jax.sharding import PartitionSpec as P

LANES = 128
SUB = 32
F32 = jnp.float32
BF16 = jnp.bfloat16
EXACT = lax.Precision.HIGHEST
VMEM_LIMIT = 40 * 1024 * 1024
PARAMS = pltpu.CompilerParams(vmem_limit_bytes=VMEM_LIMIT)


def iota(shape, axis):
    return lax.broadcasted_iota(jnp.int32, shape, axis)


def over(value, size):
    return lax.shift_right_logical(value, size.bit_length() - 1)


def within(value, size):
    return lax.bitwise_and(value, size - 1)


def mxu(left, right):
    return jnp.dot(left, right, preferred_element_type=F32)


def mxu_t(left, right):
    return lax.dot_general(left, right, (((1,), (1,)), ((), ())), preferred_element_type=F32)


def exact_dot(left, right):
    return jnp.dot(left, right, precision=EXACT, preferred_element_type=F32)


def gate(left, right):
    return (left.astype(F32) * right.astype(F32)).astype(BF16)


def reversal(size):
    return jnp.where(iota((size, size), 0) + iota((size, size), 1) == size - 1, 1.0, 0.0).astype(BF16)


def split(value, pieces):
    parts = []
    for _ in range(pieces):
        parts.append(value.astype(BF16))
        value = value - parts[-1].astype(F32)
    return jnp.concatenate(parts, axis=0)


def join(stacked, rows):
    total = stacked[:rows].astype(F32)
    for start in range(rows, stacked.shape[0], rows):
        total = total + stacked[start : start + rows].astype(F32)
    return total


def flat_rows(table, poles):
    table = table.T
    groups = table.shape[0]
    per_row = LANES // poles
    spread = jnp.where(iota((poles, LANES), 0) == within(iota((poles, LANES), 1), poles), 1.0, 0.0)
    wide = exact_dot(table, spread)
    keep = within(iota((groups, LANES), 0), per_row) == over(iota((groups, LANES), 1), poles)
    wide = jnp.where(keep, wide, 0.0)
    return jnp.sum(wide.reshape(groups // per_row, per_row, LANES), axis=1)


def members(groups, first, span, width):
    return jnp.where(iota((groups, width), 0) == first + over(iota((groups, width), 1), span), 1.0, 0.0).astype(BF16)


def shard_start(groups):
    return pl.multiple_of(lax.axis_index("ch") * groups, LANES)


def states_kernel(all_params_ref, q_any, k_any, v_any, c_any, send_ref, keep_ref, gated_ref, dgate_ref, turned_ref,
                  rows_ref, table_ref, q_ref, k_ref, v_ref, c_ref, sems, *, group, poles, inner):
    tokens, _ = gated_ref.shape
    per_block = LANES // group
    _, blocks, _ = rows_ref.shape
    half_blocks = blocks // 2
    groups = blocks * per_block
    wide = inner * LANES
    core = lax.rem(lax.axis_index("ctx"), 2)
    sources = ((k_any, k_ref), (v_any, v_ref), (c_any, c_ref), (q_any, q_ref))
    half_steps = half_blocks // inner

    def copies(turn, step):
        start = lax.rem(core + 1 + turn, 2) * half_blocks + step * inner
        cut = pl.ds(pl.multiple_of(start * LANES, LANES), wide)
        return [
            pltpu.make_async_copy(far.at[:, cut], near.at[:, cut], sems.at[n, turn * half_steps + step])
            for n, (far, near) in enumerate(sources)
        ]

    first = shard_start(groups)
    for turn in range(2):
        for step in range(half_steps):
            for copy in copies(turn, step):
                copy.start()
    for n in range(2):
        table_ref[n] = all_params_ref[n, :, pl.ds(first, groups)]
    rows_ref[0] = jnp.exp(flat_rows(table_ref[0], poles))
    rows_ref[1] = flat_rows(table_ref[1], poles)

    flip = reversal(tokens)
    back_pos = (tokens - 1 - iota((tokens, LANES), 0)).astype(F32)
    back_lane = (tokens - 1 - iota((1, tokens), 1)).astype(F32)
    wide_group = over(within(iota((poles, 2 * LANES), 1), LANES), group)
    lanes = [slice(j * LANES, (j + 1) * LANES) for j in range(inner)]

    for turn, msg_ref in enumerate((send_ref, keep_ref)):
        base = lax.rem(core + 1 + turn, 2) * half_blocks

        def body(step, carry, base=base, msg_ref=msg_ref, turn=turn):
            start = base + step * inner
            cut = pl.ds(pl.multiple_of(start * LANES, LANES), wide)
            for copy in copies(turn, step):
                copy.wait()
            gated, dgate = gate(k_ref[:, cut], v_ref[:, cut]), gate(c_ref[:, cut], q_ref[:, cut])
            gated_ref[:, cut] = gated
            dgate_ref[:, cut] = dgate
            turned = mxu(flip, dgate).astype(BF16)
            turned_ref[:, cut] = turned
            tables = [jnp.exp(-rows_ref[0, pl.ds(start + j, 1), :] * back_pos).T for j in range(inner)]
            found = []
            for j in range(inner):
                both = jnp.concatenate([tables[j].astype(BF16), (tables[j] * back_lane).astype(BF16)], axis=0)
                pair = jnp.concatenate([gated[:, lanes[j]], turned[:, lanes[j]]], axis=1)
                found.append(mxu(both, pair))
            for j in range(inner):
                folded = []
                for part in range(2):
                    total = found[j][part * LANES : part * LANES + poles]
                    for g in range(1, per_block):
                        row = part * LANES + g * poles
                        total = jnp.where(wide_group == g, found[j][row : row + poles], total)
                    folded.append(total)
                out = [folded[0][:, :LANES], folded[0][:, LANES:], folded[1][:, :LANES], folded[1][:, LANES:]]
                row = pl.multiple_of((step * inner + j) * 4 * poles, 4 * poles)
                msg_ref[pl.ds(row, 4 * poles), :] = jnp.concatenate(out, axis=0).astype(BF16)
            return carry

        lax.fori_loop(0, half_blocks // inner, body, 0)


def lags_kernel(lag_rates_ref, gated_ref, dgate_ref, turned_ref, *rest, second, group, poles, inner):
    if second:
        first_ref, out_ref, skip_ref = rest
    else:
        (out_ref,) = rest
    tokens, _ = gated_ref.shape
    per_block = LANES // group
    blocks, _, lag_width = lag_rates_ref.shape
    subs = tokens // SUB
    step_groups = inner * per_block
    lane_group = over(iota((SUB, LANES), 1), group)
    row, lane = iota((SUB, lag_width), 0), within(iota((SUB, lag_width), 1), SUB)
    near_side, no_wrap = row + lane <= SUB - 1, lane >= row
    lag = (SUB - 1 - within(iota((poles, lag_width), 1), SUB)).astype(F32)
    spread = members(step_groups, 0, SUB, inner * lag_width)
    steps = blocks // inner
    sums = []
    for step in range(1, steps) if second else range(1):
        outers = []
        for j in range(inner):
            lanes = slice((step * inner + j) * LANES, (step * inner + j + 1) * LANES)
            found = [None] * subs
            for k in range(subs):
                part = gated_ref[k * SUB : (k + 1) * SUB, lanes]
                stack = jnp.concatenate(
                    [jnp.where(lane_group == g, part, jnp.zeros_like(part)) for g in range(per_block)], axis=0
                )
                outer = mxu_t(turned_ref[: (subs - k) * SUB, lanes], stack)
                for n in range(subs - k):
                    far = subs - 1 - k - n
                    piece = outer[n * SUB : (n + 1) * SUB]
                    found[far] = piece if found[far] is None else found[far] + piece
            outers.append(found)
        terms = []
        for j in range(inner):
            found = outers[j] + [jnp.zeros((SUB, lag_width), F32)]
            lags = []
            for far in range(subs):
                total = jnp.where(near_side, found[far], found[far + 1])
                straight = pltpu.roll(total, 0, 1, stride=1, stride_axis=0)
                wrapped = pltpu.roll(total, lag_width - SUB, 1, stride=1, stride_axis=0)
                lags.append(jnp.sum(jnp.where(no_wrap, straight, wrapped), axis=0, keepdims=True))
            rate = lag_rates_ref[step * inner + j]
            decay = jnp.exp(-rate * SUB)
            total = jnp.zeros((poles, lag_width), F32)
            weighted = total
            for far in reversed(range(subs)):
                weighted = decay * weighted + far * lags[far]
                total = decay * total + lags[far]
            table = jnp.exp(-rate * lag)
            terms.append(
                split(jnp.concatenate([table * total, table * (lag * total + SUB * weighted)], axis=0), 2)
            )
        sums.append(mxu_t(jnp.concatenate(terms, axis=1), spread))
    sums = jnp.concatenate(sums, axis=1)
    zeros = jnp.zeros((sums.shape[0], blocks * per_block - sums.shape[1]), F32)
    sums = jnp.concatenate([zeros, sums] if second else [sums, zeros], axis=1)
    sums = join(sums, 2 * poles)
    if not second:
        out_ref[...] = sums
        return
    for b in range(blocks):
        lanes = slice(b * LANES, (b + 1) * LANES)
        product = gated_ref[:, lanes].astype(F32) * dgate_ref[:, lanes].astype(F32)
        skip_ref[b : b + 1, :] = jnp.sum(product, axis=0, keepdims=True)
    out_ref[: 2 * poles, :] = (first_ref[...] + sums).astype(BF16)
    out_ref[2 * poles :, :] = skip_ref[...].astype(BF16)


def tables_kernel(params_ref, rates_ref, lag_rates_ref, *, group, poles, inner):
    blocks, _, lag_width = lag_rates_ref.shape
    per_block = LANES // group
    step_groups = inner * per_block
    lag_wide = inner * lag_width
    pieces = split(params_ref[0], 3)
    spread = jnp.concatenate(
        [members(step_groups, 0, SUB, lag_wide), members(step_groups, 0, group, inner * LANES)], axis=1
    )
    for step in range(blocks // inner):
        spreads = mxu(pieces[:, step * step_groups : (step + 1) * step_groups], spread)
        rates = jnp.exp(join(spreads, poles))
        for j in range(inner):
            here = step * inner + j
            lag_rates_ref[here] = rates[:, j * lag_width : (j + 1) * lag_width]
            rates_ref[here] = rates[:, lag_wide + j * LANES : lag_wide + (j + 1) * LANES]


def conv_kernel(params_ref, rows_ref, skip_ref, rates_ref, lag_rates_ref, gated_ref, turned_ref, _, conv_ref,
                *, first_step, group, poles, inner):
    tokens, _ = gated_ref.shape
    per_block = LANES // group
    blocks, _, _ = rates_ref.shape
    subs = tokens // SUB
    lag_width = per_block * SUB
    first = lax.axis_index("ch") * blocks
    lead = (1 + iota((SUB, LANES), 0)).astype(F32)
    wide_group = over(within(iota((SUB, 2 * LANES), 1), LANES), group)
    state_group = over(within(iota((poles, 2 * LANES), 1), LANES), group)
    causal = iota((SUB, lag_width), 0) >= within(iota((SUB, lag_width), 1), SUB)
    lag = (SUB - 1 - within(iota((poles, lag_width), 1), SUB)).astype(F32)
    groups = blocks * per_block
    pieces = split(params_ref[1], 3).astype(F32)
    spread = members(groups, 0, SUB, inner * lag_width)

    def body(step, carry):
        start = (step + first_step) * inner
        moved = pltpu.roll(pieces, groups - start * per_block, 1).astype(BF16)
        lag_res = join(mxu(moved, spread), poles)
        lefts, lead_tables, decays, pairs, gains = [], [], [], [], []
        for j in range(inner):
            here = start + j
            table = jnp.exp(-lag_rates_ref[here] * lag)
            taps = jnp.sum(lag_res[:, j * lag_width : (j + 1) * lag_width] * table, axis=0, keepdims=True)
            taps = jnp.broadcast_to(taps, (SUB, lag_width))
            taps = pltpu.roll(taps, lag_width - SUB + 1, 1, stride=1, stride_axis=0)
            taps = jnp.where(causal, taps, 0.0).astype(BF16)
            lefts.append(jnp.concatenate([taps, table.astype(BF16)], axis=0))
            rate = rows_ref[0, pl.ds(here, 1), :]
            res = rows_ref[1, pl.ds(here, 1), :]
            lead_tables.append((res * jnp.exp(-rate * lead)).astype(BF16))
            decay = jnp.exp(-rates_ref[here] * SUB)
            decays.append(jnp.concatenate([decay, decay], axis=1))
            cut = pl.ds(pl.multiple_of(here * LANES, LANES), LANES)
            pairs.append(jnp.concatenate([gated_ref[:, cut], turned_ref[:, cut]], axis=1))
            gain = skip_ref[pl.ds(first + here, 1), :]
            gains.append(jnp.concatenate([gain, gain], axis=1))
        states = [jnp.zeros((poles, 2 * LANES), F32)] * inner
        totals = [[] for _ in range(inner)]
        for k in range(subs):
            rows = slice(k * SUB, (k + 1) * SUB)
            found = []
            for j in range(inner):
                part = pairs[j][rows]
                stack = [jnp.where(wide_group == g, part, jnp.zeros_like(part)) for g in range(per_block)]
                found.append(mxu(lefts[j], jnp.concatenate(stack, axis=0)))
            for j in range(inner):
                total = found[j][:SUB] + gains[j] * pairs[j][rows].astype(F32)
                if k:
                    held = states[j].astype(BF16)
                    stack = [jnp.where(state_group == g, held, jnp.zeros_like(held)) for g in range(per_block)]
                    total = total + mxu(lead_tables[j], jnp.concatenate(stack, axis=0))
                totals[j].append(total)
            states = [decays[j] * states[j] + found[j][SUB:] for j in range(inner)]
        for j in range(inner):
            cut = pl.ds(pl.multiple_of(2 * (step * inner + j) * LANES, LANES), 2 * LANES)
            conv_ref[:, cut] = jnp.concatenate(totals[j], axis=0)
        return carry

    lax.fori_loop(0, conv_ref.shape[1] // (2 * inner * LANES), body, 0)


def combine_kernel(*refs, level, levels, group, poles, tokens):
    last = level == levels - 1
    refs = list(refs)
    rates_ref = refs.pop(0)
    all_blocks = rates_ref.shape[0]
    blocks = all_blocks // 2
    per_block = LANES // group
    groups = all_blocks * per_block
    rows = 2 * poles
    if level == 0:
        own_ref, got_ref, sums_ref, states_ref, total_ref, near_ref = refs
    else:
        own_ref, own_tail_ref, got_ref = refs.pop(0), refs.pop(0), refs.pop(0)
        got_tail_ref = None if last else refs.pop(0)
        held_ref = refs.pop(0) if level > 1 else None
        if level == min(2, levels - 1):
            refs.pop(0)
        if last:
            near_ref, mine_ref, out_ref = refs
        else:
            states_ref, tail_ref, new_held_ref = refs[:3]
            slim_ref = refs[3] if level == levels - 2 else None
    me = lax.axis_index("ctx")
    core = lax.rem(me, 2)
    is_right = lax.rem(lax.shift_right_logical(me, level), 2) == 1
    before = lax.rem(me, 2**level) - (core if level else 0)
    gap_left = (tokens * before).astype(F32)
    gap_right = (tokens * (2**level - 2 - before)).astype(F32)
    gap = jnp.where(is_right, gap_left, gap_right)
    span = float(tokens * 2**level)
    next_right = lax.rem(lax.shift_right_logical(me, level + 1), 2) == 1

    def quarters(ref, b):
        value = ref[2 * b * rows : 2 * (b + 1) * rows].astype(F32)
        return [value[n * poles : (n + 1) * poles] for n in range(4)]

    wide_terms = []
    for b in range(blocks):
        rate = rates_ref[core * blocks + b]
        own_f, own_b, own_fm, own_bm = quarters(own_ref, b)
        if last:
            got = got_ref[b * rows : (b + 1) * rows].astype(F32)
            got_f = got_b = got[:poles]
            got_fm = got_bm = got[poles:]
        else:
            got_f, got_b, got_fm, got_bm = quarters(got_ref, b)
        left_f = jnp.where(is_right, got_f, own_f)
        left_fm = jnp.where(is_right, got_fm, own_fm)
        right_b = jnp.where(is_right, own_b, got_b)
        right_bm = jnp.where(is_right, own_bm, got_bm)
        once = jnp.exp(-rate)
        cross_res = once * (right_b * left_f)
        cross_mom = once * (right_bm * left_f + right_b * (left_fm + left_f))
        wide_terms.append(split(jnp.concatenate([cross_res, cross_mom], axis=0), 2))
        if level == 0:
            near_ref[b] = jnp.concatenate([left_f, right_b], axis=0)
        else:
            carry = jnp.exp(-rate * gap) * jnp.where(is_right, left_f, right_b)
            zero = jnp.zeros_like(carry)
            hold = jnp.concatenate([jnp.where(is_right, carry, zero), jnp.where(is_right, zero, carry)], axis=0)
            if level > 1:
                hold = hold + held_ref[b]
            if last:
                step = jnp.exp(-rate * tokens)
                near = near_ref[b]
                first_core = jnp.concatenate([hold[:poles], near[poles:] + step * hold[poles:]], axis=0)
                second_core = jnp.concatenate([near[:poles] + step * hold[:poles], hold[poles:]], axis=0)
                mine_ref[b] = jnp.where(core > 0, second_core, first_core).astype(BF16)
                out_ref[b * rows : (b + 1) * rows, :] = jnp.where(core > 0, first_core, second_core).astype(BF16)
            else:
                new_held_ref[b] = hold
        if not last:
            right_f = jnp.where(is_right, own_f, got_f)
            right_fm = jnp.where(is_right, own_fm, got_fm)
            left_b = jnp.where(is_right, got_b, own_b)
            left_bm = jnp.where(is_right, got_bm, own_bm)
            decay = jnp.exp(-rate * span)
            new_f, new_b = decay * left_f + right_f, left_b + decay * right_b
            new_fm = decay * (left_fm + span * left_f) + right_fm
            new_bm = left_bm + decay * (right_bm + span * right_b)
            here = slice(b * rows, (b + 1) * rows)
            new = jnp.concatenate([new_f, new_b, new_fm, new_bm], axis=0).astype(BF16)
            states_ref[2 * b * rows : 2 * (b + 1) * rows, :] = new
            if level == levels - 2 and level:
                chosen = [jnp.where(next_right, new_b, new_f), jnp.where(next_right, new_bm, new_fm)]
                slim_ref[here, :] = jnp.concatenate(chosen, axis=0).astype(BF16)
    cross = join(mxu_t(jnp.concatenate(wide_terms, axis=1), members(groups, 0, group, blocks * LANES)), rows)
    cross = jnp.where(core > 0, pltpu.roll(cross, groups // 2, 1), cross)
    tail = blocks * rows
    if level == 0:
        total_ref[...] = cross + sums_ref[...]
        return
    got_tail = got_ref[tail:, :] if last else got_tail_ref[...]
    both = own_tail_ref[...].astype(F32) + got_tail.astype(F32)
    rests = jnp.concatenate([both[:rows] + cross, both[rows:]], axis=0).astype(BF16)
    if last:
        out_ref[tail:, :] = rests
    else:
        tail_ref[...] = rests
        if slim_ref is not None:
            slim_ref[tail:, :] = rests


def merge_kernel(params_ref, own_ref, got_ref, _, out_ref, *, poles, length):
    groups = out_ref.shape[1]
    start = own_ref.shape[0] - out_ref.shape[0]
    both = own_ref[start:, :].astype(F32) + got_ref[start:, :].astype(F32)
    factor = -jnp.exp(params_ref[0]) * params_ref[1]
    scaled = [
        both[:poles] / length,
        factor * both[poles : 2 * poles] / math.sqrt(length),
        both[2 * poles :] / math.sqrt(length),
    ]
    out_ref[...] = jnp.concatenate(scaled, axis=0).astype(BF16)


def output_kernel(rows_ref, conv_ref, last_ref, mine_ref, got_ref, k_ref, v_ref, c_ref, gq_ref, gk_ref, gv_ref,
                  *, group, poles):
    tokens, width = gq_ref.shape
    per_block = LANES // group
    step = pl.program_id(0)
    steps = pl.num_programs(0)
    inner = width // LANES
    half_blocks = mine_ref.shape[0]
    core = lax.rem(lax.axis_index("ctx"), 2)
    flip = reversal(tokens)
    ahead = (1 + iota((tokens, LANES), 0)).astype(F32)
    state_group = over(within(iota((poles, 2 * LANES), 1), LANES), group)
    start = step * inner
    is_mine = over(start, half_blocks) == core
    cut = pl.ds(pl.multiple_of(start * LANES, LANES), width)

    def emit(conv_ref, base):
        totals = []
        for j in range(inner):
            here = start + j
            rate = rows_ref[0, pl.ds(here, 1), :]
            res = rows_ref[1, pl.ds(here, 1), :]
            table = (res * jnp.exp(-rate * ahead)).astype(BF16)
            place = within(here, half_blocks)
            held = jnp.where(
                is_mine, mine_ref[place], got_ref[pl.ds(pl.multiple_of(place * 2 * poles, 2 * poles), 2 * poles), :]
            )
            states = jnp.concatenate([held[:poles], held[poles:]], axis=1)
            stack = jnp.concatenate(
                [jnp.where(state_group == g, states, jnp.zeros_like(states)) for g in range(per_block)], axis=0
            )
            both = pl.ds(pl.multiple_of(2 * (here - base) * LANES, LANES), 2 * LANES)
            totals.append((conv_ref[:, both] + mxu(table, stack)).astype(BF16))
        hidden = jnp.concatenate([t[:, :LANES] for t in totals], axis=1)
        flow = mxu(flip, jnp.concatenate([t[:, LANES:] for t in totals], axis=1))
        gq_ref[...] = (c_ref[:, cut].astype(F32) * hidden.astype(F32)).astype(BF16)
        gk_ref[...] = (flow * v_ref[:, cut].astype(F32)).astype(BF16)
        gv_ref[...] = (flow * k_ref[:, cut].astype(F32)).astype(BF16)

    @pl.when(step < steps - 1)
    def _():
        emit(conv_ref, 0)

    @pl.when(step == steps - 1)
    def _():
        emit(last_ref, (steps - 1) * inner)


def assemble_kernel(*refs, poles):
    *slots, res_ref, log_ref, skip_ref = refs
    me = lax.axis_index("ch")
    groups = slots[0].shape[1]
    rows = slots[0].shape[0] - 2 * poles
    for mask, slot in enumerate(slots):
        source = lax.bitwise_xor(me, mask)
        value = slot[...].astype(F32)
        cut = pl.ds(pl.multiple_of(source * groups, LANES), groups)
        res_ref[:, cut] = value[:poles]
        log_ref[:, cut] = value[poles : 2 * poles]
        skip_ref[pl.ds(pl.multiple_of(source * rows, 8), rows), :] = value[2 * poles :]


def local(queries, key_input, value_input, cotangent, residues, log_rates, skip_gain):
    tokens, width = queries.shape
    parts = lax.axis_size("ctx")
    shards = lax.axis_size("ch")
    levels = parts.bit_length() - 1
    all_groups, poles = residues.shape
    groups = all_groups // shards
    group = width // groups
    blocks = width // LANES
    inner = 4
    steps = blocks // inner
    half_blocks = blocks // 2
    lag_width = LANES // group * SUB
    sizes = dict(group=group, poles=poles)
    half_rows, tail = half_blocks * 2 * poles, 2 * poles + blocks

    vmem = pl.BlockSpec(memory_space=pltpu.VMEM)
    anywhere = pl.BlockSpec(memory_space=pl.ANY)
    log_rates, residues = log_rates.T, residues.T
    def shape(*dims, dtype=F32):
        return jax.ShapeDtypeStruct(dims, dtype)

    def swap(value, level):
        return lax.ppermute(value, "ctx", [(i, i ^ (1 << level)) for i in range(parts)])

    far = pl.BlockSpec(memory_space=pl.ANY)
    outgoing, message, gated, dgate, turned, rows, params = pl.pallas_call(
        lambda *refs: states_kernel(*refs, inner=inner, **sizes),
        in_specs=[vmem] + [far] * 4,
        out_specs=[vmem] * 7,
        out_shape=[
            shape(2 * half_rows, LANES, dtype=BF16),
            shape(2 * half_rows, LANES, dtype=BF16),
            shape(tokens, width, dtype=BF16),
            shape(tokens, width, dtype=BF16),
            shape(tokens, width, dtype=BF16),
            shape(2, blocks, LANES),
            shape(2, poles, groups),
        ],
        scratch_shapes=[pltpu.VMEM((tokens, width), BF16)] * 4
        + [pltpu.SemaphoreType.DMA((4, steps))],
        compiler_params=pltpu.CompilerParams(vmem_limit_bytes=53000 * 1024),
        name="states",
    )(jnp.stack([log_rates, residues]), queries, key_input, value_input, cotangent)

    rates, lag_rates = pl.pallas_call(
        lambda *refs: tables_kernel(*refs, inner=inner, **sizes),
        in_specs=[vmem],
        out_specs=[vmem] * 2,
        out_shape=[shape(blocks, poles, LANES), shape(blocks, poles, lag_width)],
        compiler_params=PARAMS,
        cost_estimate=pl.CostEstimate(flops=10**9, bytes_accessed=10**6, transcendentals=10**5),
        name="tables",
    )(params)

    work = pl.CostEstimate(
        flops=16 * tokens * tokens * width, bytes_accessed=12 * tokens * width, transcendentals=tokens * width
    )

    def local_sums(second, *more):
        return pl.pallas_call(
            lambda *refs: lags_kernel(*refs, second=second, inner=inner, **sizes),
            in_specs=[vmem] * (4 + len(more)),
            out_specs=vmem,
            out_shape=shape(tail, LANES, dtype=BF16) if second else shape(2 * poles, LANES),
            scratch_shapes=[pltpu.VMEM((blocks, LANES), F32)] if second else [],
            compiler_params=PARAMS,
            cost_estimate=work,
            name="lags",
        )(lag_rates, gated, dgate, turned, *more)

    def convolve(first_step, count, after):
        skip_rows = skip_gain.reshape(-1, LANES)
        return pl.pallas_call(
            lambda *refs: conv_kernel(*refs, first_step=first_step, inner=inner, **sizes),
            in_specs=[vmem] * 7 + [anywhere],
            out_specs=vmem,
            out_shape=shape(tokens, 2 * count * inner * LANES),
            compiler_params=PARAMS,
            cost_estimate=work,
            name="conv",
        )(params, rows, skip_rows, rates, lag_rates, gated, turned, after)

    def combine(level, operands, outs):
        return pl.pallas_call(
            lambda *refs: combine_kernel(*refs, level=level, levels=levels, tokens=tokens, **sizes),
            in_specs=[anywhere if x is conv else vmem for x in operands],
            out_specs=[vmem] * len(outs),
            out_shape=outs,
            compiler_params=PARAMS,
            name="combine",
        )(*operands)

    conv = None
    states_shape = shape(2 * half_rows, LANES, dtype=BF16)
    tail_shape = shape(tail, LANES, dtype=BF16)
    slim_shape = shape(half_rows + tail, LANES, dtype=BF16)
    held_shape = shape(half_blocks, 2 * poles, LANES)
    got = swap(outgoing, 0)
    states, total, near = combine(
        0, [rates, message, got, local_sums(0)], [states_shape, shape(2 * poles, LANES), held_shape]
    )
    held = slim = None
    for level in range(1, levels):
        last = level == levels - 1
        if last and slim is not None:
            received = [swap(slim, level)]
        else:
            received = [swap(states, level)]
            if level == 1:
                carried = local_sums(1, total)
            received.append(swap(carried, level))
        operands = [rates, states, carried, *received]
        if level > 1:
            operands.append(held)
        if level == min(2, levels - 1):
            conv = convolve(0, steps - 1, near if held is None else held)
            operands.append(conv)
        if last:
            outs = [shape(half_blocks, 2 * poles, LANES, dtype=BF16), slim_shape]
            mine, outgoing = combine(level, [*operands, near], outs)
        else:
            outs = [states_shape, tail_shape, held_shape]
            if level == levels - 2:
                outs.append(slim_shape)
            states, carried, held, *more = combine(level, operands, outs)
            slim = more[0] if more else None
    got = swap(outgoing, 0)
    last_conv = convolve(steps - 1, 1, outgoing)
    merged = pl.pallas_call(
        lambda *refs: merge_kernel(*refs, poles=poles, length=tokens * parts),
        in_specs=[vmem] * 3 + [anywhere],
        out_specs=vmem,
        out_shape=shape(tail, LANES, dtype=BF16),
        compiler_params=PARAMS,
        name="merge",
    )(params, outgoing, got, last_conv)

    gathered = [merged]
    for mask in range(1, shards):
        gathered.append(lax.ppermute(merged, "ch", [(i, i ^ mask) for i in range(shards)]))

    main = pl.BlockSpec((tokens, inner * LANES), lambda i: (0, i))
    grad_query, grad_key, grad_value = pl.pallas_call(
        lambda *refs: output_kernel(*refs, **sizes),
        grid=(steps,),
        in_specs=[vmem] * 8,
        out_specs=[main] * 3,
        out_shape=[shape(tokens, width, dtype=BF16)] * 3,
        compiler_params=PARAMS,
        cost_estimate=work,
        name="outputs",
    )(rows, conv, last_conv, mine, got, key_input, value_input, cotangent)

    grad_residue, grad_lograte, grad_skip = pl.pallas_call(
        lambda *refs: assemble_kernel(*refs, poles=poles),
        in_specs=[vmem] * shards,
        out_specs=[vmem] * 3,
        out_shape=[shape(poles, all_groups), shape(poles, all_groups), shape(shards * blocks, LANES)],
        compiler_params=PARAMS,
        name="assemble",
    )(*gathered)
    return (grad_query, grad_key, grad_value, grad_residue.T, grad_lograte.T, grad_skip.reshape(-1))


def solution(mesh):
    placed = (P("ctx", "ch"), P("ctx", "ch"), P("ctx", "ch"), P("ctx", "ch"), P(), P(), P())
    return jax.shard_map(
        local,
        mesh=mesh,
        in_specs=placed,
        out_specs=(P("ctx", "ch"), P("ctx", "ch"), P("ctx", "ch"), P(), P(), P()),
        check_vma=False,
    )
```

```python
import math

import jax
import jax.numpy as jnp
from jax import lax
from jax.experimental import pallas as pl
from jax.experimental.pallas import tpu as pltpu
from jax.sharding import PartitionSpec as P

LANES = 128
SUB = 32
F32 = jnp.float32
BF16 = jnp.bfloat16
EXACT = lax.Precision.HIGHEST
VMEM_LIMIT = 40 * 1024 * 1024
PARAMS = pltpu.CompilerParams(vmem_limit_bytes=VMEM_LIMIT)


def iota(shape, axis):
    return lax.broadcasted_iota(jnp.int32, shape, axis)


def over(value, size):
    return lax.shift_right_logical(value, size.bit_length() - 1)


def within(value, size):
    return lax.bitwise_and(value, size - 1)


def mxu(left, right):
    return jnp.dot(left, right, preferred_element_type=F32)


def mxu_t(left, right):
    return lax.dot_general(left, right, (((1,), (1,)), ((), ())), preferred_element_type=F32)


def exact_dot(left, right):
    return jnp.dot(left, right, precision=EXACT, preferred_element_type=F32)


def gate(left, right):
    return (left.astype(F32) * right.astype(F32)).astype(BF16)


def reversal(size):
    return jnp.where(iota((size, size), 0) + iota((size, size), 1) == size - 1, 1.0, 0.0).astype(BF16)


def split(value, pieces):
    parts = []
    for _ in range(pieces):
        parts.append(value.astype(BF16))
        value = value - parts[-1].astype(F32)
    return jnp.concatenate(parts, axis=0)


def join(stacked, rows):
    total = stacked[:rows].astype(F32)
    for start in range(rows, stacked.shape[0], rows):
        total = total + stacked[start : start + rows].astype(F32)
    return total


def flat_rows(table, poles):
    table = table.T
    groups = table.shape[0]
    per_row = LANES // poles
    spread = jnp.where(iota((poles, LANES), 0) == within(iota((poles, LANES), 1), poles), 1.0, 0.0)
    wide = exact_dot(table, spread)
    keep = within(iota((groups, LANES), 0), per_row) == over(iota((groups, LANES), 1), poles)
    wide = jnp.where(keep, wide, 0.0)
    return jnp.sum(wide.reshape(groups // per_row, per_row, LANES), axis=1)


def members(groups, first, span, width):
    return jnp.where(iota((groups, width), 0) == first + over(iota((groups, width), 1), span), 1.0, 0.0).astype(BF16)


def shard_start(groups):
    return pl.multiple_of(lax.axis_index("ch") * groups, LANES)


def states_kernel(all_params_ref, q_any, k_any, v_any, c_any, send_ref, keep_ref, gated_ref, dgate_ref, turned_ref,
                  rows_ref, table_ref, q_ref, k_ref, v_ref, c_ref, both_ref, sems, *,
                  group, poles, inner):
    tokens, _ = gated_ref.shape
    per_block = LANES // group
    _, blocks, _ = rows_ref.shape
    half_blocks = blocks // 2
    groups = blocks * per_block
    wide = inner * LANES
    core = lax.rem(lax.axis_index("ctx"), 2)
    sources = ((k_any, k_ref), (v_any, v_ref), (c_any, c_ref), (q_any, q_ref))
    half_steps = half_blocks // inner

    def copies(turn, step):
        start = lax.rem(core + 1 + turn, 2) * half_blocks + step * inner
        cut = pl.ds(pl.multiple_of(start * LANES, LANES), wide)
        return [
            pltpu.make_async_copy(far.at[:, cut], near.at[:, cut], sems.at[n, turn * half_steps + step])
            for n, (far, near) in enumerate(sources)
        ]

    first = shard_start(groups)
    for turn in range(2):
        for step in range(half_steps):
            for copy in copies(turn, step):
                copy.start()
    for n in range(2):
        table_ref[n] = all_params_ref[n, :, pl.ds(first, groups)]
    rows_ref[0] = jnp.exp(flat_rows(table_ref[0], poles))
    rows_ref[1] = flat_rows(table_ref[1], poles)

    flip = reversal(tokens)
    back_pos = (tokens - 1 - iota((tokens, LANES), 0)).astype(F32)
    back_lane = (tokens - 1 - iota((1, tokens), 1)).astype(F32)
    wide_group = over(within(iota((poles, 2 * LANES), 1), LANES), group)
    lanes = [slice(j * LANES, (j + 1) * LANES) for j in range(inner)]
    for b in range(blocks):
        table = jnp.exp(-rows_ref[0, b : b + 1, :] * back_pos).T
        both_ref[b, :LANES] = table.astype(BF16)
        both_ref[b, LANES:] = (table * back_lane).astype(BF16)

    for turn, msg_ref in enumerate((send_ref, keep_ref)):
        base = lax.rem(core + 1 + turn, 2) * half_blocks

        def body(step, carry, base=base, msg_ref=msg_ref, turn=turn):
            start = base + step * inner
            cut = pl.ds(pl.multiple_of(start * LANES, LANES), wide)
            for copy in copies(turn, step):
                copy.wait()
            gated, dgate = gate(k_ref[:, cut], v_ref[:, cut]), gate(c_ref[:, cut], q_ref[:, cut])
            gated_ref[:, cut] = gated
            dgate_ref[:, cut] = dgate
            turned = mxu(flip, dgate).astype(BF16)
            turned_ref[:, cut] = turned
            found = []
            for j in range(inner):
                pair = jnp.concatenate([gated[:, lanes[j]], turned[:, lanes[j]]], axis=1)
                found.append(mxu(both_ref[start + j], pair))
            for j in range(inner):
                folded = []
                for part in range(2):
                    total = found[j][part * LANES : part * LANES + poles]
                    for g in range(1, per_block):
                        row = part * LANES + g * poles
                        total = jnp.where(wide_group == g, found[j][row : row + poles], total)
                    folded.append(total)
                out = [folded[0][:, :LANES], folded[0][:, LANES:], folded[1][:, :LANES], folded[1][:, LANES:]]
                row = pl.multiple_of((step * inner + j) * 4 * poles, 4 * poles)
                msg_ref[pl.ds(row, 4 * poles), :] = jnp.concatenate(out, axis=0).astype(BF16)
            return carry

        lax.fori_loop(0, half_blocks // inner, body, 0)


def lags_kernel(lag_rates_ref, gated_ref, dgate_ref, turned_ref, *rest, second, group, poles, inner):
    if second:
        first_ref, out_ref, skip_ref = rest
    else:
        (out_ref,) = rest
    tokens, _ = gated_ref.shape
    per_block = LANES // group
    blocks, _, lag_width = lag_rates_ref.shape
    subs = tokens // SUB
    step_groups = inner * per_block
    lane_group = over(iota((SUB, LANES), 1), group)
    row, lane = iota((SUB, lag_width), 0), within(iota((SUB, lag_width), 1), SUB)
    near_side, no_wrap = row + lane <= SUB - 1, lane >= row
    lag = (SUB - 1 - within(iota((poles, lag_width), 1), SUB)).astype(F32)
    spread = members(step_groups, 0, SUB, inner * lag_width)
    steps = blocks // inner
    sums = []
    for step in range(1, steps) if second else range(1):
        outers = []
        for j in range(inner):
            lanes = slice((step * inner + j) * LANES, (step * inner + j + 1) * LANES)
            found = [None] * subs
            for k in range(subs):
                part = gated_ref[k * SUB : (k + 1) * SUB, lanes]
                stack = jnp.concatenate(
                    [jnp.where(lane_group == g, part, jnp.zeros_like(part)) for g in range(per_block)], axis=0
                )
                outer = mxu_t(turned_ref[: (subs - k) * SUB, lanes], stack)
                for n in range(subs - k):
                    far = subs - 1 - k - n
                    piece = outer[n * SUB : (n + 1) * SUB]
                    found[far] = piece if found[far] is None else found[far] + piece
            outers.append(found)
        terms = []
        for j in range(inner):
            found = outers[j] + [jnp.zeros((SUB, lag_width), F32)]
            lags = []
            for far in range(subs):
                total = jnp.where(near_side, found[far], found[far + 1])
                straight = pltpu.roll(total, 0, 1, stride=1, stride_axis=0)
                wrapped = pltpu.roll(total, lag_width - SUB, 1, stride=1, stride_axis=0)
                lags.append(jnp.sum(jnp.where(no_wrap, straight, wrapped), axis=0, keepdims=True))
            rate = lag_rates_ref[step * inner + j]
            decay = jnp.exp(-rate * SUB)
            total = jnp.zeros((poles, lag_width), F32)
            weighted = total
            for far in reversed(range(subs)):
                weighted = decay * weighted + far * lags[far]
                total = decay * total + lags[far]
            table = jnp.exp(-rate * lag)
            terms.append(
                split(jnp.concatenate([table * total, table * (lag * total + SUB * weighted)], axis=0), 2)
            )
        sums.append(mxu_t(jnp.concatenate(terms, axis=1), spread))
    sums = jnp.concatenate(sums, axis=1)
    zeros = jnp.zeros((sums.shape[0], blocks * per_block - sums.shape[1]), F32)
    sums = jnp.concatenate([zeros, sums] if second else [sums, zeros], axis=1)
    sums = join(sums, 2 * poles)
    if not second:
        out_ref[...] = sums
        return
    for b in range(blocks):
        lanes = slice(b * LANES, (b + 1) * LANES)
        product = gated_ref[:, lanes].astype(F32) * dgate_ref[:, lanes].astype(F32)
        skip_ref[b : b + 1, :] = jnp.sum(product, axis=0, keepdims=True)
    out_ref[: 2 * poles, :] = (first_ref[...] + sums).astype(BF16)
    out_ref[2 * poles :, :] = skip_ref[...].astype(BF16)


def tables_kernel(params_ref, rates_ref, lag_rates_ref, *, group, poles, inner):
    blocks, _, lag_width = lag_rates_ref.shape
    per_block = LANES // group
    step_groups = inner * per_block
    lag_wide = inner * lag_width
    pieces = split(params_ref[0], 3)
    spread = jnp.concatenate(
        [members(step_groups, 0, SUB, lag_wide), members(step_groups, 0, group, inner * LANES)], axis=1
    )
    for step in range(blocks // inner):
        spreads = mxu(pieces[:, step * step_groups : (step + 1) * step_groups], spread)
        rates = jnp.exp(join(spreads, poles))
        for j in range(inner):
            here = step * inner + j
            lag_rates_ref[here] = rates[:, j * lag_width : (j + 1) * lag_width]
            rates_ref[here] = rates[:, lag_wide + j * LANES : lag_wide + (j + 1) * LANES]


def conv_kernel(params_ref, rows_ref, skip_ref, rates_ref, lag_rates_ref, gated_ref, turned_ref, _, conv_ref,
                *, first_step, group, poles, inner):
    tokens, _ = gated_ref.shape
    per_block = LANES // group
    blocks, _, _ = rates_ref.shape
    subs = tokens // SUB
    lag_width = per_block * SUB
    first = lax.axis_index("ch") * blocks
    lead = (1 + iota((SUB, LANES), 0)).astype(F32)
    wide_group = over(within(iota((SUB, 2 * LANES), 1), LANES), group)
    state_group = over(within(iota((poles, 2 * LANES), 1), LANES), group)
    causal = iota((SUB, lag_width), 0) >= within(iota((SUB, lag_width), 1), SUB)
    lag = (SUB - 1 - within(iota((poles, lag_width), 1), SUB)).astype(F32)
    groups = blocks * per_block
    pieces = split(params_ref[1], 3).astype(F32)
    spread = members(groups, 0, SUB, inner * lag_width)

    def body(step, carry):
        start = (step + first_step) * inner
        moved = pltpu.roll(pieces, groups - start * per_block, 1).astype(BF16)
        lag_res = join(mxu(moved, spread), poles)
        lefts, lead_tables, decays, pairs, gains = [], [], [], [], []
        for j in range(inner):
            here = start + j
            table = jnp.exp(-lag_rates_ref[here] * lag)
            taps = jnp.sum(lag_res[:, j * lag_width : (j + 1) * lag_width] * table, axis=0, keepdims=True)
            taps = jnp.broadcast_to(taps, (SUB, lag_width))
            taps = pltpu.roll(taps, lag_width - SUB + 1, 1, stride=1, stride_axis=0)
            taps = jnp.where(causal, taps, 0.0).astype(BF16)
            lefts.append(jnp.concatenate([taps, table.astype(BF16)], axis=0))
            rate = rows_ref[0, pl.ds(here, 1), :]
            res = rows_ref[1, pl.ds(here, 1), :]
            lead_tables.append((res * jnp.exp(-rate * lead)).astype(BF16))
            decay = jnp.exp(-rates_ref[here] * SUB)
            decays.append(jnp.concatenate([decay, decay], axis=1))
            cut = pl.ds(pl.multiple_of(here * LANES, LANES), LANES)
            pairs.append(jnp.concatenate([gated_ref[:, cut], turned_ref[:, cut]], axis=1))
            gain = skip_ref[pl.ds(first + here, 1), :]
            gains.append(jnp.concatenate([gain, gain], axis=1))
        states = [jnp.zeros((poles, 2 * LANES), F32)] * inner
        totals = [[] for _ in range(inner)]
        for k in range(subs):
            rows = slice(k * SUB, (k + 1) * SUB)
            found = []
            for j in range(inner):
                part = pairs[j][rows]
                stack = [jnp.where(wide_group == g, part, jnp.zeros_like(part)) for g in range(per_block)]
                found.append(mxu(lefts[j], jnp.concatenate(stack, axis=0)))
            for j in range(inner):
                total = found[j][:SUB] + gains[j] * pairs[j][rows].astype(F32)
                if k:
                    held = states[j].astype(BF16)
                    stack = [jnp.where(state_group == g, held, jnp.zeros_like(held)) for g in range(per_block)]
                    total = total + mxu(lead_tables[j], jnp.concatenate(stack, axis=0))
                totals[j].append(total)
            states = [decays[j] * states[j] + found[j][SUB:] for j in range(inner)]
        for j in range(inner):
            cut = pl.ds(pl.multiple_of(2 * (step * inner + j) * LANES, LANES), 2 * LANES)
            conv_ref[:, cut] = jnp.concatenate(totals[j], axis=0)
        return carry

    lax.fori_loop(0, conv_ref.shape[1] // (2 * inner * LANES), body, 0)


def combine_kernel(*refs, level, levels, group, poles, tokens):
    last = level == levels - 1
    refs = list(refs)
    rates_ref = refs.pop(0)
    all_blocks = rates_ref.shape[0]
    blocks = all_blocks // 2
    per_block = LANES // group
    groups = all_blocks * per_block
    rows = 2 * poles
    if level == 0:
        own_ref, got_ref, sums_ref, states_ref, total_ref, near_ref = refs
    else:
        own_ref, own_tail_ref, got_ref = refs.pop(0), refs.pop(0), refs.pop(0)
        got_tail_ref = None if last else refs.pop(0)
        held_ref = refs.pop(0) if level > 1 else None
        if level == min(2, levels - 1):
            refs.pop(0)
        if last:
            near_ref, mine_ref, out_ref = refs
        else:
            states_ref, tail_ref, new_held_ref = refs[:3]
            slim_ref = refs[3] if level == levels - 2 else None
    me = lax.axis_index("ctx")
    core = lax.rem(me, 2)
    is_right = lax.rem(lax.shift_right_logical(me, level), 2) == 1
    before = lax.rem(me, 2**level) - (core if level else 0)
    gap_left = (tokens * before).astype(F32)
    gap_right = (tokens * (2**level - 2 - before)).astype(F32)
    gap = jnp.where(is_right, gap_left, gap_right)
    span = float(tokens * 2**level)
    next_right = lax.rem(lax.shift_right_logical(me, level + 1), 2) == 1

    def quarters(ref, b):
        value = ref[2 * b * rows : 2 * (b + 1) * rows].astype(F32)
        return [value[n * poles : (n + 1) * poles] for n in range(4)]

    wide_terms = []
    for b in range(blocks):
        rate = rates_ref[core * blocks + b]
        own_f, own_b, own_fm, own_bm = quarters(own_ref, b)
        if last:
            got = got_ref[b * rows : (b + 1) * rows].astype(F32)
            got_f = got_b = got[:poles]
            got_fm = got_bm = got[poles:]
        else:
            got_f, got_b, got_fm, got_bm = quarters(got_ref, b)
        left_f = jnp.where(is_right, got_f, own_f)
        left_fm = jnp.where(is_right, got_fm, own_fm)
        right_b = jnp.where(is_right, own_b, got_b)
        right_bm = jnp.where(is_right, own_bm, got_bm)
        once = jnp.exp(-rate)
        cross_res = once * (right_b * left_f)
        cross_mom = once * (right_bm * left_f + right_b * (left_fm + left_f))
        wide_terms.append(split(jnp.concatenate([cross_res, cross_mom], axis=0), 2))
        if level == 0:
            near_ref[b] = jnp.concatenate([left_f, right_b], axis=0)
        else:
            carry = jnp.exp(-rate * gap) * jnp.where(is_right, left_f, right_b)
            zero = jnp.zeros_like(carry)
            hold = jnp.concatenate([jnp.where(is_right, carry, zero), jnp.where(is_right, zero, carry)], axis=0)
            if level > 1:
                hold = hold + held_ref[b]
            if last:
                step = jnp.exp(-rate * tokens)
                near = near_ref[b]
                first_core = jnp.concatenate([hold[:poles], near[poles:] + step * hold[poles:]], axis=0)
                second_core = jnp.concatenate([near[:poles] + step * hold[:poles], hold[poles:]], axis=0)
                mine_ref[b] = jnp.where(core > 0, second_core, first_core).astype(BF16)
                out_ref[b * rows : (b + 1) * rows, :] = jnp.where(core > 0, first_core, second_core).astype(BF16)
            else:
                new_held_ref[b] = hold
        if not last:
            right_f = jnp.where(is_right, own_f, got_f)
            right_fm = jnp.where(is_right, own_fm, got_fm)
            left_b = jnp.where(is_right, got_b, own_b)
            left_bm = jnp.where(is_right, got_bm, own_bm)
            decay = jnp.exp(-rate * span)
            new_f, new_b = decay * left_f + right_f, left_b + decay * right_b
            new_fm = decay * (left_fm + span * left_f) + right_fm
            new_bm = left_bm + decay * (right_bm + span * right_b)
            here = slice(b * rows, (b + 1) * rows)
            new = jnp.concatenate([new_f, new_b, new_fm, new_bm], axis=0).astype(BF16)
            states_ref[2 * b * rows : 2 * (b + 1) * rows, :] = new
            if level == levels - 2 and level:
                chosen = [jnp.where(next_right, new_b, new_f), jnp.where(next_right, new_bm, new_fm)]
                slim_ref[here, :] = jnp.concatenate(chosen, axis=0).astype(BF16)
    cross = join(mxu_t(jnp.concatenate(wide_terms, axis=1), members(groups, 0, group, blocks * LANES)), rows)
    cross = jnp.where(core > 0, pltpu.roll(cross, groups // 2, 1), cross)
    tail = blocks * rows
    if level == 0:
        total_ref[...] = cross + sums_ref[...]
        return
    got_tail = got_ref[tail:, :] if last else got_tail_ref[...]
    both = own_tail_ref[...].astype(F32) + got_tail.astype(F32)
    rests = jnp.concatenate([both[:rows] + cross, both[rows:]], axis=0).astype(BF16)
    if last:
        out_ref[tail:, :] = rests
    else:
        tail_ref[...] = rests
        if slim_ref is not None:
            slim_ref[tail:, :] = rests


def merge_kernel(params_ref, own_ref, got_ref, _, out_ref, *, poles, length):
    groups = out_ref.shape[1]
    start = own_ref.shape[0] - out_ref.shape[0]
    both = own_ref[start:, :].astype(F32) + got_ref[start:, :].astype(F32)
    factor = -jnp.exp(params_ref[0]) * params_ref[1]
    scaled = [
        both[:poles] / length,
        factor * both[poles : 2 * poles] / math.sqrt(length),
        both[2 * poles :] / math.sqrt(length),
    ]
    out_ref[...] = jnp.concatenate(scaled, axis=0).astype(BF16)


def output_kernel(rows_ref, conv_ref, last_ref, mine_ref, got_ref, k_ref, v_ref, c_ref, gq_ref, gk_ref, gv_ref,
                  *, group, poles):
    tokens, width = gq_ref.shape
    per_block = LANES // group
    step = pl.program_id(0)
    steps = pl.num_programs(0)
    inner = width // LANES
    half_blocks = mine_ref.shape[0]
    core = lax.rem(lax.axis_index("ctx"), 2)
    flip = reversal(tokens)
    ahead = (1 + iota((tokens, LANES), 0)).astype(F32)
    state_group = over(within(iota((poles, 2 * LANES), 1), LANES), group)
    start = step * inner
    is_mine = over(start, half_blocks) == core
    cut = pl.ds(pl.multiple_of(start * LANES, LANES), width)

    def emit(conv_ref, base):
        totals = []
        for j in range(inner):
            here = start + j
            rate = rows_ref[0, pl.ds(here, 1), :]
            res = rows_ref[1, pl.ds(here, 1), :]
            table = (res * jnp.exp(-rate * ahead)).astype(BF16)
            place = within(here, half_blocks)
            held = jnp.where(
                is_mine, mine_ref[place], got_ref[pl.ds(pl.multiple_of(place * 2 * poles, 2 * poles), 2 * poles), :]
            )
            states = jnp.concatenate([held[:poles], held[poles:]], axis=1)
            stack = jnp.concatenate(
                [jnp.where(state_group == g, states, jnp.zeros_like(states)) for g in range(per_block)], axis=0
            )
            both = pl.ds(pl.multiple_of(2 * (here - base) * LANES, LANES), 2 * LANES)
            totals.append((conv_ref[:, both] + mxu(table, stack)).astype(BF16))
        hidden = jnp.concatenate([t[:, :LANES] for t in totals], axis=1)
        flow = mxu(flip, jnp.concatenate([t[:, LANES:] for t in totals], axis=1))
        gq_ref[...] = (c_ref[:, cut].astype(F32) * hidden.astype(F32)).astype(BF16)
        gk_ref[...] = (flow * v_ref[:, cut].astype(F32)).astype(BF16)
        gv_ref[...] = (flow * k_ref[:, cut].astype(F32)).astype(BF16)

    @pl.when(step < steps - 1)
    def _():
        emit(conv_ref, 0)

    @pl.when(step == steps - 1)
    def _():
        emit(last_ref, (steps - 1) * inner)


def assemble_kernel(*refs, poles):
    *slots, res_ref, log_ref, skip_ref = refs
    me = lax.axis_index("ch")
    groups = slots[0].shape[1]
    rows = slots[0].shape[0] - 2 * poles
    for mask, slot in enumerate(slots):
        source = lax.bitwise_xor(me, mask)
        value = slot[...].astype(F32)
        cut = pl.ds(pl.multiple_of(source * groups, LANES), groups)
        res_ref[:, cut] = value[:poles]
        log_ref[:, cut] = value[poles : 2 * poles]
        skip_ref[pl.ds(pl.multiple_of(source * rows, 8), rows), :] = value[2 * poles :]


def local(queries, key_input, value_input, cotangent, residues, log_rates, skip_gain):
    tokens, width = queries.shape
    parts = lax.axis_size("ctx")
    shards = lax.axis_size("ch")
    levels = parts.bit_length() - 1
    all_groups, poles = residues.shape
    groups = all_groups // shards
    group = width // groups
    blocks = width // LANES
    inner = 4
    steps = blocks // inner
    half_blocks = blocks // 2
    lag_width = LANES // group * SUB
    sizes = dict(group=group, poles=poles)
    half_rows, tail = half_blocks * 2 * poles, 2 * poles + blocks

    vmem = pl.BlockSpec(memory_space=pltpu.VMEM)
    anywhere = pl.BlockSpec(memory_space=pl.ANY)
    log_rates, residues = log_rates.T, residues.T
    def shape(*dims, dtype=F32):
        return jax.ShapeDtypeStruct(dims, dtype)

    def swap(value, level):
        return lax.ppermute(value, "ctx", [(i, i ^ (1 << level)) for i in range(parts)])

    far = pl.BlockSpec(memory_space=pl.ANY)
    outgoing, message, gated, dgate, turned, rows, params = pl.pallas_call(
        lambda *refs: states_kernel(*refs, inner=inner, **sizes),
        in_specs=[vmem] + [far] * 4,
        out_specs=[vmem] * 7,
        out_shape=[
            shape(2 * half_rows, LANES, dtype=BF16),
            shape(2 * half_rows, LANES, dtype=BF16),
            shape(tokens, width, dtype=BF16),
            shape(tokens, width, dtype=BF16),
            shape(tokens, width, dtype=BF16),
            shape(2, blocks, LANES),
            shape(2, poles, groups),
        ],
        scratch_shapes=[pltpu.VMEM((tokens, width), BF16)] * 4
        + [pltpu.VMEM((blocks, 2 * LANES, tokens), BF16), pltpu.SemaphoreType.DMA((4, steps))],
        compiler_params=pltpu.CompilerParams(vmem_limit_bytes=53000 * 1024),
        name="states",
    )(jnp.stack([log_rates, residues]), queries, key_input, value_input, cotangent)

    rates, lag_rates = pl.pallas_call(
        lambda *refs: tables_kernel(*refs, inner=inner, **sizes),
        in_specs=[vmem],
        out_specs=[vmem] * 2,
        out_shape=[shape(blocks, poles, LANES), shape(blocks, poles, lag_width)],
        compiler_params=PARAMS,
        cost_estimate=pl.CostEstimate(flops=10**9, bytes_accessed=10**6, transcendentals=10**5),
        name="tables",
    )(params)

    work = pl.CostEstimate(
        flops=16 * tokens * tokens * width, bytes_accessed=12 * tokens * width, transcendentals=tokens * width
    )

    def local_sums(second, *more):
        return pl.pallas_call(
            lambda *refs: lags_kernel(*refs, second=second, inner=inner, **sizes),
            in_specs=[vmem] * (4 + len(more)),
            out_specs=vmem,
            out_shape=shape(tail, LANES, dtype=BF16) if second else shape(2 * poles, LANES),
            scratch_shapes=[pltpu.VMEM((blocks, LANES), F32)] if second else [],
            compiler_params=PARAMS,
            cost_estimate=work,
            name="lags",
        )(lag_rates, gated, dgate, turned, *more)

    def convolve(first_step, count, after):
        skip_rows = skip_gain.reshape(-1, LANES)
        return pl.pallas_call(
            lambda *refs: conv_kernel(*refs, first_step=first_step, inner=inner, **sizes),
            in_specs=[vmem] * 7 + [anywhere],
            out_specs=vmem,
            out_shape=shape(tokens, 2 * count * inner * LANES),
            compiler_params=PARAMS,
            cost_estimate=work,
            name="conv",
        )(params, rows, skip_rows, rates, lag_rates, gated, turned, after)

    def combine(level, operands, outs):
        return pl.pallas_call(
            lambda *refs: combine_kernel(*refs, level=level, levels=levels, tokens=tokens, **sizes),
            in_specs=[anywhere if x is conv else vmem for x in operands],
            out_specs=[vmem] * len(outs),
            out_shape=outs,
            compiler_params=PARAMS,
            name="combine",
        )(*operands)

    conv = None
    states_shape = shape(2 * half_rows, LANES, dtype=BF16)
    tail_shape = shape(tail, LANES, dtype=BF16)
    slim_shape = shape(half_rows + tail, LANES, dtype=BF16)
    held_shape = shape(half_blocks, 2 * poles, LANES)
    got = swap(outgoing, 0)
    states, total, near = combine(
        0, [rates, message, got, local_sums(0)], [states_shape, shape(2 * poles, LANES), held_shape]
    )
    held = slim = None
    for level in range(1, levels):
        last = level == levels - 1
        if last and slim is not None:
            received = [swap(slim, level)]
        else:
            received = [swap(states, level)]
            if level == 1:
                carried = local_sums(1, total)
            received.append(swap(carried, level))
        operands = [rates, states, carried, *received]
        if level > 1:
            operands.append(held)
        if level == min(2, levels - 1):
            conv = convolve(0, steps - 1, near if held is None else held)
            operands.append(conv)
        if last:
            outs = [shape(half_blocks, 2 * poles, LANES, dtype=BF16), slim_shape]
            mine, outgoing = combine(level, [*operands, near], outs)
        else:
            outs = [states_shape, tail_shape, held_shape]
            if level == levels - 2:
                outs.append(slim_shape)
            states, carried, held, *more = combine(level, operands, outs)
            slim = more[0] if more else None
    got = swap(outgoing, 0)
    last_conv = convolve(steps - 1, 1, outgoing)
    merged = pl.pallas_call(
        lambda *refs: merge_kernel(*refs, poles=poles, length=tokens * parts),
        in_specs=[vmem] * 3 + [anywhere],
        out_specs=vmem,
        out_shape=shape(tail, LANES, dtype=BF16),
        compiler_params=PARAMS,
        name="merge",
    )(params, outgoing, got, last_conv)

    gathered = [merged]
    for mask in range(1, shards):
        gathered.append(lax.ppermute(merged, "ch", [(i, i ^ mask) for i in range(shards)]))

    main = pl.BlockSpec((tokens, inner * LANES), lambda i: (0, i))
    grad_query, grad_key, grad_value = pl.pallas_call(
        lambda *refs: output_kernel(*refs, **sizes),
        grid=(steps,),
        in_specs=[vmem] * 8,
        out_specs=[main] * 3,
        out_shape=[shape(tokens, width, dtype=BF16)] * 3,
        compiler_params=PARAMS,
        cost_estimate=work,
        name="outputs",
    )(rows, conv, last_conv, mine, got, key_input, value_input, cotangent)

    grad_residue, grad_lograte, grad_skip = pl.pallas_call(
        lambda *refs: assemble_kernel(*refs, poles=poles),
        in_specs=[vmem] * shards,
        out_specs=[vmem] * 3,
        out_shape=[shape(poles, all_groups), shape(poles, all_groups), shape(shards * blocks, LANES)],
        compiler_params=PARAMS,
        name="assemble",
    )(*gathered)
    return (grad_query, grad_key, grad_value, grad_residue.T, grad_lograte.T, grad_skip.reshape(-1))


def solution(mesh):
    placed = (P("ctx", "ch"), P("ctx", "ch"), P("ctx", "ch"), P("ctx", "ch"), P(), P(), P())
    return jax.shard_map(
        local,
        mesh=mesh,
        in_specs=placed,
        out_specs=(P("ctx", "ch"), P("ctx", "ch"), P("ctx", "ch"), P(), P(), P()),
        check_vma=False,
    )
```

```python
import math

import jax
import jax.numpy as jnp
from jax import lax
from jax.experimental import pallas as pl
from jax.experimental.pallas import tpu as pltpu
from jax.sharding import PartitionSpec as P

LANES = 128
SUB = 32
F32 = jnp.float32
BF16 = jnp.bfloat16
EXACT = lax.Precision.HIGHEST
VMEM_LIMIT = 40 * 1024 * 1024
GATES_LIMIT = 53400 * 1024
PARAMS = pltpu.CompilerParams(vmem_limit_bytes=VMEM_LIMIT)


def iota(shape, axis):
    return lax.broadcasted_iota(jnp.int32, shape, axis)


def over(value, size):
    return lax.shift_right_logical(value, size.bit_length() - 1)


def within(value, size):
    return lax.bitwise_and(value, size - 1)


def mxu(left, right):
    return jnp.dot(left, right, preferred_element_type=F32)


def mxu_t(left, right):
    return lax.dot_general(left, right, (((1,), (1,)), ((), ())), preferred_element_type=F32)


def exact_dot(left, right):
    return jnp.dot(left, right, precision=EXACT, preferred_element_type=F32)


def gate(left, right):
    return (left.astype(F32) * right.astype(F32)).astype(BF16)


def reversal(size):
    return jnp.where(iota((size, size), 0) + iota((size, size), 1) == size - 1, 1.0, 0.0).astype(BF16)


def split(value, pieces):
    parts = []
    for _ in range(pieces):
        parts.append(value.astype(BF16))
        value = value - parts[-1].astype(F32)
    return jnp.concatenate(parts, axis=0)


def join(stacked, rows):
    total = stacked[:rows].astype(F32)
    for start in range(rows, stacked.shape[0], rows):
        total = total + stacked[start : start + rows].astype(F32)
    return total


def flat_rows(table, poles):
    table = table.T
    groups = table.shape[0]
    per_row = LANES // poles
    spread = jnp.where(iota((poles, LANES), 0) == within(iota((poles, LANES), 1), poles), 1.0, 0.0)
    wide = exact_dot(table, spread)
    keep = within(iota((groups, LANES), 0), per_row) == over(iota((groups, LANES), 1), poles)
    wide = jnp.where(keep, wide, 0.0)
    return jnp.sum(wide.reshape(groups // per_row, per_row, LANES), axis=1)


def members(groups, first, span, width):
    return jnp.where(iota((groups, width), 0) == first + over(iota((groups, width), 1), span), 1.0, 0.0).astype(BF16)


def shard_start(groups):
    return pl.multiple_of(lax.axis_index("ch") * groups, LANES)


def gates_kernel(q_any, k_any, v_any, c_any, gated_ref, dgate_ref, turned_ref, q_ref, k_ref, v_ref, c_ref, sems, *, steps):
    tokens, width = q_ref.shape
    wide = width // steps
    sources = ((k_any, k_ref), (v_any, v_ref), (c_any, c_ref), (q_any, q_ref))
    cuts = [slice(step * wide, (step + 1) * wide) for step in range(steps)]
    copies = [
        [pltpu.make_async_copy(far.at[:, cut], near.at[:, cut], sems.at[n, step]) for n, (far, near) in enumerate(sources)]
        for step, cut in enumerate(cuts)
    ]
    for step in copies:
        for copy in step:
            copy.start()
    flip = reversal(tokens)
    for step, cut in enumerate(cuts):
        for copy in copies[step]:
            copy.wait()
        dgate = gate(c_ref[:, cut], q_ref[:, cut])
        dgate_ref[:, cut] = dgate
        gated_ref[:, cut] = gate(k_ref[:, cut], v_ref[:, cut])
        turned_ref[:, cut] = mxu(flip, dgate).astype(BF16)


def states_kernel(logs_ref, res_ref, gated_ref, turned_ref, send_ref, keep_ref, rows_ref, table_ref,
                  *, group, poles, inner):
    tokens, _ = gated_ref.shape
    per_block = LANES // group
    _, blocks, _ = rows_ref.shape
    half_blocks = blocks // 2
    groups = blocks * per_block
    wide = inner * LANES
    core = lax.rem(lax.axis_index("ctx"), 2)
    first = shard_start(groups)
    for n, ref in enumerate((logs_ref, res_ref)):
        table_ref[n] = ref[:, pl.ds(first, groups)]
    rows_ref[0] = jnp.exp(flat_rows(table_ref[0], poles))
    rows_ref[1] = flat_rows(table_ref[1], poles)

    back_pos = (tokens - 1 - iota((tokens, LANES), 0)).astype(F32)
    back_lane = (tokens - 1 - iota((1, tokens), 1)).astype(F32)
    wide_group = over(within(iota((poles, 2 * LANES), 1), LANES), group)
    lanes = [slice(j * LANES, (j + 1) * LANES) for j in range(inner)]

    for turn, msg_ref in enumerate((send_ref, keep_ref)):
        base = lax.rem(core + 1 + turn, 2) * half_blocks

        def body(step, carry, base=base, msg_ref=msg_ref):
            start = base + step * inner
            cut = pl.ds(pl.multiple_of(start * LANES, LANES), wide)
            gated, turned = gated_ref[:, cut], turned_ref[:, cut]
            tables = [jnp.exp(-rows_ref[0, pl.ds(start + j, 1), :] * back_pos).T for j in range(inner)]
            found = []
            for j in range(inner):
                both = jnp.concatenate([tables[j].astype(BF16), (tables[j] * back_lane).astype(BF16)], axis=0)
                pair = jnp.concatenate([gated[:, lanes[j]], turned[:, lanes[j]]], axis=1)
                found.append(mxu(both, pair))
            for j in range(inner):
                folded = []
                for part in range(2):
                    total = found[j][part * LANES : part * LANES + poles]
                    for g in range(1, per_block):
                        row = part * LANES + g * poles
                        total = jnp.where(wide_group == g, found[j][row : row + poles], total)
                    folded.append(total)
                out = [folded[0][:, :LANES], folded[0][:, LANES:], folded[1][:, :LANES], folded[1][:, LANES:]]
                row = pl.multiple_of((step * inner + j) * 4 * poles, 4 * poles)
                msg_ref[pl.ds(row, 4 * poles), :] = jnp.concatenate(out, axis=0).astype(BF16)
            return carry

        lax.fori_loop(0, half_blocks // inner, body, 0)


def lags_kernel(lag_rates_ref, gated_ref, dgate_ref, turned_ref, *rest, second, group, poles, inner):
    if second:
        first_ref, out_ref, skip_ref = rest
    else:
        (out_ref,) = rest
    tokens, _ = gated_ref.shape
    per_block = LANES // group
    blocks, _, lag_width = lag_rates_ref.shape
    subs = tokens // SUB
    step_groups = inner * per_block
    lane_group = over(iota((SUB, LANES), 1), group)
    row, lane = iota((SUB, lag_width), 0), within(iota((SUB, lag_width), 1), SUB)
    near_side, no_wrap = row + lane <= SUB - 1, lane >= row
    lag = (SUB - 1 - within(iota((poles, lag_width), 1), SUB)).astype(F32)
    spread = members(step_groups, 0, SUB, inner * lag_width)
    steps = blocks // inner
    sums = []
    for step in range(1, steps) if second else range(1):
        outers = []
        for j in range(inner):
            lanes = slice((step * inner + j) * LANES, (step * inner + j + 1) * LANES)
            found = [None] * subs
            for k in range(subs):
                part = gated_ref[k * SUB : (k + 1) * SUB, lanes]
                stack = jnp.concatenate(
                    [jnp.where(lane_group == g, part, jnp.zeros_like(part)) for g in range(per_block)], axis=0
                )
                outer = mxu_t(turned_ref[: (subs - k) * SUB, lanes], stack)
                for n in range(subs - k):
                    far = subs - 1 - k - n
                    piece = outer[n * SUB : (n + 1) * SUB]
                    found[far] = piece if found[far] is None else found[far] + piece
            outers.append(found)
        terms = []
        for j in range(inner):
            found = outers[j] + [jnp.zeros((SUB, lag_width), F32)]
            lags = []
            for far in range(subs):
                total = jnp.where(near_side, found[far], found[far + 1])
                straight = pltpu.roll(total, 0, 1, stride=1, stride_axis=0)
                wrapped = pltpu.roll(total, lag_width - SUB, 1, stride=1, stride_axis=0)
                lags.append(jnp.sum(jnp.where(no_wrap, straight, wrapped), axis=0, keepdims=True))
            rate = lag_rates_ref[step * inner + j]
            decay = jnp.exp(-rate * SUB)
            total = jnp.zeros((poles, lag_width), F32)
            weighted = total
            for far in reversed(range(subs)):
                weighted = decay * weighted + far * lags[far]
                total = decay * total + lags[far]
            table = jnp.exp(-rate * lag)
            terms.append(
                split(jnp.concatenate([table * total, table * (lag * total + SUB * weighted)], axis=0), 2)
            )
        sums.append(mxu_t(jnp.concatenate(terms, axis=1), spread))
    sums = jnp.concatenate(sums, axis=1)
    zeros = jnp.zeros((sums.shape[0], blocks * per_block - sums.shape[1]), F32)
    sums = jnp.concatenate([zeros, sums] if second else [sums, zeros], axis=1)
    sums = join(sums, 2 * poles)
    if not second:
        out_ref[...] = sums
        return
    for b in range(blocks):
        lanes = slice(b * LANES, (b + 1) * LANES)
        product = gated_ref[:, lanes].astype(F32) * dgate_ref[:, lanes].astype(F32)
        skip_ref[b : b + 1, :] = jnp.sum(product, axis=0, keepdims=True)
    out_ref[: 2 * poles, :] = (first_ref[...] + sums).astype(BF16)
    out_ref[2 * poles :, :] = skip_ref[...].astype(BF16)


def tables_kernel(params_ref, rates_ref, lag_rates_ref, *, group, poles, inner):
    blocks, _, lag_width = lag_rates_ref.shape
    per_block = LANES // group
    step_groups = inner * per_block
    lag_wide = inner * lag_width
    pieces = split(params_ref[0], 3)
    spread = jnp.concatenate(
        [members(step_groups, 0, SUB, lag_wide), members(step_groups, 0, group, inner * LANES)], axis=1
    )
    for step in range(blocks // inner):
        spreads = mxu(pieces[:, step * step_groups : (step + 1) * step_groups], spread)
        rates = jnp.exp(join(spreads, poles))
        for j in range(inner):
            here = step * inner + j
            lag_rates_ref[here] = rates[:, j * lag_width : (j + 1) * lag_width]
            rates_ref[here] = rates[:, lag_wide + j * LANES : lag_wide + (j + 1) * LANES]


def conv_kernel(params_ref, rows_ref, skip_ref, rates_ref, lag_rates_ref, gated_ref, turned_ref, _, conv_ref,
                *, first_step, group, poles, inner):
    tokens, _ = gated_ref.shape
    per_block = LANES // group
    blocks, _, _ = rates_ref.shape
    subs = tokens // SUB
    lag_width = per_block * SUB
    first = lax.axis_index("ch") * blocks
    lead = (1 + iota((SUB, LANES), 0)).astype(F32)
    wide_group = over(within(iota((SUB, 2 * LANES), 1), LANES), group)
    state_group = over(within(iota((poles, 2 * LANES), 1), LANES), group)
    causal = iota((SUB, lag_width), 0) >= within(iota((SUB, lag_width), 1), SUB)
    lag = (SUB - 1 - within(iota((poles, lag_width), 1), SUB)).astype(F32)
    groups = blocks * per_block
    pieces = split(params_ref[1], 3).astype(F32)
    spread = members(groups, 0, SUB, inner * lag_width)

    def body(step, carry):
        start = (step + first_step) * inner
        moved = pltpu.roll(pieces, groups - start * per_block, 1).astype(BF16)
        lag_res = join(mxu(moved, spread), poles)
        lefts, lead_tables, decays, pairs, gains = [], [], [], [], []
        for j in range(inner):
            here = start + j
            table = jnp.exp(-lag_rates_ref[here] * lag)
            taps = jnp.sum(lag_res[:, j * lag_width : (j + 1) * lag_width] * table, axis=0, keepdims=True)
            taps = jnp.broadcast_to(taps, (SUB, lag_width))
            taps = pltpu.roll(taps, lag_width - SUB + 1, 1, stride=1, stride_axis=0)
            taps = jnp.where(causal, taps, 0.0).astype(BF16)
            lefts.append(jnp.concatenate([taps, table.astype(BF16)], axis=0))
            rate = rows_ref[0, pl.ds(here, 1), :]
            res = rows_ref[1, pl.ds(here, 1), :]
            lead_tables.append((res * jnp.exp(-rate * lead)).astype(BF16))
            decay = jnp.exp(-rates_ref[here] * SUB)
            decays.append(jnp.concatenate([decay, decay], axis=1))
            cut = pl.ds(pl.multiple_of(here * LANES, LANES), LANES)
            pairs.append(jnp.concatenate([gated_ref[:, cut], turned_ref[:, cut]], axis=1))
            gain = skip_ref[pl.ds(first + here, 1), :]
            gains.append(jnp.concatenate([gain, gain], axis=1))
        states = [jnp.zeros((poles, 2 * LANES), F32)] * inner
        totals = [[] for _ in range(inner)]
        for k in range(subs):
            rows = slice(k * SUB, (k + 1) * SUB)
            found = []
            for j in range(inner):
                part = pairs[j][rows]
                stack = [jnp.where(wide_group == g, part, jnp.zeros_like(part)) for g in range(per_block)]
                found.append(mxu(lefts[j], jnp.concatenate(stack, axis=0)))
            for j in range(inner):
                total = found[j][:SUB] + gains[j] * pairs[j][rows].astype(F32)
                if k:
                    held = states[j].astype(BF16)
                    stack = [jnp.where(state_group == g, held, jnp.zeros_like(held)) for g in range(per_block)]
                    total = total + mxu(lead_tables[j], jnp.concatenate(stack, axis=0))
                totals[j].append(total)
            states = [decays[j] * states[j] + found[j][SUB:] for j in range(inner)]
        for j in range(inner):
            cut = pl.ds(pl.multiple_of(2 * (step * inner + j) * LANES, LANES), 2 * LANES)
            conv_ref[:, cut] = jnp.concatenate(totals[j], axis=0)
        return carry

    lax.fori_loop(0, conv_ref.shape[1] // (2 * inner * LANES), body, 0)


def combine_kernel(*refs, level, levels, group, poles, tokens):
    last = level == levels - 1
    refs = list(refs)
    rates_ref = refs.pop(0)
    all_blocks = rates_ref.shape[0]
    blocks = all_blocks // 2
    per_block = LANES // group
    groups = all_blocks * per_block
    rows = 2 * poles
    if level == 0:
        own_ref, got_ref, sums_ref, states_ref, total_ref, near_ref = refs
    else:
        own_ref, own_tail_ref, got_ref = refs.pop(0), refs.pop(0), refs.pop(0)
        got_tail_ref = None if last else refs.pop(0)
        held_ref = refs.pop(0) if level > 1 else None
        if level == min(2, levels - 1):
            refs.pop(0)
        if last:
            near_ref, mine_ref, out_ref = refs
        else:
            states_ref, tail_ref, new_held_ref = refs[:3]
            slim_ref = refs[3] if level == levels - 2 else None
    me = lax.axis_index("ctx")
    core = lax.rem(me, 2)
    is_right = lax.rem(lax.shift_right_logical(me, level), 2) == 1
    before = lax.rem(me, 2**level) - (core if level else 0)
    gap_left = (tokens * before).astype(F32)
    gap_right = (tokens * (2**level - 2 - before)).astype(F32)
    gap = jnp.where(is_right, gap_left, gap_right)
    span = float(tokens * 2**level)
    next_right = lax.rem(lax.shift_right_logical(me, level + 1), 2) == 1

    def quarters(ref, b):
        value = ref[2 * b * rows : 2 * (b + 1) * rows].astype(F32)
        return [value[n * poles : (n + 1) * poles] for n in range(4)]

    wide_terms = []
    for b in range(blocks):
        rate = rates_ref[core * blocks + b]
        own_f, own_b, own_fm, own_bm = quarters(own_ref, b)
        if last:
            got = got_ref[b * rows : (b + 1) * rows].astype(F32)
            got_f = got_b = got[:poles]
            got_fm = got_bm = got[poles:]
        else:
            got_f, got_b, got_fm, got_bm = quarters(got_ref, b)
        left_f = jnp.where(is_right, got_f, own_f)
        left_fm = jnp.where(is_right, got_fm, own_fm)
        right_b = jnp.where(is_right, own_b, got_b)
        right_bm = jnp.where(is_right, own_bm, got_bm)
        once = jnp.exp(-rate)
        cross_res = once * (right_b * left_f)
        cross_mom = once * (right_bm * left_f + right_b * (left_fm + left_f))
        wide_terms.append(split(jnp.concatenate([cross_res, cross_mom], axis=0), 2))
        if level == 0:
            near_ref[b] = jnp.concatenate([left_f, right_b], axis=0)
        else:
            carry = jnp.exp(-rate * gap) * jnp.where(is_right, left_f, right_b)
            zero = jnp.zeros_like(carry)
            hold = jnp.concatenate([jnp.where(is_right, carry, zero), jnp.where(is_right, zero, carry)], axis=0)
            if level > 1:
                hold = hold + held_ref[b]
            if last:
                step = jnp.exp(-rate * tokens)
                near = near_ref[b]
                first_core = jnp.concatenate([hold[:poles], near[poles:] + step * hold[poles:]], axis=0)
                second_core = jnp.concatenate([near[:poles] + step * hold[:poles], hold[poles:]], axis=0)
                mine_ref[b] = jnp.where(core > 0, second_core, first_core).astype(BF16)
                out_ref[b * rows : (b + 1) * rows, :] = jnp.where(core > 0, first_core, second_core).astype(BF16)
            else:
                new_held_ref[b] = hold
        if not last:
            right_f = jnp.where(is_right, own_f, got_f)
            right_fm = jnp.where(is_right, own_fm, got_fm)
            left_b = jnp.where(is_right, got_b, own_b)
            left_bm = jnp.where(is_right, got_bm, own_bm)
            decay = jnp.exp(-rate * span)
            new_f, new_b = decay * left_f + right_f, left_b + decay * right_b
            new_fm = decay * (left_fm + span * left_f) + right_fm
            new_bm = left_bm + decay * (right_bm + span * right_b)
            here = slice(b * rows, (b + 1) * rows)
            new = jnp.concatenate([new_f, new_b, new_fm, new_bm], axis=0).astype(BF16)
            states_ref[2 * b * rows : 2 * (b + 1) * rows, :] = new
            if level == levels - 2 and level:
                chosen = [jnp.where(next_right, new_b, new_f), jnp.where(next_right, new_bm, new_fm)]
                slim_ref[here, :] = jnp.concatenate(chosen, axis=0).astype(BF16)
    cross = join(mxu_t(jnp.concatenate(wide_terms, axis=1), members(groups, 0, group, blocks * LANES)), rows)
    cross = jnp.where(core > 0, pltpu.roll(cross, groups // 2, 1), cross)
    tail = blocks * rows
    if level == 0:
        total_ref[...] = cross + sums_ref[...]
        return
    got_tail = got_ref[tail:, :] if last else got_tail_ref[...]
    both = own_tail_ref[...].astype(F32) + got_tail.astype(F32)
    rests = jnp.concatenate([both[:rows] + cross, both[rows:]], axis=0).astype(BF16)
    if last:
        out_ref[tail:, :] = rests
    else:
        tail_ref[...] = rests
        if slim_ref is not None:
            slim_ref[tail:, :] = rests


def merge_kernel(params_ref, own_ref, got_ref, _, out_ref, *, poles, length):
    groups = out_ref.shape[1]
    start = own_ref.shape[0] - out_ref.shape[0]
    both = own_ref[start:, :].astype(F32) + got_ref[start:, :].astype(F32)
    factor = -jnp.exp(params_ref[0]) * params_ref[1]
    scaled = [
        both[:poles] / length,
        factor * both[poles : 2 * poles] / math.sqrt(length),
        both[2 * poles :] / math.sqrt(length),
    ]
    out_ref[...] = jnp.concatenate(scaled, axis=0).astype(BF16)


def output_kernel(rows_ref, conv_ref, last_ref, mine_ref, got_ref, k_ref, v_ref, c_ref, gq_ref, gk_ref, gv_ref,
                  *, group, poles):
    tokens, width = gq_ref.shape
    per_block = LANES // group
    step = pl.program_id(0)
    steps = pl.num_programs(0)
    inner = width // LANES
    half_blocks = mine_ref.shape[0]
    core = lax.rem(lax.axis_index("ctx"), 2)
    flip = reversal(tokens)
    ahead = (1 + iota((tokens, LANES), 0)).astype(F32)
    state_group = over(within(iota((poles, 2 * LANES), 1), LANES), group)
    start = step * inner
    is_mine = over(start, half_blocks) == core
    cut = pl.ds(pl.multiple_of(start * LANES, LANES), width)

    def emit(conv_ref, base):
        totals = []
        for j in range(inner):
            here = start + j
            rate = rows_ref[0, pl.ds(here, 1), :]
            res = rows_ref[1, pl.ds(here, 1), :]
            table = (res * jnp.exp(-rate * ahead)).astype(BF16)
            place = within(here, half_blocks)
            held = jnp.where(
                is_mine, mine_ref[place], got_ref[pl.ds(pl.multiple_of(place * 2 * poles, 2 * poles), 2 * poles), :]
            )
            states = jnp.concatenate([held[:poles], held[poles:]], axis=1)
            stack = jnp.concatenate(
                [jnp.where(state_group == g, states, jnp.zeros_like(states)) for g in range(per_block)], axis=0
            )
            both = pl.ds(pl.multiple_of(2 * (here - base) * LANES, LANES), 2 * LANES)
            totals.append((conv_ref[:, both] + mxu(table, stack)).astype(BF16))
        hidden = jnp.concatenate([t[:, :LANES] for t in totals], axis=1)
        flow = mxu(flip, jnp.concatenate([t[:, LANES:] for t in totals], axis=1))
        gq_ref[...] = (c_ref[:, cut].astype(F32) * hidden.astype(F32)).astype(BF16)
        gk_ref[...] = (flow * v_ref[:, cut].astype(F32)).astype(BF16)
        gv_ref[...] = (flow * k_ref[:, cut].astype(F32)).astype(BF16)

    @pl.when(step < steps - 1)
    def _():
        emit(conv_ref, 0)

    @pl.when(step == steps - 1)
    def _():
        emit(last_ref, (steps - 1) * inner)


def assemble_kernel(*refs, poles):
    *slots, res_ref, log_ref, skip_ref = refs
    me = lax.axis_index("ch")
    groups = slots[0].shape[1]
    rows = slots[0].shape[0] - 2 * poles
    for mask, slot in enumerate(slots):
        source = lax.bitwise_xor(me, mask)
        value = slot[...].astype(F32)
        cut = pl.ds(pl.multiple_of(source * groups, LANES), groups)
        res_ref[:, cut] = value[:poles]
        log_ref[:, cut] = value[poles : 2 * poles]
        skip_ref[pl.ds(pl.multiple_of(source * rows, 8), rows), :] = value[2 * poles :]


def local(queries, key_input, value_input, cotangent, residues, log_rates, skip_gain):
    tokens, width = queries.shape
    parts = lax.axis_size("ctx")
    shards = lax.axis_size("ch")
    levels = parts.bit_length() - 1
    all_groups, poles = residues.shape
    groups = all_groups // shards
    group = width // groups
    blocks = width // LANES
    inner = 4
    steps = blocks // inner
    half_blocks = blocks // 2
    lag_width = LANES // group * SUB
    sizes = dict(group=group, poles=poles)
    half_rows, tail = half_blocks * 2 * poles, 2 * poles + blocks

    vmem = pl.BlockSpec(memory_space=pltpu.VMEM)
    anywhere = pl.BlockSpec(memory_space=pl.ANY)
    log_rates, residues = log_rates.T, residues.T
    def shape(*dims, dtype=F32):
        return jax.ShapeDtypeStruct(dims, dtype)

    def swap(value, level):
        return lax.ppermute(value, "ctx", [(i, i ^ (1 << level)) for i in range(parts)])

    operand = shape(tokens, width, dtype=BF16)
    gated, dgate, turned = pl.pallas_call(
        lambda *refs: gates_kernel(*refs, steps=steps),
        in_specs=[anywhere] * 4,
        out_specs=[vmem] * 3,
        out_shape=[operand] * 3,
        scratch_shapes=[pltpu.VMEM((tokens, width), BF16)] * 4 + [pltpu.SemaphoreType.DMA((4, steps))],
        compiler_params=pltpu.CompilerParams(vmem_limit_bytes=GATES_LIMIT),
        name="gates",
    )(queries, key_input, value_input, cotangent)
    outgoing, message, rows, params = pl.pallas_call(
        lambda *refs: states_kernel(*refs, inner=inner, **sizes),
        in_specs=[vmem] * 4,
        out_specs=[vmem] * 4,
        out_shape=[
            shape(2 * half_rows, LANES, dtype=BF16),
            shape(2 * half_rows, LANES, dtype=BF16),
            shape(2, blocks, LANES),
            shape(2, poles, groups),
        ],
        compiler_params=PARAMS,
        name="states",
    )(log_rates, residues, gated, turned)

    rates, lag_rates = pl.pallas_call(
        lambda *refs: tables_kernel(*refs, inner=inner, **sizes),
        in_specs=[vmem],
        out_specs=[vmem] * 2,
        out_shape=[shape(blocks, poles, LANES), shape(blocks, poles, lag_width)],
        compiler_params=PARAMS,
        cost_estimate=pl.CostEstimate(flops=10**9, bytes_accessed=10**6, transcendentals=10**5),
        name="tables",
    )(params)

    work = pl.CostEstimate(
        flops=16 * tokens * tokens * width, bytes_accessed=12 * tokens * width, transcendentals=tokens * width
    )

    def local_sums(second, *more):
        return pl.pallas_call(
            lambda *refs: lags_kernel(*refs, second=second, inner=inner, **sizes),
            in_specs=[vmem] * (4 + len(more)),
            out_specs=vmem,
            out_shape=shape(tail, LANES, dtype=BF16) if second else shape(2 * poles, LANES),
            scratch_shapes=[pltpu.VMEM((blocks, LANES), F32)] if second else [],
            compiler_params=PARAMS,
            cost_estimate=work,
            name="lags",
        )(lag_rates, gated, dgate, turned, *more)

    def convolve(first_step, count, after):
        skip_rows = skip_gain.reshape(-1, LANES)
        return pl.pallas_call(
            lambda *refs: conv_kernel(*refs, first_step=first_step, inner=inner, **sizes),
            in_specs=[vmem] * 7 + [anywhere],
            out_specs=vmem,
            out_shape=shape(tokens, 2 * count * inner * LANES),
            compiler_params=PARAMS,
            cost_estimate=work,
            name="conv",
        )(params, rows, skip_rows, rates, lag_rates, gated, turned, after)

    def combine(level, operands, outs):
        return pl.pallas_call(
            lambda *refs: combine_kernel(*refs, level=level, levels=levels, tokens=tokens, **sizes),
            in_specs=[anywhere if x is conv else vmem for x in operands],
            out_specs=[vmem] * len(outs),
            out_shape=outs,
            compiler_params=PARAMS,
            name="combine",
        )(*operands)

    conv = None
    states_shape = shape(2 * half_rows, LANES, dtype=BF16)
    tail_shape = shape(tail, LANES, dtype=BF16)
    slim_shape = shape(half_rows + tail, LANES, dtype=BF16)
    held_shape = shape(half_blocks, 2 * poles, LANES)
    got = swap(outgoing, 0)
    states, total, near = combine(
        0, [rates, message, got, local_sums(0)], [states_shape, shape(2 * poles, LANES), held_shape]
    )
    held = slim = None
    for level in range(1, levels):
        last = level == levels - 1
        if last and slim is not None:
            received = [swap(slim, level)]
        else:
            received = [swap(states, level)]
            if level == 1:
                carried = local_sums(1, total)
            received.append(swap(carried, level))
        operands = [rates, states, carried, *received]
        if level > 1:
            operands.append(held)
        if level == min(2, levels - 1):
            conv = convolve(0, steps - 1, near if held is None else held)
            operands.append(conv)
        if last:
            outs = [shape(half_blocks, 2 * poles, LANES, dtype=BF16), slim_shape]
            mine, outgoing = combine(level, [*operands, near], outs)
        else:
            outs = [states_shape, tail_shape, held_shape]
            if level == levels - 2:
                outs.append(slim_shape)
            states, carried, held, *more = combine(level, operands, outs)
            slim = more[0] if more else None
    got = swap(outgoing, 0)
    last_conv = convolve(steps - 1, 1, outgoing)
    merged = pl.pallas_call(
        lambda *refs: merge_kernel(*refs, poles=poles, length=tokens * parts),
        in_specs=[vmem] * 3 + [anywhere],
        out_specs=vmem,
        out_shape=shape(tail, LANES, dtype=BF16),
        compiler_params=PARAMS,
        name="merge",
    )(params, outgoing, got, last_conv)

    gathered = [merged]
    for mask in range(1, shards):
        gathered.append(lax.ppermute(merged, "ch", [(i, i ^ mask) for i in range(shards)]))

    main = pl.BlockSpec((tokens, inner * LANES), lambda i: (0, i))
    grad_query, grad_key, grad_value = pl.pallas_call(
        lambda *refs: output_kernel(*refs, **sizes),
        grid=(steps,),
        in_specs=[vmem] * 8,
        out_specs=[main] * 3,
        out_shape=[shape(tokens, width, dtype=BF16)] * 3,
        compiler_params=PARAMS,
        cost_estimate=work,
        name="outputs",
    )(rows, conv, last_conv, mine, got, key_input, value_input, cotangent)

    grad_residue, grad_lograte, grad_skip = pl.pallas_call(
        lambda *refs: assemble_kernel(*refs, poles=poles),
        in_specs=[vmem] * shards,
        out_specs=[vmem] * 3,
        out_shape=[shape(poles, all_groups), shape(poles, all_groups), shape(shards * blocks, LANES)],
        compiler_params=PARAMS,
        name="assemble",
    )(*gathered)
    return (grad_query, grad_key, grad_value, grad_residue.T, grad_lograte.T, grad_skip.reshape(-1))


def solution(mesh):
    placed = (P("ctx", "ch"), P("ctx", "ch"), P("ctx", "ch"), P("ctx", "ch"), P(), P(), P())
    return jax.shard_map(
        local,
        mesh=mesh,
        in_specs=placed,
        out_specs=(P("ctx", "ch"), P("ctx", "ch"), P("ctx", "ch"), P(), P(), P()),
        check_vma=False,
    )
```

```python
import math

import jax
import jax.numpy as jnp
from jax import lax
from jax.experimental import pallas as pl
from jax.experimental.pallas import tpu as pltpu
from jax.sharding import PartitionSpec as P

LANES = 128
SUB = 32
F32 = jnp.float32
BF16 = jnp.bfloat16
EXACT = lax.Precision.HIGHEST
VMEM_LIMIT = 40 * 1024 * 1024
GATES_LIMIT = 53900 * 1024
PARAMS = pltpu.CompilerParams(vmem_limit_bytes=VMEM_LIMIT)


def iota(shape, axis):
    return lax.broadcasted_iota(jnp.int32, shape, axis)


def over(value, size):
    return lax.shift_right_logical(value, size.bit_length() - 1)


def within(value, size):
    return lax.bitwise_and(value, size - 1)


def mxu(left, right):
    return jnp.dot(left, right, preferred_element_type=F32)


def mxu_t(left, right):
    return lax.dot_general(left, right, (((1,), (1,)), ((), ())), preferred_element_type=F32)


def exact_dot(left, right):
    return jnp.dot(left, right, precision=EXACT, preferred_element_type=F32)


def gate(left, right):
    return (left.astype(F32) * right.astype(F32)).astype(BF16)


def reversal(size):
    return jnp.where(iota((size, size), 0) + iota((size, size), 1) == size - 1, 1.0, 0.0).astype(BF16)


def split(value, pieces):
    parts = []
    for _ in range(pieces):
        parts.append(value.astype(BF16))
        value = value - parts[-1].astype(F32)
    return jnp.concatenate(parts, axis=0)


def join(stacked, rows):
    total = stacked[:rows].astype(F32)
    for start in range(rows, stacked.shape[0], rows):
        total = total + stacked[start : start + rows].astype(F32)
    return total


def flat_rows(table, poles):
    table = table.T
    groups = table.shape[0]
    per_row = LANES // poles
    spread = jnp.where(iota((poles, LANES), 0) == within(iota((poles, LANES), 1), poles), 1.0, 0.0)
    wide = exact_dot(table, spread)
    keep = within(iota((groups, LANES), 0), per_row) == over(iota((groups, LANES), 1), poles)
    wide = jnp.where(keep, wide, 0.0)
    return jnp.sum(wide.reshape(groups // per_row, per_row, LANES), axis=1)


def members(groups, first, span, width):
    return jnp.where(iota((groups, width), 0) == first + over(iota((groups, width), 1), span), 1.0, 0.0).astype(BF16)


def shard_start(groups):
    return pl.multiple_of(lax.axis_index("ch") * groups, LANES)


def diagonals(gated, turned, group):
    tokens = gated.shape[0]
    per_block = LANES // group
    lag_width = per_block * SUB
    subs = tokens // SUB
    lane_group = over(iota((SUB, LANES), 1), group)
    row, lane = iota((SUB, lag_width), 0), within(iota((SUB, lag_width), 1), SUB)
    near_side, no_wrap = row + lane <= SUB - 1, lane >= row
    found = [None] * subs + [jnp.zeros((SUB, lag_width), F32)]
    for k in range(subs):
        part = gated[k * SUB : (k + 1) * SUB]
        stack = jnp.concatenate(
            [jnp.where(lane_group == g, part, jnp.zeros_like(part)) for g in range(per_block)], axis=0
        )
        outer = mxu_t(turned[: (subs - k) * SUB], stack)
        for n in range(subs - k):
            far = subs - 1 - k - n
            piece = outer[n * SUB : (n + 1) * SUB]
            found[far] = piece if found[far] is None else found[far] + piece

    def rows():
        for far in range(subs):
            total = jnp.where(near_side, found[far], found[far + 1])
            straight = pltpu.roll(total, 0, 1, stride=1, stride_axis=0)
            wrapped = pltpu.roll(total, lag_width - SUB, 1, stride=1, stride_axis=0)
            yield jnp.sum(jnp.where(no_wrap, straight, wrapped), axis=0, keepdims=True)

    return rows


def gates_kernel(q_any, k_any, v_any, c_any, gated_ref, turned_ref, lags_ref, skip_ref, q_ref, k_ref, v_ref, c_ref, sems,
                 *, steps, group):
    tokens, width = q_ref.shape
    wide = width // steps
    sources = ((k_any, k_ref), (v_any, v_ref), (c_any, c_ref), (q_any, q_ref))
    cuts = [slice(step * wide, (step + 1) * wide) for step in range(steps)]
    copies = [
        [pltpu.make_async_copy(far.at[:, cut], near.at[:, cut], sems.at[n, step]) for n, (far, near) in enumerate(sources)]
        for step, cut in enumerate(cuts)
    ]
    for step in copies:
        for copy in step:
            copy.start()
    flip = reversal(tokens)
    for step, cut in enumerate(cuts):
        for copy in copies[step]:
            copy.wait()
        gated, dgate = gate(k_ref[:, cut], v_ref[:, cut]), gate(c_ref[:, cut], q_ref[:, cut])
        gated_ref[:, cut] = gated
        turned = mxu(flip, dgate).astype(BF16)
        turned_ref[:, cut] = turned
        skip = jnp.sum(gated.astype(F32) * dgate.astype(F32), axis=0, keepdims=True)
        lanes = [slice(j * LANES, (j + 1) * LANES) for j in range(wide // LANES)]
        found = [diagonals(gated[:, here], turned[:, here], group) for here in lanes]
        for j, here in enumerate(lanes):
            block = step * len(lanes) + j
            skip_ref[block : block + 1, :] = skip[:, here]
            for far, row in enumerate(found[j]()):
                lags_ref[block, far : far + 1, :] = row


def states_kernel(logs_ref, res_ref, gated_ref, turned_ref, send_ref, keep_ref, rows_ref, table_ref,
                  *, group, poles, inner):
    tokens, _ = gated_ref.shape
    per_block = LANES // group
    _, blocks, _ = rows_ref.shape
    half_blocks = blocks // 2
    groups = blocks * per_block
    wide = inner * LANES
    core = lax.rem(lax.axis_index("ctx"), 2)
    first = shard_start(groups)
    for n, ref in enumerate((logs_ref, res_ref)):
        table_ref[n] = ref[:, pl.ds(first, groups)]
    rows_ref[0] = jnp.exp(flat_rows(table_ref[0], poles))
    rows_ref[1] = flat_rows(table_ref[1], poles)

    back_pos = (tokens - 1 - iota((tokens, LANES), 0)).astype(F32)
    back_lane = (tokens - 1 - iota((1, tokens), 1)).astype(F32)
    wide_group = over(within(iota((poles, 2 * LANES), 1), LANES), group)
    lanes = [slice(j * LANES, (j + 1) * LANES) for j in range(inner)]

    for turn, msg_ref in enumerate((send_ref, keep_ref)):
        base = lax.rem(core + 1 + turn, 2) * half_blocks

        def body(step, carry, base=base, msg_ref=msg_ref):
            start = base + step * inner
            cut = pl.ds(pl.multiple_of(start * LANES, LANES), wide)
            gated, turned = gated_ref[:, cut], turned_ref[:, cut]
            tables = [jnp.exp(-rows_ref[0, pl.ds(start + j, 1), :] * back_pos).T for j in range(inner)]
            found = []
            for j in range(inner):
                both = jnp.concatenate([tables[j].astype(BF16), (tables[j] * back_lane).astype(BF16)], axis=0)
                pair = jnp.concatenate([gated[:, lanes[j]], turned[:, lanes[j]]], axis=1)
                found.append(mxu(both, pair))
            for j in range(inner):
                folded = []
                for part in range(2):
                    total = found[j][part * LANES : part * LANES + poles]
                    for g in range(1, per_block):
                        row = part * LANES + g * poles
                        total = jnp.where(wide_group == g, found[j][row : row + poles], total)
                    folded.append(total)
                out = [folded[0][:, :LANES], folded[0][:, LANES:], folded[1][:, :LANES], folded[1][:, LANES:]]
                row = pl.multiple_of((step * inner + j) * 4 * poles, 4 * poles)
                msg_ref[pl.ds(row, 4 * poles), :] = jnp.concatenate(out, axis=0).astype(BF16)
            return carry

        lax.fori_loop(0, half_blocks // inner, body, 0)


def lags_kernel(lag_rates_ref, lags_ref, sums_ref, *, group, poles, inner):
    blocks, subs, lag_width = lags_ref.shape
    per_block = LANES // group
    lag = (SUB - 1 - within(iota((poles, lag_width), 1), SUB)).astype(F32)
    spread = members(inner * per_block, 0, SUB, inner * lag_width)
    sums = []
    for step in range(blocks // inner):
        terms = []
        for j in range(inner):
            block = step * inner + j
            rate = lag_rates_ref[block]
            decay = jnp.exp(-rate * SUB)
            total = jnp.zeros((poles, lag_width), F32)
            weighted = total
            for far in reversed(range(subs)):
                row = lags_ref[block, far : far + 1, :]
                weighted = decay * weighted + far * row
                total = decay * total + row
            table = jnp.exp(-rate * lag)
            terms.append(
                split(jnp.concatenate([table * total, table * (lag * total + SUB * weighted)], axis=0), 2)
            )
        sums.append(mxu_t(jnp.concatenate(terms, axis=1), spread))
    sums_ref[...] = join(jnp.concatenate(sums, axis=1), 2 * poles)


def tables_kernel(params_ref, rates_ref, lag_rates_ref, *, group, poles, inner):
    blocks, _, lag_width = lag_rates_ref.shape
    per_block = LANES // group
    step_groups = inner * per_block
    lag_wide = inner * lag_width
    pieces = split(params_ref[0], 3)
    spread = jnp.concatenate(
        [members(step_groups, 0, SUB, lag_wide), members(step_groups, 0, group, inner * LANES)], axis=1
    )
    for step in range(blocks // inner):
        spreads = mxu(pieces[:, step * step_groups : (step + 1) * step_groups], spread)
        rates = jnp.exp(join(spreads, poles))
        for j in range(inner):
            here = step * inner + j
            lag_rates_ref[here] = rates[:, j * lag_width : (j + 1) * lag_width]
            rates_ref[here] = rates[:, lag_wide + j * LANES : lag_wide + (j + 1) * LANES]


def conv_kernel(params_ref, rows_ref, skip_ref, rates_ref, lag_rates_ref, gated_ref, turned_ref, _, conv_ref,
                *, first_step, group, poles, inner):
    tokens, _ = gated_ref.shape
    per_block = LANES // group
    blocks, _, _ = rates_ref.shape
    subs = tokens // SUB
    lag_width = per_block * SUB
    first = lax.axis_index("ch") * blocks
    lead = (1 + iota((SUB, LANES), 0)).astype(F32)
    wide_group = over(within(iota((SUB, 2 * LANES), 1), LANES), group)
    state_group = over(within(iota((poles, 2 * LANES), 1), LANES), group)
    causal = iota((SUB, lag_width), 0) >= within(iota((SUB, lag_width), 1), SUB)
    lag = (SUB - 1 - within(iota((poles, lag_width), 1), SUB)).astype(F32)
    groups = blocks * per_block
    pieces = split(params_ref[1], 3).astype(F32)
    spread = members(groups, 0, SUB, inner * lag_width)

    def body(step, carry):
        start = (step + first_step) * inner
        moved = pltpu.roll(pieces, groups - start * per_block, 1).astype(BF16)
        lag_res = join(mxu(moved, spread), poles)
        lefts, lead_tables, decays, pairs, gains = [], [], [], [], []
        for j in range(inner):
            here = start + j
            table = jnp.exp(-lag_rates_ref[here] * lag)
            taps = jnp.sum(lag_res[:, j * lag_width : (j + 1) * lag_width] * table, axis=0, keepdims=True)
            taps = jnp.broadcast_to(taps, (SUB, lag_width))
            taps = pltpu.roll(taps, lag_width - SUB + 1, 1, stride=1, stride_axis=0)
            taps = jnp.where(causal, taps, 0.0).astype(BF16)
            lefts.append(jnp.concatenate([taps, table.astype(BF16)], axis=0))
            rate = rows_ref[0, pl.ds(here, 1), :]
            res = rows_ref[1, pl.ds(here, 1), :]
            lead_tables.append((res * jnp.exp(-rate * lead)).astype(BF16))
            decay = jnp.exp(-rates_ref[here] * SUB)
            decays.append(jnp.concatenate([decay, decay], axis=1))
            cut = pl.ds(pl.multiple_of(here * LANES, LANES), LANES)
            pairs.append(jnp.concatenate([gated_ref[:, cut], turned_ref[:, cut]], axis=1))
            gain = skip_ref[pl.ds(first + here, 1), :]
            gains.append(jnp.concatenate([gain, gain], axis=1))
        states = [jnp.zeros((poles, 2 * LANES), F32)] * inner
        totals = [[] for _ in range(inner)]
        for k in range(subs):
            rows = slice(k * SUB, (k + 1) * SUB)
            found = []
            for j in range(inner):
                part = pairs[j][rows]
                stack = [jnp.where(wide_group == g, part, jnp.zeros_like(part)) for g in range(per_block)]
                found.append(mxu(lefts[j], jnp.concatenate(stack, axis=0)))
            for j in range(inner):
                total = found[j][:SUB] + gains[j] * pairs[j][rows].astype(F32)
                if k:
                    held = states[j].astype(BF16)
                    stack = [jnp.where(state_group == g, held, jnp.zeros_like(held)) for g in range(per_block)]
                    total = total + mxu(lead_tables[j], jnp.concatenate(stack, axis=0))
                totals[j].append(total)
            states = [decays[j] * states[j] + found[j][SUB:] for j in range(inner)]
        for j in range(inner):
            cut = pl.ds(pl.multiple_of(2 * (step * inner + j) * LANES, LANES), 2 * LANES)
            conv_ref[:, cut] = jnp.concatenate(totals[j], axis=0)
        return carry

    lax.fori_loop(0, conv_ref.shape[1] // (2 * inner * LANES), body, 0)


def combine_kernel(*refs, level, levels, group, poles, tokens):
    last = level == levels - 1
    refs = list(refs)
    rates_ref = refs.pop(0)
    all_blocks = rates_ref.shape[0]
    blocks = all_blocks // 2
    per_block = LANES // group
    groups = all_blocks * per_block
    rows = 2 * poles
    if level == 0:
        own_ref, got_ref, sums_ref, skip_ref, states_ref, near_ref = refs
    else:
        own_ref, got_ref = refs.pop(0), refs.pop(0)
        held_ref = refs.pop(0) if level > 1 else None
        if level == 1:
            refs.pop(0)
        if last:
            near_ref, mine_ref, out_ref = refs
        else:
            states_ref, new_held_ref = refs[:2]
            slim_ref = refs[2] if level == levels - 2 else None
    me = lax.axis_index("ctx")
    core = lax.rem(me, 2)
    is_right = lax.rem(lax.shift_right_logical(me, level), 2) == 1
    before = lax.rem(me, 2**level) - (core if level else 0)
    gap_left = (tokens * before).astype(F32)
    gap_right = (tokens * (2**level - 2 - before)).astype(F32)
    gap = jnp.where(is_right, gap_left, gap_right)
    span = float(tokens * 2**level)
    next_right = lax.rem(lax.shift_right_logical(me, level + 1), 2) == 1

    def quarters(ref, b):
        value = ref[2 * b * rows : 2 * (b + 1) * rows].astype(F32)
        return [value[n * poles : (n + 1) * poles] for n in range(4)]

    wide_terms = []
    for b in range(blocks):
        rate = rates_ref[core * blocks + b]
        own_f, own_b, own_fm, own_bm = quarters(own_ref, b)
        if last:
            got = got_ref[b * rows : (b + 1) * rows].astype(F32)
            got_f = got_b = got[:poles]
            got_fm = got_bm = got[poles:]
        else:
            got_f, got_b, got_fm, got_bm = quarters(got_ref, b)
        left_f = jnp.where(is_right, got_f, own_f)
        left_fm = jnp.where(is_right, got_fm, own_fm)
        right_b = jnp.where(is_right, own_b, got_b)
        right_bm = jnp.where(is_right, own_bm, got_bm)
        once = jnp.exp(-rate)
        cross_res = once * (right_b * left_f)
        cross_mom = once * (right_bm * left_f + right_b * (left_fm + left_f))
        wide_terms.append(split(jnp.concatenate([cross_res, cross_mom], axis=0), 2))
        if level == 0:
            near_ref[b] = jnp.concatenate([left_f, right_b], axis=0)
        else:
            carry = jnp.exp(-rate * gap) * jnp.where(is_right, left_f, right_b)
            zero = jnp.zeros_like(carry)
            hold = jnp.concatenate([jnp.where(is_right, carry, zero), jnp.where(is_right, zero, carry)], axis=0)
            if level > 1:
                hold = hold + held_ref[b]
            if last:
                step = jnp.exp(-rate * tokens)
                near = near_ref[b]
                first_core = jnp.concatenate([hold[:poles], near[poles:] + step * hold[poles:]], axis=0)
                second_core = jnp.concatenate([near[:poles] + step * hold[:poles], hold[poles:]], axis=0)
                mine_ref[b] = jnp.where(core > 0, second_core, first_core).astype(BF16)
                out_ref[b * rows : (b + 1) * rows, :] = jnp.where(core > 0, first_core, second_core).astype(BF16)
            else:
                new_held_ref[b] = hold
        if not last:
            right_f = jnp.where(is_right, own_f, got_f)
            right_fm = jnp.where(is_right, own_fm, got_fm)
            left_b = jnp.where(is_right, got_b, own_b)
            left_bm = jnp.where(is_right, got_bm, own_bm)
            decay = jnp.exp(-rate * span)
            new_f, new_b = decay * left_f + right_f, left_b + decay * right_b
            new_fm = decay * (left_fm + span * left_f) + right_fm
            new_bm = left_bm + decay * (right_bm + span * right_b)
            here = slice(b * rows, (b + 1) * rows)
            new = jnp.concatenate([new_f, new_b, new_fm, new_bm], axis=0).astype(BF16)
            states_ref[2 * b * rows : 2 * (b + 1) * rows, :] = new
            if level == levels - 2 and level:
                chosen = [jnp.where(next_right, new_b, new_f), jnp.where(next_right, new_bm, new_fm)]
                slim_ref[here, :] = jnp.concatenate(chosen, axis=0).astype(BF16)
    cross = join(mxu_t(jnp.concatenate(wide_terms, axis=1), members(groups, 0, group, blocks * LANES)), rows)
    cross = jnp.where(core > 0, pltpu.roll(cross, groups // 2, 1), cross)
    tail = blocks * rows
    if level == 0:
        rests = jnp.concatenate([cross + sums_ref[...], skip_ref[...]], axis=0).astype(BF16)
    else:
        got_start = tail if last else 2 * tail
        both = own_ref[2 * tail :, :].astype(F32) + got_ref[got_start:, :].astype(F32)
        rests = jnp.concatenate([both[:rows] + cross, both[rows:]], axis=0).astype(BF16)
    if last:
        out_ref[tail:, :] = rests
        return
    states_ref[2 * tail :, :] = rests
    if level and slim_ref is not None:
        slim_ref[tail:, :] = rests


def merge_kernel(params_ref, own_ref, got_ref, _, out_ref, *, poles, length):
    groups = out_ref.shape[1]
    start = own_ref.shape[0] - out_ref.shape[0]
    both = own_ref[start:, :].astype(F32) + got_ref[start:, :].astype(F32)
    factor = -jnp.exp(params_ref[0]) * params_ref[1]
    scaled = [
        both[:poles] / length,
        factor * both[poles : 2 * poles] / math.sqrt(length),
        both[2 * poles :] / math.sqrt(length),
    ]
    out_ref[...] = jnp.concatenate(scaled, axis=0).astype(BF16)


def output_kernel(rows_ref, conv_ref, last_ref, mine_ref, got_ref, k_ref, v_ref, c_ref, gq_ref, gk_ref, gv_ref,
                  *, group, poles):
    tokens, width = gq_ref.shape
    per_block = LANES // group
    step = pl.program_id(0)
    steps = pl.num_programs(0)
    inner = width // LANES
    half_blocks = mine_ref.shape[0]
    core = lax.rem(lax.axis_index("ctx"), 2)
    flip = reversal(tokens)
    ahead = (1 + iota((tokens, LANES), 0)).astype(F32)
    state_group = over(within(iota((poles, 2 * LANES), 1), LANES), group)
    start = step * inner
    is_mine = over(start, half_blocks) == core
    cut = pl.ds(pl.multiple_of(start * LANES, LANES), width)

    def emit(conv_ref, base):
        totals = []
        for j in range(inner):
            here = start + j
            rate = rows_ref[0, pl.ds(here, 1), :]
            res = rows_ref[1, pl.ds(here, 1), :]
            table = (res * jnp.exp(-rate * ahead)).astype(BF16)
            place = within(here, half_blocks)
            held = jnp.where(
                is_mine, mine_ref[place], got_ref[pl.ds(pl.multiple_of(place * 2 * poles, 2 * poles), 2 * poles), :]
            )
            states = jnp.concatenate([held[:poles], held[poles:]], axis=1)
            stack = jnp.concatenate(
                [jnp.where(state_group == g, states, jnp.zeros_like(states)) for g in range(per_block)], axis=0
            )
            both = pl.ds(pl.multiple_of(2 * (here - base) * LANES, LANES), 2 * LANES)
            totals.append((conv_ref[:, both] + mxu(table, stack)).astype(BF16))
        hidden = jnp.concatenate([t[:, :LANES] for t in totals], axis=1)
        flow = mxu(flip, jnp.concatenate([t[:, LANES:] for t in totals], axis=1))
        gq_ref[...] = (c_ref[:, cut].astype(F32) * hidden.astype(F32)).astype(BF16)
        gk_ref[...] = (flow * v_ref[:, cut].astype(F32)).astype(BF16)
        gv_ref[...] = (flow * k_ref[:, cut].astype(F32)).astype(BF16)

    @pl.when(step < steps - 1)
    def _():
        emit(conv_ref, 0)

    @pl.when(step == steps - 1)
    def _():
        emit(last_ref, (steps - 1) * inner)


def assemble_kernel(*refs, poles):
    *slots, res_ref, log_ref, skip_ref = refs
    me = lax.axis_index("ch")
    groups = slots[0].shape[1]
    rows = slots[0].shape[0] - 2 * poles
    for mask, slot in enumerate(slots):
        source = lax.bitwise_xor(me, mask)
        value = slot[...].astype(F32)
        cut = pl.ds(pl.multiple_of(source * groups, LANES), groups)
        res_ref[:, cut] = value[:poles]
        log_ref[:, cut] = value[poles : 2 * poles]
        skip_ref[pl.ds(pl.multiple_of(source * rows, 8), rows), :] = value[2 * poles :]


def local(queries, key_input, value_input, cotangent, residues, log_rates, skip_gain):
    tokens, width = queries.shape
    parts = lax.axis_size("ctx")
    shards = lax.axis_size("ch")
    levels = parts.bit_length() - 1
    all_groups, poles = residues.shape
    groups = all_groups // shards
    group = width // groups
    blocks = width // LANES
    inner = 4
    steps = blocks // inner
    half_blocks = blocks // 2
    lag_width = LANES // group * SUB
    sizes = dict(group=group, poles=poles)
    half_rows, tail = half_blocks * 2 * poles, 2 * poles + blocks

    vmem = pl.BlockSpec(memory_space=pltpu.VMEM)
    anywhere = pl.BlockSpec(memory_space=pl.ANY)
    log_rates, residues = log_rates.T, residues.T
    def shape(*dims, dtype=F32):
        return jax.ShapeDtypeStruct(dims, dtype)

    def swap(value, level):
        return lax.ppermute(value, "ctx", [(i, i ^ (1 << level)) for i in range(parts)])

    operand = shape(tokens, width, dtype=BF16)
    gated, turned, lags, skips = pl.pallas_call(
        lambda *refs: gates_kernel(*refs, steps=steps, group=group),
        in_specs=[anywhere] * 4,
        out_specs=[vmem] * 4,
        out_shape=[operand, operand, shape(blocks, tokens // SUB, lag_width), shape(blocks, LANES)],
        scratch_shapes=[pltpu.VMEM((tokens, width), BF16)] * 4 + [pltpu.SemaphoreType.DMA((4, steps))],
        compiler_params=pltpu.CompilerParams(vmem_limit_bytes=GATES_LIMIT),
        name="gates",
    )(queries, key_input, value_input, cotangent)
    outgoing, message, rows, params = pl.pallas_call(
        lambda *refs: states_kernel(*refs, inner=inner, **sizes),
        in_specs=[vmem] * 4,
        out_specs=[vmem] * 4,
        out_shape=[
            shape(2 * half_rows, LANES, dtype=BF16),
            shape(2 * half_rows, LANES, dtype=BF16),
            shape(2, blocks, LANES),
            shape(2, poles, groups),
        ],
        compiler_params=PARAMS,
        name="states",
    )(log_rates, residues, gated, turned)

    rates, lag_rates = pl.pallas_call(
        lambda *refs: tables_kernel(*refs, inner=inner, **sizes),
        in_specs=[vmem],
        out_specs=[vmem] * 2,
        out_shape=[shape(blocks, poles, LANES), shape(blocks, poles, lag_width)],
        compiler_params=PARAMS,
        cost_estimate=pl.CostEstimate(flops=10**9, bytes_accessed=10**6, transcendentals=10**5),
        name="tables",
    )(params)

    work = pl.CostEstimate(
        flops=16 * tokens * tokens * width, bytes_accessed=12 * tokens * width, transcendentals=tokens * width
    )

    sums = pl.pallas_call(
        lambda *refs: lags_kernel(*refs, inner=inner, **sizes),
        in_specs=[vmem] * 2,
        out_specs=vmem,
        out_shape=shape(2 * poles, LANES),
        compiler_params=PARAMS,
        cost_estimate=work,
        name="lags",
    )(lag_rates, lags)

    def convolve(first_step, count, after):
        skip_rows = skip_gain.reshape(-1, LANES)
        return pl.pallas_call(
            lambda *refs: conv_kernel(*refs, first_step=first_step, inner=inner, **sizes),
            in_specs=[vmem] * 7 + [anywhere],
            out_specs=vmem,
            out_shape=shape(tokens, 2 * count * inner * LANES),
            compiler_params=PARAMS,
            cost_estimate=work,
            name="conv",
        )(params, rows, skip_rows, rates, lag_rates, gated, turned, after)

    def combine(level, operands, outs):
        return pl.pallas_call(
            lambda *refs: combine_kernel(*refs, level=level, levels=levels, tokens=tokens, **sizes),
            in_specs=[anywhere if x is conv else vmem for x in operands],
            out_specs=[vmem] * len(outs),
            out_shape=outs,
            compiler_params=PARAMS,
            name="combine",
        )(*operands)

    conv = None
    states_shape = shape(2 * half_rows + tail, LANES, dtype=BF16)
    slim_shape = shape(half_rows + tail, LANES, dtype=BF16)
    held_shape = shape(half_blocks, 2 * poles, LANES)
    got = swap(outgoing, 0)
    states, near = combine(0, [rates, message, got, sums, skips], [states_shape, held_shape])
    held, outgoing = None, states
    for level in range(1, levels):
        last = level == levels - 1
        operands = [rates, states, swap(outgoing, level)]
        if level > 1:
            operands.append(held)
        else:
            conv = convolve(0, steps - 1, near)
            operands.append(conv)
        if last:
            outs = [shape(half_blocks, 2 * poles, LANES, dtype=BF16), slim_shape]
            mine, outgoing = combine(level, [*operands, near], outs)
        else:
            outs = [states_shape, held_shape]
            if level == levels - 2:
                outs.append(slim_shape)
            states, held, *slim = combine(level, operands, outs)
            outgoing = slim[0] if slim else states
    got = swap(outgoing, 0)
    last_conv = convolve(steps - 1, 1, outgoing)
    merged = pl.pallas_call(
        lambda *refs: merge_kernel(*refs, poles=poles, length=tokens * parts),
        in_specs=[vmem] * 3 + [anywhere],
        out_specs=vmem,
        out_shape=shape(tail, LANES, dtype=BF16),
        compiler_params=PARAMS,
        name="merge",
    )(params, outgoing, got, last_conv)

    gathered = [merged]
    for mask in range(1, shards):
        gathered.append(lax.ppermute(merged, "ch", [(i, i ^ mask) for i in range(shards)]))

    main = pl.BlockSpec((tokens, inner * LANES), lambda i: (0, i))
    grad_query, grad_key, grad_value = pl.pallas_call(
        lambda *refs: output_kernel(*refs, **sizes),
        grid=(steps,),
        in_specs=[vmem] * 8,
        out_specs=[main] * 3,
        out_shape=[shape(tokens, width, dtype=BF16)] * 3,
        compiler_params=PARAMS,
        cost_estimate=work,
        name="outputs",
    )(rows, conv, last_conv, mine, got, key_input, value_input, cotangent)

    grad_residue, grad_lograte, grad_skip = pl.pallas_call(
        lambda *refs: assemble_kernel(*refs, poles=poles),
        in_specs=[vmem] * shards,
        out_specs=[vmem] * 3,
        out_shape=[shape(poles, all_groups), shape(poles, all_groups), shape(shards * blocks, LANES)],
        compiler_params=PARAMS,
        name="assemble",
    )(*gathered)
    return (grad_query, grad_key, grad_value, grad_residue.T, grad_lograte.T, grad_skip.reshape(-1))


def solution(mesh):
    placed = (P("ctx", "ch"), P("ctx", "ch"), P("ctx", "ch"), P("ctx", "ch"), P(), P(), P())
    return jax.shard_map(
        local,
        mesh=mesh,
        in_specs=placed,
        out_specs=(P("ctx", "ch"), P("ctx", "ch"), P("ctx", "ch"), P(), P(), P()),
        check_vma=False,
    )
```

```python
import math

import jax
import jax.numpy as jnp
from jax import lax
from jax.experimental import pallas as pl
from jax.experimental.pallas import tpu as pltpu
from jax.sharding import PartitionSpec as P

LANES = 128
SUB = 32
F32 = jnp.float32
BF16 = jnp.bfloat16
EXACT = lax.Precision.HIGHEST
VMEM_LIMIT = 40 * 1024 * 1024
GATES_LIMIT = 53200 * 1024
PARAMS = pltpu.CompilerParams(vmem_limit_bytes=VMEM_LIMIT)


def iota(shape, axis):
    return lax.broadcasted_iota(jnp.int32, shape, axis)


def over(value, size):
    return lax.shift_right_logical(value, size.bit_length() - 1)


def within(value, size):
    return lax.bitwise_and(value, size - 1)


def mxu(left, right):
    return jnp.dot(left, right, preferred_element_type=F32)


def mxu_t(left, right):
    return lax.dot_general(left, right, (((1,), (1,)), ((), ())), preferred_element_type=F32)


def exact_dot(left, right):
    return jnp.dot(left, right, precision=EXACT, preferred_element_type=F32)


def gate(left, right):
    return (left.astype(F32) * right.astype(F32)).astype(BF16)


def reversal(size):
    return jnp.where(iota((size, size), 0) + iota((size, size), 1) == size - 1, 1.0, 0.0).astype(BF16)


def split(value, pieces):
    parts = []
    for _ in range(pieces):
        parts.append(value.astype(BF16))
        value = value - parts[-1].astype(F32)
    return jnp.concatenate(parts, axis=0)


def join(stacked, rows):
    total = stacked[:rows].astype(F32)
    for start in range(rows, stacked.shape[0], rows):
        total = total + stacked[start : start + rows].astype(F32)
    return total


def flat_rows(table, poles):
    table = table.T
    groups = table.shape[0]
    per_row = LANES // poles
    spread = jnp.where(iota((poles, LANES), 0) == within(iota((poles, LANES), 1), poles), 1.0, 0.0)
    wide = exact_dot(table, spread)
    keep = within(iota((groups, LANES), 0), per_row) == over(iota((groups, LANES), 1), poles)
    wide = jnp.where(keep, wide, 0.0)
    return jnp.sum(wide.reshape(groups // per_row, per_row, LANES), axis=1)


def members(groups, first, span, width):
    return jnp.where(iota((groups, width), 0) == first + over(iota((groups, width), 1), span), 1.0, 0.0).astype(BF16)


def shard_start(groups):
    return pl.multiple_of(lax.axis_index("ch") * groups, LANES)


def column_copies(sources, sems, half, half_steps, wide):
    found = []
    for step in range(half_steps):
        near_cut = pl.ds(step * wide, wide)
        cut = pl.ds(pl.multiple_of((half * half_steps + step) * wide, LANES), wide)
        found.append(
            [
                pltpu.make_async_copy(far.at[:, cut], near.at[:, near_cut], sems.at[n, step])
                for n, (far, near) in enumerate(sources)
            ]
        )
    return found


def gate_step(copies, near, step, start, wide, flip, gated_ref, dgate_ref, turned_ref):
    for copy in copies[step]:
        copy.wait()
    near_cut = slice(step * wide, (step + 1) * wide)
    q_ref, k_ref, v_ref, c_ref = near
    cut = pl.ds(pl.multiple_of(start * LANES, LANES), wide)
    dgate = gate(c_ref[:, near_cut], q_ref[:, near_cut])
    gated = gate(k_ref[:, near_cut], v_ref[:, near_cut])
    turned = mxu(flip, dgate).astype(BF16)
    gated_ref[:, cut], dgate_ref[:, cut], turned_ref[:, cut] = gated, dgate, turned
    return gated, turned


def gates_kernel(q_any, k_any, v_any, c_any, gated_ref, dgate_ref, turned_ref, q_ref, k_ref, v_ref, c_ref, sems, *, inner):
    tokens, half_width = q_ref.shape
    wide = inner * LANES
    half_steps = half_width // wide
    half = 1 - lax.rem(lax.axis_index("ctx"), 2)
    near = (q_ref, k_ref, v_ref, c_ref)
    copies = column_copies(tuple(zip((q_any, k_any, v_any, c_any), near)), sems, half, half_steps, wide)
    for step in copies:
        for copy in step:
            copy.start()
    flip = reversal(tokens)
    for step in range(half_steps):
        start = (half * half_steps + step) * inner
        gate_step(copies, near, step, start, wide, flip, gated_ref, dgate_ref, turned_ref)


def states_kernel(logs_ref, res_ref, q_any, k_any, v_any, c_any, gated_in, _, turned_in, send_ref, keep_ref, gated_ref,
                  dgate_ref, turned_ref, rows_ref, table_ref, q_ref, k_ref, v_ref, c_ref, sems, *, group, poles, inner):
    tokens, _ = gated_ref.shape
    per_block = LANES // group
    _, blocks, _ = rows_ref.shape
    half_blocks = blocks // 2
    groups = blocks * per_block
    wide = inner * LANES
    core = lax.rem(lax.axis_index("ctx"), 2)
    half_steps = half_blocks // inner
    near = (q_ref, k_ref, v_ref, c_ref)
    copies = column_copies(tuple(zip((q_any, k_any, v_any, c_any), near)), sems, core, half_steps, wide)
    for step in copies:
        for copy in step:
            copy.start()
    first = shard_start(groups)
    for n, ref in enumerate((logs_ref, res_ref)):
        table_ref[n] = ref[:, pl.ds(first, groups)]
    rows_ref[0] = jnp.exp(flat_rows(table_ref[0], poles))
    rows_ref[1] = flat_rows(table_ref[1], poles)

    flip = reversal(tokens)
    back_pos = (tokens - 1 - iota((tokens, LANES), 0)).astype(F32)
    back_lane = (tokens - 1 - iota((1, tokens), 1)).astype(F32)
    wide_group = over(within(iota((poles, 2 * LANES), 1), LANES), group)
    lanes = [slice(j * LANES, (j + 1) * LANES) for j in range(inner)]

    for turn, msg_ref in enumerate((send_ref, keep_ref)):
        base = lax.rem(core + 1 + turn, 2) * half_blocks

        for step in range(half_steps):
            start = base + step * inner
            if turn == 0:
                cut = pl.ds(pl.multiple_of(start * LANES, LANES), wide)
                gated, turned = gated_in[:, cut], turned_in[:, cut]
            else:
                gated, turned = gate_step(copies, near, step, start, wide, flip, gated_ref, dgate_ref, turned_ref)
            tables = [jnp.exp(-rows_ref[0, pl.ds(start + j, 1), :] * back_pos).T for j in range(inner)]
            found = []
            for j in range(inner):
                both = jnp.concatenate([tables[j].astype(BF16), (tables[j] * back_lane).astype(BF16)], axis=0)
                pair = jnp.concatenate([gated[:, lanes[j]], turned[:, lanes[j]]], axis=1)
                found.append(mxu(both, pair))
            for j in range(inner):
                folded = []
                for part in range(2):
                    total = found[j][part * LANES : part * LANES + poles]
                    for g in range(1, per_block):
                        row = part * LANES + g * poles
                        total = jnp.where(wide_group == g, found[j][row : row + poles], total)
                    folded.append(total)
                out = [folded[0][:, :LANES], folded[0][:, LANES:], folded[1][:, :LANES], folded[1][:, LANES:]]
                row = (step * inner + j) * 4 * poles
                msg_ref[row : row + 4 * poles, :] = jnp.concatenate(out, axis=0).astype(BF16)


def lags_kernel(lag_rates_ref, gated_ref, dgate_ref, turned_ref, *rest, second, group, poles, inner):
    if second:
        first_ref, out_ref, skip_ref = rest
    else:
        (out_ref,) = rest
    tokens, _ = gated_ref.shape
    per_block = LANES // group
    blocks, _, lag_width = lag_rates_ref.shape
    subs = tokens // SUB
    step_groups = inner * per_block
    lane_group = over(iota((SUB, LANES), 1), group)
    row, lane = iota((SUB, lag_width), 0), within(iota((SUB, lag_width), 1), SUB)
    near_side, no_wrap = row + lane <= SUB - 1, lane >= row
    lag = (SUB - 1 - within(iota((poles, lag_width), 1), SUB)).astype(F32)
    spread = members(step_groups, 0, SUB, inner * lag_width)
    steps = blocks // inner
    sums = []
    for step in range(1, steps) if second else range(1):
        outers = []
        for j in range(inner):
            lanes = slice((step * inner + j) * LANES, (step * inner + j + 1) * LANES)
            found = [None] * subs
            for k in range(subs):
                part = gated_ref[k * SUB : (k + 1) * SUB, lanes]
                stack = jnp.concatenate(
                    [jnp.where(lane_group == g, part, jnp.zeros_like(part)) for g in range(per_block)], axis=0
                )
                outer = mxu_t(turned_ref[: (subs - k) * SUB, lanes], stack)
                for n in range(subs - k):
                    far = subs - 1 - k - n
                    piece = outer[n * SUB : (n + 1) * SUB]
                    found[far] = piece if found[far] is None else found[far] + piece
            outers.append(found)
        terms = []
        for j in range(inner):
            found = outers[j] + [jnp.zeros((SUB, lag_width), F32)]
            lags = []
            for far in range(subs):
                total = jnp.where(near_side, found[far], found[far + 1])
                straight = pltpu.roll(total, 0, 1, stride=1, stride_axis=0)
                wrapped = pltpu.roll(total, lag_width - SUB, 1, stride=1, stride_axis=0)
                lags.append(jnp.sum(jnp.where(no_wrap, straight, wrapped), axis=0, keepdims=True))
            rate = lag_rates_ref[step * inner + j]
            decay = jnp.exp(-rate * SUB)
            total = jnp.zeros((poles, lag_width), F32)
            weighted = total
            for far in reversed(range(subs)):
                weighted = decay * weighted + far * lags[far]
                total = decay * total + lags[far]
            table = jnp.exp(-rate * lag)
            terms.append(
                split(jnp.concatenate([table * total, table * (lag * total + SUB * weighted)], axis=0), 2)
            )
        sums.append(mxu_t(jnp.concatenate(terms, axis=1), spread))
    sums = jnp.concatenate(sums, axis=1)
    zeros = jnp.zeros((sums.shape[0], blocks * per_block - sums.shape[1]), F32)
    sums = jnp.concatenate([zeros, sums] if second else [sums, zeros], axis=1)
    sums = join(sums, 2 * poles)
    if not second:
        out_ref[...] = sums
        return
    for b in range(blocks):
        lanes = slice(b * LANES, (b + 1) * LANES)
        product = gated_ref[:, lanes].astype(F32) * dgate_ref[:, lanes].astype(F32)
        skip_ref[b : b + 1, :] = jnp.sum(product, axis=0, keepdims=True)
    out_ref[: 2 * poles, :] = (first_ref[...] + sums).astype(BF16)
    out_ref[2 * poles :, :] = skip_ref[...].astype(BF16)


def tables_kernel(params_ref, rates_ref, lag_rates_ref, *, group, poles, inner):
    blocks, _, lag_width = lag_rates_ref.shape
    per_block = LANES // group
    step_groups = inner * per_block
    lag_wide = inner * lag_width
    pieces = split(params_ref[0], 3)
    spread = jnp.concatenate(
        [members(step_groups, 0, SUB, lag_wide), members(step_groups, 0, group, inner * LANES)], axis=1
    )
    for step in range(blocks // inner):
        spreads = mxu(pieces[:, step * step_groups : (step + 1) * step_groups], spread)
        rates = jnp.exp(join(spreads, poles))
        for j in range(inner):
            here = step * inner + j
            lag_rates_ref[here] = rates[:, j * lag_width : (j + 1) * lag_width]
            rates_ref[here] = rates[:, lag_wide + j * LANES : lag_wide + (j + 1) * LANES]


def conv_kernel(params_ref, rows_ref, skip_ref, rates_ref, lag_rates_ref, gated_ref, turned_ref, _, conv_ref,
                *, first_step, group, poles, inner):
    tokens, _ = gated_ref.shape
    per_block = LANES // group
    blocks, _, _ = rates_ref.shape
    subs = tokens // SUB
    lag_width = per_block * SUB
    first = lax.axis_index("ch") * blocks
    lead = (1 + iota((SUB, LANES), 0)).astype(F32)
    wide_group = over(within(iota((SUB, 2 * LANES), 1), LANES), group)
    state_group = over(within(iota((poles, 2 * LANES), 1), LANES), group)
    causal = iota((SUB, lag_width), 0) >= within(iota((SUB, lag_width), 1), SUB)
    lag = (SUB - 1 - within(iota((poles, lag_width), 1), SUB)).astype(F32)
    groups = blocks * per_block
    pieces = split(params_ref[1], 3).astype(F32)
    spread = members(groups, 0, SUB, inner * lag_width)

    def body(step, carry):
        start = (step + first_step) * inner
        moved = pltpu.roll(pieces, groups - start * per_block, 1).astype(BF16)
        lag_res = join(mxu(moved, spread), poles)
        lefts, lead_tables, decays, pairs, gains = [], [], [], [], []
        for j in range(inner):
            here = start + j
            table = jnp.exp(-lag_rates_ref[here] * lag)
            taps = jnp.sum(lag_res[:, j * lag_width : (j + 1) * lag_width] * table, axis=0, keepdims=True)
            taps = jnp.broadcast_to(taps, (SUB, lag_width))
            taps = pltpu.roll(taps, lag_width - SUB + 1, 1, stride=1, stride_axis=0)
            taps = jnp.where(causal, taps, 0.0).astype(BF16)
            lefts.append(jnp.concatenate([taps, table.astype(BF16)], axis=0))
            rate = rows_ref[0, pl.ds(here, 1), :]
            res = rows_ref[1, pl.ds(here, 1), :]
            lead_tables.append((res * jnp.exp(-rate * lead)).astype(BF16))
            decay = jnp.exp(-rates_ref[here] * SUB)
            decays.append(jnp.concatenate([decay, decay], axis=1))
            cut = pl.ds(pl.multiple_of(here * LANES, LANES), LANES)
            pairs.append(jnp.concatenate([gated_ref[:, cut], turned_ref[:, cut]], axis=1))
            gain = skip_ref[pl.ds(first + here, 1), :]
            gains.append(jnp.concatenate([gain, gain], axis=1))
        states = [jnp.zeros((poles, 2 * LANES), F32)] * inner
        totals = [[] for _ in range(inner)]
        for k in range(subs):
            rows = slice(k * SUB, (k + 1) * SUB)
            found = []
            for j in range(inner):
                part = pairs[j][rows]
                stack = [jnp.where(wide_group == g, part, jnp.zeros_like(part)) for g in range(per_block)]
                found.append(mxu(lefts[j], jnp.concatenate(stack, axis=0)))
            for j in range(inner):
                total = found[j][:SUB] + gains[j] * pairs[j][rows].astype(F32)
                if k:
                    held = states[j].astype(BF16)
                    stack = [jnp.where(state_group == g, held, jnp.zeros_like(held)) for g in range(per_block)]
                    total = total + mxu(lead_tables[j], jnp.concatenate(stack, axis=0))
                totals[j].append(total)
            states = [decays[j] * states[j] + found[j][SUB:] for j in range(inner)]
        for j in range(inner):
            cut = pl.ds(pl.multiple_of(2 * (step * inner + j) * LANES, LANES), 2 * LANES)
            conv_ref[:, cut] = jnp.concatenate(totals[j], axis=0)
        return carry

    lax.fori_loop(0, conv_ref.shape[1] // (2 * inner * LANES), body, 0)


def combine_kernel(*refs, level, levels, group, poles, tokens):
    last = level == levels - 1
    refs = list(refs)
    rates_ref = refs.pop(0)
    all_blocks = rates_ref.shape[0]
    blocks = all_blocks // 2
    per_block = LANES // group
    groups = all_blocks * per_block
    rows = 2 * poles
    if level == 0:
        own_ref, got_ref, sums_ref, states_ref, total_ref, near_ref = refs
    else:
        own_ref, own_tail_ref, got_ref = refs.pop(0), refs.pop(0), refs.pop(0)
        got_tail_ref = None if last else refs.pop(0)
        held_ref = refs.pop(0) if level > 1 else None
        if level == min(2, levels - 1):
            refs.pop(0)
        if last:
            near_ref, mine_ref, out_ref = refs
        else:
            states_ref, tail_ref, new_held_ref = refs[:3]
            slim_ref = refs[3] if level == levels - 2 else None
    me = lax.axis_index("ctx")
    core = lax.rem(me, 2)
    is_right = lax.rem(lax.shift_right_logical(me, level), 2) == 1
    before = lax.rem(me, 2**level) - (core if level else 0)
    gap_left = (tokens * before).astype(F32)
    gap_right = (tokens * (2**level - 2 - before)).astype(F32)
    gap = jnp.where(is_right, gap_left, gap_right)
    span = float(tokens * 2**level)
    next_right = lax.rem(lax.shift_right_logical(me, level + 1), 2) == 1

    def quarters(ref, b):
        value = ref[2 * b * rows : 2 * (b + 1) * rows].astype(F32)
        return [value[n * poles : (n + 1) * poles] for n in range(4)]

    wide_terms = []
    for b in range(blocks):
        rate = rates_ref[core * blocks + b]
        own_f, own_b, own_fm, own_bm = quarters(own_ref, b)
        if last:
            got = got_ref[b * rows : (b + 1) * rows].astype(F32)
            got_f = got_b = got[:poles]
            got_fm = got_bm = got[poles:]
        else:
            got_f, got_b, got_fm, got_bm = quarters(got_ref, b)
        left_f = jnp.where(is_right, got_f, own_f)
        left_fm = jnp.where(is_right, got_fm, own_fm)
        right_b = jnp.where(is_right, own_b, got_b)
        right_bm = jnp.where(is_right, own_bm, got_bm)
        once = jnp.exp(-rate)
        cross_res = once * (right_b * left_f)
        cross_mom = once * (right_bm * left_f + right_b * (left_fm + left_f))
        wide_terms.append(split(jnp.concatenate([cross_res, cross_mom], axis=0), 2))
        if level == 0:
            near_ref[b] = jnp.concatenate([left_f, right_b], axis=0)
        else:
            carry = jnp.exp(-rate * gap) * jnp.where(is_right, left_f, right_b)
            zero = jnp.zeros_like(carry)
            hold = jnp.concatenate([jnp.where(is_right, carry, zero), jnp.where(is_right, zero, carry)], axis=0)
            if level > 1:
                hold = hold + held_ref[b]
            if last:
                step = jnp.exp(-rate * tokens)
                near = near_ref[b]
                first_core = jnp.concatenate([hold[:poles], near[poles:] + step * hold[poles:]], axis=0)
                second_core = jnp.concatenate([near[:poles] + step * hold[:poles], hold[poles:]], axis=0)
                mine_ref[b] = jnp.where(core > 0, second_core, first_core).astype(BF16)
                out_ref[b * rows : (b + 1) * rows, :] = jnp.where(core > 0, first_core, second_core).astype(BF16)
            else:
                new_held_ref[b] = hold
        if not last:
            right_f = jnp.where(is_right, own_f, got_f)
            right_fm = jnp.where(is_right, own_fm, got_fm)
            left_b = jnp.where(is_right, got_b, own_b)
            left_bm = jnp.where(is_right, got_bm, own_bm)
            decay = jnp.exp(-rate * span)
            new_f, new_b = decay * left_f + right_f, left_b + decay * right_b
            new_fm = decay * (left_fm + span * left_f) + right_fm
            new_bm = left_bm + decay * (right_bm + span * right_b)
            here = slice(b * rows, (b + 1) * rows)
            new = jnp.concatenate([new_f, new_b, new_fm, new_bm], axis=0).astype(BF16)
            states_ref[2 * b * rows : 2 * (b + 1) * rows, :] = new
            if level == levels - 2 and level:
                chosen = [jnp.where(next_right, new_b, new_f), jnp.where(next_right, new_bm, new_fm)]
                slim_ref[here, :] = jnp.concatenate(chosen, axis=0).astype(BF16)
    cross = join(mxu_t(jnp.concatenate(wide_terms, axis=1), members(groups, 0, group, blocks * LANES)), rows)
    cross = jnp.where(core > 0, pltpu.roll(cross, groups // 2, 1), cross)
    tail = blocks * rows
    if level == 0:
        total_ref[...] = cross + sums_ref[...]
        return
    got_tail = got_ref[tail:, :] if last else got_tail_ref[...]
    both = own_tail_ref[...].astype(F32) + got_tail.astype(F32)
    rests = jnp.concatenate([both[:rows] + cross, both[rows:]], axis=0).astype(BF16)
    if last:
        out_ref[tail:, :] = rests
    else:
        tail_ref[...] = rests
        if slim_ref is not None:
            slim_ref[tail:, :] = rests


def merge_kernel(params_ref, own_ref, got_ref, _, out_ref, *, poles, length):
    groups = out_ref.shape[1]
    start = own_ref.shape[0] - out_ref.shape[0]
    both = own_ref[start:, :].astype(F32) + got_ref[start:, :].astype(F32)
    factor = -jnp.exp(params_ref[0]) * params_ref[1]
    scaled = [
        both[:poles] / length,
        factor * both[poles : 2 * poles] / math.sqrt(length),
        both[2 * poles :] / math.sqrt(length),
    ]
    out_ref[...] = jnp.concatenate(scaled, axis=0).astype(BF16)


def output_kernel(rows_ref, conv_ref, last_ref, mine_ref, got_ref, k_ref, v_ref, c_ref, gq_ref, gk_ref, gv_ref,
                  *, group, poles):
    tokens, width = gq_ref.shape
    per_block = LANES // group
    step = pl.program_id(0)
    steps = pl.num_programs(0)
    inner = width // LANES
    half_blocks = mine_ref.shape[0]
    core = lax.rem(lax.axis_index("ctx"), 2)
    flip = reversal(tokens)
    ahead = (1 + iota((tokens, LANES), 0)).astype(F32)
    state_group = over(within(iota((poles, 2 * LANES), 1), LANES), group)
    start = step * inner
    is_mine = over(start, half_blocks) == core
    cut = pl.ds(pl.multiple_of(start * LANES, LANES), width)

    def emit(conv_ref, base):
        totals = []
        for j in range(inner):
            here = start + j
            rate = rows_ref[0, pl.ds(here, 1), :]
            res = rows_ref[1, pl.ds(here, 1), :]
            table = (res * jnp.exp(-rate * ahead)).astype(BF16)
            place = within(here, half_blocks)
            held = jnp.where(
                is_mine, mine_ref[place], got_ref[pl.ds(pl.multiple_of(place * 2 * poles, 2 * poles), 2 * poles), :]
            )
            states = jnp.concatenate([held[:poles], held[poles:]], axis=1)
            stack = jnp.concatenate(
                [jnp.where(state_group == g, states, jnp.zeros_like(states)) for g in range(per_block)], axis=0
            )
            both = pl.ds(pl.multiple_of(2 * (here - base) * LANES, LANES), 2 * LANES)
            totals.append((conv_ref[:, both] + mxu(table, stack)).astype(BF16))
        hidden = jnp.concatenate([t[:, :LANES] for t in totals], axis=1)
        flow = mxu(flip, jnp.concatenate([t[:, LANES:] for t in totals], axis=1))
        gq_ref[...] = (c_ref[:, cut].astype(F32) * hidden.astype(F32)).astype(BF16)
        gk_ref[...] = (flow * v_ref[:, cut].astype(F32)).astype(BF16)
        gv_ref[...] = (flow * k_ref[:, cut].astype(F32)).astype(BF16)

    @pl.when(step < steps - 1)
    def _():
        emit(conv_ref, 0)

    @pl.when(step == steps - 1)
    def _():
        emit(last_ref, (steps - 1) * inner)


def assemble_kernel(*refs, poles):
    *slots, res_ref, log_ref, skip_ref = refs
    me = lax.axis_index("ch")
    groups = slots[0].shape[1]
    rows = slots[0].shape[0] - 2 * poles
    for mask, slot in enumerate(slots):
        source = lax.bitwise_xor(me, mask)
        value = slot[...].astype(F32)
        cut = pl.ds(pl.multiple_of(source * groups, LANES), groups)
        res_ref[:, cut] = value[:poles]
        log_ref[:, cut] = value[poles : 2 * poles]
        skip_ref[pl.ds(pl.multiple_of(source * rows, 8), rows), :] = value[2 * poles :]


def local(queries, key_input, value_input, cotangent, residues, log_rates, skip_gain):
    tokens, width = queries.shape
    parts = lax.axis_size("ctx")
    shards = lax.axis_size("ch")
    levels = parts.bit_length() - 1
    all_groups, poles = residues.shape
    groups = all_groups // shards
    group = width // groups
    blocks = width // LANES
    inner = 4
    steps = blocks // inner
    half_blocks = blocks // 2
    lag_width = LANES // group * SUB
    sizes = dict(group=group, poles=poles)
    half_rows, tail = half_blocks * 2 * poles, 2 * poles + blocks

    vmem = pl.BlockSpec(memory_space=pltpu.VMEM)
    anywhere = pl.BlockSpec(memory_space=pl.ANY)
    log_rates, residues = log_rates.T, residues.T
    def shape(*dims, dtype=F32):
        return jax.ShapeDtypeStruct(dims, dtype)

    def swap(value, level):
        return lax.ppermute(value, "ctx", [(i, i ^ (1 << level)) for i in range(parts)])

    operand = shape(tokens, width, dtype=BF16)
    scratch = [pltpu.VMEM((tokens, width // 2), BF16)] * 4 + [pltpu.SemaphoreType.DMA((4, steps // 2))]
    inputs = (queries, key_input, value_input, cotangent)
    gates = pl.pallas_call(
        lambda *refs: gates_kernel(*refs, inner=inner),
        in_specs=[anywhere] * 4,
        out_specs=[vmem] * 3,
        out_shape=[operand] * 3,
        scratch_shapes=scratch,
        compiler_params=pltpu.CompilerParams(vmem_limit_bytes=GATES_LIMIT),
        name="gates",
    )(*inputs)
    outgoing, message, gated, dgate, turned, rows, params = pl.pallas_call(
        lambda *refs: states_kernel(*refs, inner=inner, **sizes),
        in_specs=[vmem] * 2 + [anywhere] * 4 + [vmem] * 3,
        out_specs=[vmem] * 7,
        out_shape=[
            shape(2 * half_rows, LANES, dtype=BF16),
            shape(2 * half_rows, LANES, dtype=BF16),
            operand,
            operand,
            operand,
            shape(2, blocks, LANES),
            shape(2, poles, groups),
        ],
        input_output_aliases={6: 2, 7: 3, 8: 4},
        scratch_shapes=scratch,
        compiler_params=pltpu.CompilerParams(vmem_limit_bytes=GATES_LIMIT),
        name="states",
    )(log_rates, residues, *inputs, *gates)

    rates, lag_rates = pl.pallas_call(
        lambda *refs: tables_kernel(*refs, inner=inner, **sizes),
        in_specs=[vmem],
        out_specs=[vmem] * 2,
        out_shape=[shape(blocks, poles, LANES), shape(blocks, poles, lag_width)],
        compiler_params=PARAMS,
        cost_estimate=pl.CostEstimate(flops=10**9, bytes_accessed=10**6, transcendentals=10**5),
        name="tables",
    )(params)

    work = pl.CostEstimate(
        flops=16 * tokens * tokens * width, bytes_accessed=12 * tokens * width, transcendentals=tokens * width
    )

    def local_sums(second, *more):
        return pl.pallas_call(
            lambda *refs: lags_kernel(*refs, second=second, inner=inner, **sizes),
            in_specs=[vmem] * (4 + len(more)),
            out_specs=vmem,
            out_shape=shape(tail, LANES, dtype=BF16) if second else shape(2 * poles, LANES),
            scratch_shapes=[pltpu.VMEM((blocks, LANES), F32)] if second else [],
            compiler_params=PARAMS,
            cost_estimate=work,
            name="lags",
        )(lag_rates, gated, dgate, turned, *more)

    def convolve(first_step, count, after):
        skip_rows = skip_gain.reshape(-1, LANES)
        return pl.pallas_call(
            lambda *refs: conv_kernel(*refs, first_step=first_step, inner=inner, **sizes),
            in_specs=[vmem] * 7 + [anywhere],
            out_specs=vmem,
            out_shape=shape(tokens, 2 * count * inner * LANES),
            compiler_params=PARAMS,
            cost_estimate=work,
            name="conv",
        )(params, rows, skip_rows, rates, lag_rates, gated, turned, after)

    def combine(level, operands, outs):
        return pl.pallas_call(
            lambda *refs: combine_kernel(*refs, level=level, levels=levels, tokens=tokens, **sizes),
            in_specs=[anywhere if x is conv else vmem for x in operands],
            out_specs=[vmem] * len(outs),
            out_shape=outs,
            compiler_params=PARAMS,
            name="combine",
        )(*operands)

    conv = None
    states_shape = shape(2 * half_rows, LANES, dtype=BF16)
    tail_shape = shape(tail, LANES, dtype=BF16)
    slim_shape = shape(half_rows + tail, LANES, dtype=BF16)
    held_shape = shape(half_blocks, 2 * poles, LANES)
    got = swap(outgoing, 0)
    states, total, near = combine(
        0, [rates, message, got, local_sums(0)], [states_shape, shape(2 * poles, LANES), held_shape]
    )
    held = slim = None
    for level in range(1, levels):
        last = level == levels - 1
        if last and slim is not None:
            received = [swap(slim, level)]
        else:
            received = [swap(states, level)]
            if level == 1:
                carried = local_sums(1, total)
            received.append(swap(carried, level))
        operands = [rates, states, carried, *received]
        if level > 1:
            operands.append(held)
        if level == min(2, levels - 1):
            conv = convolve(0, steps - 1, near if held is None else held)
            operands.append(conv)
        if last:
            outs = [shape(half_blocks, 2 * poles, LANES, dtype=BF16), slim_shape]
            mine, outgoing = combine(level, [*operands, near], outs)
        else:
            outs = [states_shape, tail_shape, held_shape]
            if level == levels - 2:
                outs.append(slim_shape)
            states, carried, held, *more = combine(level, operands, outs)
            slim = more[0] if more else None
    got = swap(outgoing, 0)
    last_conv = convolve(steps - 1, 1, outgoing)
    merged = pl.pallas_call(
        lambda *refs: merge_kernel(*refs, poles=poles, length=tokens * parts),
        in_specs=[vmem] * 3 + [anywhere],
        out_specs=vmem,
        out_shape=shape(tail, LANES, dtype=BF16),
        compiler_params=PARAMS,
        name="merge",
    )(params, outgoing, got, last_conv)

    gathered = [merged]
    for mask in range(1, shards):
        gathered.append(lax.ppermute(merged, "ch", [(i, i ^ mask) for i in range(shards)]))

    main = pl.BlockSpec((tokens, inner * LANES), lambda i: (0, i))
    grad_query, grad_key, grad_value = pl.pallas_call(
        lambda *refs: output_kernel(*refs, **sizes),
        grid=(steps,),
        in_specs=[vmem] * 8,
        out_specs=[main] * 3,
        out_shape=[shape(tokens, width, dtype=BF16)] * 3,
        compiler_params=PARAMS,
        cost_estimate=work,
        name="outputs",
    )(rows, conv, last_conv, mine, got, key_input, value_input, cotangent)

    grad_residue, grad_lograte, grad_skip = pl.pallas_call(
        lambda *refs: assemble_kernel(*refs, poles=poles),
        in_specs=[vmem] * shards,
        out_specs=[vmem] * 3,
        out_shape=[shape(poles, all_groups), shape(poles, all_groups), shape(shards * blocks, LANES)],
        compiler_params=PARAMS,
        name="assemble",
    )(*gathered)
    return (grad_query, grad_key, grad_value, grad_residue.T, grad_lograte.T, grad_skip.reshape(-1))


def solution(mesh):
    placed = (P("ctx", "ch"), P("ctx", "ch"), P("ctx", "ch"), P("ctx", "ch"), P(), P(), P())
    return jax.shard_map(
        local,
        mesh=mesh,
        in_specs=placed,
        out_specs=(P("ctx", "ch"), P("ctx", "ch"), P("ctx", "ch"), P(), P(), P()),
        check_vma=False,
    )
```

```python
import math

import jax
import jax.numpy as jnp
from jax import lax
from jax.experimental import pallas as pl
from jax.experimental.pallas import tpu as pltpu
from jax.sharding import PartitionSpec as P

LANES = 128
SUB = 32
F32 = jnp.float32
BF16 = jnp.bfloat16
EXACT = lax.Precision.HIGHEST
VMEM_LIMIT = 40 * 1024 * 1024
PARAMS = pltpu.CompilerParams(vmem_limit_bytes=VMEM_LIMIT)


def iota(shape, axis):
    return lax.broadcasted_iota(jnp.int32, shape, axis)


def over(value, size):
    return lax.shift_right_logical(value, size.bit_length() - 1)


def within(value, size):
    return lax.bitwise_and(value, size - 1)


def mxu(left, right):
    return jnp.dot(left, right, preferred_element_type=F32)


def mxu_t(left, right):
    return lax.dot_general(left, right, (((1,), (1,)), ((), ())), preferred_element_type=F32)


def exact_dot(left, right):
    return jnp.dot(left, right, precision=EXACT, preferred_element_type=F32)


def gate(left, right):
    return (left.astype(F32) * right.astype(F32)).astype(BF16)


def reversal(size):
    return jnp.where(iota((size, size), 0) + iota((size, size), 1) == size - 1, 1.0, 0.0).astype(BF16)


def split(value, pieces):
    parts = []
    for _ in range(pieces):
        parts.append(value.astype(BF16))
        value = value - parts[-1].astype(F32)
    return jnp.concatenate(parts, axis=0)


def join(stacked, rows):
    total = stacked[:rows].astype(F32)
    for start in range(rows, stacked.shape[0], rows):
        total = total + stacked[start : start + rows].astype(F32)
    return total


def flat_rows(table, poles):
    table = table.T
    groups = table.shape[0]
    per_row = LANES // poles
    spread = jnp.where(iota((poles, LANES), 0) == within(iota((poles, LANES), 1), poles), 1.0, 0.0)
    wide = exact_dot(table, spread)
    keep = within(iota((groups, LANES), 0), per_row) == over(iota((groups, LANES), 1), poles)
    wide = jnp.where(keep, wide, 0.0)
    return jnp.sum(wide.reshape(groups // per_row, per_row, LANES), axis=1)


def members(groups, first, span, width):
    return jnp.where(iota((groups, width), 0) == first + over(iota((groups, width), 1), span), 1.0, 0.0).astype(BF16)


def shard_start(groups):
    return pl.multiple_of(lax.axis_index("ch") * groups, LANES)


def states_kernel(all_params_ref, q_any, k_any, v_any, c_any, send_ref, keep_ref, gated_ref, dgate_ref, turned_ref,
                  rows_ref, table_ref, q_ref, k_ref, v_ref, c_ref, sems, *, group, poles, inner):
    tokens, _ = gated_ref.shape
    per_block = LANES // group
    _, blocks, _ = rows_ref.shape
    half_blocks = blocks // 2
    groups = blocks * per_block
    wide = inner * LANES
    core = lax.rem(lax.axis_index("ctx"), 2)
    sources = ((k_any, k_ref), (v_any, v_ref), (c_any, c_ref), (q_any, q_ref))
    half_steps = half_blocks // inner

    def copies(turn, step):
        start = lax.rem(core + 1 + turn, 2) * half_blocks + step * inner
        cut = pl.ds(pl.multiple_of(start * LANES, LANES), wide)
        return [
            pltpu.make_async_copy(far.at[:, cut], near.at[:, cut], sems.at[n, turn * half_steps + step])
            for n, (far, near) in enumerate(sources)
        ]

    first = shard_start(groups)
    for turn in range(2):
        for step in range(half_steps):
            for copy in copies(turn, step):
                copy.start()
    for n in range(2):
        table_ref[n] = all_params_ref[n, :, pl.ds(first, groups)]
    rows_ref[0] = jnp.exp(flat_rows(table_ref[0], poles))
    rows_ref[1] = flat_rows(table_ref[1], poles)

    flip = reversal(tokens)
    back_pos = (tokens - 1 - iota((tokens, LANES), 0)).astype(F32)
    back_lane = (tokens - 1 - iota((1, tokens), 1)).astype(F32)
    wide_group = over(within(iota((poles, 2 * LANES), 1), LANES), group)
    lanes = [slice(j * LANES, (j + 1) * LANES) for j in range(inner)]

    for turn, msg_ref in enumerate((send_ref, keep_ref)):
        base = lax.rem(core + 1 + turn, 2) * half_blocks

        def body(step, carry, base=base, msg_ref=msg_ref, turn=turn):
            start = base + step * inner
            cut = pl.ds(pl.multiple_of(start * LANES, LANES), wide)
            for copy in copies(turn, step):
                copy.wait()
            gated, dgate = gate(k_ref[:, cut], v_ref[:, cut]), gate(c_ref[:, cut], q_ref[:, cut])
            gated_ref[:, cut] = gated
            dgate_ref[:, cut] = dgate
            turned = mxu(flip, dgate).astype(BF16)
            turned_ref[:, cut] = turned
            tables = [jnp.exp(-rows_ref[0, pl.ds(start + j, 1), :] * back_pos).T for j in range(inner)]
            found = []
            for j in range(inner):
                both = jnp.concatenate([tables[j].astype(BF16), (tables[j] * back_lane).astype(BF16)], axis=0)
                pair = jnp.concatenate([gated[:, lanes[j]], turned[:, lanes[j]]], axis=1)
                found.append(mxu(both, pair))
            for j in range(inner):
                folded = []
                for part in range(2):
                    total = found[j][part * LANES : part * LANES + poles]
                    for g in range(1, per_block):
                        row = part * LANES + g * poles
                        total = jnp.where(wide_group == g, found[j][row : row + poles], total)
                    folded.append(total)
                out = [folded[0][:, :LANES], folded[0][:, LANES:], folded[1][:, :LANES], folded[1][:, LANES:]]
                row = (step * inner + j) * 4 * poles
                msg_ref[row : row + 4 * poles, :] = jnp.concatenate(out, axis=0).astype(BF16)
            return carry

        for step in range(half_steps):
            body(step, 0)


def lags_kernel(lag_rates_ref, gated_ref, dgate_ref, turned_ref, *rest, second, group, poles, inner):
    if second:
        first_ref, out_ref, skip_ref = rest
    else:
        (out_ref,) = rest
    tokens, _ = gated_ref.shape
    per_block = LANES // group
    blocks, _, lag_width = lag_rates_ref.shape
    subs = tokens // SUB
    step_groups = inner * per_block
    lane_group = over(iota((SUB, LANES), 1), group)
    row, lane = iota((SUB, lag_width), 0), within(iota((SUB, lag_width), 1), SUB)
    near_side, no_wrap = row + lane <= SUB - 1, lane >= row
    lag = (SUB - 1 - within(iota((poles, lag_width), 1), SUB)).astype(F32)
    spread = members(step_groups, 0, SUB, inner * lag_width)
    steps = blocks // inner
    sums = []
    for step in range(1, steps) if second else range(1):
        outers = []
        for j in range(inner):
            lanes = slice((step * inner + j) * LANES, (step * inner + j + 1) * LANES)
            found = [None] * subs
            for k in range(subs):
                part = gated_ref[k * SUB : (k + 1) * SUB, lanes]
                stack = jnp.concatenate(
                    [jnp.where(lane_group == g, part, jnp.zeros_like(part)) for g in range(per_block)], axis=0
                )
                outer = mxu_t(turned_ref[: (subs - k) * SUB, lanes], stack)
                for n in range(subs - k):
                    far = subs - 1 - k - n
                    piece = outer[n * SUB : (n + 1) * SUB]
                    found[far] = piece if found[far] is None else found[far] + piece
            outers.append(found)
        terms = []
        for j in range(inner):
            found = outers[j] + [jnp.zeros((SUB, lag_width), F32)]
            lags = []
            for far in range(subs):
                total = jnp.where(near_side, found[far], found[far + 1])
                straight = pltpu.roll(total, 0, 1, stride=1, stride_axis=0)
                wrapped = pltpu.roll(total, lag_width - SUB, 1, stride=1, stride_axis=0)
                lags.append(jnp.sum(jnp.where(no_wrap, straight, wrapped), axis=0, keepdims=True))
            rate = lag_rates_ref[step * inner + j]
            decay = jnp.exp(-rate * SUB)
            total = jnp.zeros((poles, lag_width), F32)
            weighted = total
            for far in reversed(range(subs)):
                weighted = decay * weighted + far * lags[far]
                total = decay * total + lags[far]
            table = jnp.exp(-rate * lag)
            terms.append(
                split(jnp.concatenate([table * total, table * (lag * total + SUB * weighted)], axis=0), 2)
            )
        sums.append(mxu_t(jnp.concatenate(terms, axis=1), spread))
    sums = jnp.concatenate(sums, axis=1)
    zeros = jnp.zeros((sums.shape[0], blocks * per_block - sums.shape[1]), F32)
    sums = jnp.concatenate([zeros, sums] if second else [sums, zeros], axis=1)
    sums = join(sums, 2 * poles)
    if not second:
        out_ref[...] = sums
        return
    for b in range(blocks):
        lanes = slice(b * LANES, (b + 1) * LANES)
        product = gated_ref[:, lanes].astype(F32) * dgate_ref[:, lanes].astype(F32)
        skip_ref[b : b + 1, :] = jnp.sum(product, axis=0, keepdims=True)
    out_ref[: 2 * poles, :] = (first_ref[...] + sums).astype(BF16)
    out_ref[2 * poles :, :] = skip_ref[...].astype(BF16)


def tables_kernel(params_ref, rates_ref, lag_rates_ref, *, group, poles, inner):
    blocks, _, lag_width = lag_rates_ref.shape
    per_block = LANES // group
    step_groups = inner * per_block
    lag_wide = inner * lag_width
    pieces = split(params_ref[0], 3)
    spread = jnp.concatenate(
        [members(step_groups, 0, SUB, lag_wide), members(step_groups, 0, group, inner * LANES)], axis=1
    )
    for step in range(blocks // inner):
        spreads = mxu(pieces[:, step * step_groups : (step + 1) * step_groups], spread)
        rates = jnp.exp(join(spreads, poles))
        for j in range(inner):
            here = step * inner + j
            lag_rates_ref[here] = rates[:, j * lag_width : (j + 1) * lag_width]
            rates_ref[here] = rates[:, lag_wide + j * LANES : lag_wide + (j + 1) * LANES]


def conv_kernel(params_ref, rows_ref, skip_ref, rates_ref, lag_rates_ref, gated_ref, turned_ref, _, conv_ref,
                *, first_step, group, poles, inner):
    tokens, _ = gated_ref.shape
    per_block = LANES // group
    blocks, _, _ = rates_ref.shape
    subs = tokens // SUB
    lag_width = per_block * SUB
    first = lax.axis_index("ch") * blocks
    lead = (1 + iota((SUB, LANES), 0)).astype(F32)
    wide_group = over(within(iota((SUB, 2 * LANES), 1), LANES), group)
    state_group = over(within(iota((poles, 2 * LANES), 1), LANES), group)
    causal = iota((SUB, lag_width), 0) >= within(iota((SUB, lag_width), 1), SUB)
    lag = (SUB - 1 - within(iota((poles, lag_width), 1), SUB)).astype(F32)
    groups = blocks * per_block
    pieces = split(params_ref[1], 3).astype(F32)
    spread = members(groups, 0, SUB, inner * lag_width)

    def body(step, carry):
        start = (step + first_step) * inner
        moved = pltpu.roll(pieces, groups - start * per_block, 1).astype(BF16)
        lag_res = join(mxu(moved, spread), poles)
        lefts, lead_tables, decays, pairs, gains = [], [], [], [], []
        for j in range(inner):
            here = start + j
            table = jnp.exp(-lag_rates_ref[here] * lag)
            taps = jnp.sum(lag_res[:, j * lag_width : (j + 1) * lag_width] * table, axis=0, keepdims=True)
            taps = jnp.broadcast_to(taps, (SUB, lag_width))
            taps = pltpu.roll(taps, lag_width - SUB + 1, 1, stride=1, stride_axis=0)
            taps = jnp.where(causal, taps, 0.0).astype(BF16)
            lefts.append(jnp.concatenate([taps, table.astype(BF16)], axis=0))
            rate = rows_ref[0, pl.ds(here, 1), :]
            res = rows_ref[1, pl.ds(here, 1), :]
            lead_tables.append((res * jnp.exp(-rate * lead)).astype(BF16))
            decay = jnp.exp(-rates_ref[here] * SUB)
            decays.append(jnp.concatenate([decay, decay], axis=1))
            cut = pl.ds(pl.multiple_of(here * LANES, LANES), LANES)
            pairs.append(jnp.concatenate([gated_ref[:, cut], turned_ref[:, cut]], axis=1))
            gain = skip_ref[pl.ds(first + here, 1), :]
            gains.append(jnp.concatenate([gain, gain], axis=1))
        states = [jnp.zeros((poles, 2 * LANES), F32)] * inner
        totals = [[] for _ in range(inner)]
        for k in range(subs):
            rows = slice(k * SUB, (k + 1) * SUB)
            found = []
            for j in range(inner):
                part = pairs[j][rows]
                stack = [jnp.where(wide_group == g, part, jnp.zeros_like(part)) for g in range(per_block)]
                found.append(mxu(lefts[j], jnp.concatenate(stack, axis=0)))
            for j in range(inner):
                total = found[j][:SUB] + gains[j] * pairs[j][rows].astype(F32)
                if k:
                    held = states[j].astype(BF16)
                    stack = [jnp.where(state_group == g, held, jnp.zeros_like(held)) for g in range(per_block)]
                    total = total + mxu(lead_tables[j], jnp.concatenate(stack, axis=0))
                totals[j].append(total)
            states = [decays[j] * states[j] + found[j][SUB:] for j in range(inner)]
        for j in range(inner):
            cut = pl.ds(pl.multiple_of(2 * (step * inner + j) * LANES, LANES), 2 * LANES)
            conv_ref[:, cut] = jnp.concatenate(totals[j], axis=0)
        return carry

    lax.fori_loop(0, conv_ref.shape[1] // (2 * inner * LANES), body, 0)


def combine_kernel(*refs, level, levels, group, poles, tokens):
    last = level == levels - 1
    refs = list(refs)
    rates_ref = refs.pop(0)
    all_blocks = rates_ref.shape[0]
    blocks = all_blocks // 2
    per_block = LANES // group
    groups = all_blocks * per_block
    rows = 2 * poles
    if level == 0:
        own_ref, got_ref, sums_ref, states_ref, total_ref, near_ref = refs
    else:
        own_ref, own_tail_ref, got_ref = refs.pop(0), refs.pop(0), refs.pop(0)
        got_tail_ref = None if last else refs.pop(0)
        held_ref = refs.pop(0) if level > 1 else None
        if level == min(2, levels - 1):
            refs.pop(0)
        if last:
            near_ref, mine_ref, out_ref = refs
        else:
            states_ref, tail_ref, new_held_ref = refs[:3]
            slim_ref = refs[3] if level == levels - 2 else None
    me = lax.axis_index("ctx")
    core = lax.rem(me, 2)
    is_right = lax.rem(lax.shift_right_logical(me, level), 2) == 1
    before = lax.rem(me, 2**level) - (core if level else 0)
    gap_left = (tokens * before).astype(F32)
    gap_right = (tokens * (2**level - 2 - before)).astype(F32)
    gap = jnp.where(is_right, gap_left, gap_right)
    span = float(tokens * 2**level)
    next_right = lax.rem(lax.shift_right_logical(me, level + 1), 2) == 1

    def quarters(ref, b):
        value = ref[2 * b * rows : 2 * (b + 1) * rows].astype(F32)
        return [value[n * poles : (n + 1) * poles] for n in range(4)]

    wide_terms = []
    for b in range(blocks):
        rate = rates_ref[core * blocks + b]
        own_f, own_b, own_fm, own_bm = quarters(own_ref, b)
        if last:
            got = got_ref[b * rows : (b + 1) * rows].astype(F32)
            got_f = got_b = got[:poles]
            got_fm = got_bm = got[poles:]
        else:
            got_f, got_b, got_fm, got_bm = quarters(got_ref, b)
        left_f = jnp.where(is_right, got_f, own_f)
        left_fm = jnp.where(is_right, got_fm, own_fm)
        right_b = jnp.where(is_right, own_b, got_b)
        right_bm = jnp.where(is_right, own_bm, got_bm)
        once = jnp.exp(-rate)
        cross_res = once * (right_b * left_f)
        cross_mom = once * (right_bm * left_f + right_b * (left_fm + left_f))
        wide_terms.append(split(jnp.concatenate([cross_res, cross_mom], axis=0), 2))
        if level == 0:
            near_ref[b] = jnp.concatenate([left_f, right_b], axis=0)
        else:
            carry = jnp.exp(-rate * gap) * jnp.where(is_right, left_f, right_b)
            zero = jnp.zeros_like(carry)
            hold = jnp.concatenate([jnp.where(is_right, carry, zero), jnp.where(is_right, zero, carry)], axis=0)
            if level > 1:
                hold = hold + held_ref[b]
            if last:
                step = jnp.exp(-rate * tokens)
                near = near_ref[b]
                first_core = jnp.concatenate([hold[:poles], near[poles:] + step * hold[poles:]], axis=0)
                second_core = jnp.concatenate([near[:poles] + step * hold[:poles], hold[poles:]], axis=0)
                mine_ref[b] = jnp.where(core > 0, second_core, first_core).astype(BF16)
                out_ref[b * rows : (b + 1) * rows, :] = jnp.where(core > 0, first_core, second_core).astype(BF16)
            else:
                new_held_ref[b] = hold
        if not last:
            right_f = jnp.where(is_right, own_f, got_f)
            right_fm = jnp.where(is_right, own_fm, got_fm)
            left_b = jnp.where(is_right, got_b, own_b)
            left_bm = jnp.where(is_right, got_bm, own_bm)
            decay = jnp.exp(-rate * span)
            new_f, new_b = decay * left_f + right_f, left_b + decay * right_b
            new_fm = decay * (left_fm + span * left_f) + right_fm
            new_bm = left_bm + decay * (right_bm + span * right_b)
            here = slice(b * rows, (b + 1) * rows)
            new = jnp.concatenate([new_f, new_b, new_fm, new_bm], axis=0).astype(BF16)
            states_ref[2 * b * rows : 2 * (b + 1) * rows, :] = new
            if level == levels - 2 and level:
                chosen = [jnp.where(next_right, new_b, new_f), jnp.where(next_right, new_bm, new_fm)]
                slim_ref[here, :] = jnp.concatenate(chosen, axis=0).astype(BF16)
    cross = join(mxu_t(jnp.concatenate(wide_terms, axis=1), members(groups, 0, group, blocks * LANES)), rows)
    cross = jnp.where(core > 0, pltpu.roll(cross, groups // 2, 1), cross)
    tail = blocks * rows
    if level == 0:
        total_ref[...] = cross + sums_ref[...]
        return
    got_tail = got_ref[tail:, :] if last else got_tail_ref[...]
    both = own_tail_ref[...].astype(F32) + got_tail.astype(F32)
    rests = jnp.concatenate([both[:rows] + cross, both[rows:]], axis=0).astype(BF16)
    if last:
        out_ref[tail:, :] = rests
    else:
        tail_ref[...] = rests
        if slim_ref is not None:
            slim_ref[tail:, :] = rests


def merge_kernel(params_ref, own_ref, got_ref, _, out_ref, *, poles, length):
    groups = out_ref.shape[1]
    start = own_ref.shape[0] - out_ref.shape[0]
    both = own_ref[start:, :].astype(F32) + got_ref[start:, :].astype(F32)
    factor = -jnp.exp(params_ref[0]) * params_ref[1]
    scaled = [
        both[:poles] / length,
        factor * both[poles : 2 * poles] / math.sqrt(length),
        both[2 * poles :] / math.sqrt(length),
    ]
    out_ref[...] = jnp.concatenate(scaled, axis=0).astype(BF16)


def output_kernel(rows_ref, conv_ref, last_ref, mine_ref, got_ref, k_ref, v_ref, c_ref, gq_ref, gk_ref, gv_ref,
                  *, group, poles):
    tokens, width = gq_ref.shape
    per_block = LANES // group
    step = pl.program_id(0)
    steps = pl.num_programs(0)
    inner = width // LANES
    half_blocks = mine_ref.shape[0]
    core = lax.rem(lax.axis_index("ctx"), 2)
    flip = reversal(tokens)
    ahead = (1 + iota((tokens, LANES), 0)).astype(F32)
    state_group = over(within(iota((poles, 2 * LANES), 1), LANES), group)
    start = step * inner
    is_mine = over(start, half_blocks) == core
    cut = pl.ds(pl.multiple_of(start * LANES, LANES), width)

    def emit(conv_ref, base):
        totals = []
        for j in range(inner):
            here = start + j
            rate = rows_ref[0, pl.ds(here, 1), :]
            res = rows_ref[1, pl.ds(here, 1), :]
            table = (res * jnp.exp(-rate * ahead)).astype(BF16)
            place = within(here, half_blocks)
            held = jnp.where(
                is_mine, mine_ref[place], got_ref[pl.ds(pl.multiple_of(place * 2 * poles, 2 * poles), 2 * poles), :]
            )
            states = jnp.concatenate([held[:poles], held[poles:]], axis=1)
            stack = jnp.concatenate(
                [jnp.where(state_group == g, states, jnp.zeros_like(states)) for g in range(per_block)], axis=0
            )
            both = pl.ds(pl.multiple_of(2 * (here - base) * LANES, LANES), 2 * LANES)
            totals.append((conv_ref[:, both] + mxu(table, stack)).astype(BF16))
        hidden = jnp.concatenate([t[:, :LANES] for t in totals], axis=1)
        flow = mxu(flip, jnp.concatenate([t[:, LANES:] for t in totals], axis=1))
        gq_ref[...] = (c_ref[:, cut].astype(F32) * hidden.astype(F32)).astype(BF16)
        gk_ref[...] = (flow * v_ref[:, cut].astype(F32)).astype(BF16)
        gv_ref[...] = (flow * k_ref[:, cut].astype(F32)).astype(BF16)

    @pl.when(step < steps - 1)
    def _():
        emit(conv_ref, 0)

    @pl.when(step == steps - 1)
    def _():
        emit(last_ref, (steps - 1) * inner)


def assemble_kernel(*refs, poles):
    *slots, res_ref, log_ref, skip_ref = refs
    me = lax.axis_index("ch")
    groups = slots[0].shape[1]
    rows = slots[0].shape[0] - 2 * poles
    for mask, slot in enumerate(slots):
        source = lax.bitwise_xor(me, mask)
        value = slot[...].astype(F32)
        cut = pl.ds(pl.multiple_of(source * groups, LANES), groups)
        res_ref[:, cut] = value[:poles]
        log_ref[:, cut] = value[poles : 2 * poles]
        skip_ref[pl.ds(pl.multiple_of(source * rows, 8), rows), :] = value[2 * poles :]


def local(queries, key_input, value_input, cotangent, residues, log_rates, skip_gain):
    tokens, width = queries.shape
    parts = lax.axis_size("ctx")
    shards = lax.axis_size("ch")
    levels = parts.bit_length() - 1
    all_groups, poles = residues.shape
    groups = all_groups // shards
    group = width // groups
    blocks = width // LANES
    inner = 4
    steps = blocks // inner
    half_blocks = blocks // 2
    lag_width = LANES // group * SUB
    sizes = dict(group=group, poles=poles)
    half_rows, tail = half_blocks * 2 * poles, 2 * poles + blocks

    vmem = pl.BlockSpec(memory_space=pltpu.VMEM)
    anywhere = pl.BlockSpec(memory_space=pl.ANY)
    log_rates, residues = log_rates.T, residues.T
    def shape(*dims, dtype=F32):
        return jax.ShapeDtypeStruct(dims, dtype)

    def swap(value, level):
        return lax.ppermute(value, "ctx", [(i, i ^ (1 << level)) for i in range(parts)])

    far = pl.BlockSpec(memory_space=pl.ANY)
    outgoing, message, gated, dgate, turned, rows, params = pl.pallas_call(
        lambda *refs: states_kernel(*refs, inner=inner, **sizes),
        in_specs=[vmem] + [far] * 4,
        out_specs=[vmem] * 7,
        out_shape=[
            shape(2 * half_rows, LANES, dtype=BF16),
            shape(2 * half_rows, LANES, dtype=BF16),
            shape(tokens, width, dtype=BF16),
            shape(tokens, width, dtype=BF16),
            shape(tokens, width, dtype=BF16),
            shape(2, blocks, LANES),
            shape(2, poles, groups),
        ],
        scratch_shapes=[pltpu.VMEM((tokens, width), BF16)] * 4
        + [pltpu.SemaphoreType.DMA((4, steps))],
        compiler_params=pltpu.CompilerParams(vmem_limit_bytes=53000 * 1024),
        name="states",
    )(jnp.stack([log_rates, residues]), queries, key_input, value_input, cotangent)

    rates, lag_rates = pl.pallas_call(
        lambda *refs: tables_kernel(*refs, inner=inner, **sizes),
        in_specs=[vmem],
        out_specs=[vmem] * 2,
        out_shape=[shape(blocks, poles, LANES), shape(blocks, poles, lag_width)],
        compiler_params=PARAMS,
        cost_estimate=pl.CostEstimate(flops=10**9, bytes_accessed=10**6, transcendentals=10**5),
        name="tables",
    )(params)

    work = pl.CostEstimate(
        flops=16 * tokens * tokens * width, bytes_accessed=12 * tokens * width, transcendentals=tokens * width
    )

    def local_sums(second, *more):
        return pl.pallas_call(
            lambda *refs: lags_kernel(*refs, second=second, inner=inner, **sizes),
            in_specs=[vmem] * (4 + len(more)),
            out_specs=vmem,
            out_shape=shape(tail, LANES, dtype=BF16) if second else shape(2 * poles, LANES),
            scratch_shapes=[pltpu.VMEM((blocks, LANES), F32)] if second else [],
            compiler_params=PARAMS,
            cost_estimate=work,
            name="lags",
        )(lag_rates, gated, dgate, turned, *more)

    def convolve(first_step, count, after):
        skip_rows = skip_gain.reshape(-1, LANES)
        return pl.pallas_call(
            lambda *refs: conv_kernel(*refs, first_step=first_step, inner=inner, **sizes),
            in_specs=[vmem] * 7 + [anywhere],
            out_specs=vmem,
            out_shape=shape(tokens, 2 * count * inner * LANES),
            compiler_params=PARAMS,
            cost_estimate=work,
            name="conv",
        )(params, rows, skip_rows, rates, lag_rates, gated, turned, after)

    def combine(level, operands, outs):
        return pl.pallas_call(
            lambda *refs: combine_kernel(*refs, level=level, levels=levels, tokens=tokens, **sizes),
            in_specs=[anywhere if x is conv else vmem for x in operands],
            out_specs=[vmem] * len(outs),
            out_shape=outs,
            compiler_params=PARAMS,
            name="combine",
        )(*operands)

    conv = None
    states_shape = shape(2 * half_rows, LANES, dtype=BF16)
    tail_shape = shape(tail, LANES, dtype=BF16)
    slim_shape = shape(half_rows + tail, LANES, dtype=BF16)
    held_shape = shape(half_blocks, 2 * poles, LANES)
    got = swap(outgoing, 0)
    states, total, near = combine(
        0, [rates, message, got, local_sums(0)], [states_shape, shape(2 * poles, LANES), held_shape]
    )
    held = slim = None
    for level in range(1, levels):
        last = level == levels - 1
        if last and slim is not None:
            received = [swap(slim, level)]
        else:
            received = [swap(states, level)]
            if level == 1:
                carried = local_sums(1, total)
            received.append(swap(carried, level))
        operands = [rates, states, carried, *received]
        if level > 1:
            operands.append(held)
        if level == min(2, levels - 1):
            conv = convolve(0, steps - 1, near if held is None else held)
            operands.append(conv)
        if last:
            outs = [shape(half_blocks, 2 * poles, LANES, dtype=BF16), slim_shape]
            mine, outgoing = combine(level, [*operands, near], outs)
        else:
            outs = [states_shape, tail_shape, held_shape]
            if level == levels - 2:
                outs.append(slim_shape)
            states, carried, held, *more = combine(level, operands, outs)
            slim = more[0] if more else None
    got = swap(outgoing, 0)
    last_conv = convolve(steps - 1, 1, outgoing)
    merged = pl.pallas_call(
        lambda *refs: merge_kernel(*refs, poles=poles, length=tokens * parts),
        in_specs=[vmem] * 3 + [anywhere],
        out_specs=vmem,
        out_shape=shape(tail, LANES, dtype=BF16),
        compiler_params=PARAMS,
        name="merge",
    )(params, outgoing, got, last_conv)

    gathered = [merged]
    for mask in range(1, shards):
        gathered.append(lax.ppermute(merged, "ch", [(i, i ^ mask) for i in range(shards)]))

    main = pl.BlockSpec((tokens, inner * LANES), lambda i: (0, i))
    grad_query, grad_key, grad_value = pl.pallas_call(
        lambda *refs: output_kernel(*refs, **sizes),
        grid=(steps,),
        in_specs=[vmem] * 8,
        out_specs=[main] * 3,
        out_shape=[shape(tokens, width, dtype=BF16)] * 3,
        compiler_params=PARAMS,
        cost_estimate=work,
        name="outputs",
    )(rows, conv, last_conv, mine, got, key_input, value_input, cotangent)

    grad_residue, grad_lograte, grad_skip = pl.pallas_call(
        lambda *refs: assemble_kernel(*refs, poles=poles),
        in_specs=[vmem] * shards,
        out_specs=[vmem] * 3,
        out_shape=[shape(poles, all_groups), shape(poles, all_groups), shape(shards * blocks, LANES)],
        compiler_params=PARAMS,
        name="assemble",
    )(*gathered)
    return (grad_query, grad_key, grad_value, grad_residue.T, grad_lograte.T, grad_skip.reshape(-1))


def solution(mesh):
    placed = (P("ctx", "ch"), P("ctx", "ch"), P("ctx", "ch"), P("ctx", "ch"), P(), P(), P())
    return jax.shard_map(
        local,
        mesh=mesh,
        in_specs=placed,
        out_specs=(P("ctx", "ch"), P("ctx", "ch"), P("ctx", "ch"), P(), P(), P()),
        check_vma=False,
    )
```

```python
import math

import jax
import jax.numpy as jnp
from jax import lax
from jax.experimental import pallas as pl
from jax.experimental.pallas import tpu as pltpu
from jax.sharding import PartitionSpec as P

LANES = 128
SUB = 32
F32 = jnp.float32
BF16 = jnp.bfloat16
EXACT = lax.Precision.HIGHEST
VMEM_LIMIT = 40 * 1024 * 1024
PARAMS = pltpu.CompilerParams(vmem_limit_bytes=VMEM_LIMIT)


def iota(shape, axis):
    return lax.broadcasted_iota(jnp.int32, shape, axis)


def over(value, size):
    return lax.shift_right_logical(value, size.bit_length() - 1)


def within(value, size):
    return lax.bitwise_and(value, size - 1)


def mxu(left, right):
    return jnp.dot(left, right, preferred_element_type=F32)


def mxu_t(left, right):
    return lax.dot_general(left, right, (((1,), (1,)), ((), ())), preferred_element_type=F32)


def exact_dot(left, right):
    return jnp.dot(left, right, precision=EXACT, preferred_element_type=F32)


def gate(left, right):
    return (left.astype(F32) * right.astype(F32)).astype(BF16)


def reversal(size):
    return jnp.where(iota((size, size), 0) + iota((size, size), 1) == size - 1, 1.0, 0.0).astype(BF16)


def split(value, pieces):
    parts = []
    for _ in range(pieces):
        parts.append(value.astype(BF16))
        value = value - parts[-1].astype(F32)
    return jnp.concatenate(parts, axis=0)


def join(stacked, rows):
    total = stacked[:rows].astype(F32)
    for start in range(rows, stacked.shape[0], rows):
        total = total + stacked[start : start + rows].astype(F32)
    return total


def flat_rows(table, poles):
    table = table.T
    groups = table.shape[0]
    per_row = LANES // poles
    spread = jnp.where(iota((poles, LANES), 0) == within(iota((poles, LANES), 1), poles), 1.0, 0.0)
    wide = exact_dot(table, spread)
    keep = within(iota((groups, LANES), 0), per_row) == over(iota((groups, LANES), 1), poles)
    wide = jnp.where(keep, wide, 0.0)
    return jnp.sum(wide.reshape(groups // per_row, per_row, LANES), axis=1)


def members(groups, first, span, width):
    return jnp.where(iota((groups, width), 0) == first + over(iota((groups, width), 1), span), 1.0, 0.0).astype(BF16)


def shard_start(groups):
    return pl.multiple_of(lax.axis_index("ch") * groups, LANES)


def states_kernel(all_params_ref, q_any, k_any, v_any, c_any, send_ref, keep_ref, gated_ref, dgate_ref, turned_ref,
                  rows_ref, table_ref, q_ref, k_ref, v_ref, c_ref, sems, *, group, poles, inner):
    tokens, _ = gated_ref.shape
    per_block = LANES // group
    _, blocks, _ = rows_ref.shape
    half_blocks = blocks // 2
    groups = blocks * per_block
    wide = inner * LANES
    core = lax.rem(lax.axis_index("ctx"), 2)
    sources = ((k_any, k_ref), (v_any, v_ref), (c_any, c_ref), (q_any, q_ref))
    half_steps = half_blocks // inner

    def copies(turn, step):
        start = lax.rem(core + 1 + turn, 2) * half_blocks + step * inner
        cut = pl.ds(pl.multiple_of(start * LANES, LANES), wide)
        return [
            pltpu.make_async_copy(far.at[:, cut], near.at[:, cut], sems.at[n, turn * half_steps + step])
            for n, (far, near) in enumerate(sources)
        ]

    first = shard_start(groups)
    for turn in range(2):
        for step in range(half_steps):
            for copy in copies(turn, step):
                copy.start()
    for n in range(2):
        table_ref[n] = all_params_ref[n, :, pl.ds(first, groups)]
    rows_ref[0] = jnp.exp(flat_rows(table_ref[0], poles))
    rows_ref[1] = flat_rows(table_ref[1], poles)

    flip = reversal(tokens)
    back_pos = (tokens - 1 - iota((tokens, LANES), 0)).astype(F32)
    back_lane = (tokens - 1 - iota((1, tokens), 1)).astype(F32)
    wide_group = over(within(iota((poles, 2 * LANES), 1), LANES), group)
    lanes = [slice(j * LANES, (j + 1) * LANES) for j in range(inner)]

    for turn, msg_ref in enumerate((send_ref, keep_ref)):
        base = lax.rem(core + 1 + turn, 2) * half_blocks

        def body(step, carry, base=base, msg_ref=msg_ref, turn=turn):
            start = base + step * inner
            cut = pl.ds(pl.multiple_of(start * LANES, LANES), wide)
            for copy in copies(turn, step):
                copy.wait()
            gated, dgate = gate(k_ref[:, cut], v_ref[:, cut]), gate(c_ref[:, cut], q_ref[:, cut])
            gated_ref[:, cut] = gated
            dgate_ref[:, cut] = dgate
            turned = mxu(flip, dgate).astype(BF16)
            turned_ref[:, cut] = turned
            tables = [jnp.exp(-rows_ref[0, pl.ds(start + j, 1), :] * back_pos).T for j in range(inner)]
            found = []
            for j in range(inner):
                both = jnp.concatenate([tables[j].astype(BF16), (tables[j] * back_lane).astype(BF16)], axis=0)
                pair = jnp.concatenate([gated[:, lanes[j]], turned[:, lanes[j]]], axis=1)
                found.append(mxu(both, pair))
            for j in range(inner):
                folded = []
                for part in range(2):
                    total = found[j][part * LANES : part * LANES + poles]
                    for g in range(1, per_block):
                        row = part * LANES + g * poles
                        total = jnp.where(wide_group == g, found[j][row : row + poles], total)
                    folded.append(total)
                out = [folded[0][:, :LANES], folded[0][:, LANES:], folded[1][:, :LANES], folded[1][:, LANES:]]
                row = (step * inner + j) * 4 * poles
                msg_ref[row : row + 4 * poles, :] = jnp.concatenate(out, axis=0).astype(BF16)
            return carry

        for step in range(half_steps):
            body(step, 0)


def lags_kernel(lag_rates_ref, gated_ref, dgate_ref, turned_ref, *rest, second, group, poles, inner):
    if second:
        first_ref, out_ref, skip_ref = rest
    else:
        (out_ref,) = rest
    tokens, _ = gated_ref.shape
    per_block = LANES // group
    blocks, _, lag_width = lag_rates_ref.shape
    subs = tokens // SUB
    step_groups = inner * per_block
    lane_group = over(iota((SUB, LANES), 1), group)
    row, lane = iota((SUB, lag_width), 0), within(iota((SUB, lag_width), 1), SUB)
    near_side, no_wrap = row + lane <= SUB - 1, lane >= row
    lag = (SUB - 1 - within(iota((poles, lag_width), 1), SUB)).astype(F32)
    spread = members(step_groups, 0, SUB, inner * lag_width)
    steps = blocks // inner
    sums = []
    for step in range(1, steps) if second else range(1):
        outers = []
        for j in range(inner):
            lanes = slice((step * inner + j) * LANES, (step * inner + j + 1) * LANES)
            found = [None] * subs
            for k in range(subs):
                part = gated_ref[k * SUB : (k + 1) * SUB, lanes]
                stack = jnp.concatenate(
                    [jnp.where(lane_group == g, part, jnp.zeros_like(part)) for g in range(per_block)], axis=0
                )
                outer = mxu_t(turned_ref[: (subs - k) * SUB, lanes], stack)
                for n in range(subs - k):
                    far = subs - 1 - k - n
                    piece = outer[n * SUB : (n + 1) * SUB]
                    found[far] = piece if found[far] is None else found[far] + piece
            outers.append(found)
        terms = []
        for j in range(inner):
            found = outers[j] + [jnp.zeros((SUB, lag_width), F32)]
            lags = []
            for far in range(subs):
                total = jnp.where(near_side, found[far], found[far + 1])
                straight = pltpu.roll(total, 0, 1, stride=1, stride_axis=0)
                wrapped = pltpu.roll(total, lag_width - SUB, 1, stride=1, stride_axis=0)
                lags.append(jnp.sum(jnp.where(no_wrap, straight, wrapped), axis=0, keepdims=True))
            rate = lag_rates_ref[step * inner + j]
            decay = jnp.exp(-rate * SUB)
            total = jnp.zeros((poles, lag_width), F32)
            weighted = total
            for far in reversed(range(subs)):
                weighted = decay * weighted + far * lags[far]
                total = decay * total + lags[far]
            table = jnp.exp(-rate * lag)
            terms.append(
                split(jnp.concatenate([table * total, table * (lag * total + SUB * weighted)], axis=0), 2)
            )
        sums.append(mxu_t(jnp.concatenate(terms, axis=1), spread))
    sums = jnp.concatenate(sums, axis=1)
    zeros = jnp.zeros((sums.shape[0], blocks * per_block - sums.shape[1]), F32)
    sums = jnp.concatenate([zeros, sums] if second else [sums, zeros], axis=1)
    sums = join(sums, 2 * poles)
    if not second:
        out_ref[...] = sums
        return
    for b in range(blocks):
        lanes = slice(b * LANES, (b + 1) * LANES)
        product = gated_ref[:, lanes].astype(F32) * dgate_ref[:, lanes].astype(F32)
        skip_ref[b : b + 1, :] = jnp.sum(product, axis=0, keepdims=True)
    out_ref[: 2 * poles, :] = (first_ref[...] + sums).astype(BF16)
    out_ref[2 * poles :, :] = skip_ref[...].astype(BF16)


def tables_kernel(params_ref, rates_ref, lag_rates_ref, *, group, poles, inner):
    blocks, _, lag_width = lag_rates_ref.shape
    per_block = LANES // group
    step_groups = inner * per_block
    lag_wide = inner * lag_width
    pieces = split(params_ref[0], 3)
    spread = jnp.concatenate(
        [members(step_groups, 0, SUB, lag_wide), members(step_groups, 0, group, inner * LANES)], axis=1
    )
    for step in range(blocks // inner):
        spreads = mxu(pieces[:, step * step_groups : (step + 1) * step_groups], spread)
        rates = jnp.exp(join(spreads, poles))
        for j in range(inner):
            here = step * inner + j
            lag_rates_ref[here] = rates[:, j * lag_width : (j + 1) * lag_width]
            rates_ref[here] = rates[:, lag_wide + j * LANES : lag_wide + (j + 1) * LANES]


def conv_kernel(params_ref, rows_ref, skip_ref, rates_ref, lag_rates_ref, gated_ref, turned_ref, _, conv_ref,
                *, first_step, group, poles, inner):
    tokens, _ = gated_ref.shape
    per_block = LANES // group
    blocks, _, _ = rates_ref.shape
    subs = tokens // SUB
    lag_width = per_block * SUB
    first = lax.axis_index("ch") * blocks
    lead = (1 + iota((SUB, LANES), 0)).astype(F32)
    wide_group = over(within(iota((SUB, 2 * LANES), 1), LANES), group)
    state_group = over(within(iota((poles, 2 * LANES), 1), LANES), group)
    causal = iota((SUB, lag_width), 0) >= within(iota((SUB, lag_width), 1), SUB)
    lag = (SUB - 1 - within(iota((poles, lag_width), 1), SUB)).astype(F32)
    groups = blocks * per_block
    pieces = split(params_ref[1], 3).astype(F32)
    spread = members(groups, 0, SUB, inner * lag_width)

    def body(step, carry):
        start = (step + first_step) * inner
        moved = pltpu.roll(pieces, groups - start * per_block, 1).astype(BF16)
        lag_res = join(mxu(moved, spread), poles)
        lefts, lead_tables, decays, pairs, gains = [], [], [], [], []
        for j in range(inner):
            here = start + j
            table = jnp.exp(-lag_rates_ref[here] * lag)
            taps = jnp.sum(lag_res[:, j * lag_width : (j + 1) * lag_width] * table, axis=0, keepdims=True)
            taps = jnp.broadcast_to(taps, (SUB, lag_width))
            taps = pltpu.roll(taps, lag_width - SUB + 1, 1, stride=1, stride_axis=0)
            taps = jnp.where(causal, taps, 0.0).astype(BF16)
            lefts.append(jnp.concatenate([taps, table.astype(BF16)], axis=0))
            rate = rows_ref[0, pl.ds(here, 1), :]
            res = rows_ref[1, pl.ds(here, 1), :]
            lead_tables.append((res * jnp.exp(-rate * lead)).astype(BF16))
            decay = jnp.exp(-rates_ref[here] * SUB)
            decays.append(jnp.concatenate([decay, decay], axis=1))
            cut = pl.ds(pl.multiple_of(here * LANES, LANES), LANES)
            pairs.append(jnp.concatenate([gated_ref[:, cut], turned_ref[:, cut]], axis=1))
            gain = skip_ref[pl.ds(first + here, 1), :]
            gains.append(jnp.concatenate([gain, gain], axis=1))
        states = [jnp.zeros((poles, 2 * LANES), F32)] * inner
        totals = [[] for _ in range(inner)]
        for k in range(subs):
            rows = slice(k * SUB, (k + 1) * SUB)
            found = []
            for j in range(inner):
                part = pairs[j][rows]
                stack = [jnp.where(wide_group == g, part, jnp.zeros_like(part)) for g in range(per_block)]
                found.append(mxu(lefts[j], jnp.concatenate(stack, axis=0)))
            for j in range(inner):
                total = found[j][:SUB] + gains[j] * pairs[j][rows].astype(F32)
                if k:
                    held = states[j].astype(BF16)
                    stack = [jnp.where(state_group == g, held, jnp.zeros_like(held)) for g in range(per_block)]
                    total = total + mxu(lead_tables[j], jnp.concatenate(stack, axis=0))
                totals[j].append(total)
            states = [decays[j] * states[j] + found[j][SUB:] for j in range(inner)]
        for j in range(inner):
            cut = pl.ds(pl.multiple_of(2 * (step * inner + j) * LANES, LANES), 2 * LANES)
            conv_ref[:, cut] = jnp.concatenate(totals[j], axis=0)
        return carry

    lax.fori_loop(0, conv_ref.shape[1] // (2 * inner * LANES), body, 0)


def combine_kernel(*refs, level, levels, group, poles, tokens):
    last = level == levels - 1
    refs = list(refs)
    rates_ref = refs.pop(0)
    all_blocks = rates_ref.shape[0]
    blocks = all_blocks // 2
    per_block = LANES // group
    groups = all_blocks * per_block
    rows = 2 * poles
    if level == 0:
        own_ref, got_ref, sums_ref, states_ref, total_ref, near_ref = refs
    else:
        own_ref, own_tail_ref, got_ref = refs.pop(0), refs.pop(0), refs.pop(0)
        got_tail_ref = None if last else refs.pop(0)
        held_ref = refs.pop(0) if level > 1 else None
        if level == min(2, levels - 1):
            refs.pop(0)
        if last:
            near_ref, mine_ref, out_ref = refs
        else:
            states_ref, tail_ref, new_held_ref = refs[:3]
            slim_ref = refs[3] if level == levels - 2 else None
    me = lax.axis_index("ctx")
    core = lax.rem(me, 2)
    is_right = lax.rem(lax.shift_right_logical(me, level), 2) == 1
    before = lax.rem(me, 2**level) - (core if level else 0)
    gap_left = (tokens * before).astype(F32)
    gap_right = (tokens * (2**level - 2 - before)).astype(F32)
    gap = jnp.where(is_right, gap_left, gap_right)
    span = float(tokens * 2**level)
    next_right = lax.rem(lax.shift_right_logical(me, level + 1), 2) == 1

    def quarters(ref, b):
        value = ref[2 * b * rows : 2 * (b + 1) * rows].astype(F32)
        return [value[n * poles : (n + 1) * poles] for n in range(4)]

    wide_terms = []
    for b in range(blocks):
        rate = rates_ref[core * blocks + b]
        own_f, own_b, own_fm, own_bm = quarters(own_ref, b)
        if last:
            got = got_ref[b * rows : (b + 1) * rows].astype(F32)
            got_f = got_b = got[:poles]
            got_fm = got_bm = got[poles:]
        else:
            got_f, got_b, got_fm, got_bm = quarters(got_ref, b)
        left_f = jnp.where(is_right, got_f, own_f)
        left_fm = jnp.where(is_right, got_fm, own_fm)
        right_b = jnp.where(is_right, own_b, got_b)
        right_bm = jnp.where(is_right, own_bm, got_bm)
        once = jnp.exp(-rate)
        cross_res = once * (right_b * left_f)
        cross_mom = once * (right_bm * left_f + right_b * (left_fm + left_f))
        wide_terms.append(split(jnp.concatenate([cross_res, cross_mom], axis=0), 2))
        if level == 0:
            near_ref[b] = jnp.concatenate([left_f, right_b], axis=0)
        else:
            carry = jnp.exp(-rate * gap) * jnp.where(is_right, left_f, right_b)
            zero = jnp.zeros_like(carry)
            hold = jnp.concatenate([jnp.where(is_right, carry, zero), jnp.where(is_right, zero, carry)], axis=0)
            if level > 1:
                hold = hold + held_ref[b]
            if last:
                step = jnp.exp(-rate * tokens)
                near = near_ref[b]
                first_core = jnp.concatenate([hold[:poles], near[poles:] + step * hold[poles:]], axis=0)
                second_core = jnp.concatenate([near[:poles] + step * hold[:poles], hold[poles:]], axis=0)
                mine_ref[b] = jnp.where(core > 0, second_core, first_core).astype(BF16)
                out_ref[b * rows : (b + 1) * rows, :] = jnp.where(core > 0, first_core, second_core).astype(BF16)
            else:
                new_held_ref[b] = hold
        if not last:
            right_f = jnp.where(is_right, own_f, got_f)
            right_fm = jnp.where(is_right, own_fm, got_fm)
            left_b = jnp.where(is_right, got_b, own_b)
            left_bm = jnp.where(is_right, got_bm, own_bm)
            decay = jnp.exp(-rate * span)
            new_f, new_b = decay * left_f + right_f, left_b + decay * right_b
            new_fm = decay * (left_fm + span * left_f) + right_fm
            new_bm = left_bm + decay * (right_bm + span * right_b)
            here = slice(b * rows, (b + 1) * rows)
            new = jnp.concatenate([new_f, new_b, new_fm, new_bm], axis=0).astype(BF16)
            states_ref[2 * b * rows : 2 * (b + 1) * rows, :] = new
            if level == levels - 2 and level:
                chosen = [jnp.where(next_right, new_b, new_f), jnp.where(next_right, new_bm, new_fm)]
                slim_ref[here, :] = jnp.concatenate(chosen, axis=0).astype(BF16)
    cross = join(mxu_t(jnp.concatenate(wide_terms, axis=1), members(groups, 0, group, blocks * LANES)), rows)
    cross = jnp.where(core > 0, pltpu.roll(cross, groups // 2, 1), cross)
    tail = blocks * rows
    if level == 0:
        total_ref[...] = cross + sums_ref[...]
        return
    got_tail = got_ref[tail:, :] if last else got_tail_ref[...]
    both = own_tail_ref[...].astype(F32) + got_tail.astype(F32)
    rests = jnp.concatenate([both[:rows] + cross, both[rows:]], axis=0).astype(BF16)
    if last:
        out_ref[tail:, :] = rests
    else:
        tail_ref[...] = rests
        if slim_ref is not None:
            slim_ref[tail:, :] = rests


def merge_kernel(params_ref, own_ref, got_ref, _, out_ref, *, poles, length):
    groups = out_ref.shape[1]
    start = own_ref.shape[0] - out_ref.shape[0]
    both = own_ref[start:, :].astype(F32) + got_ref[start:, :].astype(F32)
    factor = -jnp.exp(params_ref[0]) * params_ref[1]
    scaled = [
        both[:poles] / length,
        factor * both[poles : 2 * poles] / math.sqrt(length),
        both[2 * poles :] / math.sqrt(length),
    ]
    out_ref[...] = jnp.concatenate(scaled, axis=0).astype(BF16)


def output_kernel(rows_ref, conv_ref, last_ref, mine_ref, got_ref, k_ref, v_ref, c_ref, gq_ref, gk_ref, gv_ref,
                  *, group, poles):
    tokens, width = gq_ref.shape
    per_block = LANES // group
    step = pl.program_id(0)
    steps = pl.num_programs(0)
    inner = width // LANES
    half_blocks = mine_ref.shape[0]
    core = lax.rem(lax.axis_index("ctx"), 2)
    flip = reversal(tokens)
    ahead = (1 + iota((tokens, LANES), 0)).astype(F32)
    state_group = over(within(iota((poles, 2 * LANES), 1), LANES), group)
    start = step * inner
    is_mine = over(start, half_blocks) == core
    cut = pl.ds(pl.multiple_of(start * LANES, LANES), width)

    def emit(conv_ref, base):
        totals = []
        for j in range(inner):
            here = start + j
            rate = rows_ref[0, pl.ds(here, 1), :]
            res = rows_ref[1, pl.ds(here, 1), :]
            table = (res * jnp.exp(-rate * ahead)).astype(BF16)
            place = within(here, half_blocks)
            held = jnp.where(
                is_mine, mine_ref[place], got_ref[pl.ds(pl.multiple_of(place * 2 * poles, 2 * poles), 2 * poles), :]
            )
            states = jnp.concatenate([held[:poles], held[poles:]], axis=1)
            stack = jnp.concatenate(
                [jnp.where(state_group == g, states, jnp.zeros_like(states)) for g in range(per_block)], axis=0
            )
            both = pl.ds(pl.multiple_of(2 * (here - base) * LANES, LANES), 2 * LANES)
            totals.append((conv_ref[:, both] + mxu(table, stack)).astype(BF16))
        hidden = jnp.concatenate([t[:, :LANES] for t in totals], axis=1)
        flow = mxu(flip, jnp.concatenate([t[:, LANES:] for t in totals], axis=1))
        gq_ref[...] = (c_ref[:, cut].astype(F32) * hidden.astype(F32)).astype(BF16)
        gk_ref[...] = (flow * v_ref[:, cut].astype(F32)).astype(BF16)
        gv_ref[...] = (flow * k_ref[:, cut].astype(F32)).astype(BF16)

    @pl.when(step < steps - 1)
    def _():
        emit(conv_ref, 0)

    @pl.when(step == steps - 1)
    def _():
        emit(last_ref, (steps - 1) * inner)


def assemble_kernel(*refs, poles):
    *slots, res_ref, log_ref, skip_ref = refs
    me = lax.axis_index("ch")
    groups = slots[0].shape[1]
    rows = slots[0].shape[0] - 2 * poles
    for mask, slot in enumerate(slots):
        source = lax.bitwise_xor(me, mask)
        value = slot[...].astype(F32)
        cut = pl.ds(pl.multiple_of(source * groups, LANES), groups)
        res_ref[:, cut] = value[:poles]
        log_ref[:, cut] = value[poles : 2 * poles]
        skip_ref[pl.ds(pl.multiple_of(source * rows, 8), rows), :] = value[2 * poles :]


def local(queries, key_input, value_input, cotangent, residues, log_rates, skip_gain):
    tokens, width = queries.shape
    parts = lax.axis_size("ctx")
    shards = lax.axis_size("ch")
    levels = parts.bit_length() - 1
    all_groups, poles = residues.shape
    groups = all_groups // shards
    group = width // groups
    blocks = width // LANES
    inner = 4
    steps = blocks // inner
    half_blocks = blocks // 2
    lag_width = LANES // group * SUB
    sizes = dict(group=group, poles=poles)
    half_rows, tail = half_blocks * 2 * poles, 2 * poles + blocks

    vmem = pl.BlockSpec(memory_space=pltpu.VMEM)
    anywhere = pl.BlockSpec(memory_space=pl.ANY)
    log_rates, residues = log_rates.T, residues.T
    def shape(*dims, dtype=F32):
        return jax.ShapeDtypeStruct(dims, dtype)

    def swap(value, level):
        return lax.ppermute(value, "ctx", [(i, i ^ (1 << level)) for i in range(parts)])

    far = pl.BlockSpec(memory_space=pl.ANY)
    outgoing, message, gated, dgate, turned, rows, params = pl.pallas_call(
        lambda *refs: states_kernel(*refs, inner=inner // 2, **sizes),
        in_specs=[vmem] + [far] * 4,
        out_specs=[vmem] * 7,
        out_shape=[
            shape(2 * half_rows, LANES, dtype=BF16),
            shape(2 * half_rows, LANES, dtype=BF16),
            shape(tokens, width, dtype=BF16),
            shape(tokens, width, dtype=BF16),
            shape(tokens, width, dtype=BF16),
            shape(2, blocks, LANES),
            shape(2, poles, groups),
        ],
        scratch_shapes=[pltpu.VMEM((tokens, width), BF16)] * 4
        + [pltpu.SemaphoreType.DMA((4, 2 * steps))],
        compiler_params=pltpu.CompilerParams(vmem_limit_bytes=53000 * 1024),
        name="states",
    )(jnp.stack([log_rates, residues]), queries, key_input, value_input, cotangent)

    rates, lag_rates = pl.pallas_call(
        lambda *refs: tables_kernel(*refs, inner=inner, **sizes),
        in_specs=[vmem],
        out_specs=[vmem] * 2,
        out_shape=[shape(blocks, poles, LANES), shape(blocks, poles, lag_width)],
        compiler_params=PARAMS,
        cost_estimate=pl.CostEstimate(flops=10**9, bytes_accessed=10**6, transcendentals=10**5),
        name="tables",
    )(params)

    work = pl.CostEstimate(
        flops=16 * tokens * tokens * width, bytes_accessed=12 * tokens * width, transcendentals=tokens * width
    )

    def local_sums(second, *more):
        return pl.pallas_call(
            lambda *refs: lags_kernel(*refs, second=second, inner=inner, **sizes),
            in_specs=[vmem] * (4 + len(more)),
            out_specs=vmem,
            out_shape=shape(tail, LANES, dtype=BF16) if second else shape(2 * poles, LANES),
            scratch_shapes=[pltpu.VMEM((blocks, LANES), F32)] if second else [],
            compiler_params=PARAMS,
            cost_estimate=work,
            name="lags",
        )(lag_rates, gated, dgate, turned, *more)

    def convolve(first_step, count, after):
        skip_rows = skip_gain.reshape(-1, LANES)
        return pl.pallas_call(
            lambda *refs: conv_kernel(*refs, first_step=first_step, inner=inner, **sizes),
            in_specs=[vmem] * 7 + [anywhere],
            out_specs=vmem,
            out_shape=shape(tokens, 2 * count * inner * LANES),
            compiler_params=PARAMS,
            cost_estimate=work,
            name="conv",
        )(params, rows, skip_rows, rates, lag_rates, gated, turned, after)

    def combine(level, operands, outs):
        return pl.pallas_call(
            lambda *refs: combine_kernel(*refs, level=level, levels=levels, tokens=tokens, **sizes),
            in_specs=[anywhere if x is conv else vmem for x in operands],
            out_specs=[vmem] * len(outs),
            out_shape=outs,
            compiler_params=PARAMS,
            name="combine",
        )(*operands)

    conv = None
    states_shape = shape(2 * half_rows, LANES, dtype=BF16)
    tail_shape = shape(tail, LANES, dtype=BF16)
    slim_shape = shape(half_rows + tail, LANES, dtype=BF16)
    held_shape = shape(half_blocks, 2 * poles, LANES)
    got = swap(outgoing, 0)
    states, total, near = combine(
        0, [rates, message, got, local_sums(0)], [states_shape, shape(2 * poles, LANES), held_shape]
    )
    held = slim = None
    for level in range(1, levels):
        last = level == levels - 1
        if last and slim is not None:
            received = [swap(slim, level)]
        else:
            received = [swap(states, level)]
            if level == 1:
                carried = local_sums(1, total)
            received.append(swap(carried, level))
        operands = [rates, states, carried, *received]
        if level > 1:
            operands.append(held)
        if level == min(2, levels - 1):
            conv = convolve(0, steps - 1, near if held is None else held)
            operands.append(conv)
        if last:
            outs = [shape(half_blocks, 2 * poles, LANES, dtype=BF16), slim_shape]
            mine, outgoing = combine(level, [*operands, near], outs)
        else:
            outs = [states_shape, tail_shape, held_shape]
            if level == levels - 2:
                outs.append(slim_shape)
            states, carried, held, *more = combine(level, operands, outs)
            slim = more[0] if more else None
    got = swap(outgoing, 0)
    last_conv = convolve(steps - 1, 1, outgoing)
    merged = pl.pallas_call(
        lambda *refs: merge_kernel(*refs, poles=poles, length=tokens * parts),
        in_specs=[vmem] * 3 + [anywhere],
        out_specs=vmem,
        out_shape=shape(tail, LANES, dtype=BF16),
        compiler_params=PARAMS,
        name="merge",
    )(params, outgoing, got, last_conv)

    gathered = [merged]
    for mask in range(1, shards):
        gathered.append(lax.ppermute(merged, "ch", [(i, i ^ mask) for i in range(shards)]))

    main = pl.BlockSpec((tokens, inner * LANES), lambda i: (0, i))
    grad_query, grad_key, grad_value = pl.pallas_call(
        lambda *refs: output_kernel(*refs, **sizes),
        grid=(steps,),
        in_specs=[vmem] * 8,
        out_specs=[main] * 3,
        out_shape=[shape(tokens, width, dtype=BF16)] * 3,
        compiler_params=PARAMS,
        cost_estimate=work,
        name="outputs",
    )(rows, conv, last_conv, mine, got, key_input, value_input, cotangent)

    grad_residue, grad_lograte, grad_skip = pl.pallas_call(
        lambda *refs: assemble_kernel(*refs, poles=poles),
        in_specs=[vmem] * shards,
        out_specs=[vmem] * 3,
        out_shape=[shape(poles, all_groups), shape(poles, all_groups), shape(shards * blocks, LANES)],
        compiler_params=PARAMS,
        name="assemble",
    )(*gathered)
    return (grad_query, grad_key, grad_value, grad_residue.T, grad_lograte.T, grad_skip.reshape(-1))


def solution(mesh):
    placed = (P("ctx", "ch"), P("ctx", "ch"), P("ctx", "ch"), P("ctx", "ch"), P(), P(), P())
    return jax.shard_map(
        local,
        mesh=mesh,
        in_specs=placed,
        out_specs=(P("ctx", "ch"), P("ctx", "ch"), P("ctx", "ch"), P(), P(), P()),
        check_vma=False,
    )
```
